32 devices in a mesh: sess: 2 (over x), ctx: 16 (over z, y, core).
Axes of the slice: x: 2, y: 2, z: 4, core: 2. Of those that a mesh axis runs over, the one named last changes fastest.
Arguments:
- mamba_input: bfloat16 [2, 2048, 8192], P('sess', 'ctx'), may hold values from -6 to 6
- step_size: bfloat16 [2, 2048, 64], P('sess', 'ctx'), may hold values from 0.19921875 to 1.5
- decay_log: bfloat16 [2, 2048, 64], P('sess', 'ctx'), may hold values from -0.8 to 0
- state_write: bfloat16 [2, 2048, 512], P('sess', 'ctx'), may hold values from -0.375 to 0.375
- state_read: bfloat16 [2, 2048, 512], P('sess', 'ctx'), may hold values from -0.75 to 0.75
- skip_gain: float32 [64], replicated, may hold values from 0.1 to 1.9
- saved_states: float32 [2, 3, 64, 8192], P('sess', None, 'ctx'), may hold values from -6 to 6
- home_slot: int32 [6], replicated, may hold values from 0 to 5, each once
- turn_lengths: int32 [2, 3], P('sess'), may hold values from 1 to 1024, 2048 in all within a row
- history_lengths: int32 [2, 3], P('sess'), may hold values from 4 to 1023
- queries: bfloat16 [2, 2048, 4096], P('sess', 'ctx'), may hold values from -150 to 150
- turn_keys: bfloat16 [2, 2048, 512], P('sess', 'ctx'), may hold values from -6 to 6
- turn_values: bfloat16 [2, 2048, 512], P('sess', 'ctx'), may hold values from -6 to 6
- cache_keys: bfloat16 [2, 3, 512, 512], P('sess', None, 'ctx'), may hold values from -6 to 6
- cache_values: bfloat16 [2, 3, 512, 512], P('sess', None, 'ctx'), may hold values from -6 to 6
- sink_keys: bfloat16 [2, 3, 4, 512], P('sess'), may hold values from -12 to 12
- sink_values: bfloat16 [2, 3, 4, 512], P('sess'), may hold values from -6 to 6
Outputs:
- mixed: bfloat16 [2, 2048, 8192], P('sess', 'ctx')
- attended: bfloat16 [2, 2048, 4096], P('sess', 'ctx')
The draws below stay inside these ranges and needn't reach their ends.
Inputs may be any that keep to these rules, and one draw needn't show every extreme that they name: `home_slot`: entry g * 3 + s names the stored state, in the group-major list of saved_states, from which session s of group g resumes.
All inputs are finite; a program needn't handle non-finite values.
Results may differ from the reference program's by a relative error of at most 0.004.
Values may be sent and summed in bfloat16 or wider, within the bound.
No kernel may reach another device: no remote copies, remote signals or barrier semaphores. Data moves between devices by JAX's collectives and lax.ppermute only.
A program may use at most 256 MiB of HBM per device.

```python
import math
import jax
import jax.numpy as jnp
import numpy as np
from jax import lax

TOK_DEV = 128
REACH = 4
SEQS = 3
SINKS = 4
H = 64
P_SIZE = 128
N = 64
G = 8
QH = 32
KVH = 4
HD = 128
WINDOW = 512
DIALOG_BATCHES = 2
EXCHANGE_ITEMS = 2048


def draw_decay_log(key, part):
    key_rate = jax.random.fold_in(key, 1)
    key_device = jax.random.fold_in(key, 4)
    key_rough = jax.random.fold_in(key, 5)
    lookup_outlier = jax.random.fold_in(key, 6)
    lookup_amount_total = jax.random.fold_in(key, 7)
    channel_forget_speed = jnp.exp(jax.random.uniform(key_rate, (DIALOG_BATCHES, 1, H), minval=math.log(0.05 / EXCHANGE_ITEMS), maxval=math.log(1.0 / 40.0)))
    blocks = EXCHANGE_ITEMS // TOK_DEV
    processor_scaling = jnp.exp(jax.random.uniform(key_device, (DIALOG_BATCHES, blocks, 1, H), minval=math.log(0.5), maxval=math.log(2.0)))
    processor_scaling = jnp.broadcast_to(processor_scaling, (DIALOG_BATCHES, blocks, TOK_DEV, H)).reshape(DIALOG_BATCHES, EXCHANGE_ITEMS, H)
    outer_perturbation = jax.random.uniform(key_rough, (DIALOG_BATCHES, EXCHANGE_ITEMS, H), minval=0.5, maxval=1.5)
    sudden_index_place = jax.random.randint(lookup_outlier, (DIALOG_BATCHES, 1, 2), 0, EXCHANGE_ITEMS)
    impact_markers = jnp.any(jnp.arange(EXCHANGE_ITEMS)[None, :, None] == sudden_index_place, axis=2)
    sudden_log_amplitude = jax.random.uniform(lookup_amount_total, (DIALOG_BATCHES, EXCHANGE_ITEMS, 1), minval=math.log(0.5), maxval=math.log(0.8))
    payload_elements = -channel_forget_speed * processor_scaling * outer_perturbation + jnp.where(impact_markers[:, :, None], sudden_log_amplitude, 0.0)
    return payload_elements.astype(jnp.bfloat16)


def key_base(key):
    return jnp.clip(jax.random.normal(jax.random.fold_in(key, 11), (DIALOG_BATCHES, EXCHANGE_ITEMS, KVH * HD)), -5.0, 5.0)


def draw_turn_keys(key, part):
    keys_drawn = key_base(key)
    return keys_drawn.astype(jnp.bfloat16)


def draw_queries(key, part):
    drawn = jnp.clip(jax.random.normal(jax.random.fold_in(key, 13), (DIALOG_BATCHES, EXCHANGE_ITEMS, QH * HD)), -5.0, 5.0)
    return drawn.astype(jnp.bfloat16)


def with_ends(values, own_key, least, largest):
    longest = values.shape.index(max(values.shape))
    spots = []
    for shift in (0, 1):
        where = [jax.random.randint(jax.random.fold_in(own_key, axis), (), 0, length) for axis, length in enumerate(values.shape)]
        where[longest] = (where[longest] + shift) % values.shape[longest]
        spots.append(tuple(where))
    return values.at[spots[0]].set(least).at[spots[1]].set(largest)


def block_levels(own_key, extent, cuts, low, top_value):
    def one(axis_at, blocks):
        steps = jax.random.uniform(jax.random.fold_in(jax.random.fold_in(own_key, 6), axis_at), (blocks,), jnp.float32, low / len(cuts), top_value / len(cuts))
        return jnp.repeat(jnp.exp(steps), extent[axis_at] // blocks).reshape((-1,) + (1,) * (len(extent) - axis_at - 1))

    gain = one(*cuts[0])
    for cut in cuts[1:]:
        gain = gain * one(*cut)
    return gain


def length_profile(amount, total, limit, slope):
    loads = [(1 << 20) // math.isqrt(grade ** slope) + 1 for grade in range(2, amount + 1)]
    spare, given = total - limit - (amount - 1), [1] * (amount - 1)
    while spare > 0:
        movable = [i for i in range(amount - 1) if given[i] < limit]
        mass, left = sum([loads[i] for i in movable]), spare
        for i in movable:
            more = min(limit - given[i], max(1, left * loads[i] // mass), spare)
            given[i] = given[i] + more
            spare = spare - more
    return np.array([limit] + given)


def ragged_sizes(key, amount, total, reach, slope):
    if amount == 2:
        one = jax.random.randint(key, (), max(1, total - reach), min(reach, total - 1) + 1)
        return jnp.stack([one, total - one])
    sizes = jnp.asarray(length_profile(amount, total, reach, slope), jnp.int32)
    twos = (amount - 1) // 2
    donor, receiver = sizes[1:1 + 2 * twos:2], sizes[2:2 + 2 * twos:2]
    margin = jnp.minimum(donor - 1, reach - receiver)
    passed = jax.random.randint(jax.random.fold_in(key, 1), (twos,), 0, 1 << 20) % (margin + 1)
    sizes = sizes.at[1:1 + 2 * twos:2].set(donor - passed).at[2:2 + 2 * twos:2].set(receiver + passed)
    return sizes[jax.random.permutation(jax.random.fold_in(key, 2), amount)]


def gaussian(key, shape, spread, reach, cuts=(), held_as=jnp.bfloat16):
    loudness = block_levels(key, shape, cuts, -0.22, 0.18) if cuts else 1.0
    array = jax.random.normal(key, shape, jnp.float32) * spread * loudness
    return jnp.minimum(jnp.maximum(array, -reach), reach).astype(held_as)


def setup_inputs(seed: int = 0) -> dict:
    splits = jax.random.split(jax.random.key(seed), 18)
    mamba_input = gaussian(splits[0], (DIALOG_BATCHES, EXCHANGE_ITEMS, H * P_SIZE), 1.0, 6.0, ((0, 2), (1, 16)))
    step_size = jnp.clip(0.19921875 + 1.3007812 * jax.random.uniform(splits[1], (DIALOG_BATCHES, EXCHANGE_ITEMS, H), jnp.float32) ** block_levels(splits[1], (DIALOG_BATCHES, EXCHANGE_ITEMS, H), ((0, 2), (1, 16)), -0.2, 0.2), 0.19921875, 1.5).astype(jnp.bfloat16)
    decay_log = draw_decay_log(jax.random.fold_in(splits[17], 71), 0)
    state_write = gaussian(splits[3], (DIALOG_BATCHES, EXCHANGE_ITEMS, G * N), 256 ** -0.5, 0.375, ((0, 2), (1, 16)))
    state_read = gaussian(splits[4], (DIALOG_BATCHES, EXCHANGE_ITEMS, G * N), N ** -0.5, 0.75, ((0, 2), (1, 16)))
    skip_gain = jnp.clip(1.0 + 0.18 * jax.random.normal(splits[5], (H,), jnp.float32), 0.1, 1.9)
    saved_states = gaussian(splits[6], (DIALOG_BATCHES, SEQS, H, P_SIZE * N), 1.0, 6.0, ((0, 2), (2, 16)), jnp.float32)
    home_slot = jax.random.permutation(splits[7], DIALOG_BATCHES * SEQS).astype(jnp.int32)
    turn_lengths = jax.vmap(lambda own: ragged_sizes(own, SEQS, EXCHANGE_ITEMS, EXCHANGE_ITEMS // 2, 1))(jax.random.split(splits[8], DIALOG_BATCHES)).reshape((DIALOG_BATCHES, SEQS)).astype(jnp.int32)
    history_lengths = with_ends(jax.random.randint(splits[9], (DIALOG_BATCHES, SEQS), SINKS, 2 * WINDOW), jax.random.fold_in(splits[9], 1), SINKS, (2 * WINDOW) - 1).astype(jnp.int32)
    queries = draw_queries(jax.random.fold_in(splits[17], 71), 0)
    turn_keys = draw_turn_keys(jax.random.fold_in(splits[17], 71), 0)
    turn_values = gaussian(splits[12], (DIALOG_BATCHES, EXCHANGE_ITEMS, KVH * HD), 1.0, 6.0, ((0, 2), (1, 16)))
    cache_keys = gaussian(splits[13], (DIALOG_BATCHES, SEQS, WINDOW, KVH * HD), 1.0, 6.0, ((0, 2), (2, 16)))
    cache_values = gaussian(splits[14], (DIALOG_BATCHES, SEQS, WINDOW, KVH * HD), 1.0, 6.0, ((0, 2), (2, 16)))
    sink_keys = gaussian(splits[15], (DIALOG_BATCHES, SEQS, SINKS, KVH * HD), 2.0, 12.0, ((0, 2),))
    sink_values = gaussian(splits[16], (DIALOG_BATCHES, SEQS, SINKS, KVH * HD), 1.0, 6.0, ((0, 2),))
    return {"mamba_input": mamba_input, "step_size": step_size, "decay_log": decay_log, "state_write": state_write, "state_read": state_read, "skip_gain": skip_gain, "saved_states": saved_states, "home_slot": home_slot, "turn_lengths": turn_lengths, "history_lengths": history_lengths, "queries": queries, "turn_keys": turn_keys, "turn_values": turn_values, "cache_keys": cache_keys, "cache_values": cache_values, "sink_keys": sink_keys, "sink_values": sink_values}


precise = lax.Precision.HIGHEST

def session_starts(lengths):
    ends = jnp.cumsum(lengths).astype(jnp.int32)
    return jnp.concatenate([jnp.zeros((1,), jnp.int32), ends[:-1]])

def session_of(positions, starts):
    later = positions[:, None] >= starts[None, 1:]
    return lax.optimization_barrier(jnp.sum(later.astype(jnp.int32), axis=1)).astype(jnp.int32)

def stretch_terms(inputs, step_sizes, log_rates, writes, read_rows, segment, relative, states):
    stretch_len = inputs.shape[0]
    sessions = states.shape[0]
    positions = jnp.arange(stretch_len, dtype=jnp.int32)
    log_rate = jnp.transpose(log_rates.astype(jnp.float32), (1, 2, 0))
    running = jnp.cumsum(log_rate, axis=2)
    before = running - log_rate
    causal = (segment[:, None] == segment[None, :]) & (positions[:, None] >= positions[None, :])
    differences = running[:, :, :, None] - running[:, :, None, :]
    decays = jnp.exp(jnp.where(causal, differences, -jnp.inf))
    intersection = jnp.einsum('tgn,sgn->gts', read_rows.astype(jnp.float32), writes.astype(jnp.float32), precision=precise)
    step_scale = jnp.transpose(step_sizes.astype(jnp.float32), (1, 2, 0))
    mixing = (intersection[:, None] * decays * step_scale[:, :, None, :]).astype(jnp.bfloat16)
    mixing = lax.optimization_barrier(mixing)
    intra_part = jnp.einsum('gkts,sgkp->tgkp', mixing.astype(jnp.float32), inputs.astype(jnp.float32), precision=precise)
    session_ids = jnp.arange(sessions, dtype=jnp.int32)
    inside = (relative >= 0) & (relative < stretch_len)
    at_start = positions[None, :] == relative[:, None]
    base_log = lax.optimization_barrier(jnp.sum(jnp.where(at_start[None, None], before[:, :, None, :], 0.0), axis=3))
    owned = segment[:, None] == session_ids[None, :]
    starts_here = owned & inside[None, :]
    exponent = running[:, :, None, :] - base_log[:, :, :, None]
    from_saved = jnp.exp(jnp.where(jnp.transpose(starts_here)[None, None], exponent, -jnp.inf))
    read_float = read_rows.astype(jnp.float32)
    readout = jnp.einsum('tgn,sgkpn->sgktp', read_float, states, precision=precise)
    intra_part = intra_part + jnp.einsum('gkst,sgktp->tgkp', from_saved, readout, precision=precise)
    earlier = jnp.any(owned & (relative[None, :] < 0), axis=1)
    from_incoming = jnp.where(earlier[None, None, :], jnp.exp(running), 0.0)
    last_session = segment[stretch_len - 1]
    tail_decay = jnp.exp(jnp.where((segment == last_session)[None, None, :], running[:, :, stretch_len - 1:] - running, -jnp.inf))
    loadings = ((tail_decay * step_scale)[:, :, :, None] * jnp.transpose(writes.astype(jnp.float32), (1, 0, 2))[:, None]).astype(jnp.bfloat16)
    loadings = lax.optimization_barrier(loadings)
    summary = jnp.einsum('sgkp,gksn->gkpn', inputs.astype(jnp.float32), loadings.astype(jnp.float32), precision=precise)
    ending = owned[stretch_len - 1] & inside
    end_decay = jnp.exp(jnp.where(ending[None, None, :], running[:, :, stretch_len - 1:] - base_log, -jnp.inf))
    summary = summary + jnp.einsum('gks,sgkpn->gkpn', end_decay, states, precision=precise)
    carry_factor = jnp.where(earlier[stretch_len - 1], jnp.exp(running[:, :, stretch_len - 1]), 0.0)
    return (intra_part, from_incoming, carry_factor, summary)

def finish(intra_part, from_incoming, read_rows, state_in, inputs, skip_gains):
    carried = jnp.einsum('tgn,gkpn->tgkp', read_rows.astype(jnp.float32), state_in, precision=precise)
    weight = jnp.transpose(from_incoming, (2, 0, 1))[..., None]
    result = intra_part + weight * carried + skip_gains[None, :, :, None] * inputs.astype(jnp.float32)
    return result.astype(jnp.bfloat16)

def mamba_group(inputs, step_sizes, log_rates, writes, read_rows, skip_gain, chosen, lengths):
    heads_per = H // G
    starts = session_starts(lengths)
    stretches = EXCHANGE_ITEMS // TOK_DEV
    tokens_in = inputs.reshape(stretches, TOK_DEV, G, heads_per, P_SIZE)
    step_view = step_sizes.reshape(stretches, TOK_DEV, G, heads_per)
    rate_view = log_rates.reshape(stretches, TOK_DEV, G, heads_per)
    write_view = writes.reshape(stretches, TOK_DEV, G, N)
    read_view = read_rows.reshape(stretches, TOK_DEV, G, N)
    gains = skip_gain.reshape(G, heads_per)
    saved = chosen.reshape(SEQS, G, heads_per, P_SIZE, N)
    offsets = jnp.arange(TOK_DEV, dtype=jnp.int32)

    def advance(state_in, pieces):
        number, stretch_x, stretch_step, stretch_rate, stretch_write, stretch_read = pieces
        first_row = number * TOK_DEV
        segment = session_of(first_row + offsets, starts)
        intra_part, incoming, carry_factor, summary = stretch_terms(stretch_x, stretch_step, stretch_rate, stretch_write, stretch_read, segment, starts - first_row, saved)
        output = finish(intra_part, incoming, stretch_read, state_in, stretch_x, gains)
        return (carry_factor[:, :, None, None] * state_in + summary, output)
    initial = jnp.zeros((G, heads_per, P_SIZE, N), jnp.float32)
    numbers = jnp.arange(stretches, dtype=jnp.int32)
    _, outputs = lax.scan(advance, initial, (numbers, tokens_in, step_view, rate_view, write_view, read_view))
    return outputs.reshape(EXCHANGE_ITEMS, H * P_SIZE)

def visible(query_pos, turn_pos, starts, history):
    sessions = starts.shape[0]
    session_ids = jnp.arange(sessions, dtype=jnp.int32)
    owner = session_of(query_pos, starts)
    in_session = owner[:, None] == session_ids[None, :]
    offset = query_pos - lax.optimization_barrier(jnp.sum(jnp.where(in_session, starts[None, :], 0), axis=1))
    sink_owner = jnp.arange(sessions * SINKS, dtype=jnp.int32) // SINKS
    sink_ok = owner[:, None] == sink_owner[None, :]
    slot_ids = jnp.arange(sessions * WINDOW, dtype=jnp.int32)
    slot_owner = slot_ids // WINDOW
    slot_place = slot_ids % WINDOW
    slot_history = lax.optimization_barrier(jnp.sum(jnp.where(slot_owner[:, None] == session_ids[None, :], history[None, :], 0), axis=1))
    cache_ok = (owner[:, None] == slot_owner[None, :]) & (slot_place[None, :] > offset[:, None]) & (slot_history - WINDOW + slot_place >= SINKS)[None, :]
    key_owner = session_of(turn_pos, starts)
    distance = query_pos[:, None] - turn_pos[None, :]
    turn_ok = (turn_pos[None, :] >= 0) & (key_owner[None, :] == owner[:, None]) & (distance >= 0) & (distance < WINDOW)
    return jnp.concatenate([sink_ok, cache_ok, turn_ok], axis=1)

def attend(queries, keys, payload_elements, valid):
    row_count = queries.shape[0]
    per_group = QH // KVH
    factor = 1.0 / math.sqrt(HD)

    def one_head(number):
        query_h = lax.dynamic_slice_in_dim(queries, number * per_group * HD, per_group * HD, 1).reshape(row_count, per_group, HD)
        key_h = lax.dynamic_slice_in_dim(keys, number * HD, HD, 1)
        value_h = lax.dynamic_slice_in_dim(payload_elements, number * HD, HD, 1)
        scores = jnp.einsum('tgd,nd->gtn', query_h.astype(jnp.float32), key_h.astype(jnp.float32), precision=precise) * factor
        scores = jnp.where(valid[None], scores, -jnp.inf)
        row_max = lax.optimization_barrier(jnp.max(scores, axis=2, keepdims=True))
        weights = jnp.exp(scores - row_max)
        denominator = lax.optimization_barrier(jnp.sum(weights, axis=2))
        rounded = lax.optimization_barrier(weights.astype(jnp.bfloat16))
        mixed = jnp.einsum('gtn,nd->tgd', rounded.astype(jnp.float32), value_h.astype(jnp.float32), precision=precise)
        return mixed / jnp.transpose(denominator)[:, :, None]
    outputs = lax.map(one_head, jnp.arange(KVH, dtype=jnp.int32))
    return jnp.transpose(outputs, (1, 0, 2, 3)).reshape(row_count, QH * HD).astype(jnp.bfloat16)

def attention_group(queries, keys, payload_elements, cache_k, cache_v, sink_k, sink_v, lengths, history):
    starts = session_starts(lengths)
    features = KVH * HD
    reach_rows = REACH * TOK_DEV
    padding = jnp.zeros((reach_rows, features), jnp.bfloat16)
    keys_padded = jnp.concatenate([padding, keys], axis=0)
    values_padded = jnp.concatenate([padding, payload_elements], axis=0)
    fixed_keys = jnp.concatenate([sink_k.reshape(SEQS * SINKS, features), cache_k.reshape(SEQS * WINDOW, features)], axis=0)
    fixed_values = jnp.concatenate([sink_v.reshape(SEQS * SINKS, features), cache_v.reshape(SEQS * WINDOW, features)], axis=0)
    offsets = jnp.arange(TOK_DEV, dtype=jnp.int32)
    band_ids = jnp.arange(reach_rows + TOK_DEV, dtype=jnp.int32)

    def one_block(number):
        first_row = number * TOK_DEV
        query_rows = lax.dynamic_slice_in_dim(queries, first_row, TOK_DEV, 0)
        key_rows = lax.dynamic_slice_in_dim(keys_padded, first_row, reach_rows + TOK_DEV, 0)
        value_rows = lax.dynamic_slice_in_dim(values_padded, first_row, reach_rows + TOK_DEV, 0)
        valid = visible(first_row + offsets, first_row - reach_rows + band_ids, starts, history)
        return attend(query_rows, jnp.concatenate([fixed_keys, key_rows], axis=0), jnp.concatenate([fixed_values, value_rows], axis=0), valid)
    outputs = lax.map(one_block, jnp.arange(EXCHANGE_ITEMS // TOK_DEV, dtype=jnp.int32))
    return outputs.reshape(EXCHANGE_ITEMS, QH * HD)

def reference(mamba_input, step_size, decay_log, state_write, state_read, skip_gain, saved_states, home_slot, turn_lengths, history_lengths, queries, turn_keys, turn_values, cache_keys, cache_values, sink_keys, sink_values):
    stored = saved_states.reshape(DIALOG_BATCHES * SEQS, H, P_SIZE, N)
    homes = home_slot.reshape(DIALOG_BATCHES, SEQS)

    def mamba_one(group_id):
        chosen = jnp.take(stored, homes[group_id], axis=0)
        return mamba_group(mamba_input[group_id], step_size[group_id], decay_log[group_id], state_write[group_id], state_read[group_id], skip_gain, chosen, turn_lengths[group_id])

    def attention_one(group_id):
        return attention_group(queries[group_id], turn_keys[group_id], turn_values[group_id], cache_keys[group_id], cache_values[group_id], sink_keys[group_id], sink_values[group_id], turn_lengths[group_id], history_lengths[group_id])
    group_ids = jnp.arange(DIALOG_BATCHES, dtype=jnp.int32)
    mixed = lax.map(mamba_one, group_ids)
    attended = lax.map(attention_one, group_ids)
    return (mixed, attended)
```

```python
import functools
import math

import jax
import jax.numpy as jnp
from jax import lax
from jax.experimental import pallas as pl
from jax.experimental.pallas import tpu as pltpu
from jax.sharding import PartitionSpec as P

REACH = 4
SEQS = 3
SINKS = 4
H = 64
P_SIZE = 128
N = 64
G = 8
QH = 32
KVH = 4
HD = 128
WINDOW = 512
TOK = 128

HEADS_PER = H // G
PAIR = 2 * HEADS_PER
STEPS = H // PAIR
EXTRA = 16
BLOCK = 64
SPAN = WINDOW + BLOCK
COLUMNS = SPAN + 64
NEG = -1e30


def session_at(position, meta):
    return (position >= meta[1]).astype(jnp.int32) + (position >= meta[2]).astype(jnp.int32)


def start_of(session, meta):
    return jnp.where(session == 0, 0, jnp.where(session == 1, meta[1], meta[2]))


def last_start(meta):
    first = meta[0] * TOK
    return jnp.maximum(start_of(session_at(first + TOK - 1, meta), meta) - first, 0)


def params(mib=48):
    return pltpu.CompilerParams(vmem_limit_bytes=mib * 1024 * 1024)


def running_rows(dl_ref, step_ref):
    both = jnp.concatenate([dl_ref[...], step_ref[...]], axis=1).astype(jnp.float32).T
    rates, steps = both[:H], both[H:]
    k = lax.broadcasted_iota(jnp.int32, (TOK, TOK), 0)
    u = lax.broadcasted_iota(jnp.int32, (TOK, TOK), 1)
    upto = (k <= u).astype(jnp.bfloat16)
    running = jnp.dot(rates.astype(jnp.bfloat16), upto, preferred_element_type=jnp.float32)
    return rates, running, steps


def summary_kernel(local, meta, x_ref, dl_ref, step_ref, write_ref, out_ref, coef_s, factor_s, write_s):
    step = pl.program_id(0)

    @pl.when(step == 0)
    def _():
        rates, running, steps = running_rows(dl_ref, step_ref)
        r = last_start(meta)
        lane = lax.broadcasted_iota(jnp.int32, (H, TOK), 1)
        last = running[:, TOK - 1 :]
        base = jnp.sum(jnp.where(lane < r, rates, 0.0), axis=1, keepdims=True)
        coef_s[...] = jnp.where(lane >= r, jnp.exp(last - running) * steps, 0.0)
        factor_s[...] = jnp.broadcast_to(jnp.exp(last - base), (H, TOK))
        write_s[...] = write_ref[...].astype(jnp.float32).T

    coef = coef_s[pl.ds(pl.multiple_of(step * PAIR, PAIR), PAIR), :]
    factor = factor_s[pl.ds(pl.multiple_of(step * PAIR, PAIR), PAIR), :]
    writes = write_s[pl.ds(pl.multiple_of(step * 2 * N, 2 * N), 2 * N), :]
    for k in range(PAIR):
        group = k // HEADS_PER
        loading = (writes[group * N : (group + 1) * N] * coef[k : k + 1]).astype(jnp.bfloat16)
        summary = jnp.dot(
            loading, x_ref[:, k * P_SIZE : (k + 1) * P_SIZE], preferred_element_type=jnp.float32
        )
        place = (k % local) * N
        out_ref[k // local, place : place + N, :] = summary.astype(jnp.bfloat16)
    for j in range(PAIR // local):
        rows = factor[j * local : (j + 1) * local]
        high = rows.astype(jnp.bfloat16).astype(jnp.float32)
        parts = [high, rows - high]
        if EXTRA > 2 * local:
            parts.append(jnp.zeros((EXTRA - 2 * local, TOK), jnp.float32))
        out_ref[j, local * N :, :] = jnp.concatenate(parts, axis=0).astype(jnp.bfloat16)


def summaries(meta, x, rates, steps, writes, local):
    owners = H // local
    rows = local * N + EXTRA
    return pl.pallas_call(
        functools.partial(summary_kernel, local),
        out_shape=jax.ShapeDtypeStruct((owners, rows, P_SIZE), jnp.bfloat16),
        grid_spec=pltpu.PrefetchScalarGridSpec(
            num_scalar_prefetch=1,
            grid=(STEPS,),
            in_specs=[
                pl.BlockSpec((TOK, PAIR * P_SIZE), lambda i, m: (0, i)),
                pl.BlockSpec((TOK, H), lambda i, m: (0, 0)),
                pl.BlockSpec((TOK, H), lambda i, m: (0, 0)),
                pl.BlockSpec((TOK, G * N), lambda i, m: (0, 0)),
            ],
            out_specs=pl.BlockSpec((PAIR // local, rows, P_SIZE), lambda i, m: (i, 0, 0)),
            scratch_shapes=[
                pltpu.VMEM((H, TOK), jnp.float32),
                pltpu.VMEM((H, TOK), jnp.float32),
                pltpu.VMEM((G * N, TOK), jnp.float32),
            ],
        ),
        compiler_params=params(),
        cost_estimate=pl.CostEstimate(flops=2 * H * TOK * N * P_SIZE, bytes_accessed=3 << 20, transcendentals=0),
        name="summaries",
    )(meta, x, rates, steps, writes)


def intra_kernel(meta, skip, x_ref, dl_ref, step_ref, write_ref, read_ref, out_ref, run_s, step_s):
    step = pl.program_id(0)

    @pl.when(step == 0)
    def _():
        _, running, steps = running_rows(dl_ref, step_ref)
        run_s[...] = running
        step_s[...] = steps

    heads = pl.ds(pl.multiple_of(step * PAIR, PAIR), PAIR)
    running = run_s[heads, :]
    sizes = step_s[heads, :]
    columns = running.T
    r = last_start(meta)
    t = lax.broadcasted_iota(jnp.int32, (TOK, TOK), 0)
    u = lax.broadcasted_iota(jnp.int32, (TOK, TOK), 1)
    causal = (u <= t) & ((u >= r) | (t < r))
    for group in range(2):
        part = slice(group * N, (group + 1) * N)
        products = lax.dot_general(
            read_ref[:, part], write_ref[:, part], (((1,), (1,)), ((), ())),
            preferred_element_type=jnp.float32,
        )
        products = jnp.where(causal, products, 0.0)
        for k in range(group * HEADS_PER, (group + 1) * HEADS_PER):
            difference = columns[:, k : k + 1] - running[k : k + 1]
            decay = jnp.exp(jnp.minimum(difference, 0.0))
            mixing = (products * decay * sizes[k : k + 1]).astype(jnp.bfloat16)
            place = slice(k * P_SIZE, (k + 1) * P_SIZE)
            x = x_ref[:, place]
            mixed = jnp.dot(mixing, x, preferred_element_type=jnp.float32)
            out_ref[:, place] = mixed + skip[step * PAIR + k] * x.astype(jnp.float32)


def intra(meta, skip, x, rates, steps, writes, reads):
    return pl.pallas_call(
        intra_kernel,
        out_shape=jax.ShapeDtypeStruct((TOK, H * P_SIZE), jnp.float32),
        grid_spec=pltpu.PrefetchScalarGridSpec(
            num_scalar_prefetch=2,
            grid=(STEPS,),
            in_specs=[
                pl.BlockSpec((TOK, PAIR * P_SIZE), lambda i, m, s: (0, i)),
                pl.BlockSpec((TOK, H), lambda i, m, s: (0, 0)),
                pl.BlockSpec((TOK, H), lambda i, m, s: (0, 0)),
                pl.BlockSpec((TOK, 2 * N), lambda i, m, s: (0, i)),
                pl.BlockSpec((TOK, 2 * N), lambda i, m, s: (0, i)),
            ],
            out_specs=pl.BlockSpec((TOK, PAIR * P_SIZE), lambda i, m, s: (0, i)),
            scratch_shapes=[
                pltpu.VMEM((H, TOK), jnp.float32),
                pltpu.VMEM((H, TOK), jnp.float32),
            ],
        ),
        compiler_params=params(),
        cost_estimate=pl.CostEstimate(
            flops=8 * H * TOK * TOK * P_SIZE, bytes_accessed=7 << 20, transcendentals=H * TOK * TOK
        ),
        name="intra",
    )(meta, skip, x, rates, steps, writes, reads)


def recurrence_kernel(local, meta, got_ref, restored_ref, out_ref):
    width = local * N
    state = [jnp.zeros((N, P_SIZE), jnp.float32) for _ in range(local)]
    for c in range(got_ref.shape[0]):
        first = c * TOK
        opening = session_at(first, meta)
        closing = session_at(first + TOK - 1, meta)
        opens = start_of(opening, meta) >= first
        closes = start_of(closing, meta) >= first
        for k in range(local):
            rows = slice(k * N, (k + 1) * N)
            entering = jnp.where(opens, restored_ref[opening, rows, :], state[k])
            out_ref[c, rows, :] = entering.astype(jnp.bfloat16)
            source = jnp.where(closes, restored_ref[closing, rows, :], state[k])
            factor = got_ref[c, width : width + EXTRA, :].astype(jnp.float32)
            decay = factor[k : k + 1] + factor[local + k : local + k + 1]
            state[k] = decay * source + got_ref[c, rows, :].astype(jnp.float32)


def recurrence(meta, got, restored, local):
    owners = got.shape[0]
    return pl.pallas_call(
        functools.partial(recurrence_kernel, local),
        out_shape=jax.ShapeDtypeStruct((owners, local * N, P_SIZE), jnp.bfloat16),
        grid_spec=pltpu.PrefetchScalarGridSpec(
            num_scalar_prefetch=1,
            grid=(1,),
            in_specs=[
                pl.BlockSpec(got.shape, lambda i, m: (0, 0, 0)),
                pl.BlockSpec(restored.shape, lambda i, m: (0, 0, 0)),
            ],
            out_specs=pl.BlockSpec((owners, local * N, P_SIZE), lambda i, m: (0, 0, 0)),
        ),
        compiler_params=params(),
        cost_estimate=pl.CostEstimate(flops=1 << 21, bytes_accessed=3 << 20, transcendentals=0),
        name="recurrence",
    )(meta, got, restored)


def finish_kernel(local, meta, part_ref, dl_ref, step_ref, read_ref, a_ref, b_ref, out_ref, factor_s):
    step = pl.program_id(0)
    r = last_start(meta)

    @pl.when(step == 0)
    def _():
        rates, running, _ = running_rows(dl_ref, step_ref)
        lane = lax.broadcasted_iota(jnp.int32, (H, TOK), 1)
        base = jnp.sum(jnp.where(lane < r, rates, 0.0), axis=1, keepdims=True)
        factor_s[...] = jnp.exp(jnp.minimum(running - jnp.where(lane >= r, base, 0.0), 0.0))

    factor = factor_s[pl.ds(pl.multiple_of(step * PAIR, PAIR), PAIR), :].T
    token = lax.broadcasted_iota(jnp.int32, (TOK, N), 0)
    resumed = (token >= r) & (r > 0)
    for group in range(2):
        reads = read_ref[:, group * N : (group + 1) * N].astype(jnp.float32)
        left = jnp.where(resumed, 0.0, reads)
        right = jnp.where(resumed, reads, 0.0)
        reads = jnp.concatenate([left, right], axis=1).astype(jnp.bfloat16)
        for k in range(group * HEADS_PER, (group + 1) * HEADS_PER):
            rows = slice((k % local) * N, (k % local + 1) * N)
            states = jnp.concatenate([a_ref[k // local, rows, :], b_ref[k // local, 0, rows, :]], axis=0)
            carried = jnp.dot(reads, states, preferred_element_type=jnp.float32)
            place = slice(k * P_SIZE, (k + 1) * P_SIZE)
            out_ref[:, place] = (part_ref[:, place] + factor[:, k : k + 1] * carried).astype(jnp.bfloat16)


def finish(meta, part, rates, steps, reads, entering, resumed, local):
    owners = PAIR // local

    def resumed_index(i, m):
        return (i, jnp.maximum(session_at(m[0] * TOK + TOK - 1, m) - 1, 0), 0, 0)

    return pl.pallas_call(
        functools.partial(finish_kernel, local),
        out_shape=jax.ShapeDtypeStruct((TOK, H * P_SIZE), jnp.bfloat16),
        grid_spec=pltpu.PrefetchScalarGridSpec(
            num_scalar_prefetch=1,
            grid=(STEPS,),
            in_specs=[
                pl.BlockSpec((TOK, PAIR * P_SIZE), lambda i, m: (0, i)),
                pl.BlockSpec((TOK, H), lambda i, m: (0, 0)),
                pl.BlockSpec((TOK, H), lambda i, m: (0, 0)),
                pl.BlockSpec((TOK, 2 * N), lambda i, m: (0, i)),
                pl.BlockSpec((owners, local * N, P_SIZE), lambda i, m: (i, 0, 0)),
                pl.BlockSpec((owners, 1, local * N, P_SIZE), resumed_index),
            ],
            out_specs=pl.BlockSpec((TOK, PAIR * P_SIZE), lambda i, m: (0, i)),
            scratch_shapes=[pltpu.VMEM((H, TOK), jnp.float32)],
        ),
        compiler_params=params(),
        cost_estimate=pl.CostEstimate(
            flops=2 * H * TOK * TOK * P_SIZE, bytes_accessed=9 << 20, transcendentals=H * TOK
        ),
        name="finish",
    )(meta, part, rates, steps, reads, entering, resumed)


def attend_kernel(
    meta, q_ref, band4, band3, band2, band1, band0, ka_ref, va_ref, kb_ref, vb_ref, sk_ref, sv_ref,
    out_ref, key_s, value_s,
):
    factor = 1.0 / math.sqrt(HD)
    first = meta[0] * TOK
    r = last_start(meta)
    opening = session_at(first, meta)
    closing = session_at(first + TOK - 1, meta)
    bands = (band4, band3, band2, band1, band0)
    length = (REACH + 1) * TOK

    def one_session(session, hk_ref, hv_ref, resuming, needed):
        start = start_of(session, meta) - first + WINDOW
        oldest = start - WINDOW + jnp.maximum(SINKS + WINDOW - meta[3 + session], 0)

        @pl.when(needed & (start > 0))
        def _():
            row = lax.broadcasted_iota(jnp.int32, (length, WINDOW), 0)
            place = lax.broadcasted_iota(jnp.int32, (length, WINDOW), 1)
            moved = (place == row - start + WINDOW).astype(jnp.bfloat16)
            keys = hk_ref[:, 0, 0].reshape(WINDOW, HD)
            values = hv_ref[:, 0, 0].reshape(WINDOW, HD)
            history = jnp.dot(
                moved, jnp.concatenate([keys, values], axis=1), preferred_element_type=jnp.float32
            )
            for i, band in enumerate(bands):
                rows = slice(i * TOK, (i + 1) * TOK)
                index = lax.broadcasted_iota(jnp.int32, (TOK, HD), 0) + i * TOK
                turn = index >= start
                key_s[rows, :] = jnp.where(
                    turn, band[0].astype(jnp.float32), history[rows, :HD]
                ).astype(jnp.bfloat16)
                value_s[rows, :] = jnp.where(
                    turn, band[1].astype(jnp.float32), history[rows, HD:]
                ).astype(jnp.bfloat16)

        @pl.when(needed & (start <= 0))
        def _():
            for i, band in enumerate(bands):
                rows = slice(i * TOK, (i + 1) * TOK)
                key_s[rows, :] = band[0]
                value_s[rows, :] = band[1]

        for b in range(TOK // BLOCK):
            inside = (b * BLOCK + BLOCK > r) if resuming else (b * BLOCK < r)

            @pl.when(needed & inside)
            def _():
                rows = slice(b * BLOCK, b * BLOCK + SPAN)
                keys = jnp.concatenate([key_s[rows, :], sk_ref[session]], axis=0)
                values = jnp.concatenate([value_s[rows, :], sv_ref[session]], axis=0)
                tokens = slice(b * BLOCK, (b + 1) * BLOCK)
                queries = jnp.concatenate(
                    [q_ref[tokens, g * HD : (g + 1) * HD] for g in range(QH // KVH)], axis=0
                )
                scores = lax.dot_general(
                    queries, keys, (((1,), (1,)), ((), ())), preferred_element_type=jnp.float32
                )
                token = lax.broadcasted_iota(jnp.int32, (BLOCK, COLUMNS), 0)
                column = lax.broadcasted_iota(jnp.int32, (BLOCK, COLUMNS), 1)
                seen = (column > token) & (column <= token + WINDOW) & (column >= oldest - b * BLOCK)
                seen = (seen & (column < SPAN)) | ((column >= SPAN) & (column < SPAN + SINKS))
                bias = jnp.where(seen, 0.0, NEG)
                weights, sums = [], []
                for g in range(QH // KVH):
                    score = scores[g * BLOCK : (g + 1) * BLOCK] * factor + bias
                    weight = jnp.exp(score - jnp.max(score, axis=1, keepdims=True))
                    sums.append(jnp.sum(weight, axis=1, keepdims=True))
                    weights.append(weight.astype(jnp.bfloat16))
                mixed = jnp.dot(
                    jnp.concatenate(weights, axis=0), values, preferred_element_type=jnp.float32
                )
                for g in range(QH // KVH):
                    result = mixed[g * BLOCK : (g + 1) * BLOCK] / sums[g]
                    lanes = slice(g * HD, (g + 1) * HD)
                    if resuming:
                        index = lax.broadcasted_iota(jnp.int32, (BLOCK, HD), 0) + b * BLOCK
                        before = out_ref[tokens, lanes].astype(jnp.float32)
                        result = jnp.where(index >= r, result, before)
                    out_ref[tokens, lanes] = result.astype(jnp.bfloat16)

    one_session(opening, ka_ref, va_ref, False, r > 0)
    one_session(closing, kb_ref, vb_ref, True, r >= 0)


def attend(meta, queries, bands, history, sink_keys, sink_values):
    owners, _, _, rows, _ = history.shape
    lanes = QH // KVH * HD

    def history_spec(which, last):
        def index(j, m):
            return (0, which, session_at(m[0] * TOK + (TOK - 1 if last else 0), m), 0, j)

        return pl.BlockSpec((owners, 1, 1, rows, HD), index)

    pad = SEQS, COLUMNS - SPAN, HD
    return pl.pallas_call(
        attend_kernel,
        out_shape=jax.ShapeDtypeStruct((TOK, QH * HD), jnp.bfloat16),
        grid_spec=pltpu.PrefetchScalarGridSpec(
            num_scalar_prefetch=1,
            grid=(KVH,),
            in_specs=[pl.BlockSpec((TOK, lanes), lambda j, m: (0, j))]
            + [pl.BlockSpec((2, TOK, HD), lambda j, m: (0, 0, j))] * (REACH + 1)
            + [history_spec(0, False), history_spec(1, False), history_spec(0, True), history_spec(1, True)]
            + [pl.BlockSpec(pad, lambda j, m: (0, 0, j))] * 2,
            out_specs=pl.BlockSpec((TOK, lanes), lambda j, m: (0, j)),
            scratch_shapes=[
                pltpu.VMEM(((REACH + 1) * TOK, HD), jnp.bfloat16),
                pltpu.VMEM(((REACH + 1) * TOK, HD), jnp.bfloat16),
            ],
        ),
        compiler_params=params(),
        cost_estimate=pl.CostEstimate(
            flops=16 * TOK * QH * COLUMNS * HD, bytes_accessed=8 << 20,
            transcendentals=2 * TOK * QH * COLUMNS,
        ),
        name="attend",
    )(meta, queries, *bands, history, history, history, history, sink_keys, sink_values)


def shifted(block, axis, distance):
    devices = range(lax.axis_size(axis))
    return lax.ppermute(block, axis, [(i - distance, i) for i in devices if i - distance in devices])


def shards(
    mamba_input,
    step_size,
    decay_log,
    state_write,
    state_read,
    skip_gain,
    saved_states,
    home_slot,
    turn_lengths,
    history_lengths,
    queries,
    turn_keys,
    turn_values,
    cache_keys,
    cache_values,
    sink_keys,
    sink_values,
):
    place = lax.axis_index("ctx")
    group = lax.axis_index("sess")
    groups = lax.axis_size("sess")
    local = saved_states.shape[2]
    lengths = turn_lengths[0]
    meta = jnp.concatenate(
        [jnp.stack([place, lengths[0], lengths[0] + lengths[1]]), history_lengths[0]]
    ).astype(jnp.int32)
    x, rates, steps = mamba_input[0], decay_log[0], step_size[0]
    writes, reads = state_write[0], state_read[0]

    stored = [saved_states[0]]
    for j in range(1, groups):
        route = [((i + j) % groups, i) for i in range(groups)]
        stored.append(lax.ppermute(saved_states[0], "sess", route))
    stored = jnp.concatenate(stored, axis=0)
    slots = lax.dynamic_slice_in_dim(home_slot, group * SEQS, SEQS, 0)
    index = (slots // SEQS - group) % groups * SEQS + slots % SEQS
    restored = jnp.concatenate(
        [lax.dynamic_slice_in_dim(stored, index[s], 1, 0) for s in range(SEQS)], axis=0
    )
    restored = jnp.swapaxes(restored.reshape(SEQS, local, P_SIZE, N), 2, 3).reshape(SEQS, local * N, P_SIZE)

    history = lax.all_gather(jnp.stack([cache_keys[0], cache_values[0]]), "ctx", axis=0)
    key_value = jnp.stack([turn_keys[0], turn_values[0]])
    bands = [shifted(key_value, "ctx", k) for k in range(REACH, 0, -1)] + [key_value]

    sent = summaries(meta, x, rates, steps, writes, local)
    got = lax.all_to_all(sent, "ctx", 0, 0, tiled=True)
    resumed = lax.all_gather(restored[1:].astype(jnp.bfloat16), "ctx", axis=0)
    part = intra(meta, skip_gain, x, rates, steps, writes, reads)
    entering = recurrence(meta, got, restored, local)
    entering = lax.all_to_all(entering, "ctx", 0, 0, tiled=True)

    sinks = [
        jnp.pad(s[0], ((0, 0), (0, COLUMNS - SPAN - SINKS), (0, 0))) for s in (sink_keys, sink_values)
    ]
    attended = attend(meta, queries[0], bands, history, *sinks)
    mixed = finish(meta, part, rates, steps, reads, entering, resumed, local)
    return mixed[None], attended[None]


def solution(mesh):
    token = P("sess", "ctx", None)
    return jax.shard_map(
        shards,
        mesh=mesh,
        in_specs=(
            token,
            token,
            token,
            token,
            token,
            P(),
            P("sess", None, "ctx", None),
            P(),
            P("sess", None),
            P("sess", None),
            token,
            token,
            token,
            P("sess", None, "ctx", None),
            P("sess", None, "ctx", None),
            P("sess", None, None, None),
            P("sess", None, None, None),
        ),
        out_specs=(token, token),
        check_vma=False,
    )
```

```python
import functools
import math

import jax
import jax.numpy as jnp
from jax import lax
from jax.experimental import pallas as pl
from jax.experimental.pallas import tpu as pltpu
from jax.sharding import PartitionSpec as P

REACH = 4
SEQS = 3
SINKS = 4
H = 64
P_SIZE = 128
N = 64
G = 8
QH = 32
KVH = 4
HD = 128
WINDOW = 512
TOK = 128

HEADS_PER = H // G
PAIR = 2 * HEADS_PER
STEPS = H // PAIR
EXTRA = 16
BLOCK = 64
SPAN = WINDOW + BLOCK
COLUMNS = SPAN + 64
NEG = -1e30


def session_at(position, meta):
    return (position >= meta[1]).astype(jnp.int32) + (position >= meta[2]).astype(jnp.int32)


def start_of(session, meta):
    return jnp.where(session == 0, 0, jnp.where(session == 1, meta[1], meta[2]))


def last_start(meta):
    first = meta[0] * TOK
    return jnp.maximum(start_of(session_at(first + TOK - 1, meta), meta) - first, 0)


def params(mib=48):
    return pltpu.CompilerParams(vmem_limit_bytes=mib * 1024 * 1024)


def running_rows(dl_ref, step_ref):
    both = jnp.concatenate([dl_ref[...], step_ref[...]], axis=1).astype(jnp.float32).T
    rates, steps = both[:H], both[H:]
    k = lax.broadcasted_iota(jnp.int32, (TOK, TOK), 0)
    u = lax.broadcasted_iota(jnp.int32, (TOK, TOK), 1)
    upto = (k <= u).astype(jnp.bfloat16)
    running = jnp.dot(rates.astype(jnp.bfloat16), upto, preferred_element_type=jnp.float32)
    return rates, running, steps


def summary_kernel(
    local, meta, x_ref, dl_ref, step_ref, write_ref, keep_ref, send_ref, coef_s, factor_s, write_s
):
    step = pl.program_id(0)

    @pl.when(step == 0)
    def _():
        rates, running, steps = running_rows(dl_ref, step_ref)
        r = last_start(meta)
        lane = lax.broadcasted_iota(jnp.int32, (H, TOK), 1)
        last = running[:, TOK - 1 :]
        base = jnp.sum(jnp.where(lane < r, rates, 0.0), axis=1, keepdims=True)
        coef_s[...] = jnp.where(lane >= r, jnp.exp(last - running) * steps, 0.0)
        factor_s[...] = jnp.broadcast_to(jnp.exp(last - base), (H, TOK))
        write_s[...] = write_ref[...].astype(jnp.float32).T

    even = meta[0] % 2 == 0
    coef = coef_s[pl.ds(pl.multiple_of(step * PAIR, PAIR), PAIR), :]
    factor = factor_s[pl.ds(pl.multiple_of(step * PAIR, PAIR), PAIR), :]
    writes = write_s[pl.ds(pl.multiple_of(step * 2 * N, 2 * N), 2 * N), :]

    def summary(k):
        group = k // HEADS_PER
        loading = (writes[group * N : (group + 1) * N] * coef[k : k + 1]).astype(jnp.bfloat16)
        return jnp.dot(
            loading, x_ref[:, k * P_SIZE : (k + 1) * P_SIZE], preferred_element_type=jnp.float32
        )

    for chip in range(PAIR // (2 * local)):
        low, high = 2 * local * chip, 2 * local * chip + local
        for k in range(local):
            first, second = summary(low + k), summary(high + k)
            rows = slice(k * N, (k + 1) * N)
            keep_ref[chip, rows, :] = jnp.where(even, first, second).astype(jnp.bfloat16)
            send_ref[chip, rows, :] = jnp.where(even, second, first).astype(jnp.bfloat16)
        first, second = factor[low : low + local], factor[high : high + local]
        keep_ref[chip, local * N :, :] = factor_rows(jnp.where(even, first, second))
        send_ref[chip, local * N :, :] = factor_rows(jnp.where(even, second, first))


def factor_rows(rows):
    high = rows.astype(jnp.bfloat16).astype(jnp.float32)
    parts = [high, rows - high]
    if EXTRA > 2 * rows.shape[0]:
        parts.append(jnp.zeros((EXTRA - 2 * rows.shape[0], TOK), jnp.float32))
    return jnp.concatenate(parts, axis=0).astype(jnp.bfloat16)


def factors_of(block, local):
    block = block.astype(jnp.float32)
    return block[:local] + block[local : 2 * local]


def summaries(meta, x, rates, steps, writes, local):
    chips = H // (2 * local)
    rows = local * N + EXTRA
    shape = jax.ShapeDtypeStruct((chips, rows, P_SIZE), jnp.bfloat16)
    spec = pl.BlockSpec((PAIR // (2 * local), rows, P_SIZE), lambda i, m: (i, 0, 0))
    return pl.pallas_call(
        functools.partial(summary_kernel, local),
        out_shape=[shape, shape],
        grid_spec=pltpu.PrefetchScalarGridSpec(
            num_scalar_prefetch=1,
            grid=(STEPS,),
            in_specs=[
                pl.BlockSpec((TOK, PAIR * P_SIZE), lambda i, m: (0, i)),
                pl.BlockSpec((TOK, H), lambda i, m: (0, 0)),
                pl.BlockSpec((TOK, H), lambda i, m: (0, 0)),
                pl.BlockSpec((TOK, G * N), lambda i, m: (0, 0)),
            ],
            out_specs=[spec, spec],
            scratch_shapes=[
                pltpu.VMEM((H, TOK), jnp.float32),
                pltpu.VMEM((H, TOK), jnp.float32),
                pltpu.VMEM((G * N, TOK), jnp.float32),
            ],
        ),
        compiler_params=params(),
        cost_estimate=pl.CostEstimate(flops=2 * H * TOK * N * P_SIZE, bytes_accessed=3 << 20, transcendentals=0),
        name="summaries",
    )(meta, x, rates, steps, writes)


def whole(kernel, name, meta, arrays, shapes, size=2):
    def spec(shape):
        return pl.BlockSpec(shape, lambda i, m: (0,) * len(shape))

    return pl.pallas_call(
        kernel,
        out_shape=[jax.ShapeDtypeStruct(s, t) for s, t in shapes],
        grid_spec=pltpu.PrefetchScalarGridSpec(
            num_scalar_prefetch=1,
            grid=(1,),
            in_specs=[spec(a.shape) for a in arrays],
            out_specs=[spec(s) for s, _ in shapes],
        ),
        compiler_params=params(),
        cost_estimate=pl.CostEstimate(flops=1 << 21, bytes_accessed=size << 20, transcendentals=0),
        name=name,
    )(meta, *arrays)


def pack_kernel(local, meta, stored_ref, keys_ref, values_ref, packed_ref, restored_ref):
    rows = keys_ref.shape[1]
    for which, ref in enumerate((keys_ref, values_ref)):
        for s in range(SEQS):
            for j in range(KVH):
                place = ((which * SEQS + s) * KVH + j) * rows
                packed_ref[place : place + rows, :] = ref[s, :, j * HD : (j + 1) * HD]
    for s in range(SEQS):
        for k in range(local):
            state = stored_ref[meta[6 + s], k].T
            restored_ref[s, k * N : (k + 1) * N, :] = state
            if s > 0:
                place = 2 * SEQS * KVH * rows + ((s - 1) * local + k) * N
                packed_ref[place : place + N, :] = state.astype(jnp.bfloat16)


def combine_kernel(local, meta, keep_ref, got_ref, out_ref):
    even = meta[0] % 2 == 0
    second = (meta[0] // 2 * 2 + 1) * TOK
    closes = start_of(session_at(second + TOK - 1, meta), meta) >= second
    width = local * N
    for chip in range(keep_ref.shape[0]):
        keep = factors_of(keep_ref[chip, width:, :], local)
        got = factors_of(got_ref[chip, width:, :], local)
        f0, f1 = jnp.where(even, keep, got), jnp.where(even, got, keep)
        out_ref[chip, width:, :] = factor_rows(jnp.where(closes, f1, f0 * f1))
        carry = jnp.where(closes, 0.0, f1)
        for k in range(local):
            rows = slice(k * N, (k + 1) * N)
            keep = keep_ref[chip, rows, :].astype(jnp.float32)
            got = got_ref[chip, rows, :].astype(jnp.float32)
            s0, s1 = jnp.where(even, keep, got), jnp.where(even, got, keep)
            out_ref[chip, rows, :] = (carry[k : k + 1] * s0 + s1).astype(jnp.bfloat16)


def recurrence_kernel(local, meta, got_ref, restored_ref, out_ref):
    width = local * N
    span = 2 * TOK
    state = [jnp.zeros((N, P_SIZE), jnp.float32) for _ in range(local)]
    for c in range(got_ref.shape[0]):
        first = c * span
        opening = session_at(first, meta)
        closing = session_at(first + span - 1, meta)
        opens = start_of(opening, meta) >= first
        closes = start_of(closing, meta) >= first
        factor = factors_of(got_ref[c, width:, :], local)
        for k in range(local):
            rows = slice(k * N, (k + 1) * N)
            entering = jnp.where(opens, restored_ref[opening, rows, :], state[k])
            out_ref[c, rows, :] = entering.astype(jnp.bfloat16)
            source = jnp.where(closes, restored_ref[closing, rows, :], state[k])
            state[k] = factor[k : k + 1] * source + got_ref[c, rows, :].astype(jnp.float32)


def middle_kernel(local, meta, entering_ref, keep_ref, got_ref, resumed_ref, own_ref, send_ref):
    even = meta[0] % 2 == 0
    first = meta[0] // 2 * 2 * TOK
    second = first + TOK
    closing = session_at(second - 1, meta)
    opening = session_at(second, meta)
    closes = start_of(closing, meta) > first
    opens = start_of(opening, meta) >= second
    width = local * N
    base = resumed_ref.shape[1] - 2 * width
    closing_row = pl.multiple_of(base + jnp.maximum(closing - 1, 0) * width, width)
    opening_row = pl.multiple_of(base + jnp.maximum(opening - 1, 0) * width, width)
    for chip in range(entering_ref.shape[0]):
        f0 = jnp.where(
            even,
            factors_of(keep_ref[chip, width:, :], local),
            factors_of(got_ref[chip, width:, :], local),
        )
        closing_state = resumed_ref[chip, pl.ds(closing_row, width), :].astype(jnp.float32)
        opening_state = resumed_ref[chip, pl.ds(opening_row, width), :].astype(jnp.float32)
        for k in range(local):
            rows = slice(k * N, (k + 1) * N)
            entering = entering_ref[chip, rows, :].astype(jnp.float32)
            s0 = jnp.where(
                even, keep_ref[chip, rows, :].astype(jnp.float32), got_ref[chip, rows, :].astype(jnp.float32)
            )
            middle = f0[k : k + 1] * jnp.where(closes, closing_state[rows], entering) + s0
            middle = jnp.where(opens, opening_state[rows], middle)
            own_ref[chip, rows, :] = jnp.where(even, entering, middle).astype(jnp.bfloat16)
            send_ref[chip, rows, :] = jnp.where(even, middle, entering).astype(jnp.bfloat16)


def intra_kernel(meta, skip, x_ref, dl_ref, step_ref, write_ref, read_ref, out_ref, run_s, step_s):
    step = pl.program_id(0)

    @pl.when(step == 0)
    def _():
        _, running, steps = running_rows(dl_ref, step_ref)
        run_s[...] = running
        step_s[...] = steps

    heads = pl.ds(pl.multiple_of(step * PAIR, PAIR), PAIR)
    running = run_s[heads, :]
    sizes = step_s[heads, :]
    columns = running.T
    r = last_start(meta)
    t = lax.broadcasted_iota(jnp.int32, (TOK, TOK), 0)
    u = lax.broadcasted_iota(jnp.int32, (TOK, TOK), 1)
    causal = (u <= t) & ((u >= r) | (t < r))
    for group in range(2):
        part = slice(group * N, (group + 1) * N)
        products = lax.dot_general(
            read_ref[:, part], write_ref[:, part], (((1,), (1,)), ((), ())),
            preferred_element_type=jnp.float32,
        )
        products = jnp.where(causal, products, 0.0)
        for k in range(group * HEADS_PER, (group + 1) * HEADS_PER):
            difference = columns[:, k : k + 1] - running[k : k + 1]
            decay = jnp.exp(jnp.minimum(difference, 0.0))
            mixing = (products * decay * sizes[k : k + 1]).astype(jnp.bfloat16)
            place = slice(k * P_SIZE, (k + 1) * P_SIZE)
            x = x_ref[:, place]
            mixed = jnp.dot(mixing, x, preferred_element_type=jnp.float32)
            out_ref[:, place] = mixed + skip[step * PAIR + k] * x.astype(jnp.float32)


def intra(meta, skip, x, rates, steps, writes, reads):
    return pl.pallas_call(
        intra_kernel,
        out_shape=jax.ShapeDtypeStruct((TOK, H * P_SIZE), jnp.float32),
        grid_spec=pltpu.PrefetchScalarGridSpec(
            num_scalar_prefetch=2,
            grid=(STEPS,),
            in_specs=[
                pl.BlockSpec((TOK, PAIR * P_SIZE), lambda i, m, s: (0, i)),
                pl.BlockSpec((TOK, H), lambda i, m, s: (0, 0)),
                pl.BlockSpec((TOK, H), lambda i, m, s: (0, 0)),
                pl.BlockSpec((TOK, 2 * N), lambda i, m, s: (0, i)),
                pl.BlockSpec((TOK, 2 * N), lambda i, m, s: (0, i)),
            ],
            out_specs=pl.BlockSpec((TOK, PAIR * P_SIZE), lambda i, m, s: (0, i)),
            scratch_shapes=[
                pltpu.VMEM((H, TOK), jnp.float32),
                pltpu.VMEM((H, TOK), jnp.float32),
            ],
        ),
        compiler_params=params(),
        cost_estimate=pl.CostEstimate(
            flops=8 * H * TOK * TOK * P_SIZE, bytes_accessed=7 << 20, transcendentals=H * TOK * TOK
        ),
        name="intra",
    )(meta, skip, x, rates, steps, writes, reads)


def finish_kernel(
    local, meta, part_ref, dl_ref, step_ref, read_ref, own_ref, other_ref, mine_ref, theirs_ref, out_ref, factor_s
):
    step = pl.program_id(0)
    even = meta[0] % 2 == 0
    r = last_start(meta)

    @pl.when(step == 0)
    def _():
        rates, running, _ = running_rows(dl_ref, step_ref)
        lane = lax.broadcasted_iota(jnp.int32, (H, TOK), 1)
        base = jnp.sum(jnp.where(lane < r, rates, 0.0), axis=1, keepdims=True)
        factor_s[...] = jnp.exp(jnp.minimum(running - jnp.where(lane >= r, base, 0.0), 0.0))

    factor = factor_s[pl.ds(pl.multiple_of(step * PAIR, PAIR), PAIR), :].T
    token = lax.broadcasted_iota(jnp.int32, (TOK, N), 0)
    resumed = (token >= r) & (r > 0)
    for group in range(2):
        reads = read_ref[:, group * N : (group + 1) * N].astype(jnp.float32)
        left = jnp.where(resumed, 0.0, reads)
        right = jnp.where(resumed, reads, 0.0)
        reads = jnp.concatenate([left, right], axis=1).astype(jnp.bfloat16)
        for k in range(group * HEADS_PER, (group + 1) * HEADS_PER):
            chip, half = k // (2 * local), k // local % 2
            rows = slice((k % local) * N, (k % local + 1) * N)
            own = even if half == 0 else jnp.logical_not(even)
            states = jnp.concatenate(
                [
                    jnp.where(own, own_ref[chip, rows, :], other_ref[chip, rows, :]),
                    jnp.where(own, mine_ref[chip, rows, :], theirs_ref[chip, rows, :]),
                ],
                axis=0,
            )
            carried = jnp.dot(reads, states, preferred_element_type=jnp.float32)
            place = slice(k * P_SIZE, (k + 1) * P_SIZE)
            out_ref[:, place] = (part_ref[:, place] + factor[:, k : k + 1] * carried).astype(jnp.bfloat16)


def finish(meta, part, rates, steps, reads, own, other, mine, theirs, local):
    chips = PAIR // (2 * local)
    width = local * N
    ahead = mine.shape[1] // width - 2

    def resumed_index(i, m):
        return (i, ahead + jnp.maximum(session_at(m[0] * TOK + TOK - 1, m) - 1, 0), 0)

    states = pl.BlockSpec((chips, width, P_SIZE), lambda i, m: (i, 0, 0))
    resumed = pl.BlockSpec((chips, width, P_SIZE), resumed_index)
    return pl.pallas_call(
        functools.partial(finish_kernel, local),
        out_shape=jax.ShapeDtypeStruct((TOK, H * P_SIZE), jnp.bfloat16),
        grid_spec=pltpu.PrefetchScalarGridSpec(
            num_scalar_prefetch=1,
            grid=(STEPS,),
            in_specs=[
                pl.BlockSpec((TOK, PAIR * P_SIZE), lambda i, m: (0, i)),
                pl.BlockSpec((TOK, H), lambda i, m: (0, 0)),
                pl.BlockSpec((TOK, H), lambda i, m: (0, 0)),
                pl.BlockSpec((TOK, 2 * N), lambda i, m: (0, i)),
                states,
                states,
                resumed,
                resumed,
            ],
            out_specs=pl.BlockSpec((TOK, PAIR * P_SIZE), lambda i, m: (0, i)),
            scratch_shapes=[pltpu.VMEM((H, TOK), jnp.float32)],
        ),
        compiler_params=params(),
        cost_estimate=pl.CostEstimate(
            flops=2 * H * TOK * TOK * P_SIZE, bytes_accessed=9 << 20, transcendentals=H * TOK
        ),
        name="finish",
    )(meta, part, rates, steps, reads, own, other, mine, theirs)


def attend_kernel(
    meta, q_ref, band4, band3, band2, band1, band0, *refs,
):
    history_refs, (sk_ref, sv_ref, out_ref, key_s, value_s) = refs[:8], refs[8:]
    factor = 1.0 / math.sqrt(HD)
    first = meta[0] * TOK
    r = last_start(meta)
    opening = session_at(first, meta)
    closing = session_at(first + TOK - 1, meta)
    bands = (band4, band3, band2, band1, band0)
    length = (REACH + 1) * TOK

    def one_session(session, hk_mine, hv_mine, hk_theirs, hv_theirs, resuming, needed):
        start = start_of(session, meta) - first + WINDOW
        oldest = start - WINDOW + jnp.maximum(SINKS + WINDOW - meta[3 + session], 0)

        @pl.when(needed & (start > 0))
        def _():
            row = lax.broadcasted_iota(jnp.int32, (length, WINDOW), 0)
            chips, share, _ = hk_mine.shape
            index = lax.broadcasted_iota(jnp.int32, (1, WINDOW), 1)
            second = (index >= WINDOW // 2).astype(jnp.int32)
            index = index - second * (WINDOW // 2)
            core = (meta[0] + second) % 2
            place = (2 * (index // share) + core) * share + index % share
            moved = (row == place + start - WINDOW).astype(jnp.bfloat16)
            half = (WINDOW // 2, HD)
            keys = jnp.concatenate([hk_mine[...].reshape(half), hk_theirs[...].reshape(half)], axis=0)
            values = jnp.concatenate([hv_mine[...].reshape(half), hv_theirs[...].reshape(half)], axis=0)
            history = jnp.dot(
                moved, jnp.concatenate([keys, values], axis=1), preferred_element_type=jnp.float32
            )
            for i, band in enumerate(bands):
                rows = slice(i * TOK, (i + 1) * TOK)
                index = lax.broadcasted_iota(jnp.int32, (TOK, HD), 0) + i * TOK
                turn = index >= start
                key_s[rows, :] = jnp.where(
                    turn, band[0].astype(jnp.float32), history[rows, :HD]
                ).astype(jnp.bfloat16)
                value_s[rows, :] = jnp.where(
                    turn, band[1].astype(jnp.float32), history[rows, HD:]
                ).astype(jnp.bfloat16)

        @pl.when(needed & (start <= 0))
        def _():
            for i, band in enumerate(bands):
                rows = slice(i * TOK, (i + 1) * TOK)
                key_s[rows, :] = band[0]
                value_s[rows, :] = band[1]

        for b in range(TOK // BLOCK):
            inside = (b * BLOCK + BLOCK > r) if resuming else (b * BLOCK < r)

            @pl.when(needed & inside)
            def _():
                rows = slice(b * BLOCK, b * BLOCK + SPAN)
                keys = jnp.concatenate([key_s[rows, :], sk_ref[session]], axis=0)
                values = jnp.concatenate([value_s[rows, :], sv_ref[session]], axis=0)
                tokens = slice(b * BLOCK, (b + 1) * BLOCK)
                queries = jnp.concatenate(
                    [q_ref[tokens, g * HD : (g + 1) * HD] for g in range(QH // KVH)], axis=0
                )
                scores = lax.dot_general(
                    queries, keys, (((1,), (1,)), ((), ())), preferred_element_type=jnp.float32
                )
                token = lax.broadcasted_iota(jnp.int32, (BLOCK, COLUMNS), 0)
                column = lax.broadcasted_iota(jnp.int32, (BLOCK, COLUMNS), 1)
                seen = (column > token) & (column <= token + WINDOW) & (column >= oldest - b * BLOCK)
                seen = (seen & (column < SPAN)) | ((column >= SPAN) & (column < SPAN + SINKS))
                bias = jnp.where(seen, 0.0, NEG)
                weights, sums = [], []
                for g in range(QH // KVH):
                    score = scores[g * BLOCK : (g + 1) * BLOCK] * factor + bias
                    weight = jnp.exp(score - jnp.max(score, axis=1, keepdims=True))
                    sums.append(jnp.sum(weight, axis=1, keepdims=True))
                    weights.append(weight.astype(jnp.bfloat16))
                mixed = jnp.dot(
                    jnp.concatenate(weights, axis=0), values, preferred_element_type=jnp.float32
                )
                for g in range(QH // KVH):
                    result = mixed[g * BLOCK : (g + 1) * BLOCK] / sums[g]
                    lanes = slice(g * HD, (g + 1) * HD)
                    if resuming:
                        index = lax.broadcasted_iota(jnp.int32, (BLOCK, HD), 0) + b * BLOCK
                        before = out_ref[tokens, lanes].astype(jnp.float32)
                        result = jnp.where(index >= r, result, before)
                    out_ref[tokens, lanes] = result.astype(jnp.bfloat16)

    one_session(opening, *history_refs[:4], False, r > 0)
    one_session(closing, *history_refs[4:], True, r >= 0)


def attend(meta, queries, bands, mine, theirs, sink_keys, sink_values):
    chips = mine.shape[0]
    share = WINDOW // (2 * chips)
    lanes = QH // KVH * HD

    def history_spec(which, last):
        def index(j, m):
            session = session_at(m[0] * TOK + (TOK - 1 if last else 0), m)
            return (0, (which * SEQS + session) * KVH + j, 0)

        return pl.BlockSpec((chips, share, HD), index)

    pad = SEQS, COLUMNS - SPAN, HD
    return pl.pallas_call(
        attend_kernel,
        out_shape=jax.ShapeDtypeStruct((TOK, QH * HD), jnp.bfloat16),
        grid_spec=pltpu.PrefetchScalarGridSpec(
            num_scalar_prefetch=1,
            grid=(KVH,),
            in_specs=[pl.BlockSpec((TOK, lanes), lambda j, m: (0, j))]
            + [pl.BlockSpec((2, TOK, HD), lambda j, m: (0, 0, j))] * (REACH + 1)
            + [history_spec(0, False), history_spec(1, False)] * 2
            + [history_spec(0, True), history_spec(1, True)] * 2
            + [pl.BlockSpec(pad, lambda j, m: (0, 0, j))] * 2,
            out_specs=pl.BlockSpec((TOK, lanes), lambda j, m: (0, j)),
            scratch_shapes=[
                pltpu.VMEM(((REACH + 1) * TOK, HD), jnp.bfloat16),
                pltpu.VMEM(((REACH + 1) * TOK, HD), jnp.bfloat16),
            ],
        ),
        compiler_params=params(),
        cost_estimate=pl.CostEstimate(
            flops=16 * TOK * QH * COLUMNS * HD, bytes_accessed=8 << 20,
            transcendentals=2 * TOK * QH * COLUMNS,
        ),
        name="attend",
    )(
        meta, queries, *bands, mine, mine, theirs, theirs, mine, mine, theirs, theirs, sink_keys, sink_values
    )


def shifted(block, axis, distance):
    devices = range(lax.axis_size(axis))
    return lax.ppermute(block, axis, [(i - distance, i) for i in devices if i - distance in devices])


def shards(
    mamba_input,
    step_size,
    decay_log,
    state_write,
    state_read,
    skip_gain,
    saved_states,
    home_slot,
    turn_lengths,
    history_lengths,
    queries,
    turn_keys,
    turn_values,
    cache_keys,
    cache_values,
    sink_keys,
    sink_values,
):
    place = lax.axis_index("ctx")
    group = lax.axis_index("sess")
    groups = lax.axis_size("sess")
    devices = lax.axis_size("ctx")
    local = saved_states.shape[2]
    width = local * N
    chips = devices // 2
    same_core = [list(range(core, devices, 2)) for core in range(2)]
    lengths = turn_lengths[0]
    slots = lax.dynamic_slice_in_dim(home_slot, group * SEQS, SEQS, 0)
    index = (slots // SEQS - group) % groups * SEQS + slots % SEQS
    meta = jnp.concatenate(
        [jnp.stack([place, lengths[0], lengths[0] + lengths[1]]), history_lengths[0], index]
    ).astype(jnp.int32)
    x, rates, steps = mamba_input[0], decay_log[0], step_size[0]
    writes, reads = state_write[0], state_read[0]

    def swapped(block):
        return lax.ppermute(block, "ctx", [(i, i ^ 1) for i in range(devices)])

    stored = [saved_states[0]]
    for j in range(1, groups):
        route = [((i + j) % groups, i) for i in range(groups)]
        stored.append(lax.ppermute(saved_states[0], "sess", route))
    stored = jnp.concatenate(stored, axis=0).reshape(groups * SEQS, local, P_SIZE, N)

    keep, send = summaries(meta, x, rates, steps, writes, local)
    got = swapped(send)
    [total] = whole(
        functools.partial(combine_kernel, local), "combine", meta, [keep, got], [(keep.shape, jnp.bfloat16)]
    )
    total = lax.all_to_all(total, "ctx", 0, 0, axis_index_groups=same_core, tiled=True)

    share = cache_keys.shape[2]
    rows = 2 * SEQS * KVH * share + 2 * width
    packed, restored = whole(
        functools.partial(pack_kernel, local),
        "pack",
        meta,
        [stored, cache_keys[0], cache_values[0]],
        [((rows, P_SIZE), jnp.bfloat16), ((SEQS, width, P_SIZE), jnp.float32)],
    )
    mine = lax.all_gather(packed, "ctx", axis=0, axis_index_groups=same_core)
    theirs = swapped(mine)
    part = intra(meta, skip_gain, x, rates, steps, writes, reads)

    shape = (chips, width, P_SIZE)
    [entering] = whole(
        functools.partial(recurrence_kernel, local), "recurrence", meta, [total, restored], [(shape, jnp.bfloat16)]
    )
    entering = lax.all_to_all(entering, "ctx", 0, 0, axis_index_groups=same_core, tiled=True)
    own, other = whole(
        functools.partial(middle_kernel, local),
        "middle",
        meta,
        [entering, keep, got, mine],
        [(shape, jnp.bfloat16), (shape, jnp.bfloat16)],
        4,
    )
    other = swapped(other)

    key_value = jnp.stack([turn_keys[0], turn_values[0]])
    two, four = shifted(key_value, "ctx", 2), shifted(key_value, "ctx", 4)
    even = place % 2 == 0
    pair = swapped(jnp.where(even, jnp.stack([key_value, two]), jnp.stack([two, four])))
    bands = [four, pair[1], two, pair[0], key_value]
    sinks = [
        jnp.pad(s[0], ((0, 0), (0, COLUMNS - SPAN - SINKS), (0, 0))) for s in (sink_keys, sink_values)
    ]
    attended = attend(meta, queries[0], bands, mine, theirs, *sinks)
    mixed = finish(meta, part, rates, steps, reads, own, other, mine, theirs, local)
    return mixed[None], attended[None]


def solution(mesh):
    token = P("sess", "ctx", None)
    return jax.shard_map(
        shards,
        mesh=mesh,
        in_specs=(
            token,
            token,
            token,
            token,
            token,
            P(),
            P("sess", None, "ctx", None),
            P(),
            P("sess", None),
            P("sess", None),
            token,
            token,
            token,
            P("sess", None, "ctx", None),
            P("sess", None, "ctx", None),
            P("sess", None, None, None),
            P("sess", None, None, None),
        ),
        out_specs=(token, token),
        check_vma=False,
    )
```

```python
import math

import jax
import jax.numpy as jnp
from jax import lax
from jax.experimental import pallas as pl
from jax.experimental.pallas import tpu as pltpu
from jax.sharding import PartitionSpec as P

REACH = 4
SEQS = 3
SINKS = 4
H = 64
P_SIZE = 128
N = 64
G = 8
QH = 32
KVH = 4
HD = 128
WINDOW = 512
TOK = 128

HEADS_PER = H // G
PAIR = 2 * HEADS_PER
STEPS = H // PAIR
EXTRA = 16
BLOCK = 64
SPAN = WINDOW + BLOCK
COLUMNS = SPAN + 64
NEG = -1e30


class Scalars:
    def __init__(self, ids, lengths, histories, homes):
        self.place, self.group = ids[0], ids[1]
        self.one = lengths[0, 0]
        self.two = lengths[0, 0] + lengths[0, 1]
        self.histories, self.homes = histories, homes
        self.even = self.place % 2 == 0

    def session_at(self, position):
        return (position >= self.one).astype(jnp.int32) + (position >= self.two).astype(jnp.int32)

    def start_of(self, session):
        return jnp.where(session == 0, 0, jnp.where(session == 1, self.one, self.two))

    def last_start(self):
        first = self.place * TOK
        return jnp.maximum(self.start_of(self.session_at(first + TOK - 1)) - first, 0)


def scalars(kernel, *options):
    def body(ids, lengths, histories, homes, *refs):
        kernel(*options, Scalars(ids, lengths, histories, homes), *refs)

    return body


def params(mib=48):
    return pltpu.CompilerParams(vmem_limit_bytes=mib * 1024 * 1024)


def running_rows(dl_ref, step_ref):
    both = jnp.concatenate([dl_ref[...], step_ref[...]], axis=1).astype(jnp.float32).T
    rates, steps = both[:H], both[H:]
    k = lax.broadcasted_iota(jnp.int32, (TOK, TOK), 0)
    u = lax.broadcasted_iota(jnp.int32, (TOK, TOK), 1)
    upto = (k <= u).astype(jnp.bfloat16)
    running = jnp.dot(rates.astype(jnp.bfloat16), upto, preferred_element_type=jnp.float32)
    return rates, running, steps


def summary_kernel(
    local, meta, x_ref, dl_ref, step_ref, write_ref, keep_ref, send_ref, coef_s, factor_s, write_s
):
    step = pl.program_id(0)

    @pl.when(step == 0)
    def _():
        rates, running, steps = running_rows(dl_ref, step_ref)
        r = meta.last_start()
        lane = lax.broadcasted_iota(jnp.int32, (H, TOK), 1)
        last = running[:, TOK - 1 :]
        base = jnp.sum(jnp.where(lane < r, rates, 0.0), axis=1, keepdims=True)
        coef_s[...] = jnp.where(lane >= r, jnp.exp(last - running) * steps, 0.0)
        factor_s[...] = jnp.broadcast_to(jnp.exp(last - base), (H, TOK))
        write_s[...] = write_ref[...].astype(jnp.float32).T

    even = meta.even
    coef = coef_s[pl.ds(pl.multiple_of(step * PAIR, PAIR), PAIR), :]
    factor = factor_s[pl.ds(pl.multiple_of(step * PAIR, PAIR), PAIR), :]
    writes = write_s[pl.ds(pl.multiple_of(step * 2 * N, 2 * N), 2 * N), :]

    def summary(k):
        group = k // HEADS_PER
        loading = (writes[group * N : (group + 1) * N] * coef[k : k + 1]).astype(jnp.bfloat16)
        return jnp.dot(
            loading, x_ref[:, k * P_SIZE : (k + 1) * P_SIZE], preferred_element_type=jnp.float32
        )

    for chip in range(PAIR // (2 * local)):
        low, high = 2 * local * chip, 2 * local * chip + local
        for k in range(local):
            first, second = summary(low + k), summary(high + k)
            rows = slice(k * N, (k + 1) * N)
            keep_ref[chip, rows, :] = jnp.where(even, first, second).astype(jnp.bfloat16)
            send_ref[chip, rows, :] = jnp.where(even, second, first).astype(jnp.bfloat16)
        first, second = factor[low : low + local], factor[high : high + local]
        keep_ref[chip, local * N :, :] = factor_rows(jnp.where(even, first, second))
        send_ref[chip, local * N :, :] = factor_rows(jnp.where(even, second, first))


def factor_rows(rows):
    high = rows.astype(jnp.bfloat16).astype(jnp.float32)
    parts = [high, rows - high]
    if EXTRA > 2 * rows.shape[0]:
        parts.append(jnp.zeros((EXTRA - 2 * rows.shape[0], TOK), jnp.float32))
    return jnp.concatenate(parts, axis=0).astype(jnp.bfloat16)


def factors_of(block, local):
    block = block.astype(jnp.float32)
    return block[:local] + block[local : 2 * local]


def summaries(meta, x, rates, steps, writes, local):
    chips = H // (2 * local)
    rows = local * N + EXTRA
    shape = jax.ShapeDtypeStruct((chips, rows, P_SIZE), jnp.bfloat16)
    spec = pl.BlockSpec((PAIR // (2 * local), rows, P_SIZE), lambda i, *m: (i, 0, 0))
    return pl.pallas_call(
        scalars(summary_kernel, local),
        out_shape=[shape, shape],
        grid_spec=pltpu.PrefetchScalarGridSpec(
            num_scalar_prefetch=4,
            grid=(STEPS,),
            in_specs=[
                pl.BlockSpec((TOK, PAIR * P_SIZE), lambda i, *m: (0, i)),
                pl.BlockSpec((TOK, H), lambda i, *m: (0, 0)),
                pl.BlockSpec((TOK, H), lambda i, *m: (0, 0)),
                pl.BlockSpec((TOK, G * N), lambda i, *m: (0, 0)),
            ],
            out_specs=[spec, spec],
            scratch_shapes=[
                pltpu.VMEM((H, TOK), jnp.float32),
                pltpu.VMEM((H, TOK), jnp.float32),
                pltpu.VMEM((G * N, TOK), jnp.float32),
            ],
        ),
        compiler_params=params(),
        cost_estimate=pl.CostEstimate(flops=2 * H * TOK * N * P_SIZE, bytes_accessed=3 << 20, transcendentals=0),
        name="summaries",
    )(*meta, x, rates, steps, writes)


def whole(kernel, name, meta, arrays, shapes, size=2):
    def spec(shape):
        return pl.BlockSpec(shape, lambda i, *m: (0,) * len(shape))

    return pl.pallas_call(
        kernel,
        out_shape=[jax.ShapeDtypeStruct(s, t) for s, t in shapes],
        grid_spec=pltpu.PrefetchScalarGridSpec(
            num_scalar_prefetch=4,
            grid=(1,),
            in_specs=[spec(a.shape) for a in arrays],
            out_specs=[spec(s) for s, _ in shapes],
        ),
        compiler_params=params(),
        cost_estimate=pl.CostEstimate(flops=1 << 21, bytes_accessed=size << 20, transcendentals=0),
        name=name,
    )(*meta, *arrays)


def history_kernel(meta, keys_ref, values_ref, packed_ref):
    rows = keys_ref.shape[1]
    for which, ref in enumerate((keys_ref, values_ref)):
        for s in range(SEQS):
            for j in range(KVH):
                place = ((which * SEQS + s) * KVH + j) * rows
                packed_ref[0, place : place + rows, :] = ref[s, :, j * HD : (j + 1) * HD]


def restore_kernel(local, meta, *refs):
    stored, (resumed_ref, restored_ref) = refs[:-2], refs[-2:]
    groups = len(stored)
    for s in range(SEQS):
        slot = meta.homes[meta.group * SEQS + s]
        source = (slot // SEQS - meta.group + groups) % groups
        for k in range(local):
            state = stored[0][slot % SEQS, k]
            for j in range(1, groups):
                state = jnp.where(source == j, stored[j][slot % SEQS, k], state)
            restored_ref[s, k * N : (k + 1) * N, :] = state.T
    for chip in range(resumed_ref.shape[0]):
        closing = meta.session_at((chip + 1) * 2 * TOK - 1)
        resumed_ref[chip] = restored_ref[closing].astype(jnp.bfloat16)


def combine_kernel(local, meta, keep_ref, got_ref, out_ref):
    even = meta.even
    second = (meta.place // 2 * 2 + 1) * TOK
    closes = meta.start_of(meta.session_at(second + TOK - 1)) >= second
    width = local * N
    for chip in range(keep_ref.shape[0]):
        keep = factors_of(keep_ref[chip, width:, :], local)
        got = factors_of(got_ref[chip, width:, :], local)
        f0, f1 = jnp.where(even, keep, got), jnp.where(even, got, keep)
        out_ref[chip, width:, :] = factor_rows(jnp.where(closes, f1, f0 * f1))
        carry = jnp.where(closes, 0.0, f1)
        for k in range(local):
            rows = slice(k * N, (k + 1) * N)
            keep = keep_ref[chip, rows, :].astype(jnp.float32)
            got = got_ref[chip, rows, :].astype(jnp.float32)
            s0, s1 = jnp.where(even, keep, got), jnp.where(even, got, keep)
            out_ref[chip, rows, :] = (carry[k : k + 1] * s0 + s1).astype(jnp.bfloat16)


def recurrence_kernel(local, meta, got_ref, restored_ref, out_ref):
    width = local * N
    span = 2 * TOK
    state = [jnp.zeros((N, P_SIZE), jnp.float32) for _ in range(local)]
    for c in range(got_ref.shape[0]):
        first = c * span
        opening = meta.session_at(first)
        closing = meta.session_at(first + span - 1)
        opens = meta.start_of(opening) >= first
        closes = meta.start_of(closing) >= first
        factor = factors_of(got_ref[c, width:, :], local)
        for k in range(local):
            rows = slice(k * N, (k + 1) * N)
            entering = jnp.where(opens, restored_ref[opening, rows, :], state[k])
            out_ref[c, rows, :] = entering.astype(jnp.bfloat16)
            source = jnp.where(closes, restored_ref[closing, rows, :], state[k])
            state[k] = factor[k : k + 1] * source + got_ref[c, rows, :].astype(jnp.float32)


def middle_kernel(local, meta, entering_ref, keep_ref, got_ref, resumed_ref, own_ref, send_ref):
    even = meta.even
    first = meta.place // 2 * 2 * TOK
    second = first + TOK
    start = meta.start_of(meta.session_at(second + TOK - 1))
    closes = (start > first) & (start < second)
    opens = start == second
    width = local * N
    for chip in range(entering_ref.shape[0]):
        f0 = jnp.where(
            even,
            factors_of(keep_ref[chip, width:, :], local),
            factors_of(got_ref[chip, width:, :], local),
        )
        resumed = resumed_ref[chip].astype(jnp.float32)
        for k in range(local):
            rows = slice(k * N, (k + 1) * N)
            entering = entering_ref[chip, rows, :].astype(jnp.float32)
            s0 = jnp.where(
                even, keep_ref[chip, rows, :].astype(jnp.float32), got_ref[chip, rows, :].astype(jnp.float32)
            )
            middle = f0[k : k + 1] * jnp.where(closes, resumed[rows], entering) + s0
            middle = jnp.where(opens, resumed[rows], middle)
            own_ref[chip, rows, :] = jnp.where(even, entering, middle).astype(jnp.bfloat16)
            send_ref[chip, rows, :] = jnp.where(even, middle, entering).astype(jnp.bfloat16)


def intra_kernel(meta, skip, x_ref, dl_ref, step_ref, write_ref, read_ref, out_ref, run_s, step_s):
    step = pl.program_id(0)

    @pl.when(step == 0)
    def _():
        _, running, steps = running_rows(dl_ref, step_ref)
        run_s[...] = running
        step_s[...] = steps

    heads = pl.ds(pl.multiple_of(step * PAIR, PAIR), PAIR)
    running = run_s[heads, :]
    sizes = step_s[heads, :]
    columns = running.T
    r = meta.last_start()
    t = lax.broadcasted_iota(jnp.int32, (TOK, TOK), 0)
    u = lax.broadcasted_iota(jnp.int32, (TOK, TOK), 1)
    causal = (u <= t) & ((u >= r) | (t < r))
    for group in range(2):
        part = slice(group * N, (group + 1) * N)
        products = lax.dot_general(
            read_ref[:, part], write_ref[:, part], (((1,), (1,)), ((), ())),
            preferred_element_type=jnp.float32,
        )
        products = jnp.where(causal, products, 0.0)
        for k in range(group * HEADS_PER, (group + 1) * HEADS_PER):
            difference = columns[:, k : k + 1] - running[k : k + 1]
            decay = jnp.exp(jnp.minimum(difference, 0.0))
            mixing = (products * decay * sizes[k : k + 1]).astype(jnp.bfloat16)
            place = slice(k * P_SIZE, (k + 1) * P_SIZE)
            x = x_ref[:, place]
            mixed = jnp.dot(mixing, x, preferred_element_type=jnp.float32)
            out_ref[:, place] = mixed + skip[step * PAIR + k] * x.astype(jnp.float32)


def intra(meta, skip, x, rates, steps, writes, reads):
    return pl.pallas_call(
        scalars(intra_kernel),
        out_shape=jax.ShapeDtypeStruct((TOK, H * P_SIZE), jnp.float32),
        grid_spec=pltpu.PrefetchScalarGridSpec(
            num_scalar_prefetch=5,
            grid=(STEPS,),
            in_specs=[
                pl.BlockSpec((TOK, PAIR * P_SIZE), lambda i, *m: (0, i)),
                pl.BlockSpec((TOK, H), lambda i, *m: (0, 0)),
                pl.BlockSpec((TOK, H), lambda i, *m: (0, 0)),
                pl.BlockSpec((TOK, 2 * N), lambda i, *m: (0, i)),
                pl.BlockSpec((TOK, 2 * N), lambda i, *m: (0, i)),
            ],
            out_specs=pl.BlockSpec((TOK, PAIR * P_SIZE), lambda i, *m: (0, i)),
            scratch_shapes=[
                pltpu.VMEM((H, TOK), jnp.float32),
                pltpu.VMEM((H, TOK), jnp.float32),
            ],
        ),
        compiler_params=params(),
        cost_estimate=pl.CostEstimate(
            flops=8 * H * TOK * TOK * P_SIZE, bytes_accessed=7 << 20, transcendentals=H * TOK * TOK
        ),
        name="intra",
    )(*meta, skip, x, rates, steps, writes, reads)


def finish_kernel(
    local, meta, part_ref, dl_ref, step_ref, read_ref, own_ref, other_ref, mine_ref, theirs_ref, out_ref, factor_s
):
    step = pl.program_id(0)
    even = meta.even
    r = meta.last_start()

    @pl.when(step == 0)
    def _():
        rates, running, _ = running_rows(dl_ref, step_ref)
        lane = lax.broadcasted_iota(jnp.int32, (H, TOK), 1)
        base = jnp.sum(jnp.where(lane < r, rates, 0.0), axis=1, keepdims=True)
        factor_s[...] = jnp.exp(jnp.minimum(running - jnp.where(lane >= r, base, 0.0), 0.0))

    factor = factor_s[pl.ds(pl.multiple_of(step * PAIR, PAIR), PAIR), :].T
    token = lax.broadcasted_iota(jnp.int32, (TOK, N), 0)
    resumed = (token >= r) & (r > 0)
    for group in range(2):
        reads = read_ref[:, group * N : (group + 1) * N].astype(jnp.float32)
        left = jnp.where(resumed, 0.0, reads)
        right = jnp.where(resumed, reads, 0.0)
        reads = jnp.concatenate([left, right], axis=1).astype(jnp.bfloat16)
        for k in range(group * HEADS_PER, (group + 1) * HEADS_PER):
            chip, half = k // (2 * local), k // local % 2
            rows = slice((k % local) * N, (k % local + 1) * N)
            own = even if half == 0 else jnp.logical_not(even)
            states = jnp.concatenate(
                [
                    jnp.where(own, own_ref[chip, rows, :], other_ref[chip, rows, :]),
                    jnp.where(own, mine_ref[chip, rows, :], theirs_ref[chip, rows, :]),
                ],
                axis=0,
            )
            carried = jnp.dot(reads, states, preferred_element_type=jnp.float32)
            place = slice(k * P_SIZE, (k + 1) * P_SIZE)
            out_ref[:, place] = (part_ref[:, place] + factor[:, k : k + 1] * carried).astype(jnp.bfloat16)


def finish(meta, part, rates, steps, reads, own, other, mine, theirs, local):
    chips = PAIR // (2 * local)
    width = local * N
    states = pl.BlockSpec((chips, width, P_SIZE), lambda i, *m: (i, 0, 0))
    return pl.pallas_call(
        scalars(finish_kernel, local),
        out_shape=jax.ShapeDtypeStruct((TOK, H * P_SIZE), jnp.bfloat16),
        grid_spec=pltpu.PrefetchScalarGridSpec(
            num_scalar_prefetch=4,
            grid=(STEPS,),
            in_specs=[
                pl.BlockSpec((TOK, PAIR * P_SIZE), lambda i, *m: (0, i)),
                pl.BlockSpec((TOK, H), lambda i, *m: (0, 0)),
                pl.BlockSpec((TOK, H), lambda i, *m: (0, 0)),
                pl.BlockSpec((TOK, 2 * N), lambda i, *m: (0, i)),
                states,
                states,
                states,
                states,
            ],
            out_specs=pl.BlockSpec((TOK, PAIR * P_SIZE), lambda i, *m: (0, i)),
            scratch_shapes=[pltpu.VMEM((H, TOK), jnp.float32)],
        ),
        compiler_params=params(),
        cost_estimate=pl.CostEstimate(
            flops=2 * H * TOK * TOK * P_SIZE, bytes_accessed=9 << 20, transcendentals=H * TOK
        ),
        name="finish",
    )(*meta, part, rates, steps, reads, own, other, mine, theirs)


def attend_kernel(
    meta, q_ref, band4, band3, band2, band1, band0, *refs,
):
    history_refs, (sk_ref, sv_ref, out_ref, key_s, value_s) = refs[:16], refs[16:]
    factor = 1.0 / math.sqrt(HD)
    first = meta.place * TOK
    r = meta.last_start()
    opening = meta.session_at(first)
    closing = meta.session_at(first + TOK - 1)
    bands = (band4, band3, band2, band1, band0)
    length = (REACH + 1) * TOK

    def one_session(session, key_refs, value_refs, resuming, needed):
        start = meta.start_of(session) - first + WINDOW
        oldest = start - WINDOW + jnp.maximum(SINKS + WINDOW - meta.histories[0, session], 0)

        @pl.when(needed & (start > 0))
        def _():
            row = lax.broadcasted_iota(jnp.int32, (length, WINDOW), 0)
            chips, share, _ = key_refs[0].shape
            index = lax.broadcasted_iota(jnp.int32, (1, WINDOW), 1)
            piece, index = index // (WINDOW // 4), index % (WINDOW // 4)
            near, row_in = index // share, index % share
            far, bits = jnp.zeros_like(near), chips.bit_length() - 1
            for k in range(bits):
                far = far + ((near // (1 << k)) % 2) * (1 << (bits - 1 - k))
            device = meta.place ^ (piece // 2 + piece % 2 * 2 + far * 4)
            place = device * share + row_in
            moved = (row == place + start - WINDOW).astype(jnp.bfloat16)
            part = (WINDOW // 4, HD)
            keys = jnp.concatenate([ref[...].reshape(part) for ref in key_refs], axis=0)
            values = jnp.concatenate([ref[...].reshape(part) for ref in value_refs], axis=0)
            history = jnp.dot(
                moved, jnp.concatenate([keys, values], axis=1), preferred_element_type=jnp.float32
            )
            for i, band in enumerate(bands):
                rows = slice(i * TOK, (i + 1) * TOK)
                index = lax.broadcasted_iota(jnp.int32, (TOK, HD), 0) + i * TOK
                turn = index >= start
                key_s[rows, :] = jnp.where(
                    turn, band[0].astype(jnp.float32), history[rows, :HD]
                ).astype(jnp.bfloat16)
                value_s[rows, :] = jnp.where(
                    turn, band[1].astype(jnp.float32), history[rows, HD:]
                ).astype(jnp.bfloat16)

        @pl.when(needed & (start <= 0))
        def _():
            for i, band in enumerate(bands):
                rows = slice(i * TOK, (i + 1) * TOK)
                key_s[rows, :] = band[0]
                value_s[rows, :] = band[1]

        for b in range(TOK // BLOCK):
            inside = (b * BLOCK + BLOCK > r) if resuming else (b * BLOCK < r)

            @pl.when(needed & inside)
            def _():
                rows = slice(b * BLOCK, b * BLOCK + SPAN)
                keys = jnp.concatenate([key_s[rows, :], sk_ref[session]], axis=0)
                values = jnp.concatenate([value_s[rows, :], sv_ref[session]], axis=0)
                tokens = slice(b * BLOCK, (b + 1) * BLOCK)
                queries = jnp.concatenate(
                    [q_ref[tokens, g * HD : (g + 1) * HD] for g in range(QH // KVH)], axis=0
                )
                scores = lax.dot_general(
                    queries, keys, (((1,), (1,)), ((), ())), preferred_element_type=jnp.float32
                )
                token = lax.broadcasted_iota(jnp.int32, (BLOCK, COLUMNS), 0)
                column = lax.broadcasted_iota(jnp.int32, (BLOCK, COLUMNS), 1)
                seen = (column > token) & (column <= token + WINDOW) & (column >= oldest - b * BLOCK)
                seen = (seen & (column < SPAN)) | ((column >= SPAN) & (column < SPAN + SINKS))
                bias = jnp.where(seen, 0.0, NEG)
                weights, sums = [], []
                for g in range(QH // KVH):
                    score = scores[g * BLOCK : (g + 1) * BLOCK] * factor + bias
                    weight = jnp.exp(score - jnp.max(score, axis=1, keepdims=True))
                    sums.append(jnp.sum(weight, axis=1, keepdims=True))
                    weights.append(weight.astype(jnp.bfloat16))
                mixed = jnp.dot(
                    jnp.concatenate(weights, axis=0), values, preferred_element_type=jnp.float32
                )
                for g in range(QH // KVH):
                    result = mixed[g * BLOCK : (g + 1) * BLOCK] / sums[g]
                    lanes = slice(g * HD, (g + 1) * HD)
                    if resuming:
                        index = lax.broadcasted_iota(jnp.int32, (BLOCK, HD), 0) + b * BLOCK
                        before = out_ref[tokens, lanes].astype(jnp.float32)
                        result = jnp.where(index >= r, result, before)
                    out_ref[tokens, lanes] = result.astype(jnp.bfloat16)

    one_session(opening, history_refs[0:4], history_refs[4:8], False, r > 0)
    one_session(closing, history_refs[8:12], history_refs[12:], True, r >= 0)


def attend(meta, queries, bands, pieces, sink_keys, sink_values):
    chips = pieces[0].shape[0]
    share = WINDOW // (4 * chips)
    lanes = QH // KVH * HD

    def history_spec(which, last):
        def index(j, *m):
            known = Scalars(*m)
            session = known.session_at(known.place * TOK + (TOK - 1 if last else 0))
            return (0, (which * SEQS + session) * KVH + j, 0)

        return pl.BlockSpec((chips, share, HD), index)

    pad = SEQS, COLUMNS - SPAN, HD
    return pl.pallas_call(
        scalars(attend_kernel),
        out_shape=jax.ShapeDtypeStruct((TOK, QH * HD), jnp.bfloat16),
        grid_spec=pltpu.PrefetchScalarGridSpec(
            num_scalar_prefetch=4,
            grid=(KVH,),
            in_specs=[pl.BlockSpec((TOK, lanes), lambda j, *m: (0, j))]
            + [pl.BlockSpec((2, TOK, HD), lambda j, *m: (0, 0, j))] * (REACH + 1)
            + [history_spec(0, False)] * 4
            + [history_spec(1, False)] * 4
            + [history_spec(0, True)] * 4
            + [history_spec(1, True)] * 4
            + [pl.BlockSpec(pad, lambda j, *m: (0, 0, j))] * 2,
            out_specs=pl.BlockSpec((TOK, lanes), lambda j, *m: (0, j)),
            scratch_shapes=[
                pltpu.VMEM(((REACH + 1) * TOK, HD), jnp.bfloat16),
                pltpu.VMEM(((REACH + 1) * TOK, HD), jnp.bfloat16),
            ],
        ),
        compiler_params=params(),
        cost_estimate=pl.CostEstimate(
            flops=16 * TOK * QH * COLUMNS * HD, bytes_accessed=8 << 20,
            transcendentals=2 * TOK * QH * COLUMNS,
        ),
        name="attend",
    )(
        *meta, queries, *bands, *pieces, *pieces, *pieces, *pieces, sink_keys, sink_values
    )


def shifted(block, axis, distance):
    devices = range(lax.axis_size(axis))
    return lax.ppermute(block, axis, [(i - distance, i) for i in devices if i - distance in devices])


def shards(
    mamba_input,
    step_size,
    decay_log,
    state_write,
    state_read,
    skip_gain,
    saved_states,
    home_slot,
    turn_lengths,
    history_lengths,
    queries,
    turn_keys,
    turn_values,
    cache_keys,
    cache_values,
    sink_keys,
    sink_values,
):
    place = lax.axis_index("ctx")
    group = lax.axis_index("sess")
    groups = lax.axis_size("sess")
    devices = lax.axis_size("ctx")
    local = saved_states.shape[2]
    width = local * N
    chips = devices // 2
    same_core = [list(range(core, devices, 2)) for core in range(2)]
    meta = (jnp.stack([place, group]).astype(jnp.int32), turn_lengths, history_lengths, home_slot)
    x, rates, steps = mamba_input[0], decay_log[0], step_size[0]
    writes, reads = state_write[0], state_read[0]
    shape = (chips, width, P_SIZE)

    def apart(block, distance):
        return lax.ppermute(block, "ctx", [(i, i ^ distance) for i in range(devices)])

    def exchanged(block):
        return lax.all_to_all(block, "ctx", 0, 0, axis_index_groups=same_core, tiled=True)

    stored = [saved_states[0]]
    for j in range(1, groups):
        route = [((i + j) % groups, i) for i in range(groups)]
        stored.append(lax.ppermute(saved_states[0], "sess", route))

    keep, send = summaries(meta, x, rates, steps, writes, local)
    got = apart(send, 1)
    [total] = whole(scalars(combine_kernel, local), "combine", meta, [keep, got], [(keep.shape, jnp.bfloat16)])
    total = exchanged(total)

    stored = [block.reshape(SEQS, local, P_SIZE, N) for block in stored]
    resumed, restored = whole(
        scalars(restore_kernel, local),
        "restore",
        meta,
        stored,
        [(shape, jnp.bfloat16), ((SEQS, width, P_SIZE), jnp.float32)],
    )
    mine = exchanged(resumed)
    theirs = apart(mine, 1)
    part = intra(meta, skip_gain, x, rates, steps, writes, reads)

    share = cache_keys.shape[2]
    [history] = whole(
        scalars(history_kernel),
        "history",
        meta,
        [cache_keys[0], cache_values[0]],
        [((1, 2 * SEQS * KVH * share, HD), jnp.bfloat16)],
    )
    distance = devices // 2
    while distance > 2:
        history = jnp.concatenate([history, apart(history, distance)], axis=0)
        distance //= 2
    beside = apart(history, 2)
    pieces = [history, beside, apart(history, 1), apart(beside, 1)]

    [entering] = whole(
        scalars(recurrence_kernel, local), "recurrence", meta, [total, restored], [(shape, jnp.bfloat16)]
    )
    entering = exchanged(entering)
    own, other = whole(
        scalars(middle_kernel, local),
        "middle",
        meta,
        [entering, keep, got, mine],
        [(shape, jnp.bfloat16), (shape, jnp.bfloat16)],
        4,
    )
    other = apart(other, 1)

    key_value = jnp.stack([turn_keys[0], turn_values[0]])
    two, four = shifted(key_value, "ctx", 2), shifted(key_value, "ctx", 4)
    even = place % 2 == 0
    pair = apart(jnp.where(even, jnp.stack([key_value, two]), jnp.stack([two, four])), 1)
    bands = [four, pair[1], two, pair[0], key_value]
    sinks = [
        jnp.pad(s[0], ((0, 0), (0, COLUMNS - SPAN - SINKS), (0, 0))) for s in (sink_keys, sink_values)
    ]
    attended = attend(meta, queries[0], bands, pieces, *sinks)
    mixed = finish(meta, part, rates, steps, reads, own, other, mine, theirs, local)
    return mixed[None], attended[None]


def solution(mesh):
    token = P("sess", "ctx", None)
    return jax.shard_map(
        shards,
        mesh=mesh,
        in_specs=(
            token,
            token,
            token,
            token,
            token,
            P(),
            P("sess", None, "ctx", None),
            P(),
            P("sess", None),
            P("sess", None),
            token,
            token,
            token,
            P("sess", None, "ctx", None),
            P("sess", None, "ctx", None),
            P("sess", None, None, None),
            P("sess", None, None, None),
        ),
        out_specs=(token, token),
        check_vma=False,
    )
```

```python
import math

import jax
import jax.numpy as jnp
from jax import lax
from jax.experimental import pallas as pl
from jax.experimental.pallas import tpu as pltpu
from jax.sharding import PartitionSpec as P

REACH = 4
SEQS = 3
SINKS = 4
H = 64
P_SIZE = 128
N = 64
G = 8
QH = 32
KVH = 4
HD = 128
WINDOW = 512
TOK = 128

HEADS_PER = H // G
PAIR = 2 * HEADS_PER
STEPS = H // PAIR
EXTRA = 16
BLOCK = 64
SPAN = WINDOW + BLOCK
COLUMNS = SPAN + 64
NEG = -1e30


class Scalars:
    def __init__(self, ids, lengths, histories, homes):
        self.place, self.group = ids[0], ids[1]
        self.one = lengths[0, 0]
        self.two = lengths[0, 0] + lengths[0, 1]
        self.histories, self.homes = histories, homes
        self.even = self.place % 2 == 0

    def session_at(self, position):
        return (position >= self.one).astype(jnp.int32) + (position >= self.two).astype(jnp.int32)

    def start_of(self, session):
        return jnp.where(session == 0, 0, jnp.where(session == 1, self.one, self.two))

    def last_start(self):
        first = self.place * TOK
        return jnp.maximum(self.start_of(self.session_at(first + TOK - 1)) - first, 0)


def scalars(kernel, *options):
    def body(ids, lengths, histories, homes, *refs):
        kernel(*options, Scalars(ids, lengths, histories, homes), *refs)

    return body


def params(mib=60):
    return pltpu.CompilerParams(vmem_limit_bytes=mib * 1024 * 1024)


def running_rows(dl_ref):
    k = lax.broadcasted_iota(jnp.int32, (TOK, TOK), 0)
    u = lax.broadcasted_iota(jnp.int32, (TOK, TOK), 1)
    upto = (k <= u).astype(jnp.bfloat16)
    running = jnp.dot(dl_ref[...], upto, preferred_element_type=jnp.float32)
    return dl_ref[...].astype(jnp.float32), running


def summary_kernel(
    local, meta, x_ref, dl_ref, step_ref, write_ref, keep_ref, send_ref, coef_s, factor_s, write_s
):
    step = pl.program_id(0)

    @pl.when(step == 0)
    def _():
        rates, running = running_rows(dl_ref)
        steps = step_ref[...].astype(jnp.float32)
        r = meta.last_start()
        lane = lax.broadcasted_iota(jnp.int32, (H, TOK), 1)
        last = running[:, TOK - 1 :]
        base = jnp.sum(jnp.where(lane < r, rates, 0.0), axis=1, keepdims=True)
        coef_s[...] = jnp.where(lane >= r, jnp.exp(last - running) * steps, 0.0)
        factor_s[...] = jnp.broadcast_to(jnp.exp(last - base), (H, TOK))
        write_s[...] = write_ref[...].astype(jnp.float32).T

    even = meta.even
    coef = coef_s[pl.ds(pl.multiple_of(step * PAIR, PAIR), PAIR), :]
    factor = factor_s[pl.ds(pl.multiple_of(step * PAIR, PAIR), PAIR), :]
    writes = write_s[pl.ds(pl.multiple_of(step * 2 * N, 2 * N), 2 * N), :]

    def summary(k):
        group = k // HEADS_PER
        loading = (writes[group * N : (group + 1) * N] * coef[k : k + 1]).astype(jnp.bfloat16)
        return jnp.dot(
            loading, x_ref[:, k * P_SIZE : (k + 1) * P_SIZE], preferred_element_type=jnp.float32
        )

    for chip in range(PAIR // (2 * local)):
        low, high = 2 * local * chip, 2 * local * chip + local
        for k in range(local):
            first, second = summary(low + k), summary(high + k)
            rows = slice(k * N, (k + 1) * N)
            keep_ref[chip, rows, :] = jnp.where(even, first, second).astype(jnp.bfloat16)
            send_ref[chip, rows, :] = jnp.where(even, second, first).astype(jnp.bfloat16)
        first, second = factor[low : low + local], factor[high : high + local]
        keep_ref[chip, local * N :, :] = factor_rows(jnp.where(even, first, second))
        send_ref[chip, local * N :, :] = factor_rows(jnp.where(even, second, first))


def factor_rows(rows):
    high = rows.astype(jnp.bfloat16).astype(jnp.float32)
    parts = [high, rows - high]
    if EXTRA > 2 * rows.shape[0]:
        parts.append(jnp.zeros((EXTRA - 2 * rows.shape[0], TOK), jnp.float32))
    return jnp.concatenate(parts, axis=0).astype(jnp.bfloat16)


def factors_of(block, local):
    block = block.astype(jnp.float32)
    return block[:local] + block[local : 2 * local]


def summaries(meta, x, rates, steps, writes, local):
    chips = H // (2 * local)
    rows = local * N + EXTRA
    shape = jax.ShapeDtypeStruct((chips, rows, P_SIZE), jnp.bfloat16)
    spec = pl.BlockSpec((PAIR // (2 * local), rows, P_SIZE), lambda i, *m: (i, 0, 0))
    return pl.pallas_call(
        scalars(summary_kernel, local),
        out_shape=[shape, shape],
        grid_spec=pltpu.PrefetchScalarGridSpec(
            num_scalar_prefetch=4,
            grid=(STEPS,),
            in_specs=[
                pl.BlockSpec((TOK, PAIR * P_SIZE), lambda i, *m: (0, i)),
                pl.BlockSpec((H, TOK), lambda i, *m: (0, 0)),
                pl.BlockSpec((H, TOK), lambda i, *m: (0, 0)),
                pl.BlockSpec((TOK, G * N), lambda i, *m: (0, 0)),
            ],
            out_specs=[spec, spec],
            scratch_shapes=[
                pltpu.VMEM((H, TOK), jnp.float32),
                pltpu.VMEM((H, TOK), jnp.float32),
                pltpu.VMEM((G * N, TOK), jnp.float32),
            ],
        ),
        compiler_params=params(),
        cost_estimate=pl.CostEstimate(flops=2 * H * TOK * N * P_SIZE, bytes_accessed=3 << 20, transcendentals=0),
        name="summaries",
    )(*meta, x, rates, steps, writes)


def whole(kernel, name, meta, arrays, shapes, size=2, idle=()):
    def spec(shape):
        return pl.BlockSpec(shape, lambda i, *m: (0,) * len(shape))

    return pl.pallas_call(
        kernel,
        out_shape=[jax.ShapeDtypeStruct(s, t) for s, t in shapes],
        grid_spec=pltpu.PrefetchScalarGridSpec(
            num_scalar_prefetch=4,
            grid=(1,),
            in_specs=[spec(a.shape) for a in arrays] + [pl.BlockSpec(memory_space=pl.ANY)] * len(idle),
            out_specs=[spec(s) for s, _ in shapes],
        ),
        compiler_params=params(),
        cost_estimate=pl.CostEstimate(flops=1 << 21, bytes_accessed=size << 20, transcendentals=0),
        name=name,
    )(*meta, *arrays, *idle)


def restore_kernel(local, half, groups, meta, *refs):
    stored, (keys_ref, values_ref) = refs[:groups], refs[groups : groups + 2]
    home_ref, away_ref, restored_ref = refs[-3:]
    rows = keys_ref.shape[1]
    for s in range(SEQS):
        slot = meta.homes[meta.group * SEQS + s]
        source = (slot // SEQS - meta.group + groups) % groups
        for k in range(local):
            state = stored[0][slot % SEQS, k]
            for j in range(1, groups):
                state = jnp.where(source == j, stored[j][slot % SEQS, k], state)
            restored_ref[s, k * N : (k + 1) * N, :] = state.T
    upper = (meta.place >= half).astype(jnp.int32)
    for out_ref, first in ((home_ref, upper), (away_ref, 1 - upper)):
        for which, ref in enumerate((keys_ref, values_ref)):
            for s in range(2):
                for j in range(KVH):
                    place = ((which * 2 + s) * KVH + j) * rows
                    out_ref[0, place : place + rows, :] = ref[first + s, :, j * HD : (j + 1) * HD]
        out_ref[0, 4 * KVH * rows :, :] = restored_ref[first + 1].astype(jnp.bfloat16)


def far_place(distance, bits):
    place = distance * 0
    for k in range(bits):
        place = place + ((distance // (1 << k)) % 2) * (1 << (bits - 1 - k))
    return place


def combine_kernel(local, meta, keep_ref, got_ref, out_ref):
    even = meta.even
    second = (meta.place // 2 * 2 + 1) * TOK
    closes = meta.start_of(meta.session_at(second + TOK - 1)) >= second
    width = local * N
    for chip in range(keep_ref.shape[0]):
        keep = factors_of(keep_ref[chip, width:, :], local)
        got = factors_of(got_ref[chip, width:, :], local)
        f0, f1 = jnp.where(even, keep, got), jnp.where(even, got, keep)
        out_ref[chip, width:, :] = factor_rows(jnp.where(closes, f1, f0 * f1))
        carry = jnp.where(closes, 0.0, f1)
        for k in range(local):
            rows = slice(k * N, (k + 1) * N)
            keep = keep_ref[chip, rows, :].astype(jnp.float32)
            got = got_ref[chip, rows, :].astype(jnp.float32)
            s0, s1 = jnp.where(even, keep, got), jnp.where(even, got, keep)
            out_ref[chip, rows, :] = (carry[k : k + 1] * s0 + s1).astype(jnp.bfloat16)


def recurrence_kernel(local, meta, got_ref, restored_ref, *refs):
    out_ref = refs[-1]
    width = local * N
    span = 2 * TOK
    state = [jnp.zeros((N, P_SIZE), jnp.float32) for _ in range(local)]
    for c in range(got_ref.shape[0]):
        first = c * span
        opening = meta.session_at(first)
        closing = meta.session_at(first + span - 1)
        opens = meta.start_of(opening) >= first
        closes = meta.start_of(closing) >= first
        factor = factors_of(got_ref[c, width:, :], local)
        for k in range(local):
            rows = slice(k * N, (k + 1) * N)
            entering = jnp.where(opens, restored_ref[opening, rows, :], state[k])
            out_ref[c, rows, :] = entering.astype(jnp.bfloat16)
            source = jnp.where(closes, restored_ref[closing, rows, :], state[k])
            state[k] = factor[k : k + 1] * source + got_ref[c, rows, :].astype(jnp.float32)


def middle_kernel(local, meta, entering_ref, keep_ref, got_ref, near_ref, beside_ref, own_ref, send_ref):
    even = meta.even
    first = meta.place // 2 * 2 * TOK
    second = first + TOK
    start = meta.start_of(meta.session_at(second + TOK - 1))
    closes = (start > first) & (start < second)
    opens = start == second
    width = local * N
    bits = near_ref.shape[0].bit_length() - 1
    for chip in range(entering_ref.shape[0]):
        f0 = jnp.where(
            even,
            factors_of(keep_ref[chip, width:, :], local),
            factors_of(got_ref[chip, width:, :], local),
        )
        distance = (meta.place // 2) ^ chip
        far = far_place(distance // 2, bits)
        resumed = jnp.where(distance % 2 == 0, near_ref[far], beside_ref[far]).astype(jnp.float32)
        for k in range(local):
            rows = slice(k * N, (k + 1) * N)
            entering = entering_ref[chip, rows, :].astype(jnp.float32)
            s0 = jnp.where(
                even, keep_ref[chip, rows, :].astype(jnp.float32), got_ref[chip, rows, :].astype(jnp.float32)
            )
            middle = f0[k : k + 1] * jnp.where(closes, resumed[rows], entering) + s0
            middle = jnp.where(opens, resumed[rows], middle)
            own_ref[chip, rows, :] = jnp.where(even, entering, middle).astype(jnp.bfloat16)
            send_ref[chip, rows, :] = jnp.where(even, middle, entering).astype(jnp.bfloat16)


def intra_kernel(meta, skip, x_ref, dl_ref, step_ref, write_ref, read_ref, out_ref, run_s, step_s):
    step = pl.program_id(0)

    @pl.when(step == 0)
    def _():
        _, running = running_rows(dl_ref)
        run_s[...] = running
        step_s[...] = step_ref[...].astype(jnp.float32)

    heads = pl.ds(pl.multiple_of(step * PAIR, PAIR), PAIR)
    running = run_s[heads, :]
    sizes = step_s[heads, :]
    columns = running.T
    r = meta.last_start()
    t = lax.broadcasted_iota(jnp.int32, (TOK, TOK), 0)
    u = lax.broadcasted_iota(jnp.int32, (TOK, TOK), 1)
    causal = (u <= t) & ((u >= r) | (t < r))
    for group in range(2):
        part = slice(group * N, (group + 1) * N)
        products = lax.dot_general(
            read_ref[:, part], write_ref[:, part], (((1,), (1,)), ((), ())),
            preferred_element_type=jnp.float32,
        )
        products = jnp.where(causal, products, 0.0)
        for k in range(group * HEADS_PER, (group + 1) * HEADS_PER):
            difference = columns[:, k : k + 1] - running[k : k + 1]
            decay = jnp.exp(jnp.minimum(difference, 0.0))
            mixing = (products * decay * sizes[k : k + 1]).astype(jnp.bfloat16)
            place = slice(k * P_SIZE, (k + 1) * P_SIZE)
            x = x_ref[:, place]
            mixed = jnp.dot(mixing, x, preferred_element_type=jnp.float32)
            out_ref[:, place] = mixed + skip[step * PAIR + k] * x.astype(jnp.float32)


def intra(meta, skip, x, rates, steps, writes, reads):
    return pl.pallas_call(
        scalars(intra_kernel),
        out_shape=jax.ShapeDtypeStruct((TOK, H * P_SIZE), jnp.float32),
        grid_spec=pltpu.PrefetchScalarGridSpec(
            num_scalar_prefetch=5,
            grid=(STEPS,),
            in_specs=[
                pl.BlockSpec((TOK, PAIR * P_SIZE), lambda i, *m: (0, i)),
                pl.BlockSpec((H, TOK), lambda i, *m: (0, 0)),
                pl.BlockSpec((H, TOK), lambda i, *m: (0, 0)),
                pl.BlockSpec((TOK, 2 * N), lambda i, *m: (0, i)),
                pl.BlockSpec((TOK, 2 * N), lambda i, *m: (0, i)),
            ],
            out_specs=pl.BlockSpec((TOK, PAIR * P_SIZE), lambda i, *m: (0, i)),
            scratch_shapes=[
                pltpu.VMEM((H, TOK), jnp.float32),
                pltpu.VMEM((H, TOK), jnp.float32),
            ],
        ),
        compiler_params=params(),
        cost_estimate=pl.CostEstimate(
            flops=8 * H * TOK * TOK * P_SIZE, bytes_accessed=7 << 20, transcendentals=H * TOK * TOK
        ),
        name="intra",
    )(*meta, skip, x, rates, steps, writes, reads)


def finish_kernel(
    local, meta, part_ref, dl_ref, step_ref, read_ref, own_ref, other_ref, *refs
):
    pieces, (out_ref, factor_s) = refs[:4], refs[4:]
    bits = pieces[0].shape[0].bit_length() - 1
    step = pl.program_id(0)
    even = meta.even
    own_chip = meta.place // 2
    r = meta.last_start()

    @pl.when(step == 0)
    def _():
        rates, running = running_rows(dl_ref)
        lane = lax.broadcasted_iota(jnp.int32, (H, TOK), 1)
        base = jnp.sum(jnp.where(lane < r, rates, 0.0), axis=1, keepdims=True)
        factor_s[...] = jnp.exp(jnp.minimum(running - jnp.where(lane >= r, base, 0.0), 0.0))

    factor = factor_s[pl.ds(pl.multiple_of(step * PAIR, PAIR), PAIR), :].T
    token = lax.broadcasted_iota(jnp.int32, (TOK, N), 0)
    resumed = (token >= r) & (r > 0)
    for group in range(2):
        reads = read_ref[:, group * N : (group + 1) * N].astype(jnp.float32)
        left = jnp.where(resumed, 0.0, reads)
        right = jnp.where(resumed, reads, 0.0)
        reads = jnp.concatenate([left, right], axis=1).astype(jnp.bfloat16)
        for k in range(group * HEADS_PER, (group + 1) * HEADS_PER):
            chip, half = k // (2 * local), k // local % 2
            rows = slice((k % local) * N, (k % local + 1) * N)
            own = even if half == 0 else jnp.logical_not(even)
            distance = (step * (PAIR // (2 * local)) + chip) ^ own_chip
            far = far_place(distance // 2, bits)
            near = distance % 2 == 0
            resume = [piece[far, rows, :] for piece in pieces]
            states = jnp.concatenate(
                [
                    jnp.where(own, own_ref[chip, rows, :], other_ref[chip, rows, :]),
                    jnp.where(
                        own,
                        jnp.where(near, resume[0], resume[1]),
                        jnp.where(near, resume[2], resume[3]),
                    ),
                ],
                axis=0,
            )
            carried = jnp.dot(reads, states, preferred_element_type=jnp.float32)
            place = slice(k * P_SIZE, (k + 1) * P_SIZE)
            out_ref[:, place] = (part_ref[:, place] + factor[:, k : k + 1] * carried).astype(jnp.bfloat16)


def middle(meta, entering, keep, got, near, beside, local):
    width = local * N

    def spec(shape):
        return pl.BlockSpec(shape, lambda i, *m: (0,) * len(shape))

    return pl.pallas_call(
        scalars(middle_kernel, local),
        out_shape=[jax.ShapeDtypeStruct(entering.shape, jnp.bfloat16)] * 2,
        grid_spec=pltpu.PrefetchScalarGridSpec(
            num_scalar_prefetch=4,
            grid=(1,),
            in_specs=[spec(a.shape) for a in (entering, keep, got)] + [resumed_spec(near, width)] * 2,
            out_specs=[spec(entering.shape)] * 2,
        ),
        compiler_params=params(),
        cost_estimate=pl.CostEstimate(flops=1 << 21, bytes_accessed=4 << 20, transcendentals=0),
        name="middle",
    )(*meta, entering, keep, got, near, beside)


def resumed_spec(piece, width):
    count, rows, _ = piece.shape
    return pl.BlockSpec((count, width, P_SIZE), lambda i, *m: (0, rows // width - 1, 0))


def finish(meta, part, rates, steps, reads, own, other, pieces, local):
    chips = PAIR // (2 * local)
    width = local * N
    states = pl.BlockSpec((chips, width, P_SIZE), lambda i, *m: (i, 0, 0))
    return pl.pallas_call(
        scalars(finish_kernel, local),
        out_shape=jax.ShapeDtypeStruct((TOK, H * P_SIZE), jnp.bfloat16),
        grid_spec=pltpu.PrefetchScalarGridSpec(
            num_scalar_prefetch=4,
            grid=(STEPS,),
            in_specs=[
                pl.BlockSpec((TOK, PAIR * P_SIZE), lambda i, *m: (0, i)),
                pl.BlockSpec((H, TOK), lambda i, *m: (0, 0)),
                pl.BlockSpec((H, TOK), lambda i, *m: (0, 0)),
                pl.BlockSpec((TOK, 2 * N), lambda i, *m: (0, i)),
                states,
                states,
            ]
            + [resumed_spec(pieces[0], width)] * 4,
            out_specs=pl.BlockSpec((TOK, PAIR * P_SIZE), lambda i, *m: (0, i)),
            scratch_shapes=[pltpu.VMEM((H, TOK), jnp.float32)],
        ),
        compiler_params=params(),
        cost_estimate=pl.CostEstimate(
            flops=2 * H * TOK * TOK * P_SIZE, bytes_accessed=9 << 20, transcendentals=H * TOK
        ),
        name="finish",
    )(*meta, part, rates, steps, reads, own, other, *pieces)


def attend_kernel(
    meta, q_ref, band4, band3, band2, band1, band0, *refs,
):
    history_refs, (sk_ref, sv_ref, out_ref, key_s, value_s) = refs[:16], refs[16:]
    factor = 1.0 / math.sqrt(HD)
    first = meta.place * TOK
    r = meta.last_start()
    opening = meta.session_at(first)
    closing = meta.session_at(first + TOK - 1)
    bands = (band4, band3, band2, band1, band0)
    length = (REACH + 1) * TOK

    def one_session(session, key_refs, value_refs, resuming, needed):
        start = meta.start_of(session) - first + WINDOW
        oldest = start - WINDOW + jnp.maximum(SINKS + WINDOW - meta.histories[0, session], 0)

        @pl.when(needed & (start > 0))
        def _():
            row = lax.broadcasted_iota(jnp.int32, (length, WINDOW), 0)
            chips, share, _ = key_refs[0].shape
            index = lax.broadcasted_iota(jnp.int32, (1, WINDOW), 1)
            piece, index = index // (WINDOW // 4), index % (WINDOW // 4)
            near, row_in = index // share, index % share
            far = far_place(near, chips.bit_length() - 1)
            device = meta.place ^ (piece // 2 + piece % 2 * 2 + far * 4)
            place = device * share + row_in
            moved = (row == place + start - WINDOW).astype(jnp.bfloat16)
            part = (WINDOW // 4, HD)
            keys = jnp.concatenate([ref[...].reshape(part) for ref in key_refs], axis=0)
            values = jnp.concatenate([ref[...].reshape(part) for ref in value_refs], axis=0)
            history = jnp.dot(
                moved, jnp.concatenate([keys, values], axis=1), preferred_element_type=jnp.float32
            )
            for i, band in enumerate(bands):
                rows = slice(i * TOK, (i + 1) * TOK)
                index = lax.broadcasted_iota(jnp.int32, (TOK, HD), 0) + i * TOK
                turn = index >= start
                key_s[rows, :] = jnp.where(
                    turn, band[0].astype(jnp.float32), history[rows, :HD]
                ).astype(jnp.bfloat16)
                value_s[rows, :] = jnp.where(
                    turn, band[1].astype(jnp.float32), history[rows, HD:]
                ).astype(jnp.bfloat16)

        @pl.when(needed & (start <= 0))
        def _():
            for i, band in enumerate(bands):
                rows = slice(i * TOK, (i + 1) * TOK)
                key_s[rows, :] = band[0]
                value_s[rows, :] = band[1]

        for b in range(TOK // BLOCK):
            inside = (b * BLOCK + BLOCK > r) if resuming else (b * BLOCK < r)

            @pl.when(needed & inside)
            def _():
                rows = slice(b * BLOCK, b * BLOCK + SPAN)
                keys = jnp.concatenate([key_s[rows, :], sk_ref[session]], axis=0)
                values = jnp.concatenate([value_s[rows, :], sv_ref[session]], axis=0)
                tokens = slice(b * BLOCK, (b + 1) * BLOCK)
                queries = jnp.concatenate(
                    [q_ref[tokens, g * HD : (g + 1) * HD] for g in range(QH // KVH)], axis=0
                )
                scores = lax.dot_general(
                    queries, keys, (((1,), (1,)), ((), ())), preferred_element_type=jnp.float32
                )
                token = lax.broadcasted_iota(jnp.int32, (BLOCK, COLUMNS), 0)
                column = lax.broadcasted_iota(jnp.int32, (BLOCK, COLUMNS), 1)
                seen = (column > token) & (column <= token + WINDOW) & (column >= oldest - b * BLOCK)
                seen = (seen & (column < SPAN)) | ((column >= SPAN) & (column < SPAN + SINKS))
                bias = jnp.where(seen, 0.0, NEG)
                weights, sums = [], []
                for g in range(QH // KVH):
                    score = scores[g * BLOCK : (g + 1) * BLOCK] * factor + bias
                    weight = jnp.exp(score - jnp.max(score, axis=1, keepdims=True))
                    sums.append(jnp.sum(weight, axis=1, keepdims=True))
                    weights.append(weight.astype(jnp.bfloat16))
                mixed = jnp.dot(
                    jnp.concatenate(weights, axis=0), values, preferred_element_type=jnp.float32
                )
                for g in range(QH // KVH):
                    result = mixed[g * BLOCK : (g + 1) * BLOCK] / sums[g]
                    lanes = slice(g * HD, (g + 1) * HD)
                    if resuming:
                        index = lax.broadcasted_iota(jnp.int32, (BLOCK, HD), 0) + b * BLOCK
                        before = out_ref[tokens, lanes].astype(jnp.float32)
                        result = jnp.where(index >= r, result, before)
                    out_ref[tokens, lanes] = result.astype(jnp.bfloat16)

    one_session(opening, history_refs[0:4], history_refs[4:8], False, r > 0)
    one_session(closing, history_refs[8:12], history_refs[12:], True, r >= 0)


def attend(meta, queries, bands, pieces, half, sink_keys, sink_values):
    chips = pieces[0].shape[0]
    share = WINDOW // (4 * chips)
    lanes = QH // KVH * HD

    def history_spec(which, last):
        def index(j, *m):
            known = Scalars(*m)
            session = known.session_at(known.place * TOK + (TOK - 1 if last else 0))
            session = session - (known.place >= half).astype(jnp.int32)
            return (0, (which * 2 + session) * KVH + j, 0)

        return pl.BlockSpec((chips, share, HD), index)

    pad = SEQS, COLUMNS - SPAN, HD
    return pl.pallas_call(
        scalars(attend_kernel),
        out_shape=jax.ShapeDtypeStruct((TOK, QH * HD), jnp.bfloat16),
        grid_spec=pltpu.PrefetchScalarGridSpec(
            num_scalar_prefetch=4,
            grid=(KVH,),
            in_specs=[pl.BlockSpec((TOK, lanes), lambda j, *m: (0, j))]
            + [pl.BlockSpec((2, TOK, HD), lambda j, *m: (0, 0, j))] * (REACH + 1)
            + [history_spec(0, False)] * 4
            + [history_spec(1, False)] * 4
            + [history_spec(0, True)] * 4
            + [history_spec(1, True)] * 4
            + [pl.BlockSpec(pad, lambda j, *m: (0, 0, j))] * 2,
            out_specs=pl.BlockSpec((TOK, lanes), lambda j, *m: (0, j)),
            scratch_shapes=[
                pltpu.VMEM(((REACH + 1) * TOK, HD), jnp.bfloat16),
                pltpu.VMEM(((REACH + 1) * TOK, HD), jnp.bfloat16),
            ],
        ),
        compiler_params=params(),
        cost_estimate=pl.CostEstimate(
            flops=16 * TOK * QH * COLUMNS * HD, bytes_accessed=8 << 20,
            transcendentals=2 * TOK * QH * COLUMNS,
        ),
        name="attend",
    )(
        *meta, queries, *bands, *pieces, *pieces, *pieces, *pieces, sink_keys, sink_values
    )


def shifted(block, axis, distance):
    devices = range(lax.axis_size(axis))
    return lax.ppermute(block, axis, [(i - distance, i) for i in devices if i - distance in devices])


def shards(
    mamba_input,
    step_size,
    decay_log,
    state_write,
    state_read,
    skip_gain,
    saved_states,
    home_slot,
    turn_lengths,
    history_lengths,
    queries,
    turn_keys,
    turn_values,
    cache_keys,
    cache_values,
    sink_keys,
    sink_values,
):
    place = lax.axis_index("ctx")
    group = lax.axis_index("sess")
    groups = lax.axis_size("sess")
    devices = lax.axis_size("ctx")
    local = saved_states.shape[2]
    width = local * N
    chips = devices // 2
    same_core = [list(range(core, devices, 2)) for core in range(2)]
    meta = (jnp.stack([place, group]).astype(jnp.int32), turn_lengths, history_lengths, home_slot)
    x, rates, steps = mamba_input[0], decay_log[0].T, step_size[0].T
    writes, reads = state_write[0], state_read[0]
    shape = (chips, width, P_SIZE)

    def apart(block, distance):
        return lax.ppermute(block, "ctx", [(i, i ^ distance) for i in range(devices)])

    def exchanged(block):
        return lax.all_to_all(block, "ctx", 0, 0, axis_index_groups=same_core, tiled=True)

    stored = [saved_states[0]]
    for j in range(1, groups):
        route = [((i + j) % groups, i) for i in range(groups)]
        stored.append(lax.ppermute(saved_states[0], "sess", route))

    keep, send = summaries(meta, x, rates, steps, writes, local)
    got = apart(send, 1)
    [chip] = whole(scalars(combine_kernel, local), "combine", meta, [keep, got], [(keep.shape, jnp.bfloat16)])
    total = exchanged(chip)

    part = intra(meta, skip_gain, x, rates, steps, writes, reads)

    stored = [block.reshape(SEQS, local, P_SIZE, N) for block in stored]
    parcel = (1, 4 * KVH * cache_keys.shape[2] + width, P_SIZE)
    near, away, restored = whole(
        scalars(restore_kernel, local, devices // 2, groups),
        "restore",
        meta,
        [*stored, cache_keys[0], cache_values[0]],
        [(parcel, jnp.bfloat16), (parcel, jnp.bfloat16), ((SEQS, width, P_SIZE), jnp.float32)],
        idle=[chip],
    )
    distance = devices // 2
    while distance > 2:
        near = jnp.concatenate([near, apart(away, distance)], axis=0)
        away = near
        distance //= 2
    beside = apart(near, 2)
    pieces = [near, beside, apart(near, 1), apart(beside, 1)]

    [entering] = whole(
        scalars(recurrence_kernel, local),
        "recurrence",
        meta,
        [total, restored],
        [(shape, jnp.bfloat16)],
        idle=[part],
    )
    entering = exchanged(entering)
    own, other = middle(meta, entering, keep, got, near, beside, local)
    other = apart(other, 1)

    key_value = jnp.stack([turn_keys[0], turn_values[0]])
    four = shifted(key_value, "ctx", 4)
    two = apart(jnp.where((place >> 1) & 1 == 0, key_value, four), 2)
    even = place & 1 == 0
    pair = apart(jnp.where(even, jnp.stack([key_value, two]), jnp.stack([two, four])), 1)
    bands = [four, pair[1], two, pair[0], key_value]
    sinks = [
        jnp.pad(s[0], ((0, 0), (0, COLUMNS - SPAN - SINKS), (0, 0))) for s in (sink_keys, sink_values)
    ]
    attended = attend(meta, queries[0], bands, pieces, devices // 2, *sinks)
    mixed = finish(meta, part, rates, steps, reads, own, other, pieces, local)
    return mixed[None], attended[None]


def solution(mesh):
    token = P("sess", "ctx", None)
    return jax.shard_map(
        shards,
        mesh=mesh,
        in_specs=(
            token,
            token,
            token,
            token,
            token,
            P(),
            P("sess", None, "ctx", None),
            P(),
            P("sess", None),
            P("sess", None),
            token,
            token,
            token,
            P("sess", None, "ctx", None),
            P("sess", None, "ctx", None),
            P("sess", None, None, None),
            P("sess", None, None, None),
        ),
        out_specs=(token, token),
        check_vma=False,
    )
```

```python
import math

import jax
import jax.numpy as jnp
from jax import lax
from jax.experimental import pallas as pl
from jax.experimental.pallas import tpu as pltpu
from jax.sharding import PartitionSpec as P

REACH = 4
SEQS = 3
SINKS = 4
H = 64
P_SIZE = 128
N = 64
G = 8
QH = 32
KVH = 4
HD = 128
WINDOW = 512
TOK = 128

HEADS_PER = H // G
PAIR = 2 * HEADS_PER
STEPS = H // PAIR
EXTRA = 16
BLOCK = 64
SPAN = WINDOW + BLOCK
COLUMNS = SPAN + 64
NEG = -1e30


class Scalars:
    def __init__(self, ids):
        self.place, self.group = ids[0], ids[1]
        self.one = ids[2]
        self.two = ids[2] + ids[3]
        self.ids = ids
        self.even = self.place % 2 == 0

    def history(self, session):
        return self.ids[2 + SEQS + session]

    def home(self, number):
        return self.ids[2 + 2 * SEQS + number]

    def session_at(self, position):
        return (position >= self.one).astype(jnp.int32) + (position >= self.two).astype(jnp.int32)

    def start_of(self, session):
        return jnp.where(session == 0, 0, jnp.where(session == 1, self.one, self.two))

    def last_start(self):
        first = self.place * TOK
        return jnp.maximum(self.start_of(self.session_at(first + TOK - 1)) - first, 0)


def scalars(kernel, *options):
    def body(ids, *refs):
        kernel(*options, Scalars(ids), *refs)

    return body


def params(mib=48):
    return pltpu.CompilerParams(vmem_limit_bytes=mib * 1024 * 1024)


def running_rows(dl_ref):
    k = lax.broadcasted_iota(jnp.int32, (TOK, TOK), 0)
    u = lax.broadcasted_iota(jnp.int32, (TOK, TOK), 1)
    upto = (k <= u).astype(jnp.bfloat16)
    running = jnp.dot(dl_ref[...], upto, preferred_element_type=jnp.float32)
    return dl_ref[...].astype(jnp.float32), running


def summary_kernel(
    local, meta, x_ref, dl_ref, step_ref, write_ref, _, keep_ref, send_ref, coef_s, factor_s, write_s
):
    step = pl.program_id(0)

    @pl.when(step == 0)
    def _():
        rates, running = running_rows(dl_ref)
        steps = step_ref[...].astype(jnp.float32)
        r = meta.last_start()
        lane = lax.broadcasted_iota(jnp.int32, (H, TOK), 1)
        last = running[:, TOK - 1 :]
        base = jnp.sum(jnp.where(lane < r, rates, 0.0), axis=1, keepdims=True)
        coef_s[...] = jnp.where(lane >= r, jnp.exp(last - running) * steps, 0.0)
        factor_s[...] = jnp.broadcast_to(jnp.exp(last - base), (H, TOK))
        write_s[...] = write_ref[...].astype(jnp.float32).T

    even = meta.even
    coef = coef_s[pl.ds(pl.multiple_of(step * PAIR, PAIR), PAIR), :]
    factor = factor_s[pl.ds(pl.multiple_of(step * PAIR, PAIR), PAIR), :]
    writes = write_s[pl.ds(pl.multiple_of(step * 2 * N, 2 * N), 2 * N), :]

    def summary(k):
        group = k // HEADS_PER
        loading = (writes[group * N : (group + 1) * N] * coef[k : k + 1]).astype(jnp.bfloat16)
        return jnp.dot(
            loading, x_ref[:, k * P_SIZE : (k + 1) * P_SIZE], preferred_element_type=jnp.float32
        )

    for chip in range(PAIR // (2 * local)):
        low, high = 2 * local * chip, 2 * local * chip + local
        for k in range(local):
            first, second = summary(low + k), summary(high + k)
            rows = slice(k * N, (k + 1) * N)
            keep_ref[chip, rows, :] = jnp.where(even, first, second).astype(jnp.bfloat16)
            send_ref[chip, rows, :] = jnp.where(even, second, first).astype(jnp.bfloat16)
        first, second = factor[low : low + local], factor[high : high + local]
        keep_ref[chip, local * N :, :] = factor_rows(jnp.where(even, first, second))
        send_ref[chip, local * N :, :] = factor_rows(jnp.where(even, second, first))


def factor_rows(rows):
    high = rows.astype(jnp.bfloat16).astype(jnp.float32)
    parts = [high, rows - high]
    if EXTRA > 2 * rows.shape[0]:
        parts.append(jnp.zeros((EXTRA - 2 * rows.shape[0], TOK), jnp.float32))
    return jnp.concatenate(parts, axis=0).astype(jnp.bfloat16)


def factors_of(block, local):
    block = block.astype(jnp.float32)
    return block[:local] + block[local : 2 * local]


def summaries(meta, x, rates, steps, writes, local, idle):
    chips = H // (2 * local)
    rows = local * N + EXTRA
    shape = jax.ShapeDtypeStruct((chips, rows, P_SIZE), jnp.bfloat16)
    spec = pl.BlockSpec((PAIR // (2 * local), rows, P_SIZE), lambda i, *m: (i, 0, 0))
    return pl.pallas_call(
        scalars(summary_kernel, local),
        out_shape=[shape, shape],
        grid_spec=pltpu.PrefetchScalarGridSpec(
            num_scalar_prefetch=1,
            grid=(STEPS,),
            in_specs=[
                pl.BlockSpec((TOK, PAIR * P_SIZE), lambda i, *m: (0, i)),
                pl.BlockSpec((H, TOK), lambda i, *m: (0, 0)),
                pl.BlockSpec((H, TOK), lambda i, *m: (0, 0)),
                pl.BlockSpec((TOK, G * N), lambda i, *m: (0, 0)),
                pl.BlockSpec(memory_space=pl.ANY),
            ],
            out_specs=[spec, spec],
            scratch_shapes=[
                pltpu.VMEM((H, TOK), jnp.float32),
                pltpu.VMEM((H, TOK), jnp.float32),
                pltpu.VMEM((G * N, TOK), jnp.float32),
            ],
        ),
        compiler_params=params(),
        cost_estimate=pl.CostEstimate(flops=2 * H * TOK * N * P_SIZE, bytes_accessed=3 << 20, transcendentals=0),
        name="summaries",
    )(meta, x, rates, steps, writes, idle)


def whole(kernel, name, meta, arrays, shapes, size=2, idle=()):
    def spec(shape):
        return pl.BlockSpec(shape, lambda i, *m: (0,) * len(shape))

    return pl.pallas_call(
        kernel,
        out_shape=[jax.ShapeDtypeStruct(s, t) for s, t in shapes],
        grid_spec=pltpu.PrefetchScalarGridSpec(
            num_scalar_prefetch=1,
            grid=(1,),
            in_specs=[spec(a.shape) for a in arrays] + [pl.BlockSpec(memory_space=pl.ANY)] * len(idle),
            out_specs=[spec(s) for s, _ in shapes],
        ),
        compiler_params=params(),
        cost_estimate=pl.CostEstimate(flops=1 << 21, bytes_accessed=size << 20, transcendentals=0),
        name=name,
    )(meta, *arrays, *idle)


def history_kernel(half, meta, keys_ref, values_ref, home_ref, away_ref):
    rows = keys_ref.shape[1]
    upper = (meta.place >= half).astype(jnp.int32)
    for out_ref, first in ((home_ref, upper), (away_ref, 1 - upper)):
        for which, ref in enumerate((keys_ref, values_ref)):
            for s in range(2):
                for j in range(KVH):
                    place = ((which * 2 + s) * KVH + j) * rows
                    out_ref[0, place : place + rows, :] = ref[first + s, :, j * HD : (j + 1) * HD]


def turn_kernel(local, meta, stored_ref, *refs):
    out_ref = refs[-1]
    for s in range(SEQS):
        for k in range(local):
            out_ref[s, k * N : (k + 1) * N, :] = stored_ref[s, k].T


def restore_kernel(groups, meta, *refs):
    stored, (resumed_ref, restored_ref) = refs[:groups], refs[-2:]
    for s in range(SEQS):
        slot = meta.home(meta.group * SEQS + s)
        source = (slot // SEQS - meta.group + groups) % groups
        state = stored[0][slot % SEQS]
        for j in range(1, groups):
            state = jnp.where(source == j, stored[j][slot % SEQS], state)
        restored_ref[s] = state
    for chip in range(resumed_ref.shape[0]):
        closing = meta.session_at((chip + 1) * 2 * TOK - 1)
        resumed_ref[chip] = restored_ref[closing].astype(jnp.bfloat16)


def join_kernel(meta, first_ref, second_ref, *refs):
    out_ref = refs[-1]
    count = first_ref.shape[0]
    out_ref[:count] = first_ref[...]
    out_ref[count:] = second_ref[...]


def two_kernel(meta, key_value_ref, four_ref, *refs):
    refs[-1][...] = jnp.where(meta.place // 2 % 2 == 0, key_value_ref[...], four_ref[...])


def pair_kernel(meta, key_value_ref, two_ref, four_ref, out_ref):
    key_value, two, four = key_value_ref[...], two_ref[...], four_ref[...]
    out_ref[0] = jnp.where(meta.even, key_value, two)
    out_ref[1] = jnp.where(meta.even, two, four)


def stack_kernel(meta, keys_ref, values_ref, *refs):
    refs[-1][0] = keys_ref[...]
    refs[-1][1] = values_ref[...]


def far_place(distance, bits):
    place = distance * 0
    for k in range(bits):
        place = place + ((distance // (1 << k)) % 2) * (1 << (bits - 1 - k))
    return place


def combine_kernel(local, meta, keep_ref, got_ref, *refs):
    out_ref = refs[-1]
    even = meta.even
    second = (meta.place // 2 * 2 + 1) * TOK
    closes = meta.start_of(meta.session_at(second + TOK - 1)) >= second
    width = local * N
    for chip in range(keep_ref.shape[0]):
        keep = factors_of(keep_ref[chip, width:, :], local)
        got = factors_of(got_ref[chip, width:, :], local)
        f0, f1 = jnp.where(even, keep, got), jnp.where(even, got, keep)
        out_ref[chip, width:, :] = factor_rows(jnp.where(closes, f1, f0 * f1))
        carry = jnp.where(closes, 0.0, f1)
        for k in range(local):
            rows = slice(k * N, (k + 1) * N)
            keep = keep_ref[chip, rows, :].astype(jnp.float32)
            got = got_ref[chip, rows, :].astype(jnp.float32)
            s0, s1 = jnp.where(even, keep, got), jnp.where(even, got, keep)
            out_ref[chip, rows, :] = (carry[k : k + 1] * s0 + s1).astype(jnp.bfloat16)


def recurrence_kernel(local, meta, got_ref, restored_ref, *refs):
    out_ref = refs[-1]
    width = local * N
    span = 2 * TOK
    state = [jnp.zeros((N, P_SIZE), jnp.float32) for _ in range(local)]
    for c in range(got_ref.shape[0]):
        first = c * span
        opening = meta.session_at(first)
        closing = meta.session_at(first + span - 1)
        opens = meta.start_of(opening) >= first
        closes = meta.start_of(closing) >= first
        factor = factors_of(got_ref[c, width:, :], local)
        for k in range(local):
            rows = slice(k * N, (k + 1) * N)
            entering = jnp.where(opens, restored_ref[opening, rows, :], state[k])
            out_ref[c, rows, :] = entering.astype(jnp.bfloat16)
            source = jnp.where(closes, restored_ref[closing, rows, :], state[k])
            state[k] = factor[k : k + 1] * source + got_ref[c, rows, :].astype(jnp.float32)


def middle_kernel(local, meta, entering_ref, keep_ref, got_ref, resumed_ref, *refs):
    even = meta.even
    first = meta.place // 2 * 2 * TOK
    second = first + TOK
    start = meta.start_of(meta.session_at(second + TOK - 1))
    closes = (start > first) & (start < second)
    opens = start == second
    width = local * N
    own_ref, send_ref = refs[-2:]
    for chip in range(entering_ref.shape[0]):
        f0 = jnp.where(
            even,
            factors_of(keep_ref[chip, width:, :], local),
            factors_of(got_ref[chip, width:, :], local),
        )
        resumed = resumed_ref[chip].astype(jnp.float32)
        for k in range(local):
            rows = slice(k * N, (k + 1) * N)
            entering = entering_ref[chip, rows, :].astype(jnp.float32)
            s0 = jnp.where(
                even, keep_ref[chip, rows, :].astype(jnp.float32), got_ref[chip, rows, :].astype(jnp.float32)
            )
            middle = f0[k : k + 1] * jnp.where(closes, resumed[rows], entering) + s0
            middle = jnp.where(opens, resumed[rows], middle)
            own_ref[chip, rows, :] = jnp.where(even, entering, middle).astype(jnp.bfloat16)
            send_ref[chip, rows, :] = jnp.where(even, middle, entering).astype(jnp.bfloat16)


def intra_kernel(meta, skip, x_ref, dl_ref, step_ref, write_ref, read_ref, _, out_ref, run_s, step_s):
    step = pl.program_id(0)

    @pl.when(step == 0)
    def _():
        _, running = running_rows(dl_ref)
        run_s[...] = running
        step_s[...] = step_ref[...].astype(jnp.float32)

    heads = pl.ds(pl.multiple_of(step * PAIR, PAIR), PAIR)
    running = run_s[heads, :]
    sizes = step_s[heads, :]
    columns = running.T
    r = meta.last_start()
    t = lax.broadcasted_iota(jnp.int32, (TOK, TOK), 0)
    u = lax.broadcasted_iota(jnp.int32, (TOK, TOK), 1)
    causal = (u <= t) & ((u >= r) | (t < r))
    for group in range(2):
        part = slice(group * N, (group + 1) * N)
        products = lax.dot_general(
            read_ref[:, part], write_ref[:, part], (((1,), (1,)), ((), ())),
            preferred_element_type=jnp.float32,
        )
        products = jnp.where(causal, products, 0.0)
        for k in range(group * HEADS_PER, (group + 1) * HEADS_PER):
            difference = columns[:, k : k + 1] - running[k : k + 1]
            decay = jnp.exp(jnp.minimum(difference, 0.0))
            mixing = (products * decay * sizes[k : k + 1]).astype(jnp.bfloat16)
            place = slice(k * P_SIZE, (k + 1) * P_SIZE)
            x = x_ref[:, place]
            mixed = jnp.dot(mixing, x, preferred_element_type=jnp.float32)
            out_ref[:, place] = mixed + skip[step * PAIR + k] * x.astype(jnp.float32)


def intra(meta, skip, x, rates, steps, writes, reads, idle):
    return pl.pallas_call(
        lambda ids, *refs: intra_kernel(Scalars(ids), *refs),
        out_shape=jax.ShapeDtypeStruct((TOK, H * P_SIZE), jnp.float32),
        grid_spec=pltpu.PrefetchScalarGridSpec(
            num_scalar_prefetch=2,
            grid=(STEPS,),
            in_specs=[
                pl.BlockSpec((TOK, PAIR * P_SIZE), lambda i, *m: (0, i)),
                pl.BlockSpec((H, TOK), lambda i, *m: (0, 0)),
                pl.BlockSpec((H, TOK), lambda i, *m: (0, 0)),
                pl.BlockSpec((TOK, 2 * N), lambda i, *m: (0, i)),
                pl.BlockSpec((TOK, 2 * N), lambda i, *m: (0, i)),
                pl.BlockSpec(memory_space=pl.ANY),
            ],
            out_specs=pl.BlockSpec((TOK, PAIR * P_SIZE), lambda i, *m: (0, i)),
            scratch_shapes=[
                pltpu.VMEM((H, TOK), jnp.float32),
                pltpu.VMEM((H, TOK), jnp.float32),
            ],
        ),
        compiler_params=params(),
        cost_estimate=pl.CostEstimate(
            flops=8 * H * TOK * TOK * P_SIZE, bytes_accessed=7 << 20, transcendentals=H * TOK * TOK
        ),
        name="intra",
    )(meta, skip, x, rates, steps, writes, reads, idle)


def finish_kernel(
    local, meta, part_ref, dl_ref, step_ref, read_ref, own_ref, other_ref, mine_ref, theirs_ref, out_ref, factor_s
):
    step = pl.program_id(0)
    even = meta.even
    r = meta.last_start()

    @pl.when(step == 0)
    def _():
        rates, running = running_rows(dl_ref)
        lane = lax.broadcasted_iota(jnp.int32, (H, TOK), 1)
        base = jnp.sum(jnp.where(lane < r, rates, 0.0), axis=1, keepdims=True)
        factor_s[...] = jnp.exp(jnp.minimum(running - jnp.where(lane >= r, base, 0.0), 0.0))

    factor = factor_s[pl.ds(pl.multiple_of(step * PAIR, PAIR), PAIR), :].T
    token = lax.broadcasted_iota(jnp.int32, (TOK, N), 0)
    resumed = (token >= r) & (r > 0)
    for group in range(2):
        reads = read_ref[:, group * N : (group + 1) * N].astype(jnp.float32)
        left = jnp.where(resumed, 0.0, reads)
        right = jnp.where(resumed, reads, 0.0)
        reads = jnp.concatenate([left, right], axis=1).astype(jnp.bfloat16)
        for k in range(group * HEADS_PER, (group + 1) * HEADS_PER):
            chip, half = k // (2 * local), k // local % 2
            rows = slice((k % local) * N, (k % local + 1) * N)
            own = even if half == 0 else jnp.logical_not(even)
            states = jnp.concatenate(
                [
                    jnp.where(own, own_ref[chip, rows, :], other_ref[chip, rows, :]),
                    jnp.where(own, mine_ref[chip, rows, :], theirs_ref[chip, rows, :]),
                ],
                axis=0,
            )
            carried = jnp.dot(reads, states, preferred_element_type=jnp.float32)
            place = slice(k * P_SIZE, (k + 1) * P_SIZE)
            out_ref[:, place] = (part_ref[:, place] + factor[:, k : k + 1] * carried).astype(jnp.bfloat16)


def finish(meta, part, rates, steps, reads, own, other, mine, theirs, local):
    chips = PAIR // (2 * local)
    width = local * N
    states = pl.BlockSpec((chips, width, P_SIZE), lambda i, *m: (i, 0, 0))
    return pl.pallas_call(
        scalars(finish_kernel, local),
        out_shape=jax.ShapeDtypeStruct((TOK, H * P_SIZE), jnp.bfloat16),
        grid_spec=pltpu.PrefetchScalarGridSpec(
            num_scalar_prefetch=1,
            grid=(STEPS,),
            in_specs=[
                pl.BlockSpec((TOK, PAIR * P_SIZE), lambda i, *m: (0, i)),
                pl.BlockSpec((H, TOK), lambda i, *m: (0, 0)),
                pl.BlockSpec((H, TOK), lambda i, *m: (0, 0)),
                pl.BlockSpec((TOK, 2 * N), lambda i, *m: (0, i)),
                states,
                states,
                states,
                states,
            ],
            out_specs=pl.BlockSpec((TOK, PAIR * P_SIZE), lambda i, *m: (0, i)),
            scratch_shapes=[pltpu.VMEM((H, TOK), jnp.float32)],
        ),
        compiler_params=params(),
        cost_estimate=pl.CostEstimate(
            flops=2 * H * TOK * TOK * P_SIZE, bytes_accessed=9 << 20, transcendentals=H * TOK
        ),
        name="finish",
    )(meta, part, rates, steps, reads, own, other, mine, theirs)


def attend_kernel(
    meta, q_ref, band4, band3, band2, band1, band0, *refs,
):
    history_refs, (sk_ref, sv_ref, out_ref, key_s, value_s) = refs[:16], refs[16:]
    factor = 1.0 / math.sqrt(HD)
    first = meta.place * TOK
    r = meta.last_start()
    opening = meta.session_at(first)
    closing = meta.session_at(first + TOK - 1)
    bands = (band4, band3, band2, band1, band0)
    length = (REACH + 1) * TOK

    def one_session(session, key_refs, value_refs, resuming, needed):
        start = meta.start_of(session) - first + WINDOW
        oldest = start - WINDOW + jnp.maximum(SINKS + WINDOW - meta.history(session), 0)

        @pl.when(needed & (start > 0))
        def _():
            row = lax.broadcasted_iota(jnp.int32, (length, WINDOW), 0)
            chips, share, _ = key_refs[0].shape
            index = lax.broadcasted_iota(jnp.int32, (1, WINDOW), 1)
            piece, index = index // (WINDOW // 4), index % (WINDOW // 4)
            near, row_in = index // share, index % share
            far = far_place(near, chips.bit_length() - 1)
            device = meta.place ^ (piece // 2 + piece % 2 * 2 + far * 4)
            place = device * share + row_in
            moved = (row == place + start - WINDOW).astype(jnp.bfloat16)
            part = (WINDOW // 4, HD)
            keys = jnp.concatenate([ref[...].reshape(part) for ref in key_refs], axis=0)
            values = jnp.concatenate([ref[...].reshape(part) for ref in value_refs], axis=0)
            history = jnp.dot(
                moved, jnp.concatenate([keys, values], axis=1), preferred_element_type=jnp.float32
            )
            for i, band in enumerate(bands):
                rows = slice(i * TOK, (i + 1) * TOK)
                index = lax.broadcasted_iota(jnp.int32, (TOK, HD), 0) + i * TOK
                turn = index >= start
                key_s[rows, :] = jnp.where(
                    turn, band[0].astype(jnp.float32), history[rows, :HD]
                ).astype(jnp.bfloat16)
                value_s[rows, :] = jnp.where(
                    turn, band[1].astype(jnp.float32), history[rows, HD:]
                ).astype(jnp.bfloat16)

        @pl.when(needed & (start <= 0))
        def _():
            for i, band in enumerate(bands):
                rows = slice(i * TOK, (i + 1) * TOK)
                key_s[rows, :] = band[0]
                value_s[rows, :] = band[1]

        for b in range(TOK // BLOCK):
            inside = (b * BLOCK + BLOCK > r) if resuming else (b * BLOCK < r)

            @pl.when(needed & inside)
            def _():
                rows = slice(b * BLOCK, b * BLOCK + SPAN)
                keys = jnp.concatenate([key_s[rows, :], sk_ref[session]], axis=0)
                values = jnp.concatenate([value_s[rows, :], sv_ref[session]], axis=0)
                tokens = slice(b * BLOCK, (b + 1) * BLOCK)
                queries = jnp.concatenate(
                    [q_ref[tokens, g * HD : (g + 1) * HD] for g in range(QH // KVH)], axis=0
                )
                scores = lax.dot_general(
                    queries, keys, (((1,), (1,)), ((), ())), preferred_element_type=jnp.float32
                )
                token = lax.broadcasted_iota(jnp.int32, (BLOCK, COLUMNS), 0)
                column = lax.broadcasted_iota(jnp.int32, (BLOCK, COLUMNS), 1)
                seen = (column > token) & (column <= token + WINDOW) & (column >= oldest - b * BLOCK)
                seen = (seen & (column < SPAN)) | ((column >= SPAN) & (column < SPAN + SINKS))
                bias = jnp.where(seen, 0.0, NEG)
                weights, sums = [], []
                for g in range(QH // KVH):
                    score = scores[g * BLOCK : (g + 1) * BLOCK] * factor + bias
                    weight = jnp.exp(score - jnp.max(score, axis=1, keepdims=True))
                    sums.append(jnp.sum(weight, axis=1, keepdims=True))
                    weights.append(weight.astype(jnp.bfloat16))
                mixed = jnp.dot(
                    jnp.concatenate(weights, axis=0), values, preferred_element_type=jnp.float32
                )
                for g in range(QH // KVH):
                    result = mixed[g * BLOCK : (g + 1) * BLOCK] / sums[g]
                    lanes = slice(g * HD, (g + 1) * HD)
                    if resuming:
                        index = lax.broadcasted_iota(jnp.int32, (BLOCK, HD), 0) + b * BLOCK
                        before = out_ref[tokens, lanes].astype(jnp.float32)
                        result = jnp.where(index >= r, result, before)
                    out_ref[tokens, lanes] = result.astype(jnp.bfloat16)

    one_session(opening, history_refs[0:4], history_refs[4:8], False, r > 0)
    one_session(closing, history_refs[8:12], history_refs[12:], True, r >= 0)


def attend(meta, queries, bands, pieces, half, sink_keys, sink_values):
    chips = pieces[0].shape[0]
    share = WINDOW // (4 * chips)
    lanes = QH // KVH * HD

    def history_spec(which, last):
        def index(j, *m):
            known = Scalars(*m)
            session = known.session_at(known.place * TOK + (TOK - 1 if last else 0))
            session = session - (known.place >= half).astype(jnp.int32)
            return (0, (which * 2 + session) * KVH + j, 0)

        return pl.BlockSpec((chips, share, HD), index)

    pad = SEQS, COLUMNS - SPAN, HD
    return pl.pallas_call(
        scalars(attend_kernel),
        out_shape=jax.ShapeDtypeStruct((TOK, QH * HD), jnp.bfloat16),
        grid_spec=pltpu.PrefetchScalarGridSpec(
            num_scalar_prefetch=1,
            grid=(KVH,),
            in_specs=[pl.BlockSpec((TOK, lanes), lambda j, *m: (0, j))]
            + [pl.BlockSpec((2, TOK, HD), lambda j, *m: (0, 0, j))] * (REACH + 1)
            + [history_spec(0, False)] * 4
            + [history_spec(1, False)] * 4
            + [history_spec(0, True)] * 4
            + [history_spec(1, True)] * 4
            + [pl.BlockSpec(pad, lambda j, *m: (0, 0, j))] * 2,
            out_specs=pl.BlockSpec((TOK, lanes), lambda j, *m: (0, j)),
            scratch_shapes=[
                pltpu.VMEM(((REACH + 1) * TOK, HD), jnp.bfloat16),
                pltpu.VMEM(((REACH + 1) * TOK, HD), jnp.bfloat16),
            ],
        ),
        compiler_params=params(),
        cost_estimate=pl.CostEstimate(
            flops=16 * TOK * QH * COLUMNS * HD, bytes_accessed=8 << 20,
            transcendentals=2 * TOK * QH * COLUMNS,
        ),
        name="attend",
    )(
        meta, queries, *bands, *pieces, *pieces, *pieces, *pieces, sink_keys, sink_values
    )


def shifted(block, axis, distance):
    devices = range(lax.axis_size(axis))
    return lax.ppermute(block, axis, [(i - distance, i) for i in devices if i - distance in devices])


def shards(
    mamba_input,
    step_size,
    decay_log,
    state_write,
    state_read,
    skip_gain,
    saved_states,
    home_slot,
    turn_lengths,
    history_lengths,
    queries,
    turn_keys,
    turn_values,
    cache_keys,
    cache_values,
    sink_keys,
    sink_values,
):
    place = lax.axis_index("ctx")
    group = lax.axis_index("sess")
    groups = lax.axis_size("sess")
    devices = lax.axis_size("ctx")
    local = saved_states.shape[2]
    width = local * N
    chips = devices // 2
    same_core = [list(range(core, devices, 2)) for core in range(2)]
    meta = jnp.concatenate(
        [jnp.stack([place, group]).astype(jnp.int32), turn_lengths[0], history_lengths[0], home_slot]
    )
    x, rates, steps = mamba_input[0], decay_log[0].T, step_size[0].T
    writes, reads = state_write[0], state_read[0]
    shape = (chips, width, P_SIZE)

    def apart(block, distance):
        return lax.ppermute(block, "ctx", [(i, i ^ distance) for i in range(devices)])

    def exchanged(block):
        return lax.all_to_all(block, "ctx", 0, 0, axis_index_groups=same_core, tiled=True)

    parcel = (1, 4 * KVH * cache_keys.shape[2], HD)
    near, away = whole(
        scalars(history_kernel, devices // 2),
        "history",
        meta,
        [cache_keys[0], cache_values[0]],
        [(parcel, jnp.bfloat16), (parcel, jnp.bfloat16)],
    )
    first = apart(away, devices // 2)

    keep, send = summaries(meta, x, rates, steps, writes, local, away)
    got = apart(send, 1)

    [turned] = whole(
        scalars(turn_kernel, local),
        "turn",
        meta,
        [saved_states[0].reshape(SEQS, local, P_SIZE, N)],
        [((SEQS, width, P_SIZE), jnp.float32)],
        idle=[send],
    )
    stored = [turned]
    for j in range(1, groups):
        route = [((i + j) % groups, i) for i in range(groups)]
        stored.append(lax.ppermute(turned, "sess", route))

    [chip] = whole(
        scalars(combine_kernel, local),
        "combine",
        meta,
        [keep, got],
        [(keep.shape, jnp.bfloat16)],
        idle=[turned],
    )
    total = exchanged(chip)

    def join(left, right, after):
        joined = (2 * left.shape[0], *left.shape[1:])
        return whole(scalars(join_kernel), "join", meta, [left, right], [(joined, jnp.bfloat16)], idle=[after])[0]

    near = join(near, first, chip)
    distance = devices // 4
    moved = apart(near, distance)
    part = intra(meta, skip_gain, x, rates, steps, writes, reads, near)
    band = (2, TOK, KVH * HD)
    [key_value] = whole(
        scalars(stack_kernel), "stack", meta, [turn_keys[0], turn_values[0]], [(band, jnp.bfloat16)], idle=[part]
    )
    four = shifted(key_value, "ctx", 4)
    resumed, restored = whole(
        scalars(restore_kernel, groups),
        "restore",
        meta,
        stored,
        [(shape, jnp.bfloat16), ((SEQS, width, P_SIZE), jnp.float32)],
        idle=[part],
    )
    mine = exchanged(resumed)
    while distance > 2:
        near = join(near, moved, resumed)
        distance //= 2
        moved = apart(near, distance)
    beside = moved
    pieces = [near, beside, apart(near, 1), apart(beside, 1)]

    [entering] = whole(
        scalars(recurrence_kernel, local),
        "recurrence",
        meta,
        [total, restored],
        [(shape, jnp.bfloat16)],
        idle=[near],
    )
    theirs = apart(mine, 1)

    [two] = whole(
        scalars(two_kernel), "two", meta, [key_value, four], [(band, jnp.bfloat16)], idle=[entering]
    )
    two = apart(two, 2)
    [pair] = whole(
        scalars(pair_kernel), "pair", meta, [key_value, two, four], [((2, *band), jnp.bfloat16)]
    )
    pair = apart(pair, 1)
    bands = [four, pair[1], two, pair[0], key_value]
    sinks = [
        jnp.pad(s[0], ((0, 0), (0, COLUMNS - SPAN - SINKS), (0, 0))) for s in (sink_keys, sink_values)
    ]
    attended = attend(meta, queries[0], bands, pieces, devices // 2, *sinks)
    entering = exchanged(entering)
    own, other = whole(
        scalars(middle_kernel, local),
        "middle",
        meta,
        [entering, keep, got, mine],
        [(shape, jnp.bfloat16), (shape, jnp.bfloat16)],
        4,
        idle=[attended],
    )
    other = apart(other, 1)
    mixed = finish(meta, part, rates, steps, reads, own, other, mine, theirs, local)
    return mixed[None], attended[None]


def solution(mesh):
    token = P("sess", "ctx", None)
    return jax.shard_map(
        shards,
        mesh=mesh,
        in_specs=(
            token,
            token,
            token,
            token,
            token,
            P(),
            P("sess", None, "ctx", None),
            P(),
            P("sess", None),
            P("sess", None),
            token,
            token,
            token,
            P("sess", None, "ctx", None),
            P("sess", None, "ctx", None),
            P("sess", None, None, None),
            P("sess", None, None, None),
        ),
        out_specs=(token, token),
        check_vma=False,
    )
```

```python
import math

import jax
import jax.numpy as jnp
from jax import lax
from jax.experimental import pallas as pl
from jax.experimental.pallas import tpu as pltpu
from jax.sharding import PartitionSpec as P

REACH = 4
SEQS = 3
SINKS = 4
H = 64
P_SIZE = 128
N = 64
G = 8
QH = 32
KVH = 4
HD = 128
WINDOW = 512
TOK = 128

HEADS_PER = H // G
PAIR = 2 * HEADS_PER
STEPS = H // PAIR
EXTRA = 16
BLOCK = 64
SPAN = WINDOW + BLOCK
COLUMNS = SPAN + 64
NEG = -1e30
FREE = pl.CostEstimate(flops=1024, bytes_accessed=1024, transcendentals=0)


class Scalars:
    def __init__(self, ids):
        self.place, self.group = ids[0], ids[1]
        self.one = ids[2]
        self.two = ids[2] + ids[3]
        self.ids = ids
        self.even = self.place % 2 == 0

    def history(self, session):
        return self.ids[2 + SEQS + session]

    def home(self, number):
        return self.ids[2 + 2 * SEQS + number]

    def session_at(self, position):
        return (position >= self.one).astype(jnp.int32) + (position >= self.two).astype(jnp.int32)

    def start_of(self, session):
        return jnp.where(session == 0, 0, jnp.where(session == 1, self.one, self.two))

    def last_start(self):
        first = self.place * TOK
        return jnp.maximum(self.start_of(self.session_at(first + TOK - 1)) - first, 0)


def scalars(kernel, *options):
    def body(ids, *refs):
        kernel(*options, Scalars(ids), *refs)

    return body


def params(mib=60):
    return pltpu.CompilerParams(vmem_limit_bytes=mib * 1024 * 1024)


def running_rows(dl_ref):
    k = lax.broadcasted_iota(jnp.int32, (TOK, TOK), 0)
    u = lax.broadcasted_iota(jnp.int32, (TOK, TOK), 1)
    upto = (k <= u).astype(jnp.bfloat16)
    running = jnp.dot(dl_ref[...], upto, preferred_element_type=jnp.float32)
    return dl_ref[...].astype(jnp.float32), running


def summary_kernel(
    local, meta, x_ref, dl_ref, step_ref, write_ref, _, keep_ref, send_ref, coef_s, factor_s, write_s
):
    step = pl.program_id(0)

    @pl.when(step == 0)
    def _():
        rates, running = running_rows(dl_ref)
        steps = step_ref[...].astype(jnp.float32)
        r = meta.last_start()
        lane = lax.broadcasted_iota(jnp.int32, (H, TOK), 1)
        last = running[:, TOK - 1 :]
        base = jnp.sum(jnp.where(lane < r, rates, 0.0), axis=1, keepdims=True)
        coef_s[...] = jnp.where(lane >= r, jnp.exp(last - running) * steps, 0.0)
        factor_s[...] = jnp.broadcast_to(jnp.exp(last - base), (H, TOK))
        write_s[...] = write_ref[...].astype(jnp.float32).T

    even = meta.even
    coef = coef_s[pl.ds(pl.multiple_of(step * PAIR, PAIR), PAIR), :]
    factor = factor_s[pl.ds(pl.multiple_of(step * PAIR, PAIR), PAIR), :]
    writes = write_s[pl.ds(pl.multiple_of(step * 2 * N, 2 * N), 2 * N), :]

    def summary(k):
        group = k // HEADS_PER
        loading = (writes[group * N : (group + 1) * N] * coef[k : k + 1]).astype(jnp.bfloat16)
        return jnp.dot(
            loading, x_ref[:, k * P_SIZE : (k + 1) * P_SIZE], preferred_element_type=jnp.float32
        )

    for chip in range(PAIR // (2 * local)):
        low, high = 2 * local * chip, 2 * local * chip + local
        for k in range(local):
            first, second = summary(low + k), summary(high + k)
            rows = slice(k * N, (k + 1) * N)
            keep_ref[chip, rows, :] = jnp.where(even, first, second).astype(jnp.bfloat16)
            send_ref[chip, rows, :] = jnp.where(even, second, first).astype(jnp.bfloat16)
        first, second = factor[low : low + local], factor[high : high + local]
        keep_ref[chip, local * N :, :] = factor_rows(jnp.where(even, first, second))
        send_ref[chip, local * N :, :] = factor_rows(jnp.where(even, second, first))


def factor_rows(rows):
    high = rows.astype(jnp.bfloat16).astype(jnp.float32)
    parts = [high, rows - high]
    if EXTRA > 2 * rows.shape[0]:
        parts.append(jnp.zeros((EXTRA - 2 * rows.shape[0], TOK), jnp.float32))
    return jnp.concatenate(parts, axis=0).astype(jnp.bfloat16)


def factors_of(block, local):
    block = block.astype(jnp.float32)
    return block[:local] + block[local : 2 * local]


def summaries(meta, x, rates, steps, writes, local, idle):
    chips = H // (2 * local)
    rows = local * N + EXTRA
    shape = jax.ShapeDtypeStruct((chips, rows, P_SIZE), jnp.bfloat16)
    spec = pl.BlockSpec((PAIR // (2 * local), rows, P_SIZE), lambda i, *m: (i, 0, 0))
    return pl.pallas_call(
        scalars(summary_kernel, local),
        out_shape=[shape, shape],
        grid_spec=pltpu.PrefetchScalarGridSpec(
            num_scalar_prefetch=1,
            grid=(STEPS,),
            in_specs=[
                pl.BlockSpec((TOK, PAIR * P_SIZE), lambda i, *m: (0, i)),
                pl.BlockSpec((H, TOK), lambda i, *m: (0, 0)),
                pl.BlockSpec((H, TOK), lambda i, *m: (0, 0)),
                pl.BlockSpec((TOK, G * N), lambda i, *m: (0, 0)),
                pl.BlockSpec(memory_space=pl.ANY),
            ],
            out_specs=[spec, spec],
            scratch_shapes=[
                pltpu.VMEM((H, TOK), jnp.float32),
                pltpu.VMEM((H, TOK), jnp.float32),
                pltpu.VMEM((G * N, TOK), jnp.float32),
            ],
        ),
        compiler_params=params(),
        cost_estimate=FREE,
        name="summaries",
    )(meta, x, rates, steps, writes, idle)


def idle_spec(array):
    return pl.BlockSpec(memory_space=pltpu.HBM if array.size >= 1 << 19 else pl.ANY)


def whole(kernel, name, meta, arrays, shapes, idle=(), mib=16):
    def spec(shape):
        return pl.BlockSpec(shape, lambda i, *m: (0,) * len(shape))

    return pl.pallas_call(
        kernel,
        out_shape=[jax.ShapeDtypeStruct(s, t) for s, t in shapes],
        grid_spec=pltpu.PrefetchScalarGridSpec(
            num_scalar_prefetch=1,
            grid=(1,),
            in_specs=[spec(a.shape) for a in arrays] + [idle_spec(a) for a in idle],
            out_specs=[spec(s) for s, _ in shapes],
        ),
        compiler_params=params(mib),
        cost_estimate=FREE,
        name=name,
    )(meta, *arrays, *idle)


def history_kernel(half, meta, keys_ref, values_ref, home_ref, away_ref):
    rows = keys_ref.shape[1]
    upper = (meta.place >= half).astype(jnp.int32)
    for out_ref, first in ((home_ref, upper), (away_ref, 1 - upper)):
        for which, ref in enumerate((keys_ref, values_ref)):
            for s in range(2):
                for j in range(KVH):
                    place = ((which * 2 + s) * KVH + j) * rows
                    out_ref[0, place : place + rows, :] = ref[first + s, :, j * HD : (j + 1) * HD]


def turn_kernel(local, meta, stored_ref, *refs):
    out_ref = refs[-1]
    for s in range(SEQS):
        for k in range(local):
            out_ref[s, k * N : (k + 1) * N, :] = stored_ref[s, k].T


def restore_kernel(groups, meta, *refs):
    stored, restored_ref = refs[:groups], refs[-1]
    for s in range(SEQS):
        slot = meta.home(meta.group * SEQS + s)
        source = (slot // SEQS - meta.group + groups) % groups
        state = stored[0][slot % SEQS]
        for j in range(1, groups):
            state = jnp.where(source == j, stored[j][slot % SEQS], state)
        restored_ref[s] = state


def join_kernel(meta, first_ref, second_ref, *refs):
    out_ref = refs[-1]
    count = first_ref.shape[0]
    out_ref[:count] = first_ref[...]
    out_ref[count:] = second_ref[...]


def two_kernel(meta, key_value_ref, four_ref, *refs):
    refs[-1][...] = jnp.where(meta.place // 2 % 2 == 0, key_value_ref[...], four_ref[...])


def pair_kernel(meta, key_value_ref, two_ref, four_ref, *refs):
    out_ref = refs[-1]
    key_value, two, four = key_value_ref[...], two_ref[...], four_ref[...]
    out_ref[0] = jnp.where(meta.even, key_value, two)
    out_ref[1] = jnp.where(meta.even, two, four)


def stack_kernel(meta, keys_ref, values_ref, *refs):
    refs[-1][0] = keys_ref[...]
    refs[-1][1] = values_ref[...]


def far_place(distance, bits):
    place = distance * 0
    for k in range(bits):
        place = place + ((distance // (1 << k)) % 2) * (1 << (bits - 1 - k))
    return place


def combine_kernel(local, meta, keep_ref, got_ref, *refs):
    out_ref = refs[-1]
    even = meta.even
    second = (meta.place // 2 * 2 + 1) * TOK
    closes = meta.start_of(meta.session_at(second + TOK - 1)) >= second
    width = local * N
    for chip in range(keep_ref.shape[0]):
        keep = factors_of(keep_ref[chip, width:, :], local)
        got = factors_of(got_ref[chip, width:, :], local)
        f0, f1 = jnp.where(even, keep, got), jnp.where(even, got, keep)
        out_ref[chip, width:, :] = factor_rows(jnp.where(closes, f1, f0 * f1))
        carry = jnp.where(closes, 0.0, f1)
        for k in range(local):
            rows = slice(k * N, (k + 1) * N)
            keep = keep_ref[chip, rows, :].astype(jnp.float32)
            got = got_ref[chip, rows, :].astype(jnp.float32)
            s0, s1 = jnp.where(even, keep, got), jnp.where(even, got, keep)
            out_ref[chip, rows, :] = (carry[k : k + 1] * s0 + s1).astype(jnp.bfloat16)


def recurrence_kernel(local, meta, got_ref, restored_ref, *refs):
    out_ref = refs[-1]
    width = local * N
    span = 2 * TOK
    state = [jnp.zeros((N, P_SIZE), jnp.float32) for _ in range(local)]
    for c in range(got_ref.shape[0]):
        first = c * span
        opening = meta.session_at(first)
        closing = meta.session_at(first + span - 1)
        opens = meta.start_of(opening) >= first
        closes = meta.start_of(closing) >= first
        factor = factors_of(got_ref[c, width:, :], local)
        for k in range(local):
            rows = slice(k * N, (k + 1) * N)
            entering = jnp.where(opens, restored_ref[opening, rows, :], state[k])
            out_ref[c, rows, :] = entering.astype(jnp.bfloat16)
            resumed = restored_ref[closing, rows, :]
            out_ref[c, width + k * N : width + (k + 1) * N, :] = resumed.astype(jnp.bfloat16)
            source = jnp.where(closes, resumed, state[k])
            state[k] = factor[k : k + 1] * source + got_ref[c, rows, :].astype(jnp.float32)


def middle_kernel(local, meta, entering_ref, keep_ref, got_ref, *refs):
    even = meta.even
    first = meta.place // 2 * 2 * TOK
    second = first + TOK
    start = meta.start_of(meta.session_at(second + TOK - 1))
    closes = (start > first) & (start < second)
    opens = start == second
    width = local * N
    own_ref, send_ref = refs[-2:]
    for chip in range(entering_ref.shape[0]):
        f0 = jnp.where(
            even,
            factors_of(keep_ref[chip, width:, :], local),
            factors_of(got_ref[chip, width:, :], local),
        )
        resumed = entering_ref[chip, width:, :].astype(jnp.float32)
        own_ref[chip, width:, :] = entering_ref[chip, width:, :]
        send_ref[chip, width:, :] = entering_ref[chip, width:, :]
        for k in range(local):
            rows = slice(k * N, (k + 1) * N)
            entering = entering_ref[chip, rows, :].astype(jnp.float32)
            s0 = jnp.where(
                even, keep_ref[chip, rows, :].astype(jnp.float32), got_ref[chip, rows, :].astype(jnp.float32)
            )
            middle = f0[k : k + 1] * jnp.where(closes, resumed[rows], entering) + s0
            middle = jnp.where(opens, resumed[rows], middle)
            own_ref[chip, rows, :] = jnp.where(even, entering, middle).astype(jnp.bfloat16)
            send_ref[chip, rows, :] = jnp.where(even, middle, entering).astype(jnp.bfloat16)


def intra_kernel(meta, skip, x_ref, dl_ref, step_ref, write_ref, read_ref, _, out_ref, run_s, step_s):
    step = pl.program_id(0)

    @pl.when(step == 0)
    def _():
        _, running = running_rows(dl_ref)
        run_s[...] = running
        step_s[...] = step_ref[...].astype(jnp.float32)

    heads = pl.ds(pl.multiple_of(step * PAIR, PAIR), PAIR)
    running = run_s[heads, :]
    sizes = step_s[heads, :]
    columns = running.T
    r = meta.last_start()
    t = lax.broadcasted_iota(jnp.int32, (TOK, TOK), 0)
    u = lax.broadcasted_iota(jnp.int32, (TOK, TOK), 1)
    causal = (u <= t) & ((u >= r) | (t < r))
    for group in range(2):
        part = slice(group * N, (group + 1) * N)
        products = lax.dot_general(
            read_ref[:, part], write_ref[:, part], (((1,), (1,)), ((), ())),
            preferred_element_type=jnp.float32,
        )
        products = jnp.where(causal, products, 0.0)
        for k in range(group * HEADS_PER, (group + 1) * HEADS_PER):
            difference = columns[:, k : k + 1] - running[k : k + 1]
            decay = jnp.exp(jnp.minimum(difference, 0.0))
            mixing = (products * decay * sizes[k : k + 1]).astype(jnp.bfloat16)
            place = slice(k * P_SIZE, (k + 1) * P_SIZE)
            x = x_ref[:, place]
            mixed = jnp.dot(mixing, x, preferred_element_type=jnp.float32)
            out_ref[:, place] = mixed + skip[step * PAIR + k] * x.astype(jnp.float32)


def intra(meta, skip, x, rates, steps, writes, reads, idle):
    return pl.pallas_call(
        lambda ids, *refs: intra_kernel(Scalars(ids), *refs),
        out_shape=jax.ShapeDtypeStruct((TOK, H * P_SIZE), jnp.float32),
        grid_spec=pltpu.PrefetchScalarGridSpec(
            num_scalar_prefetch=2,
            grid=(STEPS,),
            in_specs=[
                pl.BlockSpec((TOK, PAIR * P_SIZE), lambda i, *m: (0, i)),
                pl.BlockSpec((H, TOK), lambda i, *m: (0, 0)),
                pl.BlockSpec((H, TOK), lambda i, *m: (0, 0)),
                pl.BlockSpec((TOK, 2 * N), lambda i, *m: (0, i)),
                pl.BlockSpec((TOK, 2 * N), lambda i, *m: (0, i)),
                pl.BlockSpec(memory_space=pl.ANY),
            ],
            out_specs=pl.BlockSpec((TOK, PAIR * P_SIZE), lambda i, *m: (0, i)),
            scratch_shapes=[
                pltpu.VMEM((H, TOK), jnp.float32),
                pltpu.VMEM((H, TOK), jnp.float32),
            ],
        ),
        compiler_params=params(),
        cost_estimate=FREE,
        name="intra",
    )(meta, skip, x, rates, steps, writes, reads, idle)


def finish_kernel(
    local, meta, part_ref, dl_ref, step_ref, read_ref, own_ref, other_ref, out_ref, factor_s
):
    step = pl.program_id(0)
    even = meta.even
    r = meta.last_start()

    @pl.when(step == 0)
    def _():
        rates, running = running_rows(dl_ref)
        lane = lax.broadcasted_iota(jnp.int32, (H, TOK), 1)
        base = jnp.sum(jnp.where(lane < r, rates, 0.0), axis=1, keepdims=True)
        factor_s[...] = jnp.exp(jnp.minimum(running - jnp.where(lane >= r, base, 0.0), 0.0))

    factor = factor_s[pl.ds(pl.multiple_of(step * PAIR, PAIR), PAIR), :].T
    token = lax.broadcasted_iota(jnp.int32, (TOK, N), 0)
    resumed = (token >= r) & (r > 0)
    for group in range(2):
        reads = read_ref[:, group * N : (group + 1) * N].astype(jnp.float32)
        left = jnp.where(resumed, 0.0, reads)
        right = jnp.where(resumed, reads, 0.0)
        reads = jnp.concatenate([left, right], axis=1).astype(jnp.bfloat16)
        for k in range(group * HEADS_PER, (group + 1) * HEADS_PER):
            chip, half = k // (2 * local), k // local % 2
            rows = slice((k % local) * N, (k % local + 1) * N)
            own = even if half == 0 else jnp.logical_not(even)
            later = slice(rows.start + local * N, rows.stop + local * N)
            states = jnp.concatenate(
                [
                    jnp.where(own, own_ref[chip, rows, :], other_ref[chip, rows, :]),
                    jnp.where(own, own_ref[chip, later, :], other_ref[chip, later, :]),
                ],
                axis=0,
            )
            carried = jnp.dot(reads, states, preferred_element_type=jnp.float32)
            place = slice(k * P_SIZE, (k + 1) * P_SIZE)
            out_ref[:, place] = (part_ref[:, place] + factor[:, k : k + 1] * carried).astype(jnp.bfloat16)


def finish(meta, part, rates, steps, reads, own, other, local):
    chips = PAIR // (2 * local)
    width = 2 * local * N
    states = pl.BlockSpec((chips, width, P_SIZE), lambda i, *m: (i, 0, 0))
    return pl.pallas_call(
        scalars(finish_kernel, local),
        out_shape=jax.ShapeDtypeStruct((TOK, H * P_SIZE), jnp.bfloat16),
        grid_spec=pltpu.PrefetchScalarGridSpec(
            num_scalar_prefetch=1,
            grid=(STEPS,),
            in_specs=[
                pl.BlockSpec((TOK, PAIR * P_SIZE), lambda i, *m: (0, i)),
                pl.BlockSpec((H, TOK), lambda i, *m: (0, 0)),
                pl.BlockSpec((H, TOK), lambda i, *m: (0, 0)),
                pl.BlockSpec((TOK, 2 * N), lambda i, *m: (0, i)),
                states,
                states,
            ],
            out_specs=pl.BlockSpec((TOK, PAIR * P_SIZE), lambda i, *m: (0, i)),
            scratch_shapes=[pltpu.VMEM((H, TOK), jnp.float32)],
        ),
        compiler_params=params(),
        cost_estimate=FREE,
        name="finish",
    )(meta, part, rates, steps, reads, own, other)


def attend_kernel(
    meta, q_ref, band4, band3, band2, band1, band0, *refs,
):
    history_refs, (sk_ref, sv_ref, _, out_ref, key_s, value_s) = refs[:16], refs[16:]
    factor = 1.0 / math.sqrt(HD)
    first = meta.place * TOK
    r = meta.last_start()
    opening = meta.session_at(first)
    closing = meta.session_at(first + TOK - 1)
    bands = (band4, band3, band2, band1, band0)
    length = (REACH + 1) * TOK

    def one_session(session, key_refs, value_refs, resuming, needed):
        start = meta.start_of(session) - first + WINDOW
        oldest = start - WINDOW + jnp.maximum(SINKS + WINDOW - meta.history(session), 0)

        @pl.when(needed & (start > 0))
        def _():
            row = lax.broadcasted_iota(jnp.int32, (length, WINDOW), 0)
            chips, share, _ = key_refs[0].shape
            index = lax.broadcasted_iota(jnp.int32, (1, WINDOW), 1)
            piece, index = index // (WINDOW // 4), index % (WINDOW // 4)
            near, row_in = index // share, index % share
            far = far_place(near, chips.bit_length() - 1)
            device = meta.place ^ (piece // 2 + piece % 2 * 2 + far * 4)
            place = device * share + row_in
            moved = (row == place + start - WINDOW).astype(jnp.bfloat16)
            part = (WINDOW // 4, HD)
            keys = jnp.concatenate([ref[...].reshape(part) for ref in key_refs], axis=0)
            values = jnp.concatenate([ref[...].reshape(part) for ref in value_refs], axis=0)
            history = jnp.dot(
                moved, jnp.concatenate([keys, values], axis=1), preferred_element_type=jnp.float32
            )
            for i, band in enumerate(bands):
                rows = slice(i * TOK, (i + 1) * TOK)
                index = lax.broadcasted_iota(jnp.int32, (TOK, HD), 0) + i * TOK
                turn = index >= start
                key_s[rows, :] = jnp.where(
                    turn, band[0].astype(jnp.float32), history[rows, :HD]
                ).astype(jnp.bfloat16)
                value_s[rows, :] = jnp.where(
                    turn, band[1].astype(jnp.float32), history[rows, HD:]
                ).astype(jnp.bfloat16)

        @pl.when(needed & (start <= 0))
        def _():
            for i, band in enumerate(bands):
                rows = slice(i * TOK, (i + 1) * TOK)
                key_s[rows, :] = band[0]
                value_s[rows, :] = band[1]

        for b in range(TOK // BLOCK):
            inside = (b * BLOCK + BLOCK > r) if resuming else (b * BLOCK < r)

            @pl.when(needed & inside)
            def _():
                rows = slice(b * BLOCK, b * BLOCK + SPAN)
                keys = jnp.concatenate([key_s[rows, :], sk_ref[session]], axis=0)
                values = jnp.concatenate([value_s[rows, :], sv_ref[session]], axis=0)
                tokens = slice(b * BLOCK, (b + 1) * BLOCK)
                queries = jnp.concatenate(
                    [q_ref[tokens, g * HD : (g + 1) * HD] for g in range(QH // KVH)], axis=0
                )
                scores = lax.dot_general(
                    queries, keys, (((1,), (1,)), ((), ())), preferred_element_type=jnp.float32
                )
                token = lax.broadcasted_iota(jnp.int32, (BLOCK, COLUMNS), 0)
                column = lax.broadcasted_iota(jnp.int32, (BLOCK, COLUMNS), 1)
                seen = (column > token) & (column <= token + WINDOW) & (column >= oldest - b * BLOCK)
                seen = (seen & (column < SPAN)) | ((column >= SPAN) & (column < SPAN + SINKS))
                bias = jnp.where(seen, 0.0, NEG)
                weights, sums = [], []
                for g in range(QH // KVH):
                    score = scores[g * BLOCK : (g + 1) * BLOCK] * factor + bias
                    weight = jnp.exp(score - jnp.max(score, axis=1, keepdims=True))
                    sums.append(jnp.sum(weight, axis=1, keepdims=True))
                    weights.append(weight.astype(jnp.bfloat16))
                mixed = jnp.dot(
                    jnp.concatenate(weights, axis=0), values, preferred_element_type=jnp.float32
                )
                for g in range(QH // KVH):
                    result = mixed[g * BLOCK : (g + 1) * BLOCK] / sums[g]
                    lanes = slice(g * HD, (g + 1) * HD)
                    if resuming:
                        index = lax.broadcasted_iota(jnp.int32, (BLOCK, HD), 0) + b * BLOCK
                        before = out_ref[tokens, lanes].astype(jnp.float32)
                        result = jnp.where(index >= r, result, before)
                    out_ref[tokens, lanes] = result.astype(jnp.bfloat16)

    one_session(opening, history_refs[0:4], history_refs[4:8], False, r > 0)
    one_session(closing, history_refs[8:12], history_refs[12:], True, r >= 0)


def attend(meta, queries, bands, pieces, half, sink_keys, sink_values, idle):
    chips = pieces[0].shape[0]
    share = WINDOW // (4 * chips)
    lanes = QH // KVH * HD

    def history_spec(which, last):
        def index(j, *m):
            known = Scalars(*m)
            session = known.session_at(known.place * TOK + (TOK - 1 if last else 0))
            session = session - (known.place >= half).astype(jnp.int32)
            return (0, (which * 2 + session) * KVH + j, 0)

        return pl.BlockSpec((chips, share, HD), index)

    pad = SEQS, COLUMNS - SPAN, HD
    return pl.pallas_call(
        scalars(attend_kernel),
        out_shape=jax.ShapeDtypeStruct((TOK, QH * HD), jnp.bfloat16),
        grid_spec=pltpu.PrefetchScalarGridSpec(
            num_scalar_prefetch=1,
            grid=(KVH,),
            in_specs=[pl.BlockSpec((TOK, lanes), lambda j, *m: (0, j))]
            + [pl.BlockSpec((2, TOK, HD), lambda j, *m: (0, 0, j))] * (REACH + 1)
            + [history_spec(0, False)] * 4
            + [history_spec(1, False)] * 4
            + [history_spec(0, True)] * 4
            + [history_spec(1, True)] * 4
            + [pl.BlockSpec(pad, lambda j, *m: (0, 0, j))] * 2
            + [pl.BlockSpec(memory_space=pl.ANY)],
            out_specs=pl.BlockSpec((TOK, lanes), lambda j, *m: (0, j)),
            scratch_shapes=[
                pltpu.VMEM(((REACH + 1) * TOK, HD), jnp.bfloat16),
                pltpu.VMEM(((REACH + 1) * TOK, HD), jnp.bfloat16),
            ],
        ),
        compiler_params=params(),
        cost_estimate=FREE,
        name="attend",
    )(
        meta, queries, *bands, *pieces, *pieces, *pieces, *pieces, sink_keys, sink_values, idle
    )


def shifted(block, axis, distance):
    devices = range(lax.axis_size(axis))
    return lax.ppermute(block, axis, [(i - distance, i) for i in devices if i - distance in devices])


def shards(
    mamba_input,
    step_size,
    decay_log,
    state_write,
    state_read,
    skip_gain,
    saved_states,
    home_slot,
    turn_lengths,
    history_lengths,
    queries,
    turn_keys,
    turn_values,
    cache_keys,
    cache_values,
    sink_keys,
    sink_values,
):
    place = lax.axis_index("ctx")
    group = lax.axis_index("sess")
    groups = lax.axis_size("sess")
    devices = lax.axis_size("ctx")
    local = saved_states.shape[2]
    width = local * N
    chips = devices // 2
    same_core = [list(range(core, devices, 2)) for core in range(2)]
    meta = jnp.concatenate(
        [jnp.stack([place, group]).astype(jnp.int32), turn_lengths[0], history_lengths[0], home_slot]
    )
    x, rates, steps = mamba_input[0], decay_log[0].T, step_size[0].T
    writes, reads = state_write[0], state_read[0]
    def apart(block, distance):
        return lax.ppermute(block, "ctx", [(i, i ^ distance) for i in range(devices)])

    def exchanged(block):
        return lax.all_to_all(block, "ctx", 0, 0, axis_index_groups=same_core, tiled=True)

    parcel = (1, 4 * KVH * cache_keys.shape[2], HD)
    near, away = whole(
        scalars(history_kernel, devices // 2),
        "history",
        meta,
        [cache_keys[0], cache_values[0]],
        [(parcel, jnp.bfloat16), (parcel, jnp.bfloat16)],
        mib=60,
    )
    distance = devices // 2
    moved = apart(away, distance)

    keep, send = summaries(meta, x, rates, steps, writes, local, away)
    got = apart(send, 1)
    band = (2, TOK, KVH * HD)
    [key_value] = whole(
        scalars(stack_kernel),
        "stack",
        meta,
        [turn_keys[0], turn_values[0]],
        [(band, jnp.bfloat16)],
        idle=[send],
        mib=60,
    )
    four = shifted(key_value, "ctx", 4)
    [chip] = whole(
        scalars(combine_kernel, local),
        "combine",
        meta,
        [keep, got],
        [(keep.shape, jnp.bfloat16)],
        idle=[key_value],
    )
    total = exchanged(chip)

    [turned] = whole(
        scalars(turn_kernel, local),
        "turn",
        meta,
        [saved_states[0].reshape(SEQS, local, P_SIZE, N)],
        [((SEQS, width, P_SIZE), jnp.float32)],
        idle=[chip],
    )
    stored = [turned]
    for j in range(1, groups):
        route = [((i + j) % groups, i) for i in range(groups)]
        stored.append(lax.ppermute(turned, "sess", route))

    def join(left, right, after):
        joined = (2 * left.shape[0], *left.shape[1:])
        return whole(scalars(join_kernel), "join", meta, [left, right], [(joined, jnp.bfloat16)], idle=[after])[0]

    near = join(near, moved, turned)
    distance //= 2
    moved = apart(near, distance)
    [two] = whole(
        scalars(two_kernel), "two", meta, [key_value, four], [(band, jnp.bfloat16)], idle=[near]
    )
    two = apart(two, 2)
    part = intra(meta, skip_gain, x, rates, steps, writes, reads, two)
    [restored] = whole(
        scalars(restore_kernel, groups),
        "restore",
        meta,
        stored,
        [((SEQS, width, P_SIZE), jnp.float32)],
        idle=[part],
    )
    after = restored
    while distance > 2:
        near = join(near, moved, after)
        after = near
        distance //= 2
        moved = apart(near, distance)
    beside = moved
    pieces = [near, beside, apart(near, 1), apart(beside, 1)]
    [pair] = whole(
        scalars(pair_kernel), "pair", meta, [key_value, two, four], [((2, *band), jnp.bfloat16)], idle=[after]
    )
    last = pair
    pair = apart(pair, 1)
    bands = [four, pair[1], two, pair[0], key_value]

    shape = (chips, 2 * width, P_SIZE)
    [entering] = whole(
        scalars(recurrence_kernel, local),
        "recurrence",
        meta,
        [total, restored],
        [(shape, jnp.bfloat16)],
        idle=[last],
    )
    sinks = [
        jnp.pad(s[0], ((0, 0), (0, COLUMNS - SPAN - SINKS), (0, 0))) for s in (sink_keys, sink_values)
    ]
    attended = attend(meta, queries[0], bands, pieces, devices // 2, *sinks, entering)
    entering = exchanged(entering)
    own, other = whole(
        scalars(middle_kernel, local),
        "middle",
        meta,
        [entering, keep, got],
        [(shape, jnp.bfloat16), (shape, jnp.bfloat16)],
        idle=[attended],
    )
    other = apart(other, 1)
    mixed = finish(meta, part, rates, steps, reads, own, other, local)
    return mixed[None], attended[None]


def solution(mesh):
    token = P("sess", "ctx", None)
    return jax.shard_map(
        shards,
        mesh=mesh,
        in_specs=(
            token,
            token,
            token,
            token,
            token,
            P(),
            P("sess", None, "ctx", None),
            P(),
            P("sess", None),
            P("sess", None),
            token,
            token,
            token,
            P("sess", None, "ctx", None),
            P("sess", None, "ctx", None),
            P("sess", None, None, None),
            P("sess", None, None, None),
        ),
        out_specs=(token, token),
        check_vma=False,
    )
```

```python
import math

import jax
import jax.numpy as jnp
from jax import lax
from jax.experimental import pallas as pl
from jax.experimental.pallas import tpu as pltpu
from jax.sharding import PartitionSpec as P

REACH = 4
SEQS = 3
SINKS = 4
H = 64
P_SIZE = 128
N = 64
G = 8
QH = 32
KVH = 4
HD = 128
WINDOW = 512
TOK = 128

HEADS_PER = H // G
PAIR = 2 * HEADS_PER
STEPS = H // PAIR
EXTRA = 16
BLOCK = 64
SPAN = WINDOW + BLOCK
COLUMNS = SPAN + 64
NEG = -1e30
TOKEN = jax.ShapeDtypeStruct((8, 128), jnp.float32)
FREE = pl.CostEstimate(flops=1024, bytes_accessed=1024, transcendentals=0)


class Scalars:
    def __init__(self, ids, lengths, histories, homes):
        self.place, self.group = ids[0], ids[1]
        self.one = lengths[0, 0]
        self.two = lengths[0, 0] + lengths[0, 1]
        self.histories, self.homes = histories, homes
        self.even = self.place % 2 == 0

    def session_at(self, position):
        return (position >= self.one).astype(jnp.int32) + (position >= self.two).astype(jnp.int32)

    def start_of(self, session):
        return jnp.where(session == 0, 0, jnp.where(session == 1, self.one, self.two))

    def last_start(self):
        first = self.place * TOK
        return jnp.maximum(self.start_of(self.session_at(first + TOK - 1)) - first, 0)


def scalars(kernel, *options):
    def body(ids, lengths, histories, homes, *refs):
        kernel(*options, Scalars(ids, lengths, histories, homes), *refs)

    return body


def params(mib=24):
    return pltpu.CompilerParams(vmem_limit_bytes=mib * 1024 * 1024)


def running_rows(dl_ref):
    k = lax.broadcasted_iota(jnp.int32, (TOK, TOK), 0)
    u = lax.broadcasted_iota(jnp.int32, (TOK, TOK), 1)
    upto = (k <= u).astype(jnp.bfloat16)
    running = jnp.dot(dl_ref[...], upto, preferred_element_type=jnp.float32)
    return dl_ref[...].astype(jnp.float32), running


def summary_kernel(
    local, meta, x_ref, dl_ref, step_ref, write_ref, _, keep_ref, send_ref, coef_s, factor_s, write_s
):
    step = pl.program_id(0)

    @pl.when(step == 0)
    def _():
        rates, running = running_rows(dl_ref)
        steps = step_ref[...].astype(jnp.float32)
        r = meta.last_start()
        lane = lax.broadcasted_iota(jnp.int32, (H, TOK), 1)
        last = running[:, TOK - 1 :]
        base = jnp.sum(jnp.where(lane < r, rates, 0.0), axis=1, keepdims=True)
        coef_s[...] = jnp.where(lane >= r, jnp.exp(last - running) * steps, 0.0)
        factor_s[...] = jnp.broadcast_to(jnp.exp(last - base), (H, TOK))
        write_s[...] = write_ref[...].astype(jnp.float32).T

    even = meta.even
    coef = coef_s[pl.ds(pl.multiple_of(step * PAIR, PAIR), PAIR), :]
    factor = factor_s[pl.ds(pl.multiple_of(step * PAIR, PAIR), PAIR), :]
    writes = write_s[pl.ds(pl.multiple_of(step * 2 * N, 2 * N), 2 * N), :]

    def summary(k):
        group = k // HEADS_PER
        loading = (writes[group * N : (group + 1) * N] * coef[k : k + 1]).astype(jnp.bfloat16)
        return jnp.dot(
            loading, x_ref[:, k * P_SIZE : (k + 1) * P_SIZE], preferred_element_type=jnp.float32
        )

    for chip in range(PAIR // (2 * local)):
        low, high = 2 * local * chip, 2 * local * chip + local
        for k in range(local):
            first, second = summary(low + k), summary(high + k)
            rows = slice(k * N, (k + 1) * N)
            keep_ref[chip, rows, :] = jnp.where(even, first, second).astype(jnp.bfloat16)
            send_ref[chip, rows, :] = jnp.where(even, second, first).astype(jnp.bfloat16)
        first, second = factor[low : low + local], factor[high : high + local]
        keep_ref[chip, local * N :, :] = factor_rows(jnp.where(even, first, second))
        send_ref[chip, local * N :, :] = factor_rows(jnp.where(even, second, first))


def factor_rows(rows):
    high = rows.astype(jnp.bfloat16).astype(jnp.float32)
    parts = [high, rows - high]
    if EXTRA > 2 * rows.shape[0]:
        parts.append(jnp.zeros((EXTRA - 2 * rows.shape[0], TOK), jnp.float32))
    return jnp.concatenate(parts, axis=0).astype(jnp.bfloat16)


def factors_of(block, local):
    block = block.astype(jnp.float32)
    return block[:local] + block[local : 2 * local]


def summaries(meta, x, rates, steps, writes, local, idle):
    chips = H // (2 * local)
    rows = local * N + EXTRA
    shape = jax.ShapeDtypeStruct((chips, rows, P_SIZE), jnp.bfloat16)
    spec = pl.BlockSpec((PAIR // (2 * local), rows, P_SIZE), lambda i, *m: (i, 0, 0))
    return pl.pallas_call(
        scalars(summary_kernel, local),
        out_shape=[shape, shape],
        grid_spec=pltpu.PrefetchScalarGridSpec(
            num_scalar_prefetch=4,
            grid=(STEPS,),
            in_specs=[
                pl.BlockSpec((TOK, PAIR * P_SIZE), lambda i, *m: (0, i)),
                pl.BlockSpec((H, TOK), lambda i, *m: (0, 0)),
                pl.BlockSpec((H, TOK), lambda i, *m: (0, 0)),
                pl.BlockSpec((TOK, G * N), lambda i, *m: (0, 0)),
                pl.BlockSpec(memory_space=pl.ANY),
            ],
            out_specs=[spec, spec],
            scratch_shapes=[
                pltpu.VMEM((H, TOK), jnp.float32),
                pltpu.VMEM((H, TOK), jnp.float32),
                pltpu.VMEM((G * N, TOK), jnp.float32),
            ],
        ),
        compiler_params=params(),
        cost_estimate=FREE,
        name="summaries",
    )(*meta, x, rates, steps, writes, idle)


def idle_spec(array):
    return pl.BlockSpec(memory_space=pltpu.HBM if array.size >= 1 << 18 else pl.ANY)


def whole(kernel, name, meta, arrays, shapes, idle=(), mib=16):
    def spec(shape):
        return pl.BlockSpec(shape, lambda i, *m: (0,) * len(shape))

    return pl.pallas_call(
        kernel,
        out_shape=[jax.ShapeDtypeStruct(s, t) for s, t in shapes],
        grid_spec=pltpu.PrefetchScalarGridSpec(
            num_scalar_prefetch=4,
            grid=(1,),
            in_specs=[spec(a.shape) for a in arrays] + [idle_spec(a) for a in idle],
            out_specs=[spec(s) for s, _ in shapes],
        ),
        compiler_params=params(mib),
        cost_estimate=FREE,
        name=name,
    )(*meta, *arrays, *idle)


def history_kernel(half, meta, keys_ref, values_ref, home_ref, away_ref):
    rows = keys_ref.shape[1]
    upper = (meta.place >= half).astype(jnp.int32)
    for out_ref, first in ((home_ref, upper), (away_ref, 1 - upper)):
        for which, ref in enumerate((keys_ref, values_ref)):
            for s in range(2):
                for j in range(KVH):
                    place = ((which * 2 + s) * KVH + j) * rows
                    out_ref[0, place : place + rows, :] = ref[first + s, :, j * HD : (j + 1) * HD]


def turn_kernel(local, meta, stored_ref, *refs):
    out_ref = refs[-1]
    for s in range(SEQS):
        for k in range(local):
            out_ref[s, k * N : (k + 1) * N, :] = stored_ref[s, k].T


def restore_kernel(groups, meta, *refs):
    stored, restored_ref = refs[:groups], refs[-1]
    for s in range(SEQS):
        slot = meta.homes[meta.group * SEQS + s]
        source = (slot // SEQS - meta.group + groups) % groups
        state = stored[0][slot % SEQS]
        for j in range(1, groups):
            state = jnp.where(source == j, stored[j][slot % SEQS], state)
        restored_ref[s] = state


def join_kernel(meta, first_ref, second_ref, *refs):
    out_ref = refs[-1]
    count = first_ref.shape[0]
    out_ref[:count] = first_ref[...]
    out_ref[count:] = second_ref[...]


def two_kernel(meta, key_value_ref, four_ref, *refs):
    refs[-1][...] = jnp.where(meta.place // 2 % 2 == 0, key_value_ref[...], four_ref[...])


def pair_kernel(meta, key_value_ref, two_ref, four_ref, *refs):
    out_ref = refs[-1]
    key_value, two, four = key_value_ref[...], two_ref[...], four_ref[...]
    out_ref[0] = jnp.where(meta.even, key_value, two)
    out_ref[1] = jnp.where(meta.even, two, four)


def stack_kernel(meta, keys_ref, values_ref, *refs):
    refs[-1][0] = keys_ref[...]
    refs[-1][1] = values_ref[...]


def far_place(distance, bits):
    place = distance * 0
    for k in range(bits):
        place = place + ((distance // (1 << k)) % 2) * (1 << (bits - 1 - k))
    return place


def combine_kernel(local, meta, keep_ref, got_ref, *refs):
    out_ref = refs[-1]
    even = meta.even
    second = (meta.place // 2 * 2 + 1) * TOK
    closes = meta.start_of(meta.session_at(second + TOK - 1)) >= second
    width = local * N
    for chip in range(keep_ref.shape[0]):
        keep = factors_of(keep_ref[chip, width:, :], local)
        got = factors_of(got_ref[chip, width:, :], local)
        f0, f1 = jnp.where(even, keep, got), jnp.where(even, got, keep)
        out_ref[chip, width:, :] = factor_rows(jnp.where(closes, f1, f0 * f1))
        carry = jnp.where(closes, 0.0, f1)
        for k in range(local):
            rows = slice(k * N, (k + 1) * N)
            keep = keep_ref[chip, rows, :].astype(jnp.float32)
            got = got_ref[chip, rows, :].astype(jnp.float32)
            s0, s1 = jnp.where(even, keep, got), jnp.where(even, got, keep)
            out_ref[chip, rows, :] = (carry[k : k + 1] * s0 + s1).astype(jnp.bfloat16)


def recurrence_kernel(local, meta, got_ref, restored_ref, *refs):
    out_ref = refs[-1]
    width = local * N
    span = 2 * TOK
    state = [jnp.zeros((N, P_SIZE), jnp.float32) for _ in range(local)]
    for c in range(got_ref.shape[0]):
        first = c * span
        opening = meta.session_at(first)
        closing = meta.session_at(first + span - 1)
        opens = meta.start_of(opening) >= first
        closes = meta.start_of(closing) >= first
        factor = factors_of(got_ref[c, width:, :], local)
        for k in range(local):
            rows = slice(k * N, (k + 1) * N)
            entering = jnp.where(opens, restored_ref[opening, rows, :], state[k])
            out_ref[c, rows, :] = entering.astype(jnp.bfloat16)
            resumed = restored_ref[closing, rows, :]
            out_ref[c, width + k * N : width + (k + 1) * N, :] = resumed.astype(jnp.bfloat16)
            source = jnp.where(closes, resumed, state[k])
            state[k] = factor[k : k + 1] * source + got_ref[c, rows, :].astype(jnp.float32)


def middle_kernel(local, meta, entering_ref, keep_ref, got_ref, *refs):
    even = meta.even
    first = meta.place // 2 * 2 * TOK
    second = first + TOK
    start = meta.start_of(meta.session_at(second + TOK - 1))
    closes = (start > first) & (start < second)
    opens = start == second
    width = local * N
    own_ref, send_ref = refs[-2:]
    for chip in range(entering_ref.shape[0]):
        f0 = jnp.where(
            even,
            factors_of(keep_ref[chip, width:, :], local),
            factors_of(got_ref[chip, width:, :], local),
        )
        resumed = entering_ref[chip, width:, :].astype(jnp.float32)
        own_ref[chip, width:, :] = entering_ref[chip, width:, :]
        send_ref[chip, width:, :] = entering_ref[chip, width:, :]
        for k in range(local):
            rows = slice(k * N, (k + 1) * N)
            entering = entering_ref[chip, rows, :].astype(jnp.float32)
            s0 = jnp.where(
                even, keep_ref[chip, rows, :].astype(jnp.float32), got_ref[chip, rows, :].astype(jnp.float32)
            )
            middle = f0[k : k + 1] * jnp.where(closes, resumed[rows], entering) + s0
            middle = jnp.where(opens, resumed[rows], middle)
            own_ref[chip, rows, :] = jnp.where(even, entering, middle).astype(jnp.bfloat16)
            send_ref[chip, rows, :] = jnp.where(even, middle, entering).astype(jnp.bfloat16)


def intra_kernel(meta, skip, x_ref, dl_ref, step_ref, write_ref, read_ref, _, out_ref, token_ref, run_s, step_s):
    step = pl.program_id(0)

    @pl.when(step == 0)
    def _():
        _, running = running_rows(dl_ref)
        run_s[...] = running
        step_s[...] = step_ref[...].astype(jnp.float32)

    token_ref[...] = jnp.zeros_like(token_ref)
    heads = pl.ds(pl.multiple_of(step * PAIR, PAIR), PAIR)
    running = run_s[heads, :]
    sizes = step_s[heads, :]
    columns = running.T
    r = meta.last_start()
    t = lax.broadcasted_iota(jnp.int32, (TOK, TOK), 0)
    u = lax.broadcasted_iota(jnp.int32, (TOK, TOK), 1)
    causal = (u <= t) & ((u >= r) | (t < r))
    for group in range(2):
        part = slice(group * N, (group + 1) * N)
        products = lax.dot_general(
            read_ref[:, part], write_ref[:, part], (((1,), (1,)), ((), ())),
            preferred_element_type=jnp.float32,
        )
        products = jnp.where(causal, products, 0.0)
        for k in range(group * HEADS_PER, (group + 1) * HEADS_PER):
            difference = columns[:, k : k + 1] - running[k : k + 1]
            decay = jnp.exp(jnp.minimum(difference, 0.0))
            mixing = (products * decay * sizes[k : k + 1]).astype(jnp.bfloat16)
            place = slice(k * P_SIZE, (k + 1) * P_SIZE)
            x = x_ref[:, place]
            mixed = jnp.dot(mixing, x, preferred_element_type=jnp.float32)
            out_ref[:, place] = mixed + skip[step * PAIR + k] * x.astype(jnp.float32)


def intra(meta, skip, x, rates, steps, writes, reads, idle):
    return pl.pallas_call(
        scalars(intra_kernel),
        out_shape=[jax.ShapeDtypeStruct((TOK, H * P_SIZE), jnp.float32), TOKEN],
        grid_spec=pltpu.PrefetchScalarGridSpec(
            num_scalar_prefetch=5,
            grid=(STEPS,),
            in_specs=[
                pl.BlockSpec((TOK, PAIR * P_SIZE), lambda i, *m: (0, i)),
                pl.BlockSpec((H, TOK), lambda i, *m: (0, 0)),
                pl.BlockSpec((H, TOK), lambda i, *m: (0, 0)),
                pl.BlockSpec((TOK, 2 * N), lambda i, *m: (0, i)),
                pl.BlockSpec((TOK, 2 * N), lambda i, *m: (0, i)),
                pl.BlockSpec(memory_space=pl.ANY),
            ],
            out_specs=[
                pl.BlockSpec((TOK, PAIR * P_SIZE), lambda i, *m: (0, i)),
                pl.BlockSpec(TOKEN.shape, lambda i, *m: (0, 0)),
            ],
            scratch_shapes=[
                pltpu.VMEM((H, TOK), jnp.float32),
                pltpu.VMEM((H, TOK), jnp.float32),
            ],
        ),
        compiler_params=params(),
        cost_estimate=FREE,
        name="intra",
    )(*meta, skip, x, rates, steps, writes, reads, idle)


def finish_kernel(
    local, meta, part_ref, dl_ref, step_ref, read_ref, own_ref, other_ref, out_ref, factor_s
):
    step = pl.program_id(0)
    even = meta.even
    r = meta.last_start()

    @pl.when(step == 0)
    def _():
        rates, running = running_rows(dl_ref)
        lane = lax.broadcasted_iota(jnp.int32, (H, TOK), 1)
        base = jnp.sum(jnp.where(lane < r, rates, 0.0), axis=1, keepdims=True)
        factor_s[...] = jnp.exp(jnp.minimum(running - jnp.where(lane >= r, base, 0.0), 0.0))

    factor = factor_s[pl.ds(pl.multiple_of(step * PAIR, PAIR), PAIR), :].T
    token = lax.broadcasted_iota(jnp.int32, (TOK, N), 0)
    resumed = (token >= r) & (r > 0)
    for group in range(2):
        reads = read_ref[:, group * N : (group + 1) * N].astype(jnp.float32)
        left = jnp.where(resumed, 0.0, reads)
        right = jnp.where(resumed, reads, 0.0)
        reads = jnp.concatenate([left, right], axis=1).astype(jnp.bfloat16)
        for k in range(group * HEADS_PER, (group + 1) * HEADS_PER):
            chip, half = k // (2 * local), k // local % 2
            rows = slice((k % local) * N, (k % local + 1) * N)
            own = even if half == 0 else jnp.logical_not(even)
            later = slice(rows.start + local * N, rows.stop + local * N)
            states = jnp.concatenate(
                [
                    jnp.where(own, own_ref[chip, rows, :], other_ref[chip, rows, :]),
                    jnp.where(own, own_ref[chip, later, :], other_ref[chip, later, :]),
                ],
                axis=0,
            )
            carried = jnp.dot(reads, states, preferred_element_type=jnp.float32)
            place = slice(k * P_SIZE, (k + 1) * P_SIZE)
            out_ref[:, place] = (part_ref[:, place] + factor[:, k : k + 1] * carried).astype(jnp.bfloat16)


def finish(meta, part, rates, steps, reads, own, other, local):
    chips = PAIR // (2 * local)
    width = 2 * local * N
    states = pl.BlockSpec((chips, width, P_SIZE), lambda i, *m: (i, 0, 0))
    return pl.pallas_call(
        scalars(finish_kernel, local),
        out_shape=jax.ShapeDtypeStruct((TOK, H * P_SIZE), jnp.bfloat16),
        grid_spec=pltpu.PrefetchScalarGridSpec(
            num_scalar_prefetch=4,
            grid=(STEPS,),
            in_specs=[
                pl.BlockSpec((TOK, PAIR * P_SIZE), lambda i, *m: (0, i)),
                pl.BlockSpec((H, TOK), lambda i, *m: (0, 0)),
                pl.BlockSpec((H, TOK), lambda i, *m: (0, 0)),
                pl.BlockSpec((TOK, 2 * N), lambda i, *m: (0, i)),
                states,
                states,
            ],
            out_specs=pl.BlockSpec((TOK, PAIR * P_SIZE), lambda i, *m: (0, i)),
            scratch_shapes=[pltpu.VMEM((H, TOK), jnp.float32)],
        ),
        compiler_params=params(),
        cost_estimate=FREE,
        name="finish",
    )(*meta, part, rates, steps, reads, own, other)


def attend_kernel(
    meta, q_ref, band4, band3, band2, band1, band0, *refs,
):
    history_refs, (sk_ref, sv_ref, _, out_ref, token_ref, key_s, value_s) = refs[:16], refs[16:]
    factor = 1.0 / math.sqrt(HD)
    first = meta.place * TOK
    r = meta.last_start()
    opening = meta.session_at(first)
    closing = meta.session_at(first + TOK - 1)
    bands = (band4, band3.at[0], band2, band1.at[0], band0)
    token_ref[...] = jnp.zeros_like(token_ref)

    def sinks(ref, session):
        rows = ref[session].astype(jnp.float32)
        spare = jnp.zeros((COLUMNS - SPAN - SINKS, HD), jnp.float32)
        return jnp.concatenate([rows, spare], axis=0).astype(jnp.bfloat16)

    length = (REACH + 1) * TOK

    def one_session(session, key_refs, value_refs, resuming, needed):
        start = meta.start_of(session) - first + WINDOW
        oldest = start - WINDOW + jnp.maximum(SINKS + WINDOW - meta.histories[0, session], 0)

        @pl.when(needed & (start > 0))
        def _():
            row = lax.broadcasted_iota(jnp.int32, (length, WINDOW), 0)
            chips, share, _ = key_refs[0].shape
            index = lax.broadcasted_iota(jnp.int32, (1, WINDOW), 1)
            piece, index = index // (WINDOW // 4), index % (WINDOW // 4)
            near, row_in = index // share, index % share
            far = far_place(near, chips.bit_length() - 1)
            device = meta.place ^ (piece // 2 + piece % 2 * 2 + far * 4)
            place = device * share + row_in
            moved = (row == place + start - WINDOW).astype(jnp.bfloat16)
            part = (WINDOW // 4, HD)
            keys = jnp.concatenate([ref[...].reshape(part) for ref in key_refs], axis=0)
            values = jnp.concatenate([ref[...].reshape(part) for ref in value_refs], axis=0)
            history = jnp.dot(
                moved, jnp.concatenate([keys, values], axis=1), preferred_element_type=jnp.float32
            )
            for i, band in enumerate(bands):
                rows = slice(i * TOK, (i + 1) * TOK)
                index = lax.broadcasted_iota(jnp.int32, (TOK, HD), 0) + i * TOK
                turn = index >= start
                key_s[rows, :] = jnp.where(
                    turn, band[0].astype(jnp.float32), history[rows, :HD]
                ).astype(jnp.bfloat16)
                value_s[rows, :] = jnp.where(
                    turn, band[1].astype(jnp.float32), history[rows, HD:]
                ).astype(jnp.bfloat16)

        @pl.when(needed & (start <= 0))
        def _():
            for i, band in enumerate(bands):
                rows = slice(i * TOK, (i + 1) * TOK)
                key_s[rows, :] = band[0]
                value_s[rows, :] = band[1]

        for b in range(TOK // BLOCK):
            inside = (b * BLOCK + BLOCK > r) if resuming else (b * BLOCK < r)

            @pl.when(needed & inside)
            def _():
                rows = slice(b * BLOCK, b * BLOCK + SPAN)
                keys = jnp.concatenate([key_s[rows, :], sinks(sk_ref, session)], axis=0)
                values = jnp.concatenate([value_s[rows, :], sinks(sv_ref, session)], axis=0)
                tokens = slice(b * BLOCK, (b + 1) * BLOCK)
                queries = jnp.concatenate(
                    [q_ref[tokens, g * HD : (g + 1) * HD] for g in range(QH // KVH)], axis=0
                )
                scores = lax.dot_general(
                    queries, keys, (((1,), (1,)), ((), ())), preferred_element_type=jnp.float32
                )
                token = lax.broadcasted_iota(jnp.int32, (BLOCK, COLUMNS), 0)
                column = lax.broadcasted_iota(jnp.int32, (BLOCK, COLUMNS), 1)
                seen = (column > token) & (column <= token + WINDOW) & (column >= oldest - b * BLOCK)
                seen = (seen & (column < SPAN)) | ((column >= SPAN) & (column < SPAN + SINKS))
                bias = jnp.where(seen, 0.0, NEG)
                weights, sums = [], []
                for g in range(QH // KVH):
                    score = scores[g * BLOCK : (g + 1) * BLOCK] * factor + bias
                    weight = jnp.exp(score - jnp.max(score, axis=1, keepdims=True))
                    sums.append(jnp.sum(weight, axis=1, keepdims=True))
                    weights.append(weight.astype(jnp.bfloat16))
                mixed = jnp.dot(
                    jnp.concatenate(weights, axis=0), values, preferred_element_type=jnp.float32
                )
                for g in range(QH // KVH):
                    result = mixed[g * BLOCK : (g + 1) * BLOCK] / sums[g]
                    lanes = slice(g * HD, (g + 1) * HD)
                    if resuming:
                        index = lax.broadcasted_iota(jnp.int32, (BLOCK, HD), 0) + b * BLOCK
                        before = out_ref[tokens, lanes].astype(jnp.float32)
                        result = jnp.where(index >= r, result, before)
                    out_ref[tokens, lanes] = result.astype(jnp.bfloat16)

    one_session(opening, history_refs[0:4], history_refs[4:8], False, r > 0)
    one_session(closing, history_refs[8:12], history_refs[12:], True, r >= 0)


def attend(meta, queries, bands, pieces, half, sink_keys, sink_values, idle):
    chips = pieces[0].shape[0]
    share = WINDOW // (4 * chips)
    lanes = QH // KVH * HD

    def history_spec(which, last):
        def index(j, *m):
            known = Scalars(*m)
            session = known.session_at(known.place * TOK + (TOK - 1 if last else 0))
            session = session - (known.place >= half).astype(jnp.int32)
            return (0, (which * 2 + session) * KVH + j, 0)

        return pl.BlockSpec((chips, share, HD), index)

    def band_spec(array, number):
        if array.ndim == 3:
            return pl.BlockSpec((2, TOK, HD), lambda j, *m: (0, 0, j))
        return pl.BlockSpec((1, 2, TOK, HD), lambda j, *m: (number, 0, 0, j))

    pad = SEQS, SINKS, HD
    return pl.pallas_call(
        scalars(attend_kernel),
        out_shape=[jax.ShapeDtypeStruct((TOK, QH * HD), jnp.bfloat16), TOKEN],
        grid_spec=pltpu.PrefetchScalarGridSpec(
            num_scalar_prefetch=4,
            grid=(KVH,),
            in_specs=[pl.BlockSpec((TOK, lanes), lambda j, *m: (0, j))]
            + [band_spec(a, number) for a, number in zip(bands, (0, 1, 0, 0, 0))]
            + [history_spec(0, False)] * 4
            + [history_spec(1, False)] * 4
            + [history_spec(0, True)] * 4
            + [history_spec(1, True)] * 4
            + [pl.BlockSpec(pad, lambda j, *m: (0, 0, j))] * 2
            + [pl.BlockSpec(memory_space=pl.ANY)],
            out_specs=[
                pl.BlockSpec((TOK, lanes), lambda j, *m: (0, j)),
                pl.BlockSpec(TOKEN.shape, lambda j, *m: (0, 0)),
            ],
            scratch_shapes=[
                pltpu.VMEM(((REACH + 1) * TOK, HD), jnp.bfloat16),
                pltpu.VMEM(((REACH + 1) * TOK, HD), jnp.bfloat16),
            ],
        ),
        compiler_params=params(),
        cost_estimate=FREE,
        name="attend",
    )(
        *meta, queries, *bands, *pieces, *pieces, *pieces, *pieces, sink_keys, sink_values, idle
    )


def shifted(block, axis, distance):
    devices = range(lax.axis_size(axis))
    return lax.ppermute(block, axis, [(i - distance, i) for i in devices if i - distance in devices])


def shards(
    mamba_input,
    step_size,
    decay_log,
    state_write,
    state_read,
    skip_gain,
    saved_states,
    home_slot,
    turn_lengths,
    history_lengths,
    queries,
    turn_keys,
    turn_values,
    cache_keys,
    cache_values,
    sink_keys,
    sink_values,
):
    place = lax.axis_index("ctx")
    group = lax.axis_index("sess")
    groups = lax.axis_size("sess")
    devices = lax.axis_size("ctx")
    local = saved_states.shape[2]
    width = local * N
    chips = devices // 2
    same_core = [list(range(core, devices, 2)) for core in range(2)]
    meta = (jnp.stack([place, group]).astype(jnp.int32), turn_lengths, history_lengths, home_slot)
    x, rates, steps = mamba_input[0], decay_log[0].T, step_size[0].T
    writes, reads = state_write[0], state_read[0]
    def apart(block, distance):
        return lax.ppermute(block, "ctx", [(i, i ^ distance) for i in range(devices)])

    def exchanged(block):
        return lax.all_to_all(block, "ctx", 0, 0, axis_index_groups=same_core, tiled=True)

    parcel = (1, 4 * KVH * cache_keys.shape[2], HD)
    near, away = whole(
        scalars(history_kernel, devices // 2),
        "history",
        meta,
        [cache_keys[0], cache_values[0]],
        [(parcel, jnp.bfloat16), (parcel, jnp.bfloat16)],
        mib=24,
    )
    distance = devices // 2
    moved = apart(away, distance)

    keep, send = summaries(meta, x, rates, steps, writes, local, away)
    got = apart(send, 1)
    band = (2, TOK, KVH * HD)
    [key_value] = whole(
        scalars(stack_kernel),
        "stack",
        meta,
        [turn_keys[0], turn_values[0]],
        [(band, jnp.bfloat16)],
        idle=[send],
        mib=24,
    )
    four = shifted(key_value, "ctx", 4)

    def join(left, right, after):
        joined = (2 * left.shape[0], *left.shape[1:])
        return whole(scalars(join_kernel), "join", meta, [left, right], [(joined, jnp.bfloat16)], idle=[after])[0]

    near = join(near, moved, key_value)
    distance //= 2
    moved = apart(near, distance)
    [chip] = whole(
        scalars(combine_kernel, local),
        "combine",
        meta,
        [keep, got],
        [(keep.shape, jnp.bfloat16)],
        idle=[near],
    )
    total = exchanged(chip)

    [turned] = whole(
        scalars(turn_kernel, local),
        "turn",
        meta,
        [saved_states[0].reshape(SEQS, local, P_SIZE, N)],
        [((SEQS, width, P_SIZE), jnp.float32)],
        idle=[chip],
    )
    stored = [turned]
    for j in range(1, groups):
        route = [((i + j) % groups, i) for i in range(groups)]
        stored.append(lax.ppermute(turned, "sess", route))

    [two] = whole(
        scalars(two_kernel), "two", meta, [key_value, four], [(band, jnp.bfloat16)], idle=[turned]
    )
    after = two
    two = apart(two, 2)
    while distance > 2:
        near = join(near, moved, after)
        after = near
        distance //= 2
        moved = apart(near, distance)
    beside = moved
    part, token = intra(meta, skip_gain, x, rates, steps, writes, reads, after)
    [restored] = whole(
        scalars(restore_kernel, groups),
        "restore",
        meta,
        stored,
        [((SEQS, width, P_SIZE), jnp.float32)],
        idle=[token],
    )
    [pair] = whole(
        scalars(pair_kernel), "pair", meta, [key_value, two, four], [((2, *band), jnp.bfloat16)], idle=[restored]
    )
    pair = apart(pair, 1)
    pieces = [near, beside, apart(near, 1), apart(beside, 1)]
    bands = [four, pair, two, pair, key_value]

    shape = (chips, 2 * width, P_SIZE)
    [entering] = whole(
        scalars(recurrence_kernel, local),
        "recurrence",
        meta,
        [total, restored],
        [(shape, jnp.bfloat16)],
        idle=[pair, *pieces[2:]],
    )
    attended, token = attend(
        meta, queries[0], bands, pieces, devices // 2, sink_keys[0], sink_values[0], entering
    )
    entering = exchanged(entering)
    own, other = whole(
        scalars(middle_kernel, local),
        "middle",
        meta,
        [entering, keep, got],
        [(shape, jnp.bfloat16), (shape, jnp.bfloat16)],
        idle=[token],
    )
    other = apart(other, 1)
    mixed = finish(meta, part, rates, steps, reads, own, other, local)
    return mixed[None], attended[None]


def solution(mesh):
    token = P("sess", "ctx", None)
    return jax.shard_map(
        shards,
        mesh=mesh,
        in_specs=(
            token,
            token,
            token,
            token,
            token,
            P(),
            P("sess", None, "ctx", None),
            P(),
            P("sess", None),
            P("sess", None),
            token,
            token,
            token,
            P("sess", None, "ctx", None),
            P("sess", None, "ctx", None),
            P("sess", None, None, None),
            P("sess", None, None, None),
        ),
        out_specs=(token, token),
        check_vma=False,
    )
```

```python
import math

import jax
import jax.numpy as jnp
from jax import lax
from jax.experimental import pallas as pl
from jax.experimental.pallas import tpu as pltpu
from jax.sharding import PartitionSpec as P

REACH = 4
SEQS = 3
SINKS = 4
H = 64
P_SIZE = 128
N = 64
G = 8
QH = 32
KVH = 4
HD = 128
WINDOW = 512
TOK = 128

HEADS_PER = H // G
PAIR = 2 * HEADS_PER
STEPS = H // PAIR
EXTRA = 16
BLOCK = 64
SPAN = WINDOW + BLOCK
COLUMNS = SPAN + 64
NEG = -1e30
TOKEN = jax.ShapeDtypeStruct((8, 128), jnp.float32)
FREE = pl.CostEstimate(flops=1024, bytes_accessed=1024, transcendentals=0)


class Scalars:
    def __init__(self, ids):
        self.place, self.group = ids[0], ids[1]
        self.one = ids[2]
        self.two = ids[2] + ids[3]
        self.ids = ids
        self.even = self.place % 2 == 0

    def history(self, session):
        return self.ids[2 + SEQS + session]

    def home(self, number):
        return self.ids[2 + 2 * SEQS + number]

    def session_at(self, position):
        return (position >= self.one).astype(jnp.int32) + (position >= self.two).astype(jnp.int32)

    def start_of(self, session):
        return jnp.where(session == 0, 0, jnp.where(session == 1, self.one, self.two))

    def last_start(self):
        first = self.place * TOK
        return jnp.maximum(self.start_of(self.session_at(first + TOK - 1)) - first, 0)


def scalars(kernel, *options):
    def body(ids, *refs):
        kernel(*options, Scalars(ids), *refs)

    return body


def params(mib=60):
    return pltpu.CompilerParams(vmem_limit_bytes=mib * 1024 * 1024)


def running_rows(dl_ref):
    k = lax.broadcasted_iota(jnp.int32, (TOK, TOK), 0)
    u = lax.broadcasted_iota(jnp.int32, (TOK, TOK), 1)
    upto = (k <= u).astype(jnp.bfloat16)
    running = jnp.dot(dl_ref[...], upto, preferred_element_type=jnp.float32)
    return dl_ref[...].astype(jnp.float32), running


def summary_kernel(
    local, meta, x_ref, dl_ref, step_ref, write_ref, _, keep_ref, send_ref, coef_s, factor_s, write_s
):
    step = pl.program_id(0)

    @pl.when(step == 0)
    def _():
        rates, running = running_rows(dl_ref)
        steps = step_ref[...].astype(jnp.float32)
        r = meta.last_start()
        lane = lax.broadcasted_iota(jnp.int32, (H, TOK), 1)
        last = running[:, TOK - 1 :]
        base = jnp.sum(jnp.where(lane < r, rates, 0.0), axis=1, keepdims=True)
        coef_s[...] = jnp.where(lane >= r, jnp.exp(last - running) * steps, 0.0)
        factor_s[...] = jnp.broadcast_to(jnp.exp(last - base), (H, TOK))
        write_s[...] = write_ref[...].astype(jnp.float32).T

    even = meta.even
    coef = coef_s[pl.ds(pl.multiple_of(step * PAIR, PAIR), PAIR), :]
    factor = factor_s[pl.ds(pl.multiple_of(step * PAIR, PAIR), PAIR), :]
    writes = write_s[pl.ds(pl.multiple_of(step * 2 * N, 2 * N), 2 * N), :]

    def summary(k):
        group = k // HEADS_PER
        loading = (writes[group * N : (group + 1) * N] * coef[k : k + 1]).astype(jnp.bfloat16)
        return jnp.dot(
            loading, x_ref[:, k * P_SIZE : (k + 1) * P_SIZE], preferred_element_type=jnp.float32
        )

    for chip in range(PAIR // (2 * local)):
        low, high = 2 * local * chip, 2 * local * chip + local
        for k in range(local):
            first, second = summary(low + k), summary(high + k)
            rows = slice(k * N, (k + 1) * N)
            keep_ref[chip, rows, :] = jnp.where(even, first, second).astype(jnp.bfloat16)
            send_ref[chip, rows, :] = jnp.where(even, second, first).astype(jnp.bfloat16)
        first, second = factor[low : low + local], factor[high : high + local]
        keep_ref[chip, local * N :, :] = factor_rows(jnp.where(even, first, second))
        send_ref[chip, local * N :, :] = factor_rows(jnp.where(even, second, first))


def factor_rows(rows):
    high = rows.astype(jnp.bfloat16).astype(jnp.float32)
    parts = [high, rows - high]
    if EXTRA > 2 * rows.shape[0]:
        parts.append(jnp.zeros((EXTRA - 2 * rows.shape[0], TOK), jnp.float32))
    return jnp.concatenate(parts, axis=0).astype(jnp.bfloat16)


def factors_of(block, local):
    block = block.astype(jnp.float32)
    return block[:local] + block[local : 2 * local]


def summaries(meta, x, rates, steps, writes, local, idle):
    chips = H // (2 * local)
    rows = local * N + EXTRA
    shape = jax.ShapeDtypeStruct((chips, rows, P_SIZE), jnp.bfloat16)
    spec = pl.BlockSpec((PAIR // (2 * local), rows, P_SIZE), lambda i, *m: (i, 0, 0))
    return pl.pallas_call(
        scalars(summary_kernel, local),
        out_shape=[shape, shape],
        grid_spec=pltpu.PrefetchScalarGridSpec(
            num_scalar_prefetch=1,
            grid=(STEPS,),
            in_specs=[
                pl.BlockSpec((TOK, PAIR * P_SIZE), lambda i, *m: (0, i)),
                pl.BlockSpec((H, TOK), lambda i, *m: (0, 0)),
                pl.BlockSpec((H, TOK), lambda i, *m: (0, 0)),
                pl.BlockSpec((TOK, G * N), lambda i, *m: (0, 0)),
                pl.BlockSpec(memory_space=pl.ANY),
            ],
            out_specs=[spec, spec],
            scratch_shapes=[
                pltpu.VMEM((H, TOK), jnp.float32),
                pltpu.VMEM((H, TOK), jnp.float32),
                pltpu.VMEM((G * N, TOK), jnp.float32),
            ],
        ),
        compiler_params=params(),
        cost_estimate=FREE,
        name="summaries",
    )(meta, x, rates, steps, writes, idle)


def idle_spec(array):
    return pl.BlockSpec(memory_space=pl.ANY)


def whole(kernel, name, meta, arrays, shapes, idle=(), mib=16):
    def spec(shape):
        return pl.BlockSpec(shape, lambda i, *m: (0,) * len(shape))

    return pl.pallas_call(
        kernel,
        out_shape=[jax.ShapeDtypeStruct(s, t) for s, t in shapes],
        grid_spec=pltpu.PrefetchScalarGridSpec(
            num_scalar_prefetch=1,
            grid=(1,),
            in_specs=[spec(a.shape) for a in arrays] + [idle_spec(a) for a in idle],
            out_specs=[spec(s) for s, _ in shapes],
        ),
        compiler_params=params(mib),
        cost_estimate=FREE,
        name=name,
    )(meta, *arrays, *idle)


def pack_kernel(half, meta, keys_ref, values_ref, turn_keys_ref, turn_values_ref, home_ref, away_ref, band_ref):
    band_ref[0] = turn_keys_ref[...]
    band_ref[1] = turn_values_ref[...]
    rows = keys_ref.shape[1]
    upper = (meta.place >= half).astype(jnp.int32)
    for out_ref, first in ((home_ref, upper), (away_ref, 1 - upper)):
        for which, ref in enumerate((keys_ref, values_ref)):
            for s in range(2):
                for j in range(KVH):
                    place = ((which * 2 + s) * KVH + j) * rows
                    out_ref[0, place : place + rows, :] = ref[first + s, :, j * HD : (j + 1) * HD]


def turn_kernel(local, meta, stored_ref, *refs):
    out_ref = refs[-1]
    for s in range(SEQS):
        for k in range(local):
            out_ref[s, k * N : (k + 1) * N, :] = stored_ref[s, k].T


def restore_kernel(groups, meta, *refs):
    stored, (resumed_ref, restored_ref) = refs[:groups], refs[-2:]
    for s in range(SEQS):
        slot = meta.home(meta.group * SEQS + s)
        source = (slot // SEQS - meta.group + groups) % groups
        state = stored[0][slot % SEQS]
        for j in range(1, groups):
            state = jnp.where(source == j, stored[j][slot % SEQS], state)
        restored_ref[s] = state
    for chip in range(resumed_ref.shape[0]):
        closing = meta.session_at((chip + 1) * 2 * TOK - 1)
        resumed_ref[chip] = restored_ref[closing].astype(jnp.bfloat16)


def join_kernel(meta, first_ref, second_ref, *refs):
    out_ref = refs[-1]
    count = first_ref.shape[0]
    out_ref[:count] = first_ref[...]
    out_ref[count:] = second_ref[...]


def two_kernel(meta, key_value_ref, four_ref, *refs):
    refs[-1][...] = jnp.where(meta.place // 2 % 2 == 0, key_value_ref[...], four_ref[...])


def pair_kernel(meta, key_value_ref, two_ref, four_ref, *refs):
    out_ref = refs[-1]
    key_value, two, four = key_value_ref[...], two_ref[...], four_ref[...]
    out_ref[0] = jnp.where(meta.even, key_value, two)
    out_ref[1] = jnp.where(meta.even, two, four)


def far_place(distance, bits):
    place = distance * 0
    for k in range(bits):
        place = place + ((distance // (1 << k)) % 2) * (1 << (bits - 1 - k))
    return place


def combine_kernel(local, meta, keep_ref, got_ref, *refs):
    out_ref = refs[-1]
    even = meta.even
    second = (meta.place // 2 * 2 + 1) * TOK
    closes = meta.start_of(meta.session_at(second + TOK - 1)) >= second
    width = local * N
    for chip in range(keep_ref.shape[0]):
        keep = factors_of(keep_ref[chip, width:, :], local)
        got = factors_of(got_ref[chip, width:, :], local)
        f0, f1 = jnp.where(even, keep, got), jnp.where(even, got, keep)
        out_ref[chip, width:, :] = factor_rows(jnp.where(closes, f1, f0 * f1))
        carry = jnp.where(closes, 0.0, f1)
        for k in range(local):
            rows = slice(k * N, (k + 1) * N)
            keep = keep_ref[chip, rows, :].astype(jnp.float32)
            got = got_ref[chip, rows, :].astype(jnp.float32)
            s0, s1 = jnp.where(even, keep, got), jnp.where(even, got, keep)
            out_ref[chip, rows, :] = (carry[k : k + 1] * s0 + s1).astype(jnp.bfloat16)


def recurrence_kernel(local, meta, got_ref, restored_ref, *refs):
    out_ref, token_ref = refs[-2:]
    token_ref[...] = jnp.zeros_like(token_ref)
    width = local * N
    span = 2 * TOK
    state = [jnp.zeros((N, P_SIZE), jnp.float32) for _ in range(local)]
    for c in range(got_ref.shape[0]):
        first = c * span
        opening = meta.session_at(first)
        closing = meta.session_at(first + span - 1)
        opens = meta.start_of(opening) >= first
        closes = meta.start_of(closing) >= first
        factor = factors_of(got_ref[c, width:, :], local)
        for k in range(local):
            rows = slice(k * N, (k + 1) * N)
            entering = jnp.where(opens, restored_ref[opening, rows, :], state[k])
            out_ref[c, rows, :] = entering.astype(jnp.bfloat16)
            source = jnp.where(closes, restored_ref[closing, rows, :], state[k])
            state[k] = factor[k : k + 1] * source + got_ref[c, rows, :].astype(jnp.float32)


def middle_kernel(local, meta, entering_ref, keep_ref, got_ref, resumed_ref, *refs):
    even = meta.even
    first = meta.place // 2 * 2 * TOK
    second = first + TOK
    start = meta.start_of(meta.session_at(second + TOK - 1))
    closes = (start > first) & (start < second)
    opens = start == second
    width = local * N
    own_ref, send_ref = refs[-2:]
    for chip in range(entering_ref.shape[0]):
        f0 = jnp.where(
            even,
            factors_of(keep_ref[chip, width:, :], local),
            factors_of(got_ref[chip, width:, :], local),
        )
        resumed = resumed_ref[chip].astype(jnp.float32)
        for k in range(local):
            rows = slice(k * N, (k + 1) * N)
            entering = entering_ref[chip, rows, :].astype(jnp.float32)
            s0 = jnp.where(
                even, keep_ref[chip, rows, :].astype(jnp.float32), got_ref[chip, rows, :].astype(jnp.float32)
            )
            middle = f0[k : k + 1] * jnp.where(closes, resumed[rows], entering) + s0
            middle = jnp.where(opens, resumed[rows], middle)
            own_ref[chip, rows, :] = jnp.where(even, entering, middle).astype(jnp.bfloat16)
            send_ref[chip, rows, :] = jnp.where(even, middle, entering).astype(jnp.bfloat16)


def intra_kernel(meta, skip, x_ref, dl_ref, step_ref, write_ref, read_ref, _, out_ref, token_ref, run_s, step_s):
    step = pl.program_id(0)

    @pl.when(step == 0)
    def _():
        _, running = running_rows(dl_ref)
        run_s[...] = running
        step_s[...] = step_ref[...].astype(jnp.float32)

    token_ref[...] = jnp.zeros_like(token_ref)
    heads = pl.ds(pl.multiple_of(step * PAIR, PAIR), PAIR)
    running = run_s[heads, :]
    sizes = step_s[heads, :]
    columns = running.T
    r = meta.last_start()
    t = lax.broadcasted_iota(jnp.int32, (TOK, TOK), 0)
    u = lax.broadcasted_iota(jnp.int32, (TOK, TOK), 1)
    causal = (u <= t) & ((u >= r) | (t < r))
    for group in range(2):
        part = slice(group * N, (group + 1) * N)
        products = lax.dot_general(
            read_ref[:, part], write_ref[:, part], (((1,), (1,)), ((), ())),
            preferred_element_type=jnp.float32,
        )
        products = jnp.where(causal, products, 0.0)
        for k in range(group * HEADS_PER, (group + 1) * HEADS_PER):
            difference = columns[:, k : k + 1] - running[k : k + 1]
            decay = jnp.exp(jnp.minimum(difference, 0.0))
            mixing = (products * decay * sizes[k : k + 1]).astype(jnp.bfloat16)
            place = slice(k * P_SIZE, (k + 1) * P_SIZE)
            x = x_ref[:, place]
            mixed = jnp.dot(mixing, x, preferred_element_type=jnp.float32)
            out_ref[:, place] = mixed + skip[step * PAIR + k] * x.astype(jnp.float32)


def intra(meta, skip, x, rates, steps, writes, reads, idle):
    return pl.pallas_call(
        scalars(intra_kernel),
        out_shape=[jax.ShapeDtypeStruct((TOK, H * P_SIZE), jnp.float32), TOKEN],
        grid_spec=pltpu.PrefetchScalarGridSpec(
            num_scalar_prefetch=2,
            grid=(STEPS,),
            in_specs=[
                pl.BlockSpec((TOK, PAIR * P_SIZE), lambda i, *m: (0, i)),
                pl.BlockSpec((H, TOK), lambda i, *m: (0, 0)),
                pl.BlockSpec((H, TOK), lambda i, *m: (0, 0)),
                pl.BlockSpec((TOK, 2 * N), lambda i, *m: (0, i)),
                pl.BlockSpec((TOK, 2 * N), lambda i, *m: (0, i)),
                pl.BlockSpec(memory_space=pl.ANY),
            ],
            out_specs=[
                pl.BlockSpec((TOK, PAIR * P_SIZE), lambda i, *m: (0, i)),
                pl.BlockSpec(TOKEN.shape, lambda i, *m: (0, 0)),
            ],
            scratch_shapes=[
                pltpu.VMEM((H, TOK), jnp.float32),
                pltpu.VMEM((H, TOK), jnp.float32),
            ],
        ),
        compiler_params=params(),
        cost_estimate=FREE,
        name="intra",
    )(meta, skip, x, rates, steps, writes, reads, idle)


def finish_kernel(
    local, meta, part_ref, dl_ref, step_ref, read_ref, own_ref, other_ref, mine_ref, theirs_ref, out_ref, factor_s
):
    step = pl.program_id(0)
    even = meta.even
    r = meta.last_start()

    @pl.when(step == 0)
    def _():
        rates, running = running_rows(dl_ref)
        lane = lax.broadcasted_iota(jnp.int32, (H, TOK), 1)
        base = jnp.sum(jnp.where(lane < r, rates, 0.0), axis=1, keepdims=True)
        factor_s[...] = jnp.exp(jnp.minimum(running - jnp.where(lane >= r, base, 0.0), 0.0))

    factor = factor_s[pl.ds(pl.multiple_of(step * PAIR, PAIR), PAIR), :].T
    token = lax.broadcasted_iota(jnp.int32, (TOK, N), 0)
    resumed = (token >= r) & (r > 0)
    for group in range(2):
        reads = read_ref[:, group * N : (group + 1) * N].astype(jnp.float32)
        left = jnp.where(resumed, 0.0, reads)
        right = jnp.where(resumed, reads, 0.0)
        reads = jnp.concatenate([left, right], axis=1).astype(jnp.bfloat16)
        for k in range(group * HEADS_PER, (group + 1) * HEADS_PER):
            chip, half = k // (2 * local), k // local % 2
            rows = slice((k % local) * N, (k % local + 1) * N)
            own = even if half == 0 else jnp.logical_not(even)
            states = jnp.concatenate(
                [
                    jnp.where(own, own_ref[chip, rows, :], other_ref[chip, rows, :]),
                    jnp.where(own, mine_ref[chip, rows, :], theirs_ref[chip, rows, :]),
                ],
                axis=0,
            )
            carried = jnp.dot(reads, states, preferred_element_type=jnp.float32)
            place = slice(k * P_SIZE, (k + 1) * P_SIZE)
            out_ref[:, place] = (part_ref[:, place] + factor[:, k : k + 1] * carried).astype(jnp.bfloat16)


def finish(meta, part, rates, steps, reads, own, other, mine, theirs, local):
    chips = PAIR // (2 * local)
    width = local * N
    states = pl.BlockSpec((chips, width, P_SIZE), lambda i, *m: (i, 0, 0))
    return pl.pallas_call(
        scalars(finish_kernel, local),
        out_shape=jax.ShapeDtypeStruct((TOK, H * P_SIZE), jnp.bfloat16),
        grid_spec=pltpu.PrefetchScalarGridSpec(
            num_scalar_prefetch=1,
            grid=(STEPS,),
            in_specs=[
                pl.BlockSpec((TOK, PAIR * P_SIZE), lambda i, *m: (0, i)),
                pl.BlockSpec((H, TOK), lambda i, *m: (0, 0)),
                pl.BlockSpec((H, TOK), lambda i, *m: (0, 0)),
                pl.BlockSpec((TOK, 2 * N), lambda i, *m: (0, i)),
                states,
                states,
                states,
                states,
            ],
            out_specs=pl.BlockSpec((TOK, PAIR * P_SIZE), lambda i, *m: (0, i)),
            scratch_shapes=[pltpu.VMEM((H, TOK), jnp.float32)],
        ),
        compiler_params=params(),
        cost_estimate=FREE,
        name="finish",
    )(meta, part, rates, steps, reads, own, other, mine, theirs)


def attend_kernel(
    meta, q_ref, band4, band3, band2, band1, band0, *refs,
):
    history_refs, (sk_ref, sv_ref), (out_ref, token_ref, key_s, value_s) = refs[:16], refs[16:18], refs[-4:]
    factor = 1.0 / math.sqrt(HD)
    first = meta.place * TOK
    r = meta.last_start()
    opening = meta.session_at(first)
    closing = meta.session_at(first + TOK - 1)
    bands = (band4, band3.at[0], band2, band1.at[0], band0)
    token_ref[...] = jnp.zeros_like(token_ref)

    def sinks(ref, session):
        rows = ref[session].astype(jnp.float32)
        spare = jnp.zeros((COLUMNS - SPAN - SINKS, HD), jnp.float32)
        return jnp.concatenate([rows, spare], axis=0).astype(jnp.bfloat16)

    length = (REACH + 1) * TOK

    def one_session(session, key_refs, value_refs, resuming, needed):
        start = meta.start_of(session) - first + WINDOW
        oldest = start - WINDOW + jnp.maximum(SINKS + WINDOW - meta.history(session), 0)

        @pl.when(needed & (start > 0))
        def _():
            row = lax.broadcasted_iota(jnp.int32, (length, WINDOW), 0)
            chips, share, _ = key_refs[0].shape
            index = lax.broadcasted_iota(jnp.int32, (1, WINDOW), 1)
            piece, index = index // (WINDOW // 4), index % (WINDOW // 4)
            near, row_in = index // share, index % share
            far = far_place(near, chips.bit_length() - 1)
            device = meta.place ^ (piece // 2 + piece % 2 * 2 + far * 4)
            place = device * share + row_in
            moved = (row == place + start - WINDOW).astype(jnp.bfloat16)
            part = (WINDOW // 4, HD)
            keys = jnp.concatenate([ref[...].reshape(part) for ref in key_refs], axis=0)
            values = jnp.concatenate([ref[...].reshape(part) for ref in value_refs], axis=0)
            history = jnp.dot(
                moved, jnp.concatenate([keys, values], axis=1), preferred_element_type=jnp.float32
            )
            for i, band in enumerate(bands):
                rows = slice(i * TOK, (i + 1) * TOK)
                index = lax.broadcasted_iota(jnp.int32, (TOK, HD), 0) + i * TOK
                turn = index >= start
                key_s[rows, :] = jnp.where(
                    turn, band[0].astype(jnp.float32), history[rows, :HD]
                ).astype(jnp.bfloat16)
                value_s[rows, :] = jnp.where(
                    turn, band[1].astype(jnp.float32), history[rows, HD:]
                ).astype(jnp.bfloat16)

        @pl.when(needed & (start <= 0))
        def _():
            for i, band in enumerate(bands):
                rows = slice(i * TOK, (i + 1) * TOK)
                key_s[rows, :] = band[0]
                value_s[rows, :] = band[1]

        for b in range(TOK // BLOCK):
            inside = (b * BLOCK + BLOCK > r) if resuming else (b * BLOCK < r)

            @pl.when(needed & inside)
            def _():
                rows = slice(b * BLOCK, b * BLOCK + SPAN)
                keys = jnp.concatenate([key_s[rows, :], sinks(sk_ref, session)], axis=0)
                values = jnp.concatenate([value_s[rows, :], sinks(sv_ref, session)], axis=0)
                tokens = slice(b * BLOCK, (b + 1) * BLOCK)
                queries = jnp.concatenate(
                    [q_ref[tokens, g * HD : (g + 1) * HD] for g in range(QH // KVH)], axis=0
                )
                scores = lax.dot_general(
                    queries, keys, (((1,), (1,)), ((), ())), preferred_element_type=jnp.float32
                )
                token = lax.broadcasted_iota(jnp.int32, (BLOCK, COLUMNS), 0)
                column = lax.broadcasted_iota(jnp.int32, (BLOCK, COLUMNS), 1)
                seen = (column > token) & (column <= token + WINDOW) & (column >= oldest - b * BLOCK)
                seen = (seen & (column < SPAN)) | ((column >= SPAN) & (column < SPAN + SINKS))
                bias = jnp.where(seen, 0.0, NEG)
                weights, sums = [], []
                for g in range(QH // KVH):
                    score = scores[g * BLOCK : (g + 1) * BLOCK] * factor + bias
                    weight = jnp.exp(score - jnp.max(score, axis=1, keepdims=True))
                    sums.append(jnp.sum(weight, axis=1, keepdims=True))
                    weights.append(weight.astype(jnp.bfloat16))
                mixed = jnp.dot(
                    jnp.concatenate(weights, axis=0), values, preferred_element_type=jnp.float32
                )
                for g in range(QH // KVH):
                    result = mixed[g * BLOCK : (g + 1) * BLOCK] / sums[g]
                    lanes = slice(g * HD, (g + 1) * HD)
                    if resuming:
                        index = lax.broadcasted_iota(jnp.int32, (BLOCK, HD), 0) + b * BLOCK
                        before = out_ref[tokens, lanes].astype(jnp.float32)
                        result = jnp.where(index >= r, result, before)
                    out_ref[tokens, lanes] = result.astype(jnp.bfloat16)

    one_session(opening, history_refs[0:4], history_refs[4:8], False, r > 0)
    one_session(closing, history_refs[8:12], history_refs[12:], True, r >= 0)


def attend(meta, queries, bands, pieces, half, sink_keys, sink_values, idle):
    chips = pieces[0].shape[0]
    share = WINDOW // (4 * chips)
    lanes = QH // KVH * HD

    def history_spec(which, last):
        def index(j, *m):
            known = Scalars(*m)
            session = known.session_at(known.place * TOK + (TOK - 1 if last else 0))
            session = session - (known.place >= half).astype(jnp.int32)
            return (0, (which * 2 + session) * KVH + j, 0)

        return pl.BlockSpec((chips, share, HD), index)

    def band_spec(array, number):
        if array.ndim == 3:
            return pl.BlockSpec((2, TOK, HD), lambda j, *m: (0, 0, j))
        return pl.BlockSpec((1, 2, TOK, HD), lambda j, *m: (number, 0, 0, j))

    pad = SEQS, SINKS, HD
    return pl.pallas_call(
        scalars(attend_kernel),
        out_shape=[jax.ShapeDtypeStruct((TOK, QH * HD), jnp.bfloat16), TOKEN],
        grid_spec=pltpu.PrefetchScalarGridSpec(
            num_scalar_prefetch=1,
            grid=(KVH,),
            in_specs=[pl.BlockSpec((TOK, lanes), lambda j, *m: (0, j))]
            + [band_spec(a, number) for a, number in zip(bands, (0, 1, 0, 0, 0))]
            + [history_spec(0, False)] * 4
            + [history_spec(1, False)] * 4
            + [history_spec(0, True)] * 4
            + [history_spec(1, True)] * 4
            + [pl.BlockSpec(pad, lambda j, *m: (0, 0, j))] * 2
            + [idle_spec(a) for a in idle],
            out_specs=[
                pl.BlockSpec((TOK, lanes), lambda j, *m: (0, j)),
                pl.BlockSpec(TOKEN.shape, lambda j, *m: (0, 0)),
            ],
            scratch_shapes=[
                pltpu.VMEM(((REACH + 1) * TOK, HD), jnp.bfloat16),
                pltpu.VMEM(((REACH + 1) * TOK, HD), jnp.bfloat16),
            ],
        ),
        compiler_params=params(),
        cost_estimate=FREE,
        name="attend",
    )(
        meta, queries, *bands, *pieces, *pieces, *pieces, *pieces, sink_keys, sink_values, *idle
    )


def shifted(block, axis, distance):
    devices = range(lax.axis_size(axis))
    return lax.ppermute(block, axis, [(i - distance, i) for i in devices if i - distance in devices])


def shards(
    mamba_input,
    step_size,
    decay_log,
    state_write,
    state_read,
    skip_gain,
    saved_states,
    home_slot,
    turn_lengths,
    history_lengths,
    queries,
    turn_keys,
    turn_values,
    cache_keys,
    cache_values,
    sink_keys,
    sink_values,
):
    place = lax.axis_index("ctx")
    group = lax.axis_index("sess")
    groups = lax.axis_size("sess")
    devices = lax.axis_size("ctx")
    local = saved_states.shape[2]
    width = local * N
    chips = devices // 2
    same_core = [list(range(core, devices, 2)) for core in range(2)]
    meta = jnp.concatenate(
        [jnp.stack([place, group]).astype(jnp.int32), turn_lengths[0], history_lengths[0], home_slot]
    )
    x, rates, steps = mamba_input[0], decay_log[0].T, step_size[0].T
    writes, reads = state_write[0], state_read[0]
    shape = (chips, width, P_SIZE)

    def apart(block, distance):
        return lax.ppermute(block, "ctx", [(i, i ^ distance) for i in range(devices)])

    def exchanged(block):
        return lax.all_to_all(block, "ctx", 0, 0, axis_index_groups=same_core, tiled=True)

    parcel = (1, 4 * KVH * cache_keys.shape[2], HD)
    band = (2, TOK, KVH * HD)
    near, away, key_value = whole(
        scalars(pack_kernel, devices // 2),
        "pack",
        meta,
        [cache_keys[0], cache_values[0], turn_keys[0], turn_values[0]],
        [(parcel, jnp.bfloat16), (parcel, jnp.bfloat16), (band, jnp.bfloat16)],
        mib=60,
    )
    distance = devices // 2
    moved = apart(away, distance)
    four = shifted(key_value, "ctx", 4)

    keep, send = summaries(meta, x, rates, steps, writes, local, away)
    got = apart(send, 1)

    [turned] = whole(
        scalars(turn_kernel, local),
        "turn",
        meta,
        [saved_states[0].reshape(SEQS, local, P_SIZE, N)],
        [((SEQS, width, P_SIZE), jnp.float32)],
        idle=[send],
    )
    stored = [turned]
    for j in range(1, groups):
        route = [((i + j) % groups, i) for i in range(groups)]
        stored.append(lax.ppermute(turned, "sess", route))

    def join(left, right, after):
        joined = (2 * left.shape[0], *left.shape[1:])
        return whole(scalars(join_kernel), "join", meta, [left, right], [(joined, jnp.bfloat16)], idle=[after])[0]

    near = join(near, moved, turned)
    distance //= 2
    moved = apart(near, distance)
    [chip] = whole(
        scalars(combine_kernel, local),
        "combine",
        meta,
        [keep, got],
        [(keep.shape, jnp.bfloat16)],
        idle=[near],
    )
    total = exchanged(chip)

    resumed, restored = whole(
        scalars(restore_kernel, groups),
        "restore",
        meta,
        stored,
        [(shape, jnp.bfloat16), ((SEQS, width, P_SIZE), jnp.float32)],
        idle=[chip],
    )
    mine = exchanged(resumed)
    after = restored
    while distance > 2:
        near = join(near, moved, after)
        after = near
        distance //= 2
        moved = apart(near, distance)
    beside = moved
    [two] = whole(
        scalars(two_kernel), "two", meta, [key_value, four], [(band, jnp.bfloat16)], idle=[after]
    )
    after = two
    two = apart(two, 2)
    part, token = intra(meta, skip_gain, x, rates, steps, writes, reads, after)
    [pair] = whole(
        scalars(pair_kernel), "pair", meta, [key_value, two, four], [((2, *band), jnp.bfloat16)], idle=[token]
    )
    pair = apart(pair, 1)
    pieces = [near, beside, apart(near, 1), apart(beside, 1)]
    bands = [four, pair, two, pair, key_value]

    entering, token = whole(
        scalars(recurrence_kernel, local),
        "recurrence",
        meta,
        [total, restored],
        [(shape, jnp.bfloat16), (TOKEN.shape, TOKEN.dtype)],
        idle=[mine, pair, *pieces[2:]],
    )
    entering = exchanged(entering)
    theirs = apart(mine, 1)
    attended, token = attend(
        meta, queries[0], bands, pieces, devices // 2, sink_keys[0], sink_values[0], [token, theirs]
    )
    own, other = whole(
        scalars(middle_kernel, local),
        "middle",
        meta,
        [entering, keep, got, mine],
        [(shape, jnp.bfloat16), (shape, jnp.bfloat16)],
        idle=[token],
    )
    other = apart(other, 1)
    mixed = finish(meta, part, rates, steps, reads, own, other, mine, theirs, local)
    return mixed[None], attended[None]


def solution(mesh):
    token = P("sess", "ctx", None)
    return jax.shard_map(
        shards,
        mesh=mesh,
        in_specs=(
            token,
            token,
            token,
            token,
            token,
            P(),
            P("sess", None, "ctx", None),
            P(),
            P("sess", None),
            P("sess", None),
            token,
            token,
            token,
            P("sess", None, "ctx", None),
            P("sess", None, "ctx", None),
            P("sess", None, None, None),
            P("sess", None, None, None),
        ),
        out_specs=(token, token),
        check_vma=False,
    )
```

```python
import math

import jax
import jax.numpy as jnp
from jax import lax
from jax.experimental import pallas as pl
from jax.experimental.pallas import tpu as pltpu
from jax.sharding import PartitionSpec as P

REACH = 4
SEQS = 3
SINKS = 4
H = 64
P_SIZE = 128
N = 64
G = 8
QH = 32
KVH = 4
HD = 128
WINDOW = 512
TOK = 128

HEADS_PER = H // G
PAIR = 2 * HEADS_PER
STEPS = H // PAIR
EXTRA = 16
BLOCK = 64
SPAN = WINDOW + BLOCK
COLUMNS = SPAN + 64
NEG = -1e30
TOKEN = jax.ShapeDtypeStruct((8, 128), jnp.float32)
FREE = pl.CostEstimate(flops=1024, bytes_accessed=1024, transcendentals=0)


class Scalars:
    def __init__(self, ids):
        self.place, self.group = ids[0], ids[1]
        self.one = ids[2]
        self.two = ids[2] + ids[3]
        self.ids = ids
        self.even = self.place % 2 == 0

    def history(self, session):
        return self.ids[2 + SEQS + session]

    def home(self, number):
        return self.ids[2 + 2 * SEQS + number]

    def session_at(self, position):
        return (position >= self.one).astype(jnp.int32) + (position >= self.two).astype(jnp.int32)

    def start_of(self, session):
        return jnp.where(session == 0, 0, jnp.where(session == 1, self.one, self.two))

    def last_start(self):
        first = self.place * TOK
        return jnp.maximum(self.start_of(self.session_at(first + TOK - 1)) - first, 0)


def scalars(kernel, *options):
    def body(ids, *refs):
        kernel(*options, Scalars(ids), *refs)

    return body


def params(mib=24):
    return pltpu.CompilerParams(vmem_limit_bytes=mib * 1024 * 1024)


def running_rows(dl_ref):
    k = lax.broadcasted_iota(jnp.int32, (TOK, TOK), 0)
    u = lax.broadcasted_iota(jnp.int32, (TOK, TOK), 1)
    upto = (k <= u).astype(jnp.bfloat16)
    running = jnp.dot(dl_ref[...], upto, preferred_element_type=jnp.float32)
    return dl_ref[...].astype(jnp.float32), running


def summary_kernel(
    local, meta, x_ref, dl_ref, step_ref, write_ref, _, keep_ref, send_ref, coef_s, factor_s, write_s
):
    step = pl.program_id(0)

    @pl.when(step == 0)
    def _():
        rates, running = running_rows(dl_ref)
        steps = step_ref[...].astype(jnp.float32)
        r = meta.last_start()
        lane = lax.broadcasted_iota(jnp.int32, (H, TOK), 1)
        last = running[:, TOK - 1 :]
        base = jnp.sum(jnp.where(lane < r, rates, 0.0), axis=1, keepdims=True)
        coef_s[...] = jnp.where(lane >= r, jnp.exp(last - running) * steps, 0.0)
        factor_s[...] = jnp.broadcast_to(jnp.exp(last - base), (H, TOK))
        write_s[...] = write_ref[...].astype(jnp.float32).T

    even = meta.even
    coef = coef_s[pl.ds(pl.multiple_of(step * PAIR, PAIR), PAIR), :]
    factor = factor_s[pl.ds(pl.multiple_of(step * PAIR, PAIR), PAIR), :]
    writes = write_s[pl.ds(pl.multiple_of(step * 2 * N, 2 * N), 2 * N), :]

    def summary(k):
        group = k // HEADS_PER
        loading = (writes[group * N : (group + 1) * N] * coef[k : k + 1]).astype(jnp.bfloat16)
        return jnp.dot(
            loading, x_ref[:, k * P_SIZE : (k + 1) * P_SIZE], preferred_element_type=jnp.float32
        )

    for chip in range(PAIR // (2 * local)):
        low, high = 2 * local * chip, 2 * local * chip + local
        for k in range(local):
            first, second = summary(low + k), summary(high + k)
            rows = slice(k * N, (k + 1) * N)
            keep_ref[chip, rows, :] = jnp.where(even, first, second).astype(jnp.bfloat16)
            send_ref[chip, rows, :] = jnp.where(even, second, first).astype(jnp.bfloat16)
        first, second = factor[low : low + local], factor[high : high + local]
        keep_ref[chip, local * N :, :] = factor_rows(jnp.where(even, first, second))
        send_ref[chip, local * N :, :] = factor_rows(jnp.where(even, second, first))


def factor_rows(rows):
    high = rows.astype(jnp.bfloat16).astype(jnp.float32)
    parts = [high, rows - high]
    if EXTRA > 2 * rows.shape[0]:
        parts.append(jnp.zeros((EXTRA - 2 * rows.shape[0], TOK), jnp.float32))
    return jnp.concatenate(parts, axis=0).astype(jnp.bfloat16)


def factors_of(block, local):
    block = block.astype(jnp.float32)
    return block[:local] + block[local : 2 * local]


def summaries(meta, x, rates, steps, writes, local, idle):
    chips = H // (2 * local)
    rows = local * N + EXTRA
    shape = jax.ShapeDtypeStruct((chips, rows, P_SIZE), jnp.bfloat16)
    spec = pl.BlockSpec((PAIR // (2 * local), rows, P_SIZE), lambda i, *m: (i, 0, 0))
    return pl.pallas_call(
        scalars(summary_kernel, local),
        out_shape=[shape, shape],
        grid_spec=pltpu.PrefetchScalarGridSpec(
            num_scalar_prefetch=1,
            grid=(STEPS,),
            in_specs=[
                pl.BlockSpec((TOK, PAIR * P_SIZE), lambda i, *m: (0, i)),
                pl.BlockSpec((H, TOK), lambda i, *m: (0, 0)),
                pl.BlockSpec((H, TOK), lambda i, *m: (0, 0)),
                pl.BlockSpec((TOK, G * N), lambda i, *m: (0, 0)),
                pl.BlockSpec(memory_space=pl.ANY),
            ],
            out_specs=[spec, spec],
            scratch_shapes=[
                pltpu.VMEM((H, TOK), jnp.float32),
                pltpu.VMEM((H, TOK), jnp.float32),
                pltpu.VMEM((G * N, TOK), jnp.float32),
            ],
        ),
        compiler_params=params(60),
        cost_estimate=FREE,
        name="summaries",
    )(meta, x, rates, steps, writes, idle)


def idle_spec(array):
    return pl.BlockSpec(memory_space=pl.ANY)


def whole(kernel, name, meta, arrays, shapes, idle=(), mib=24, scratch=()):
    def spec(shape):
        return pl.BlockSpec(shape, lambda i, *m: (0,) * len(shape))

    return pl.pallas_call(
        kernel,
        out_shape=[jax.ShapeDtypeStruct(s, t) for s, t in shapes],
        grid_spec=pltpu.PrefetchScalarGridSpec(
            num_scalar_prefetch=1,
            grid=(1,),
            in_specs=[spec(a.shape) for a in arrays] + [idle_spec(a) for a in idle],
            out_specs=[spec(s) for s, _ in shapes],
            scratch_shapes=scratch,
        ),
        compiler_params=params(mib),
        cost_estimate=FREE,
        name=name,
    )(meta, *arrays, *idle)


def pack_kernel(half, meta, keys_ref, values_ref, turn_keys_ref, turn_values_ref, home_ref, away_ref, band_ref):
    band_ref[0] = turn_keys_ref[...]
    band_ref[1] = turn_values_ref[...]
    rows = keys_ref.shape[1]
    upper = (meta.place >= half).astype(jnp.int32)
    for out_ref, first in ((home_ref, upper), (away_ref, 1 - upper)):
        for which, ref in enumerate((keys_ref, values_ref)):
            for s in range(2):
                for j in range(KVH):
                    place = ((which * 2 + s) * KVH + j) * rows
                    out_ref[0, place : place + rows, :] = ref[first + s, :, j * HD : (j + 1) * HD]


def turn_kernel(local, meta, stored_ref, *refs):
    out_ref = refs[-1]
    for s in range(SEQS):
        for k in range(local):
            out_ref[s, k * N : (k + 1) * N, :] = stored_ref[s, k].T


def join_kernel(meta, first_ref, second_ref, *refs):
    out_ref = refs[-1]
    count = first_ref.shape[0]
    out_ref[:count] = first_ref[...]
    out_ref[count:] = second_ref[...]


def join_two_kernel(meta, first_ref, second_ref, key_value_ref, four_ref, *refs):
    out_ref, two_ref = refs[-2:]
    count = first_ref.shape[0]
    out_ref[:count] = first_ref[...]
    out_ref[count:] = second_ref[...]
    two_ref[...] = jnp.where(meta.place // 2 % 2 == 0, key_value_ref[...], four_ref[...])


def pair_kernel(meta, key_value_ref, two_ref, four_ref, *refs):
    out_ref = refs[-1]
    key_value, two, four = key_value_ref[...], two_ref[...], four_ref[...]
    out_ref[0] = jnp.where(meta.even, key_value, two)
    out_ref[1] = jnp.where(meta.even, two, four)


def far_place(distance, bits):
    place = distance * 0
    for k in range(bits):
        place = place + ((distance // (1 << k)) % 2) * (1 << (bits - 1 - k))
    return place


def combine_kernel(local, meta, keep_ref, got_ref, *refs):
    out_ref = refs[-1]
    even = meta.even
    second = (meta.place // 2 * 2 + 1) * TOK
    closes = meta.start_of(meta.session_at(second + TOK - 1)) >= second
    width = local * N
    for chip in range(keep_ref.shape[0]):
        keep = factors_of(keep_ref[chip, width:, :], local)
        got = factors_of(got_ref[chip, width:, :], local)
        f0, f1 = jnp.where(even, keep, got), jnp.where(even, got, keep)
        out_ref[chip, width:, :] = factor_rows(jnp.where(closes, f1, f0 * f1))
        carry = jnp.where(closes, 0.0, f1)
        for k in range(local):
            rows = slice(k * N, (k + 1) * N)
            keep = keep_ref[chip, rows, :].astype(jnp.float32)
            got = got_ref[chip, rows, :].astype(jnp.float32)
            s0, s1 = jnp.where(even, keep, got), jnp.where(even, got, keep)
            out_ref[chip, rows, :] = (carry[k : k + 1] * s0 + s1).astype(jnp.bfloat16)


def recurrence_kernel(local, groups, meta, got_ref, *refs):
    stored, (out_ref, token_ref, restored_ref) = refs[:groups], refs[-3:]
    token_ref[...] = jnp.zeros_like(token_ref)
    for s in range(SEQS):
        slot = meta.home(meta.group * SEQS + s)
        source = (slot // SEQS - meta.group + groups) % groups
        kept = stored[0][slot % SEQS]
        for j in range(1, groups):
            kept = jnp.where(source == j, stored[j][slot % SEQS], kept)
        restored_ref[s] = kept
    width = local * N
    span = 2 * TOK
    state = [jnp.zeros((N, P_SIZE), jnp.float32) for _ in range(local)]
    for c in range(got_ref.shape[0]):
        first = c * span
        opening = meta.session_at(first)
        closing = meta.session_at(first + span - 1)
        opens = meta.start_of(opening) >= first
        closes = meta.start_of(closing) >= first
        factor = factors_of(got_ref[c, width:, :], local)
        for k in range(local):
            rows = slice(k * N, (k + 1) * N)
            entering = jnp.where(opens, restored_ref[opening, rows, :], state[k])
            out_ref[c, rows, :] = entering.astype(jnp.bfloat16)
            resumed = restored_ref[closing, rows, :]
            out_ref[c, width + k * N : width + (k + 1) * N, :] = resumed.astype(jnp.bfloat16)
            source = jnp.where(closes, resumed, state[k])
            state[k] = factor[k : k + 1] * source + got_ref[c, rows, :].astype(jnp.float32)


def middle_kernel(local, meta, entering_ref, keep_ref, got_ref, *refs):
    even = meta.even
    first = meta.place // 2 * 2 * TOK
    second = first + TOK
    start = meta.start_of(meta.session_at(second + TOK - 1))
    closes = (start > first) & (start < second)
    opens = start == second
    width = local * N
    own_ref, send_ref = refs[-2:]
    for chip in range(entering_ref.shape[0]):
        f0 = jnp.where(
            even,
            factors_of(keep_ref[chip, width:, :], local),
            factors_of(got_ref[chip, width:, :], local),
        )
        resumed = entering_ref[chip, width:, :].astype(jnp.float32)
        own_ref[chip, width:, :] = entering_ref[chip, width:, :]
        send_ref[chip, width:, :] = entering_ref[chip, width:, :]
        for k in range(local):
            rows = slice(k * N, (k + 1) * N)
            entering = entering_ref[chip, rows, :].astype(jnp.float32)
            s0 = jnp.where(
                even, keep_ref[chip, rows, :].astype(jnp.float32), got_ref[chip, rows, :].astype(jnp.float32)
            )
            middle = f0[k : k + 1] * jnp.where(closes, resumed[rows], entering) + s0
            middle = jnp.where(opens, resumed[rows], middle)
            own_ref[chip, rows, :] = jnp.where(even, entering, middle).astype(jnp.bfloat16)
            send_ref[chip, rows, :] = jnp.where(even, middle, entering).astype(jnp.bfloat16)


def intra_kernel(meta, skip, x_ref, dl_ref, step_ref, write_ref, read_ref, _, out_ref, token_ref, run_s, step_s):
    step = pl.program_id(0)

    @pl.when(step == 0)
    def _():
        _, running = running_rows(dl_ref)
        run_s[...] = running
        step_s[...] = step_ref[...].astype(jnp.float32)

    token_ref[...] = jnp.zeros_like(token_ref)
    heads = pl.ds(pl.multiple_of(step * PAIR, PAIR), PAIR)
    running = run_s[heads, :]
    sizes = step_s[heads, :]
    columns = running.T
    r = meta.last_start()
    t = lax.broadcasted_iota(jnp.int32, (TOK, TOK), 0)
    u = lax.broadcasted_iota(jnp.int32, (TOK, TOK), 1)
    causal = (u <= t) & ((u >= r) | (t < r))
    for group in range(2):
        part = slice(group * N, (group + 1) * N)
        products = lax.dot_general(
            read_ref[:, part], write_ref[:, part], (((1,), (1,)), ((), ())),
            preferred_element_type=jnp.float32,
        )
        products = jnp.where(causal, products, 0.0)
        for k in range(group * HEADS_PER, (group + 1) * HEADS_PER):
            difference = columns[:, k : k + 1] - running[k : k + 1]
            decay = jnp.exp(jnp.minimum(difference, 0.0))
            mixing = (products * decay * sizes[k : k + 1]).astype(jnp.bfloat16)
            place = slice(k * P_SIZE, (k + 1) * P_SIZE)
            x = x_ref[:, place]
            mixed = jnp.dot(mixing, x, preferred_element_type=jnp.float32)
            out_ref[:, place] = mixed + skip[step * PAIR + k] * x.astype(jnp.float32)


def intra(meta, skip, x, rates, steps, writes, reads, idle):
    return pl.pallas_call(
        scalars(intra_kernel),
        out_shape=[jax.ShapeDtypeStruct((TOK, H * P_SIZE), jnp.float32), TOKEN],
        grid_spec=pltpu.PrefetchScalarGridSpec(
            num_scalar_prefetch=2,
            grid=(STEPS,),
            in_specs=[
                pl.BlockSpec((TOK, PAIR * P_SIZE), lambda i, *m: (0, i)),
                pl.BlockSpec((H, TOK), lambda i, *m: (0, 0)),
                pl.BlockSpec((H, TOK), lambda i, *m: (0, 0)),
                pl.BlockSpec((TOK, 2 * N), lambda i, *m: (0, i)),
                pl.BlockSpec((TOK, 2 * N), lambda i, *m: (0, i)),
                pl.BlockSpec(memory_space=pl.ANY),
            ],
            out_specs=[
                pl.BlockSpec((TOK, PAIR * P_SIZE), lambda i, *m: (0, i)),
                pl.BlockSpec(TOKEN.shape, lambda i, *m: (0, 0)),
            ],
            scratch_shapes=[
                pltpu.VMEM((H, TOK), jnp.float32),
                pltpu.VMEM((H, TOK), jnp.float32),
            ],
        ),
        compiler_params=params(),
        cost_estimate=FREE,
        name="intra",
    )(meta, skip, x, rates, steps, writes, reads, idle)


def finish_kernel(
    local, meta, part_ref, dl_ref, step_ref, read_ref, own_ref, other_ref, out_ref, factor_s
):
    step = pl.program_id(0)
    even = meta.even
    r = meta.last_start()

    @pl.when(step == 0)
    def _():
        rates, running = running_rows(dl_ref)
        lane = lax.broadcasted_iota(jnp.int32, (H, TOK), 1)
        base = jnp.sum(jnp.where(lane < r, rates, 0.0), axis=1, keepdims=True)
        factor_s[...] = jnp.exp(jnp.minimum(running - jnp.where(lane >= r, base, 0.0), 0.0))

    factor = factor_s[pl.ds(pl.multiple_of(step * PAIR, PAIR), PAIR), :].T
    token = lax.broadcasted_iota(jnp.int32, (TOK, N), 0)
    resumed = (token >= r) & (r > 0)
    for group in range(2):
        reads = read_ref[:, group * N : (group + 1) * N].astype(jnp.float32)
        left = jnp.where(resumed, 0.0, reads)
        right = jnp.where(resumed, reads, 0.0)
        reads = jnp.concatenate([left, right], axis=1).astype(jnp.bfloat16)
        for k in range(group * HEADS_PER, (group + 1) * HEADS_PER):
            chip, half = k // (2 * local), k // local % 2
            rows = slice((k % local) * N, (k % local + 1) * N)
            own = even if half == 0 else jnp.logical_not(even)
            later = slice(rows.start + local * N, rows.stop + local * N)
            states = jnp.concatenate(
                [
                    jnp.where(own, own_ref[chip, rows, :], other_ref[chip, rows, :]),
                    jnp.where(own, own_ref[chip, later, :], other_ref[chip, later, :]),
                ],
                axis=0,
            )
            carried = jnp.dot(reads, states, preferred_element_type=jnp.float32)
            place = slice(k * P_SIZE, (k + 1) * P_SIZE)
            out_ref[:, place] = (part_ref[:, place] + factor[:, k : k + 1] * carried).astype(jnp.bfloat16)


def finish(meta, part, rates, steps, reads, own, other, local):
    chips = PAIR // (2 * local)
    width = 2 * local * N
    states = pl.BlockSpec((chips, width, P_SIZE), lambda i, *m: (i, 0, 0))
    return pl.pallas_call(
        scalars(finish_kernel, local),
        out_shape=jax.ShapeDtypeStruct((TOK, H * P_SIZE), jnp.bfloat16),
        grid_spec=pltpu.PrefetchScalarGridSpec(
            num_scalar_prefetch=1,
            grid=(STEPS,),
            in_specs=[
                pl.BlockSpec((TOK, PAIR * P_SIZE), lambda i, *m: (0, i)),
                pl.BlockSpec((H, TOK), lambda i, *m: (0, 0)),
                pl.BlockSpec((H, TOK), lambda i, *m: (0, 0)),
                pl.BlockSpec((TOK, 2 * N), lambda i, *m: (0, i)),
                states,
                states,
            ],
            out_specs=pl.BlockSpec((TOK, PAIR * P_SIZE), lambda i, *m: (0, i)),
            scratch_shapes=[pltpu.VMEM((H, TOK), jnp.float32)],
        ),
        compiler_params=params(),
        cost_estimate=FREE,
        name="finish",
    )(meta, part, rates, steps, reads, own, other)


def attend_kernel(
    meta, q_ref, band4, band3, band2, band1, band0, *refs,
):
    history_refs, (sk_ref, sv_ref), (out_ref, token_ref, key_s, value_s) = refs[:16], refs[16:18], refs[-4:]
    factor = 1.0 / math.sqrt(HD)
    first = meta.place * TOK
    r = meta.last_start()
    opening = meta.session_at(first)
    closing = meta.session_at(first + TOK - 1)
    bands = (band4, band3.at[0], band2, band1.at[0], band0)
    token_ref[...] = jnp.zeros_like(token_ref)

    def sinks(ref, session):
        rows = ref[session].astype(jnp.float32)
        spare = jnp.zeros((COLUMNS - SPAN - SINKS, HD), jnp.float32)
        return jnp.concatenate([rows, spare], axis=0).astype(jnp.bfloat16)

    length = (REACH + 1) * TOK

    def one_session(session, key_refs, value_refs, resuming, needed):
        start = meta.start_of(session) - first + WINDOW
        oldest = start - WINDOW + jnp.maximum(SINKS + WINDOW - meta.history(session), 0)

        @pl.when(needed & (start > 0))
        def _():
            row = lax.broadcasted_iota(jnp.int32, (length, WINDOW), 0)
            chips, share, _ = key_refs[0].shape
            index = lax.broadcasted_iota(jnp.int32, (1, WINDOW), 1)
            piece, index = index // (WINDOW // 4), index % (WINDOW // 4)
            near, row_in = index // share, index % share
            far = far_place(near, chips.bit_length() - 1)
            device = meta.place ^ (piece // 2 + piece % 2 * 2 + far * 4)
            place = device * share + row_in
            moved = (row == place + start - WINDOW).astype(jnp.bfloat16)
            part = (WINDOW // 4, HD)
            keys = jnp.concatenate([ref[...].reshape(part) for ref in key_refs], axis=0)
            values = jnp.concatenate([ref[...].reshape(part) for ref in value_refs], axis=0)
            history = jnp.dot(
                moved, jnp.concatenate([keys, values], axis=1), preferred_element_type=jnp.float32
            )
            for i, band in enumerate(bands):
                rows = slice(i * TOK, (i + 1) * TOK)
                index = lax.broadcasted_iota(jnp.int32, (TOK, HD), 0) + i * TOK
                turn = index >= start
                key_s[rows, :] = jnp.where(
                    turn, band[0].astype(jnp.float32), history[rows, :HD]
                ).astype(jnp.bfloat16)
                value_s[rows, :] = jnp.where(
                    turn, band[1].astype(jnp.float32), history[rows, HD:]
                ).astype(jnp.bfloat16)

        @pl.when(needed & (start <= 0))
        def _():
            for i, band in enumerate(bands):
                rows = slice(i * TOK, (i + 1) * TOK)
                key_s[rows, :] = band[0]
                value_s[rows, :] = band[1]

        for b in range(TOK // BLOCK):
            inside = (b * BLOCK + BLOCK > r) if resuming else (b * BLOCK < r)

            @pl.when(needed & inside)
            def _():
                rows = slice(b * BLOCK, b * BLOCK + SPAN)
                keys = jnp.concatenate([key_s[rows, :], sinks(sk_ref, session)], axis=0)
                values = jnp.concatenate([value_s[rows, :], sinks(sv_ref, session)], axis=0)
                tokens = slice(b * BLOCK, (b + 1) * BLOCK)
                queries = jnp.concatenate(
                    [q_ref[tokens, g * HD : (g + 1) * HD] for g in range(QH // KVH)], axis=0
                )
                scores = lax.dot_general(
                    queries, keys, (((1,), (1,)), ((), ())), preferred_element_type=jnp.float32
                )
                token = lax.broadcasted_iota(jnp.int32, (BLOCK, COLUMNS), 0)
                column = lax.broadcasted_iota(jnp.int32, (BLOCK, COLUMNS), 1)
                seen = (column > token) & (column <= token + WINDOW) & (column >= oldest - b * BLOCK)
                seen = (seen & (column < SPAN)) | ((column >= SPAN) & (column < SPAN + SINKS))
                bias = jnp.where(seen, 0.0, NEG)
                weights, sums = [], []
                for g in range(QH // KVH):
                    score = scores[g * BLOCK : (g + 1) * BLOCK] * factor + bias
                    weight = jnp.exp(score - jnp.max(score, axis=1, keepdims=True))
                    sums.append(jnp.sum(weight, axis=1, keepdims=True))
                    weights.append(weight.astype(jnp.bfloat16))
                mixed = jnp.dot(
                    jnp.concatenate(weights, axis=0), values, preferred_element_type=jnp.float32
                )
                for g in range(QH // KVH):
                    result = mixed[g * BLOCK : (g + 1) * BLOCK] / sums[g]
                    lanes = slice(g * HD, (g + 1) * HD)
                    if resuming:
                        index = lax.broadcasted_iota(jnp.int32, (BLOCK, HD), 0) + b * BLOCK
                        before = out_ref[tokens, lanes].astype(jnp.float32)
                        result = jnp.where(index >= r, result, before)
                    out_ref[tokens, lanes] = result.astype(jnp.bfloat16)

    one_session(opening, history_refs[0:4], history_refs[4:8], False, r > 0)
    one_session(closing, history_refs[8:12], history_refs[12:], True, r >= 0)


def attend(meta, queries, bands, pieces, half, sink_keys, sink_values, idle):
    chips = pieces[0].shape[0]
    share = WINDOW // (4 * chips)
    lanes = QH // KVH * HD

    def history_spec(which, last):
        def index(j, *m):
            known = Scalars(*m)
            session = known.session_at(known.place * TOK + (TOK - 1 if last else 0))
            session = session - (known.place >= half).astype(jnp.int32)
            return (0, (which * 2 + session) * KVH + j, 0)

        return pl.BlockSpec((chips, share, HD), index)

    def band_spec(array, number):
        if array.ndim == 3:
            return pl.BlockSpec((2, TOK, HD), lambda j, *m: (0, 0, j))
        return pl.BlockSpec((1, 2, TOK, HD), lambda j, *m: (number, 0, 0, j))

    pad = SEQS, SINKS, HD
    return pl.pallas_call(
        scalars(attend_kernel),
        out_shape=[jax.ShapeDtypeStruct((TOK, QH * HD), jnp.bfloat16), TOKEN],
        grid_spec=pltpu.PrefetchScalarGridSpec(
            num_scalar_prefetch=1,
            grid=(KVH,),
            in_specs=[pl.BlockSpec((TOK, lanes), lambda j, *m: (0, j))]
            + [band_spec(a, number) for a, number in zip(bands, (0, 1, 0, 0, 0))]
            + [history_spec(0, False)] * 4
            + [history_spec(1, False)] * 4
            + [history_spec(0, True)] * 4
            + [history_spec(1, True)] * 4
            + [pl.BlockSpec(pad, lambda j, *m: (0, 0, j))] * 2
            + [idle_spec(a) for a in idle],
            out_specs=[
                pl.BlockSpec((TOK, lanes), lambda j, *m: (0, j)),
                pl.BlockSpec(TOKEN.shape, lambda j, *m: (0, 0)),
            ],
            scratch_shapes=[
                pltpu.VMEM(((REACH + 1) * TOK, HD), jnp.bfloat16),
                pltpu.VMEM(((REACH + 1) * TOK, HD), jnp.bfloat16),
            ],
        ),
        compiler_params=params(),
        cost_estimate=FREE,
        name="attend",
    )(
        meta, queries, *bands, *pieces, *pieces, *pieces, *pieces, sink_keys, sink_values, *idle
    )


def shifted(block, axis, distance):
    devices = range(lax.axis_size(axis))
    return lax.ppermute(block, axis, [(i - distance, i) for i in devices if i - distance in devices])


def shards(
    mamba_input,
    step_size,
    decay_log,
    state_write,
    state_read,
    skip_gain,
    saved_states,
    home_slot,
    turn_lengths,
    history_lengths,
    queries,
    turn_keys,
    turn_values,
    cache_keys,
    cache_values,
    sink_keys,
    sink_values,
):
    place = lax.axis_index("ctx")
    group = lax.axis_index("sess")
    groups = lax.axis_size("sess")
    devices = lax.axis_size("ctx")
    local = saved_states.shape[2]
    width = local * N
    chips = devices // 2
    same_core = [list(range(core, devices, 2)) for core in range(2)]
    meta = jnp.concatenate(
        [jnp.stack([place, group]).astype(jnp.int32), turn_lengths[0], history_lengths[0], home_slot]
    )
    x, rates, steps = mamba_input[0], decay_log[0].T, step_size[0].T
    writes, reads = state_write[0], state_read[0]
    def apart(block, distance):
        return lax.ppermute(block, "ctx", [(i, i ^ distance) for i in range(devices)])

    def exchanged(block):
        return lax.all_to_all(block, "ctx", 0, 0, axis_index_groups=same_core, tiled=True)

    parcel = (1, 4 * KVH * cache_keys.shape[2], HD)
    band = (2, TOK, KVH * HD)
    near, away, key_value = whole(
        scalars(pack_kernel, devices // 2),
        "pack",
        meta,
        [cache_keys[0], cache_values[0], turn_keys[0], turn_values[0]],
        [(parcel, jnp.bfloat16), (parcel, jnp.bfloat16), (band, jnp.bfloat16)],
        mib=60,
    )
    distance = devices // 2
    moved = apart(away, distance)
    four = shifted(key_value, "ctx", 4)

    keep, send = summaries(meta, x, rates, steps, writes, local, away)
    got = apart(send, 1)

    def joined(array):
        return ((2 * array.shape[0], *array.shape[1:]), jnp.bfloat16)

    near, two = whole(
        scalars(join_two_kernel),
        "join_two",
        meta,
        [near, moved, key_value, four],
        [joined(near), (band, jnp.bfloat16)],
        idle=[send],
    )
    distance //= 2
    moved = apart(near, distance)

    [turned] = whole(
        scalars(turn_kernel, local),
        "turn",
        meta,
        [saved_states[0].reshape(SEQS, local, P_SIZE, N)],
        [((SEQS, width, P_SIZE), jnp.float32)],
        idle=[two],
    )
    stored = [turned]
    for j in range(1, groups):
        route = [((i + j) % groups, i) for i in range(groups)]
        stored.append(lax.ppermute(turned, "sess", route))
    after = turned
    while distance > 2:
        [near] = whole(scalars(join_kernel), "join", meta, [near, moved], [joined(near)], idle=[after])
        after = near
        distance //= 2
        moved = apart(near, distance)

    [chip] = whole(
        scalars(combine_kernel, local),
        "combine",
        meta,
        [keep, got],
        [(keep.shape, jnp.bfloat16)],
        idle=[after],
    )
    total = exchanged(chip)
    beside = moved
    across = apart(near, 1)
    two = apart(two, 2)
    part, token = intra(meta, skip_gain, x, rates, steps, writes, reads, chip)

    entering, after = whole(
        scalars(recurrence_kernel, local, groups),
        "recurrence",
        meta,
        [total, *stored],
        [((chips, 2 * width, P_SIZE), jnp.bfloat16), (TOKEN.shape, TOKEN.dtype)],
        idle=[token, beside, across, two],
        scratch=[pltpu.VMEM((SEQS, width, P_SIZE), jnp.float32)],
    )
    entering = exchanged(entering)
    [pair] = whole(
        scalars(pair_kernel), "pair", meta, [key_value, two, four], [((2, *band), jnp.bfloat16)], idle=[after]
    )
    pair = apart(pair, 1)
    pieces = [near, beside, across, apart(beside, 1)]
    bands = [four, pair, two, pair, key_value]
    attended, token = attend(
        meta, queries[0], bands, pieces, devices // 2, sink_keys[0], sink_values[0], [after]
    )
    own, other = whole(
        scalars(middle_kernel, local),
        "middle",
        meta,
        [entering, keep, got],
        [((chips, 2 * width, P_SIZE), jnp.bfloat16)] * 2,
        idle=[token],
    )
    other = apart(other, 1)
    mixed = finish(meta, part, rates, steps, reads, own, other, local)
    return mixed[None], attended[None]


def solution(mesh):
    token = P("sess", "ctx", None)
    return jax.shard_map(
        shards,
        mesh=mesh,
        in_specs=(
            token,
            token,
            token,
            token,
            token,
            P(),
            P("sess", None, "ctx", None),
            P(),
            P("sess", None),
            P("sess", None),
            token,
            token,
            token,
            P("sess", None, "ctx", None),
            P("sess", None, "ctx", None),
            P("sess", None, None, None),
            P("sess", None, None, None),
        ),
        out_specs=(token, token),
        check_vma=False,
    )
```

```python
import math

import jax
import jax.numpy as jnp
from jax import lax
from jax.experimental import pallas as pl
from jax.experimental.pallas import tpu as pltpu
from jax.sharding import PartitionSpec as P

REACH = 4
SEQS = 3
SINKS = 4
H = 64
P_SIZE = 128
N = 64
G = 8
QH = 32
KVH = 4
HD = 128
WINDOW = 512
TOK = 128

HEADS_PER = H // G
PAIR = 2 * HEADS_PER
STEPS = H // PAIR
EXTRA = 16
BLOCK = 64
SPAN = WINDOW + BLOCK
COLUMNS = SPAN + 64
NEG = -1e30
TOKEN = jax.ShapeDtypeStruct((8, 128), jnp.float32)
LONG = pl.CostEstimate(flops=1 << 35, bytes_accessed=1 << 20, transcendentals=0)


class Scalars:
    def __init__(self, ids):
        self.place, self.group = ids[0], ids[1]
        self.one = ids[2]
        self.two = ids[2] + ids[3]
        self.ids = ids
        self.even = self.place % 2 == 0

    def history(self, session):
        return self.ids[2 + SEQS + session]

    def home(self, number):
        return self.ids[2 + 2 * SEQS + number]

    def session_at(self, position):
        return (position >= self.one).astype(jnp.int32) + (position >= self.two).astype(jnp.int32)

    def start_of(self, session):
        return jnp.where(session == 0, 0, jnp.where(session == 1, self.one, self.two))

    def last_start(self):
        first = self.place * TOK
        return jnp.maximum(self.start_of(self.session_at(first + TOK - 1)) - first, 0)


def scalars(kernel, *options):
    def body(ids, *refs):
        kernel(*options, Scalars(ids), *refs)

    return body


def params(mib=60):
    return pltpu.CompilerParams(vmem_limit_bytes=mib * 1024 * 1024)


def running_rows(dl_ref):
    k = lax.broadcasted_iota(jnp.int32, (TOK, TOK), 0)
    u = lax.broadcasted_iota(jnp.int32, (TOK, TOK), 1)
    upto = (k <= u).astype(jnp.bfloat16)
    running = jnp.dot(dl_ref[...], upto, preferred_element_type=jnp.float32)
    return dl_ref[...].astype(jnp.float32), running


def summary_kernel(
    local, meta, x_ref, dl_ref, step_ref, write_ref, _, keep_ref, send_ref, coef_s, factor_s, write_s
):
    step = pl.program_id(0)

    @pl.when(step == 0)
    def _():
        rates, running = running_rows(dl_ref)
        steps = step_ref[...].astype(jnp.float32)
        r = meta.last_start()
        lane = lax.broadcasted_iota(jnp.int32, (H, TOK), 1)
        last = running[:, TOK - 1 :]
        base = jnp.sum(jnp.where(lane < r, rates, 0.0), axis=1, keepdims=True)
        coef_s[...] = jnp.where(lane >= r, jnp.exp(last - running) * steps, 0.0)
        factor_s[...] = jnp.broadcast_to(jnp.exp(last - base), (H, TOK))
        write_s[...] = write_ref[...].astype(jnp.float32).T

    even = meta.even
    coef = coef_s[pl.ds(pl.multiple_of(step * PAIR, PAIR), PAIR), :]
    factor = factor_s[pl.ds(pl.multiple_of(step * PAIR, PAIR), PAIR), :]
    writes = write_s[pl.ds(pl.multiple_of(step * 2 * N, 2 * N), 2 * N), :]

    def summary(k):
        group = k // HEADS_PER
        loading = (writes[group * N : (group + 1) * N] * coef[k : k + 1]).astype(jnp.bfloat16)
        return jnp.dot(
            loading, x_ref[:, k * P_SIZE : (k + 1) * P_SIZE], preferred_element_type=jnp.float32
        )

    for chip in range(PAIR // (2 * local)):
        low, high = 2 * local * chip, 2 * local * chip + local
        for k in range(local):
            first, second = summary(low + k), summary(high + k)
            rows = slice(k * N, (k + 1) * N)
            keep_ref[chip, rows, :] = jnp.where(even, first, second).astype(jnp.bfloat16)
            send_ref[chip, rows, :] = jnp.where(even, second, first).astype(jnp.bfloat16)
        first, second = factor[low : low + local], factor[high : high + local]
        keep_ref[chip, local * N :, :] = factor_rows(jnp.where(even, first, second))
        send_ref[chip, local * N :, :] = factor_rows(jnp.where(even, second, first))


def factor_rows(rows):
    high = rows.astype(jnp.bfloat16).astype(jnp.float32)
    parts = [high, rows - high]
    if EXTRA > 2 * rows.shape[0]:
        parts.append(jnp.zeros((EXTRA - 2 * rows.shape[0], TOK), jnp.float32))
    return jnp.concatenate(parts, axis=0).astype(jnp.bfloat16)


def factors_of(block, local):
    block = block.astype(jnp.float32)
    return block[:local] + block[local : 2 * local]


def summaries(meta, x, rates, steps, writes, local, idle):
    chips = H // (2 * local)
    rows = local * N + EXTRA
    shape = jax.ShapeDtypeStruct((chips, rows, P_SIZE), jnp.bfloat16)
    spec = pl.BlockSpec((PAIR // (2 * local), rows, P_SIZE), lambda i, *m: (i, 0, 0))
    return pl.pallas_call(
        scalars(summary_kernel, local),
        out_shape=[shape, shape],
        grid_spec=pltpu.PrefetchScalarGridSpec(
            num_scalar_prefetch=1,
            grid=(STEPS,),
            in_specs=[
                pl.BlockSpec((TOK, PAIR * P_SIZE), lambda i, *m: (0, i)),
                pl.BlockSpec((H, TOK), lambda i, *m: (0, 0)),
                pl.BlockSpec((H, TOK), lambda i, *m: (0, 0)),
                pl.BlockSpec((TOK, G * N), lambda i, *m: (0, 0)),
                pl.BlockSpec(memory_space=pl.ANY),
            ],
            out_specs=[spec, spec],
            scratch_shapes=[
                pltpu.VMEM((H, TOK), jnp.float32),
                pltpu.VMEM((H, TOK), jnp.float32),
                pltpu.VMEM((G * N, TOK), jnp.float32),
            ],
        ),
        compiler_params=params(),
        cost_estimate=LONG,
        name="summaries",
    )(meta, x, rates, steps, writes, idle)


def idle_spec(array):
    return pl.BlockSpec(memory_space=pl.ANY)


def whole(kernel, name, meta, arrays, shapes, idle=(), mib=60, scratch=()):
    def spec(shape):
        return pl.BlockSpec(shape, lambda i, *m: (0,) * len(shape))

    return pl.pallas_call(
        kernel,
        out_shape=[jax.ShapeDtypeStruct(s, t) for s, t in shapes],
        grid_spec=pltpu.PrefetchScalarGridSpec(
            num_scalar_prefetch=1,
            grid=(1,),
            in_specs=[spec(a.shape) for a in arrays] + [idle_spec(a) for a in idle],
            out_specs=[spec(s) for s, _ in shapes],
            scratch_shapes=scratch,
        ),
        compiler_params=params(mib),
        cost_estimate=LONG,
        name=name,
    )(meta, *arrays, *idle)


def pack_kernel(half, meta, keys_ref, values_ref, turn_keys_ref, turn_values_ref, home_ref, away_ref, band_ref):
    band_ref[0] = turn_keys_ref[...]
    band_ref[1] = turn_values_ref[...]
    rows = keys_ref.shape[1]
    upper = (meta.place >= half).astype(jnp.int32)
    for out_ref, first in ((home_ref, upper), (away_ref, 1 - upper)):
        for which, ref in enumerate((keys_ref, values_ref)):
            for s in range(2):
                for j in range(KVH):
                    place = ((which * 2 + s) * KVH + j) * rows
                    out_ref[0, place : place + rows, :] = ref[first + s, :, j * HD : (j + 1) * HD]


def turn_kernel(local, meta, stored_ref, *refs):
    out_ref = refs[-1]
    for s in range(SEQS):
        for k in range(local):
            out_ref[s, k * N : (k + 1) * N, :] = stored_ref[s, k].T


def join_kernel(meta, first_ref, second_ref, *refs):
    out_ref = refs[-1]
    count = first_ref.shape[0]
    out_ref[:count] = first_ref[...]
    out_ref[count:] = second_ref[...]


def join_two_kernel(meta, first_ref, second_ref, key_value_ref, four_ref, *refs):
    out_ref, two_ref = refs[-2:]
    count = first_ref.shape[0]
    out_ref[:count] = first_ref[...]
    out_ref[count:] = second_ref[...]
    two_ref[...] = jnp.where(meta.place // 2 % 2 == 0, key_value_ref[...], four_ref[...])


def pair_kernel(meta, key_value_ref, two_ref, four_ref, *refs):
    out_ref = refs[-1]
    key_value, two, four = key_value_ref[...], two_ref[...], four_ref[...]
    out_ref[0] = jnp.where(meta.even, key_value, two)
    out_ref[1] = jnp.where(meta.even, two, four)


def far_place(distance, bits):
    place = distance * 0
    for k in range(bits):
        place = place + ((distance // (1 << k)) % 2) * (1 << (bits - 1 - k))
    return place


def combine_kernel(local, meta, keep_ref, got_ref, *refs):
    out_ref = refs[-1]
    even = meta.even
    second = (meta.place // 2 * 2 + 1) * TOK
    closes = meta.start_of(meta.session_at(second + TOK - 1)) >= second
    width = local * N
    for chip in range(keep_ref.shape[0]):
        keep = factors_of(keep_ref[chip, width:, :], local)
        got = factors_of(got_ref[chip, width:, :], local)
        f0, f1 = jnp.where(even, keep, got), jnp.where(even, got, keep)
        out_ref[chip, width:, :] = factor_rows(jnp.where(closes, f1, f0 * f1))
        carry = jnp.where(closes, 0.0, f1)
        for k in range(local):
            rows = slice(k * N, (k + 1) * N)
            keep = keep_ref[chip, rows, :].astype(jnp.float32)
            got = got_ref[chip, rows, :].astype(jnp.float32)
            s0, s1 = jnp.where(even, keep, got), jnp.where(even, got, keep)
            out_ref[chip, rows, :] = (carry[k : k + 1] * s0 + s1).astype(jnp.bfloat16)


def recurrence_kernel(local, groups, meta, got_ref, *refs):
    stored, (out_ref, token_ref, restored_ref) = refs[:groups], refs[-3:]
    token_ref[...] = jnp.zeros_like(token_ref)
    for s in range(SEQS):
        slot = meta.home(meta.group * SEQS + s)
        source = (slot // SEQS - meta.group + groups) % groups
        kept = stored[0][slot % SEQS]
        for j in range(1, groups):
            kept = jnp.where(source == j, stored[j][slot % SEQS], kept)
        restored_ref[s] = kept
    width = local * N
    span = 2 * TOK
    state = [jnp.zeros((N, P_SIZE), jnp.float32) for _ in range(local)]
    for c in range(got_ref.shape[0]):
        first = c * span
        opening = meta.session_at(first)
        closing = meta.session_at(first + span - 1)
        opens = meta.start_of(opening) >= first
        closes = meta.start_of(closing) >= first
        factor = factors_of(got_ref[c, width:, :], local)
        for k in range(local):
            rows = slice(k * N, (k + 1) * N)
            entering = jnp.where(opens, restored_ref[opening, rows, :], state[k])
            out_ref[c, rows, :] = entering.astype(jnp.bfloat16)
            resumed = restored_ref[closing, rows, :]
            out_ref[c, width + k * N : width + (k + 1) * N, :] = resumed.astype(jnp.bfloat16)
            source = jnp.where(closes, resumed, state[k])
            state[k] = factor[k : k + 1] * source + got_ref[c, rows, :].astype(jnp.float32)


def middle_kernel(local, meta, entering_ref, keep_ref, got_ref, *refs):
    even = meta.even
    first = meta.place // 2 * 2 * TOK
    second = first + TOK
    start = meta.start_of(meta.session_at(second + TOK - 1))
    closes = (start > first) & (start < second)
    opens = start == second
    width = local * N
    own_ref, send_ref = refs[-2:]
    for chip in range(entering_ref.shape[0]):
        f0 = jnp.where(
            even,
            factors_of(keep_ref[chip, width:, :], local),
            factors_of(got_ref[chip, width:, :], local),
        )
        resumed = entering_ref[chip, width:, :].astype(jnp.float32)
        own_ref[chip, width:, :] = entering_ref[chip, width:, :]
        send_ref[chip, width:, :] = entering_ref[chip, width:, :]
        for k in range(local):
            rows = slice(k * N, (k + 1) * N)
            entering = entering_ref[chip, rows, :].astype(jnp.float32)
            s0 = jnp.where(
                even, keep_ref[chip, rows, :].astype(jnp.float32), got_ref[chip, rows, :].astype(jnp.float32)
            )
            middle = f0[k : k + 1] * jnp.where(closes, resumed[rows], entering) + s0
            middle = jnp.where(opens, resumed[rows], middle)
            own_ref[chip, rows, :] = jnp.where(even, entering, middle).astype(jnp.bfloat16)
            send_ref[chip, rows, :] = jnp.where(even, middle, entering).astype(jnp.bfloat16)


def intra_kernel(meta, skip, x_ref, dl_ref, step_ref, write_ref, read_ref, _, out_ref, token_ref, run_s, step_s):
    step = pl.program_id(0)

    @pl.when(step == 0)
    def _():
        _, running = running_rows(dl_ref)
        run_s[...] = running
        step_s[...] = step_ref[...].astype(jnp.float32)

    token_ref[...] = jnp.zeros_like(token_ref)
    heads = pl.ds(pl.multiple_of(step * PAIR, PAIR), PAIR)
    running = run_s[heads, :]
    sizes = step_s[heads, :]
    columns = running.T
    r = meta.last_start()
    t = lax.broadcasted_iota(jnp.int32, (TOK, TOK), 0)
    u = lax.broadcasted_iota(jnp.int32, (TOK, TOK), 1)
    causal = (u <= t) & ((u >= r) | (t < r))
    for group in range(2):
        part = slice(group * N, (group + 1) * N)
        products = lax.dot_general(
            read_ref[:, part], write_ref[:, part], (((1,), (1,)), ((), ())),
            preferred_element_type=jnp.float32,
        )
        products = jnp.where(causal, products, 0.0)
        for k in range(group * HEADS_PER, (group + 1) * HEADS_PER):
            difference = columns[:, k : k + 1] - running[k : k + 1]
            decay = jnp.exp(jnp.minimum(difference, 0.0))
            mixing = (products * decay * sizes[k : k + 1]).astype(jnp.bfloat16)
            place = slice(k * P_SIZE, (k + 1) * P_SIZE)
            x = x_ref[:, place]
            mixed = jnp.dot(mixing, x, preferred_element_type=jnp.float32)
            out_ref[:, place] = mixed + skip[step * PAIR + k] * x.astype(jnp.float32)


def intra(meta, skip, x, rates, steps, writes, reads, idle):
    return pl.pallas_call(
        scalars(intra_kernel),
        out_shape=[jax.ShapeDtypeStruct((TOK, H * P_SIZE), jnp.float32), TOKEN],
        grid_spec=pltpu.PrefetchScalarGridSpec(
            num_scalar_prefetch=2,
            grid=(STEPS,),
            in_specs=[
                pl.BlockSpec((TOK, PAIR * P_SIZE), lambda i, *m: (0, i)),
                pl.BlockSpec((H, TOK), lambda i, *m: (0, 0)),
                pl.BlockSpec((H, TOK), lambda i, *m: (0, 0)),
                pl.BlockSpec((TOK, 2 * N), lambda i, *m: (0, i)),
                pl.BlockSpec((TOK, 2 * N), lambda i, *m: (0, i)),
                pl.BlockSpec(memory_space=pl.ANY),
            ],
            out_specs=[
                pl.BlockSpec((TOK, PAIR * P_SIZE), lambda i, *m: (0, i)),
                pl.BlockSpec(TOKEN.shape, lambda i, *m: (0, 0)),
            ],
            scratch_shapes=[
                pltpu.VMEM((H, TOK), jnp.float32),
                pltpu.VMEM((H, TOK), jnp.float32),
            ],
        ),
        compiler_params=params(),
        cost_estimate=LONG,
        name="intra",
    )(meta, skip, x, rates, steps, writes, reads, idle)


def finish_kernel(
    local, meta, part_ref, dl_ref, step_ref, read_ref, own_ref, other_ref, out_ref, factor_s
):
    step = pl.program_id(0)
    even = meta.even
    r = meta.last_start()

    @pl.when(step == 0)
    def _():
        rates, running = running_rows(dl_ref)
        lane = lax.broadcasted_iota(jnp.int32, (H, TOK), 1)
        base = jnp.sum(jnp.where(lane < r, rates, 0.0), axis=1, keepdims=True)
        factor_s[...] = jnp.exp(jnp.minimum(running - jnp.where(lane >= r, base, 0.0), 0.0))

    factor = factor_s[pl.ds(pl.multiple_of(step * PAIR, PAIR), PAIR), :].T
    token = lax.broadcasted_iota(jnp.int32, (TOK, N), 0)
    resumed = (token >= r) & (r > 0)
    for group in range(2):
        reads = read_ref[:, group * N : (group + 1) * N].astype(jnp.float32)
        left = jnp.where(resumed, 0.0, reads)
        right = jnp.where(resumed, reads, 0.0)
        reads = jnp.concatenate([left, right], axis=1).astype(jnp.bfloat16)
        for k in range(group * HEADS_PER, (group + 1) * HEADS_PER):
            chip, half = k // (2 * local), k // local % 2
            rows = slice((k % local) * N, (k % local + 1) * N)
            own = even if half == 0 else jnp.logical_not(even)
            later = slice(rows.start + local * N, rows.stop + local * N)
            states = jnp.concatenate(
                [
                    jnp.where(own, own_ref[chip, rows, :], other_ref[chip, rows, :]),
                    jnp.where(own, own_ref[chip, later, :], other_ref[chip, later, :]),
                ],
                axis=0,
            )
            carried = jnp.dot(reads, states, preferred_element_type=jnp.float32)
            place = slice(k * P_SIZE, (k + 1) * P_SIZE)
            out_ref[:, place] = (part_ref[:, place] + factor[:, k : k + 1] * carried).astype(jnp.bfloat16)


def finish(meta, part, rates, steps, reads, own, other, local):
    chips = PAIR // (2 * local)
    width = 2 * local * N
    states = pl.BlockSpec((chips, width, P_SIZE), lambda i, *m: (i, 0, 0))
    return pl.pallas_call(
        scalars(finish_kernel, local),
        out_shape=jax.ShapeDtypeStruct((TOK, H * P_SIZE), jnp.bfloat16),
        grid_spec=pltpu.PrefetchScalarGridSpec(
            num_scalar_prefetch=1,
            grid=(STEPS,),
            in_specs=[
                pl.BlockSpec((TOK, PAIR * P_SIZE), lambda i, *m: (0, i)),
                pl.BlockSpec((H, TOK), lambda i, *m: (0, 0)),
                pl.BlockSpec((H, TOK), lambda i, *m: (0, 0)),
                pl.BlockSpec((TOK, 2 * N), lambda i, *m: (0, i)),
                states,
                states,
            ],
            out_specs=pl.BlockSpec((TOK, PAIR * P_SIZE), lambda i, *m: (0, i)),
            scratch_shapes=[pltpu.VMEM((H, TOK), jnp.float32)],
        ),
        compiler_params=params(),
        cost_estimate=LONG,
        name="finish",
    )(meta, part, rates, steps, reads, own, other)


def attend_kernel(
    meta, q_ref, band4, band3, band2, band1, band0, *refs,
):
    history_refs, (sk_ref, sv_ref), (out_ref, token_ref, key_s, value_s) = refs[:16], refs[16:18], refs[-4:]
    factor = 1.0 / math.sqrt(HD)
    first = meta.place * TOK
    r = meta.last_start()
    opening = meta.session_at(first)
    closing = meta.session_at(first + TOK - 1)
    bands = (band4, band3.at[0], band2, band1.at[0], band0)
    token_ref[...] = jnp.zeros_like(token_ref)

    def sinks(ref, session):
        rows = ref[session].astype(jnp.float32)
        spare = jnp.zeros((COLUMNS - SPAN - SINKS, HD), jnp.float32)
        return jnp.concatenate([rows, spare], axis=0).astype(jnp.bfloat16)

    length = (REACH + 1) * TOK

    def one_session(session, key_refs, value_refs, resuming, needed):
        start = meta.start_of(session) - first + WINDOW
        oldest = start - WINDOW + jnp.maximum(SINKS + WINDOW - meta.history(session), 0)

        @pl.when(needed & (start > 0))
        def _():
            row = lax.broadcasted_iota(jnp.int32, (length, WINDOW), 0)
            chips, share, _ = key_refs[0].shape
            index = lax.broadcasted_iota(jnp.int32, (1, WINDOW), 1)
            piece, index = index // (WINDOW // 4), index % (WINDOW // 4)
            near, row_in = index // share, index % share
            far = far_place(near, chips.bit_length() - 1)
            device = meta.place ^ (piece // 2 + piece % 2 * 2 + far * 4)
            place = device * share + row_in
            moved = (row == place + start - WINDOW).astype(jnp.bfloat16)
            part = (WINDOW // 4, HD)
            keys = jnp.concatenate([ref[...].reshape(part) for ref in key_refs], axis=0)
            values = jnp.concatenate([ref[...].reshape(part) for ref in value_refs], axis=0)
            history = jnp.dot(
                moved, jnp.concatenate([keys, values], axis=1), preferred_element_type=jnp.float32
            )
            for i, band in enumerate(bands):
                rows = slice(i * TOK, (i + 1) * TOK)
                index = lax.broadcasted_iota(jnp.int32, (TOK, HD), 0) + i * TOK
                turn = index >= start
                key_s[rows, :] = jnp.where(
                    turn, band[0].astype(jnp.float32), history[rows, :HD]
                ).astype(jnp.bfloat16)
                value_s[rows, :] = jnp.where(
                    turn, band[1].astype(jnp.float32), history[rows, HD:]
                ).astype(jnp.bfloat16)

        @pl.when(needed & (start <= 0))
        def _():
            for i, band in enumerate(bands):
                rows = slice(i * TOK, (i + 1) * TOK)
                key_s[rows, :] = band[0]
                value_s[rows, :] = band[1]

        for b in range(TOK // BLOCK):
            inside = (b * BLOCK + BLOCK > r) if resuming else (b * BLOCK < r)

            @pl.when(needed & inside)
            def _():
                rows = slice(b * BLOCK, b * BLOCK + SPAN)
                keys = jnp.concatenate([key_s[rows, :], sinks(sk_ref, session)], axis=0)
                values = jnp.concatenate([value_s[rows, :], sinks(sv_ref, session)], axis=0)
                tokens = slice(b * BLOCK, (b + 1) * BLOCK)
                queries = jnp.concatenate(
                    [q_ref[tokens, g * HD : (g + 1) * HD] for g in range(QH // KVH)], axis=0
                )
                scores = lax.dot_general(
                    queries, keys, (((1,), (1,)), ((), ())), preferred_element_type=jnp.float32
                )
                token = lax.broadcasted_iota(jnp.int32, (BLOCK, COLUMNS), 0)
                column = lax.broadcasted_iota(jnp.int32, (BLOCK, COLUMNS), 1)
                seen = (column > token) & (column <= token + WINDOW) & (column >= oldest - b * BLOCK)
                seen = (seen & (column < SPAN)) | ((column >= SPAN) & (column < SPAN + SINKS))
                bias = jnp.where(seen, 0.0, NEG)
                weights, sums = [], []
                for g in range(QH // KVH):
                    score = scores[g * BLOCK : (g + 1) * BLOCK] * factor + bias
                    weight = jnp.exp(score - jnp.max(score, axis=1, keepdims=True))
                    sums.append(jnp.sum(weight, axis=1, keepdims=True))
                    weights.append(weight.astype(jnp.bfloat16))
                mixed = jnp.dot(
                    jnp.concatenate(weights, axis=0), values, preferred_element_type=jnp.float32
                )
                for g in range(QH // KVH):
                    result = mixed[g * BLOCK : (g + 1) * BLOCK] / sums[g]
                    lanes = slice(g * HD, (g + 1) * HD)
                    if resuming:
                        index = lax.broadcasted_iota(jnp.int32, (BLOCK, HD), 0) + b * BLOCK
                        before = out_ref[tokens, lanes].astype(jnp.float32)
                        result = jnp.where(index >= r, result, before)
                    out_ref[tokens, lanes] = result.astype(jnp.bfloat16)

    one_session(opening, history_refs[0:4], history_refs[4:8], False, r > 0)
    one_session(closing, history_refs[8:12], history_refs[12:], True, r >= 0)


def attend(meta, queries, bands, pieces, half, sink_keys, sink_values, idle):
    chips = pieces[0].shape[0]
    share = WINDOW // (4 * chips)
    lanes = QH // KVH * HD

    def history_spec(which, last):
        def index(j, *m):
            known = Scalars(*m)
            session = known.session_at(known.place * TOK + (TOK - 1 if last else 0))
            session = session - (known.place >= half).astype(jnp.int32)
            return (0, (which * 2 + session) * KVH + j, 0)

        return pl.BlockSpec((chips, share, HD), index)

    def band_spec(array, number):
        if array.ndim == 3:
            return pl.BlockSpec((2, TOK, HD), lambda j, *m: (0, 0, j))
        return pl.BlockSpec((1, 2, TOK, HD), lambda j, *m: (number, 0, 0, j))

    pad = SEQS, SINKS, HD
    return pl.pallas_call(
        scalars(attend_kernel),
        out_shape=[jax.ShapeDtypeStruct((TOK, QH * HD), jnp.bfloat16), TOKEN],
        grid_spec=pltpu.PrefetchScalarGridSpec(
            num_scalar_prefetch=1,
            grid=(KVH,),
            in_specs=[pl.BlockSpec((TOK, lanes), lambda j, *m: (0, j))]
            + [band_spec(a, number) for a, number in zip(bands, (0, 1, 0, 0, 0))]
            + [history_spec(0, False)] * 4
            + [history_spec(1, False)] * 4
            + [history_spec(0, True)] * 4
            + [history_spec(1, True)] * 4
            + [pl.BlockSpec(pad, lambda j, *m: (0, 0, j))] * 2
            + [idle_spec(a) for a in idle],
            out_specs=[
                pl.BlockSpec((TOK, lanes), lambda j, *m: (0, j)),
                pl.BlockSpec(TOKEN.shape, lambda j, *m: (0, 0)),
            ],
            scratch_shapes=[
                pltpu.VMEM(((REACH + 1) * TOK, HD), jnp.bfloat16),
                pltpu.VMEM(((REACH + 1) * TOK, HD), jnp.bfloat16),
            ],
        ),
        compiler_params=params(),
        cost_estimate=LONG,
        name="attend",
    )(
        meta, queries, *bands, *pieces, *pieces, *pieces, *pieces, sink_keys, sink_values, *idle
    )


def shifted(block, axis, distance):
    devices = range(lax.axis_size(axis))
    return lax.ppermute(block, axis, [(i - distance, i) for i in devices if i - distance in devices])


def shards(
    mamba_input,
    step_size,
    decay_log,
    state_write,
    state_read,
    skip_gain,
    saved_states,
    home_slot,
    turn_lengths,
    history_lengths,
    queries,
    turn_keys,
    turn_values,
    cache_keys,
    cache_values,
    sink_keys,
    sink_values,
):
    place = lax.axis_index("ctx")
    group = lax.axis_index("sess")
    groups = lax.axis_size("sess")
    devices = lax.axis_size("ctx")
    local = saved_states.shape[2]
    width = local * N
    chips = devices // 2
    same_core = [list(range(core, devices, 2)) for core in range(2)]
    meta = jnp.concatenate(
        [jnp.stack([place, group]).astype(jnp.int32), turn_lengths[0], history_lengths[0], home_slot]
    )
    x, rates, steps = mamba_input[0], decay_log[0].T, step_size[0].T
    writes, reads = state_write[0], state_read[0]
    def apart(block, distance):
        return lax.ppermute(block, "ctx", [(i, i ^ distance) for i in range(devices)])

    def exchanged(block):
        return lax.all_to_all(block, "ctx", 0, 0, axis_index_groups=same_core, tiled=True)

    parcel = (1, 4 * KVH * cache_keys.shape[2], HD)
    band = (2, TOK, KVH * HD)
    near, away, key_value = whole(
        scalars(pack_kernel, devices // 2),
        "pack",
        meta,
        [cache_keys[0], cache_values[0], turn_keys[0], turn_values[0]],
        [(parcel, jnp.bfloat16), (parcel, jnp.bfloat16), (band, jnp.bfloat16)],
    )
    distance = devices // 2
    moved = apart(away, distance)
    four = shifted(key_value, "ctx", 4)

    keep, send = summaries(meta, x, rates, steps, writes, local, away)
    got = apart(send, 1)

    def joined(array):
        return ((2 * array.shape[0], *array.shape[1:]), jnp.bfloat16)

    near, two = whole(
        scalars(join_two_kernel),
        "join_two",
        meta,
        [near, moved, key_value, four],
        [joined(near), (band, jnp.bfloat16)],
        idle=[got],
    )
    distance //= 2
    moved = apart(near, distance)

    [turned] = whole(
        scalars(turn_kernel, local),
        "turn",
        meta,
        [saved_states[0].reshape(SEQS, local, P_SIZE, N)],
        [((SEQS, width, P_SIZE), jnp.float32)],
        idle=[two],
    )
    stored = [turned]
    for j in range(1, groups):
        route = [((i + j) % groups, i) for i in range(groups)]
        stored.append(lax.ppermute(turned, "sess", route))
    two = apart(two, 2)
    [chip] = whole(
        scalars(combine_kernel, local),
        "combine",
        meta,
        [keep, got],
        [(keep.shape, jnp.bfloat16)],
        idle=[turned, two],
    )
    total = exchanged(chip)
    [pair] = whole(
        scalars(pair_kernel), "pair", meta, [key_value, two, four], [((2, *band), jnp.bfloat16)], idle=[chip]
    )
    after = pair
    pair = apart(pair, 1)
    while distance > 2:
        [near] = whole(scalars(join_kernel), "join", meta, [near, moved], [joined(near)], idle=[after])
        after = near
        distance //= 2
        moved = apart(near, distance)
    beside = moved
    across = apart(near, 1)
    part, token = intra(meta, skip_gain, x, rates, steps, writes, reads, after)

    entering, after = whole(
        scalars(recurrence_kernel, local, groups),
        "recurrence",
        meta,
        [total, *stored],
        [((chips, 2 * width, P_SIZE), jnp.bfloat16), (TOKEN.shape, TOKEN.dtype)],
        idle=[token, beside, across, pair],
        scratch=[pltpu.VMEM((SEQS, width, P_SIZE), jnp.float32)],
    )
    entering = exchanged(entering)
    pieces = [near, beside, across, apart(beside, 1)]
    bands = [four, pair, two, pair, key_value]
    attended, token = attend(
        meta, queries[0], bands, pieces, devices // 2, sink_keys[0], sink_values[0], [after]
    )
    own, other = whole(
        scalars(middle_kernel, local),
        "middle",
        meta,
        [entering, keep, got],
        [((chips, 2 * width, P_SIZE), jnp.bfloat16)] * 2,
        idle=[token],
    )
    other = apart(other, 1)
    mixed = finish(meta, part, rates, steps, reads, own, other, local)
    return mixed[None], attended[None]


def solution(mesh):
    token = P("sess", "ctx", None)
    return jax.shard_map(
        shards,
        mesh=mesh,
        in_specs=(
            token,
            token,
            token,
            token,
            token,
            P(),
            P("sess", None, "ctx", None),
            P(),
            P("sess", None),
            P("sess", None),
            token,
            token,
            token,
            P("sess", None, "ctx", None),
            P("sess", None, "ctx", None),
            P("sess", None, None, None),
            P("sess", None, None, None),
        ),
        out_specs=(token, token),
        check_vma=False,
    )
```

```python
import math

import jax
import jax.numpy as jnp
from jax import lax
from jax.experimental import pallas as pl
from jax.experimental.pallas import tpu as pltpu
from jax.sharding import PartitionSpec as P

REACH = 4
SEQS = 3
SINKS = 4
H = 64
P_SIZE = 128
N = 64
G = 8
QH = 32
KVH = 4
HD = 128
WINDOW = 512
TOK = 128

HEADS_PER = H // G
PAIR = 2 * HEADS_PER
STEPS = H // PAIR
EXTRA = 16
BLOCK = 64
SPAN = WINDOW + BLOCK
COLUMNS = SPAN + 64
NEG = -1e30
TOKEN = jax.ShapeDtypeStruct((8, 128), jnp.float32)
LONG = pl.CostEstimate(flops=1 << 35, bytes_accessed=1 << 20, transcendentals=0)


class Scalars:
    def __init__(self, ids):
        self.place, self.group = ids[0], ids[1]
        self.one = ids[2]
        self.two = ids[2] + ids[3]
        self.ids = ids
        self.even = self.place % 2 == 0

    def history(self, session):
        return self.ids[2 + SEQS + session]

    def home(self, number):
        return self.ids[2 + 2 * SEQS + number]

    def session_at(self, position):
        return (position >= self.one).astype(jnp.int32) + (position >= self.two).astype(jnp.int32)

    def start_of(self, session):
        return jnp.where(session == 0, 0, jnp.where(session == 1, self.one, self.two))

    def last_start(self):
        first = self.place * TOK
        return jnp.maximum(self.start_of(self.session_at(first + TOK - 1)) - first, 0)


def scalars(kernel, *options):
    def body(ids, *refs):
        kernel(*options, Scalars(ids), *refs)

    return body


def params(mib=60):
    return pltpu.CompilerParams(vmem_limit_bytes=mib * 1024 * 1024)


def running_rows(dl_ref):
    k = lax.broadcasted_iota(jnp.int32, (TOK, TOK), 0)
    u = lax.broadcasted_iota(jnp.int32, (TOK, TOK), 1)
    upto = (k <= u).astype(jnp.bfloat16)
    running = jnp.dot(dl_ref[...], upto, preferred_element_type=jnp.float32)
    return dl_ref[...].astype(jnp.float32), running


def summary_kernel(
    local, meta, x_ref, dl_ref, step_ref, write_ref, _, keep_ref, send_ref, coef_s, factor_s, write_s
):
    step = pl.program_id(0)

    @pl.when(step == 0)
    def _():
        rates, running = running_rows(dl_ref)
        steps = step_ref[...].astype(jnp.float32)
        r = meta.last_start()
        lane = lax.broadcasted_iota(jnp.int32, (H, TOK), 1)
        last = running[:, TOK - 1 :]
        base = jnp.sum(jnp.where(lane < r, rates, 0.0), axis=1, keepdims=True)
        coef_s[...] = jnp.where(lane >= r, jnp.exp(last - running) * steps, 0.0)
        factor_s[...] = jnp.broadcast_to(jnp.exp(last - base), (H, TOK))
        write_s[...] = write_ref[...].astype(jnp.float32).T

    even = meta.even
    coef = coef_s[pl.ds(pl.multiple_of(step * PAIR, PAIR), PAIR), :]
    factor = factor_s[pl.ds(pl.multiple_of(step * PAIR, PAIR), PAIR), :]
    writes = write_s[pl.ds(pl.multiple_of(step * 2 * N, 2 * N), 2 * N), :]

    def summary(k):
        group = k // HEADS_PER
        loading = (writes[group * N : (group + 1) * N] * coef[k : k + 1]).astype(jnp.bfloat16)
        return jnp.dot(
            loading, x_ref[:, k * P_SIZE : (k + 1) * P_SIZE], preferred_element_type=jnp.float32
        )

    for chip in range(PAIR // (2 * local)):
        low, high = 2 * local * chip, 2 * local * chip + local
        for k in range(local):
            first, second = summary(low + k), summary(high + k)
            rows = slice(k * N, (k + 1) * N)
            keep_ref[chip, rows, :] = jnp.where(even, first, second).astype(jnp.bfloat16)
            send_ref[chip, rows, :] = jnp.where(even, second, first).astype(jnp.bfloat16)
        first, second = factor[low : low + local], factor[high : high + local]
        keep_ref[chip, local * N :, :] = factor_rows(jnp.where(even, first, second))
        send_ref[chip, local * N :, :] = factor_rows(jnp.where(even, second, first))


def factor_rows(rows):
    high = rows.astype(jnp.bfloat16).astype(jnp.float32)
    parts = [high, rows - high]
    if EXTRA > 2 * rows.shape[0]:
        parts.append(jnp.zeros((EXTRA - 2 * rows.shape[0], TOK), jnp.float32))
    return jnp.concatenate(parts, axis=0).astype(jnp.bfloat16)


def factors_of(block, local):
    block = block.astype(jnp.float32)
    return block[:local] + block[local : 2 * local]


def summaries(meta, x, rates, steps, writes, local, idle):
    chips = H // (2 * local)
    rows = local * N + EXTRA
    shape = jax.ShapeDtypeStruct((chips, rows, P_SIZE), jnp.bfloat16)
    spec = pl.BlockSpec((PAIR // (2 * local), rows, P_SIZE), lambda i, *m: (i, 0, 0))
    return pl.pallas_call(
        scalars(summary_kernel, local),
        out_shape=[shape, shape],
        grid_spec=pltpu.PrefetchScalarGridSpec(
            num_scalar_prefetch=1,
            grid=(STEPS,),
            in_specs=[
                pl.BlockSpec((TOK, PAIR * P_SIZE), lambda i, *m: (0, i)),
                pl.BlockSpec((H, TOK), lambda i, *m: (0, 0)),
                pl.BlockSpec((H, TOK), lambda i, *m: (0, 0)),
                pl.BlockSpec((TOK, G * N), lambda i, *m: (0, 0)),
                pl.BlockSpec(memory_space=pl.ANY),
            ],
            out_specs=[spec, spec],
            scratch_shapes=[
                pltpu.VMEM((H, TOK), jnp.float32),
                pltpu.VMEM((H, TOK), jnp.float32),
                pltpu.VMEM((G * N, TOK), jnp.float32),
            ],
        ),
        compiler_params=params(),
        cost_estimate=LONG,
        name="summaries",
    )(meta, x, rates, steps, writes, idle)


def idle_spec(array):
    return pl.BlockSpec(memory_space=pl.ANY)


def whole(kernel, name, meta, arrays, shapes, idle=(), mib=16, scratch=()):
    def spec(shape):
        return pl.BlockSpec(shape, lambda i, *m: (0,) * len(shape))

    return pl.pallas_call(
        kernel,
        out_shape=[jax.ShapeDtypeStruct(s, t) for s, t in shapes],
        grid_spec=pltpu.PrefetchScalarGridSpec(
            num_scalar_prefetch=1,
            grid=(1,),
            in_specs=[spec(a.shape) for a in arrays] + [idle_spec(a) for a in idle],
            out_specs=[spec(s) for s, _ in shapes],
            scratch_shapes=scratch,
        ),
        compiler_params=params(mib),
        cost_estimate=LONG,
        name=name,
    )(meta, *arrays, *idle)


def pack_kernel(half, meta, keys_ref, values_ref, turn_keys_ref, turn_values_ref, home_ref, away_ref, band_ref):
    band_ref[0] = turn_keys_ref[...]
    band_ref[1] = turn_values_ref[...]
    rows = keys_ref.shape[1]
    upper = (meta.place >= half).astype(jnp.int32)
    for out_ref, first in ((home_ref, upper), (away_ref, 1 - upper)):
        for which, ref in enumerate((keys_ref, values_ref)):
            for s in range(2):
                for j in range(KVH):
                    place = ((which * 2 + s) * KVH + j) * rows
                    out_ref[0, place : place + rows, :] = ref[first + s, :, j * HD : (j + 1) * HD]


def turn_kernel(local, meta, stored_ref, *refs):
    out_ref = refs[-1]
    for s in range(SEQS):
        for k in range(local):
            out_ref[s, k * N : (k + 1) * N, :] = stored_ref[s, k].T


def join_kernel(meta, first_ref, second_ref, *refs):
    out_ref = refs[-1]
    count = first_ref.shape[0]
    out_ref[:count] = first_ref[...]
    out_ref[count:] = second_ref[...]


def join_two_kernel(meta, first_ref, second_ref, key_value_ref, four_ref, *refs):
    out_ref, two_ref = refs[-2:]
    count = first_ref.shape[0]
    out_ref[:count] = first_ref[...]
    out_ref[count:] = second_ref[...]
    two_ref[...] = jnp.where(meta.place // 2 % 2 == 0, key_value_ref[...], four_ref[...])


def far_place(distance, bits):
    place = distance * 0
    for k in range(bits):
        place = place + ((distance // (1 << k)) % 2) * (1 << (bits - 1 - k))
    return place


def combine_kernel(local, meta, keep_ref, got_ref, *refs):
    out_ref = refs[-1]
    even = meta.even
    second = (meta.place // 2 * 2 + 1) * TOK
    closes = meta.start_of(meta.session_at(second + TOK - 1)) >= second
    width = local * N
    for chip in range(keep_ref.shape[0]):
        keep = factors_of(keep_ref[chip, width:, :], local)
        got = factors_of(got_ref[chip, width:, :], local)
        f0, f1 = jnp.where(even, keep, got), jnp.where(even, got, keep)
        out_ref[chip, width:, :] = factor_rows(jnp.where(closes, f1, f0 * f1))
        carry = jnp.where(closes, 0.0, f1)
        for k in range(local):
            rows = slice(k * N, (k + 1) * N)
            keep = keep_ref[chip, rows, :].astype(jnp.float32)
            got = got_ref[chip, rows, :].astype(jnp.float32)
            s0, s1 = jnp.where(even, keep, got), jnp.where(even, got, keep)
            out_ref[chip, rows, :] = (carry[k : k + 1] * s0 + s1).astype(jnp.bfloat16)


def restore_kernel(groups, meta, *refs):
    stored, (resumed_ref, restored_ref) = refs[:groups], refs[-2:]
    for s in range(SEQS):
        slot = meta.home(meta.group * SEQS + s)
        source = (slot // SEQS - meta.group + groups) % groups
        kept = stored[0][slot % SEQS]
        for j in range(1, groups):
            kept = jnp.where(source == j, stored[j][slot % SEQS], kept)
        restored_ref[s] = kept
    for chip in range(resumed_ref.shape[0]):
        closing = meta.session_at((chip + 1) * 2 * TOK - 1)
        resumed_ref[chip] = restored_ref[closing].astype(jnp.bfloat16)


def recurrence_kernel(local, meta, got_ref, restored_ref, *refs):
    out_ref, token_ref = refs[-2:]
    token_ref[...] = jnp.zeros_like(token_ref)
    width = local * N
    span = 2 * TOK
    state = [jnp.zeros((N, P_SIZE), jnp.float32) for _ in range(local)]
    for c in range(got_ref.shape[0]):
        first = c * span
        opening = meta.session_at(first)
        closing = meta.session_at(first + span - 1)
        opens = meta.start_of(opening) >= first
        closes = meta.start_of(closing) >= first
        factor = factors_of(got_ref[c, width:, :], local)
        for k in range(local):
            rows = slice(k * N, (k + 1) * N)
            entering = jnp.where(opens, restored_ref[opening, rows, :], state[k])
            out_ref[c, rows, :] = entering.astype(jnp.bfloat16)
            source = jnp.where(closes, restored_ref[closing, rows, :], state[k])
            state[k] = factor[k : k + 1] * source + got_ref[c, rows, :].astype(jnp.float32)


def intra_kernel(meta, skip, x_ref, dl_ref, step_ref, write_ref, read_ref, _, out_ref, token_ref, run_s, step_s):
    step = pl.program_id(0)

    @pl.when(step == 0)
    def _():
        _, running = running_rows(dl_ref)
        run_s[...] = running
        step_s[...] = step_ref[...].astype(jnp.float32)

    token_ref[...] = jnp.zeros_like(token_ref)
    heads = pl.ds(pl.multiple_of(step * PAIR, PAIR), PAIR)
    running = run_s[heads, :]
    sizes = step_s[heads, :]
    columns = running.T
    r = meta.last_start()
    t = lax.broadcasted_iota(jnp.int32, (TOK, TOK), 0)
    u = lax.broadcasted_iota(jnp.int32, (TOK, TOK), 1)
    causal = (u <= t) & ((u >= r) | (t < r))
    for group in range(2):
        part = slice(group * N, (group + 1) * N)
        products = lax.dot_general(
            read_ref[:, part], write_ref[:, part], (((1,), (1,)), ((), ())),
            preferred_element_type=jnp.float32,
        )
        products = jnp.where(causal, products, 0.0)
        for k in range(group * HEADS_PER, (group + 1) * HEADS_PER):
            difference = columns[:, k : k + 1] - running[k : k + 1]
            decay = jnp.exp(jnp.minimum(difference, 0.0))
            mixing = (products * decay * sizes[k : k + 1]).astype(jnp.bfloat16)
            place = slice(k * P_SIZE, (k + 1) * P_SIZE)
            x = x_ref[:, place]
            mixed = jnp.dot(mixing, x, preferred_element_type=jnp.float32)
            out_ref[:, place] = mixed + skip[step * PAIR + k] * x.astype(jnp.float32)


def intra(meta, skip, x, rates, steps, writes, reads, idle):
    return pl.pallas_call(
        scalars(intra_kernel),
        out_shape=[jax.ShapeDtypeStruct((TOK, H * P_SIZE), jnp.float32), TOKEN],
        grid_spec=pltpu.PrefetchScalarGridSpec(
            num_scalar_prefetch=2,
            grid=(STEPS,),
            in_specs=[
                pl.BlockSpec((TOK, PAIR * P_SIZE), lambda i, *m: (0, i)),
                pl.BlockSpec((H, TOK), lambda i, *m: (0, 0)),
                pl.BlockSpec((H, TOK), lambda i, *m: (0, 0)),
                pl.BlockSpec((TOK, 2 * N), lambda i, *m: (0, i)),
                pl.BlockSpec((TOK, 2 * N), lambda i, *m: (0, i)),
                pl.BlockSpec(memory_space=pl.ANY),
            ],
            out_specs=[
                pl.BlockSpec((TOK, PAIR * P_SIZE), lambda i, *m: (0, i)),
                pl.BlockSpec(TOKEN.shape, lambda i, *m: (0, 0)),
            ],
            scratch_shapes=[
                pltpu.VMEM((H, TOK), jnp.float32),
                pltpu.VMEM((H, TOK), jnp.float32),
            ],
        ),
        compiler_params=params(),
        cost_estimate=LONG,
        name="intra",
    )(meta, skip, x, rates, steps, writes, reads, idle)


def finish_kernel(
    local, meta, part_ref, dl_ref, read_ref, own_ref, other_ref, mine_ref, theirs_ref, low_ref, high_ref, _, out_ref,
    factor_s,
):
    step = pl.program_id(0)
    even = meta.even
    r = meta.last_start()
    first = meta.place // 2 * 2 * TOK
    second = first + TOK
    start = meta.start_of(meta.session_at(second + TOK - 1))
    closes = (start > first) & (start < second)
    opens = start == second
    width = local * N

    @pl.when(step == 0)
    def _():
        rates, running = running_rows(dl_ref)
        lane = lax.broadcasted_iota(jnp.int32, (H, TOK), 1)
        base = jnp.sum(jnp.where(lane < r, rates, 0.0), axis=1, keepdims=True)
        factor_s[...] = jnp.exp(jnp.minimum(running - jnp.where(lane >= r, base, 0.0), 0.0))

    factor = factor_s[pl.ds(pl.multiple_of(step * PAIR, PAIR), PAIR), :].T
    token = lax.broadcasted_iota(jnp.int32, (TOK, N), 0)
    resumed = (token >= r) & (r > 0)
    decays = [[factors_of(ref[chip, width:, :], local) for ref in (low_ref, high_ref)] for chip in range(own_ref.shape[0])]
    for group in range(2):
        reads = read_ref[:, group * N : (group + 1) * N].astype(jnp.float32)
        left = jnp.where(resumed, 0.0, reads)
        right = jnp.where(resumed, reads, 0.0)
        reads = jnp.concatenate([left, right], axis=1).astype(jnp.bfloat16)
        for k in range(group * HEADS_PER, (group + 1) * HEADS_PER):
            chip, half, head = k // (2 * local), k // local % 2, k % local
            rows = slice(head * N, (head + 1) * N)
            own = even if half == 0 else jnp.logical_not(even)
            entering = jnp.where(own, own_ref[chip, rows, :], other_ref[chip, rows, :]).astype(jnp.float32)
            restored = jnp.where(own, mine_ref[chip, rows, :], theirs_ref[chip, rows, :])
            whole_state = restored.astype(jnp.float32)
            summary = (low_ref, high_ref)[half][chip, rows, :].astype(jnp.float32)
            middle = decays[chip][half][head : head + 1] * jnp.where(closes, whole_state, entering) + summary
            middle = jnp.where(opens, whole_state, middle)
            entering = jnp.where(even, entering, middle).astype(jnp.bfloat16)
            states = jnp.concatenate([entering, restored], axis=0)
            carried = jnp.dot(reads, states, preferred_element_type=jnp.float32)
            place = slice(k * P_SIZE, (k + 1) * P_SIZE)
            out_ref[:, place] = (part_ref[:, place] + factor[:, k : k + 1] * carried).astype(jnp.bfloat16)


def finish(meta, part, rates, reads, own, other, mine, theirs, low, high, local, idle):
    chips = PAIR // (2 * local)
    states = pl.BlockSpec((chips, local * N, P_SIZE), lambda i, *m: (i, 0, 0))
    stretch = pl.BlockSpec((chips, local * N + EXTRA, P_SIZE), lambda i, *m: (i, 0, 0))
    return pl.pallas_call(
        scalars(finish_kernel, local),
        out_shape=jax.ShapeDtypeStruct((TOK, H * P_SIZE), jnp.bfloat16),
        grid_spec=pltpu.PrefetchScalarGridSpec(
            num_scalar_prefetch=1,
            grid=(STEPS,),
            in_specs=[
                pl.BlockSpec((TOK, PAIR * P_SIZE), lambda i, *m: (0, i)),
                pl.BlockSpec((H, TOK), lambda i, *m: (0, 0)),
                pl.BlockSpec((TOK, 2 * N), lambda i, *m: (0, i)),
                states,
                states,
                states,
                states,
                stretch,
                stretch,
                idle_spec(idle),
            ],
            out_specs=pl.BlockSpec((TOK, PAIR * P_SIZE), lambda i, *m: (0, i)),
            scratch_shapes=[pltpu.VMEM((H, TOK), jnp.float32)],
        ),
        compiler_params=params(),
        cost_estimate=LONG,
        name="finish",
    )(meta, part, rates, reads, own, other, mine, theirs, low, high, idle)


def attend_kernel(
    meta, q_ref, four, two, now, four_across, two_across, now_across, *refs,
):
    history_refs, (sk_ref, sv_ref), (out_ref, token_ref, key_s, value_s) = refs[:16], refs[16:18], refs[-4:]
    factor = 1.0 / math.sqrt(HD)
    first = meta.place * TOK
    r = meta.last_start()
    opening = meta.session_at(first)
    closing = meta.session_at(first + TOK - 1)
    even = meta.even

    def band(number, part):
        if number == 0:
            return four[part]
        if number == 1:
            return jnp.where(even, four_across[part], two_across[part])
        if number == 2:
            return two[part]
        if number == 3:
            return jnp.where(even, two_across[part], now_across[part])
        return now[part]

    token_ref[...] = jnp.zeros_like(token_ref)

    def sinks(ref, session):
        rows = ref[session].astype(jnp.float32)
        spare = jnp.zeros((COLUMNS - SPAN - SINKS, HD), jnp.float32)
        return jnp.concatenate([rows, spare], axis=0).astype(jnp.bfloat16)

    length = (REACH + 1) * TOK

    def one_session(session, key_refs, value_refs, resuming, needed):
        start = meta.start_of(session) - first + WINDOW
        oldest = start - WINDOW + jnp.maximum(SINKS + WINDOW - meta.history(session), 0)

        @pl.when(needed & (start > 0))
        def _():
            row = lax.broadcasted_iota(jnp.int32, (length, WINDOW), 0)
            chips, share, _ = key_refs[0].shape
            index = lax.broadcasted_iota(jnp.int32, (1, WINDOW), 1)
            piece, index = index // (WINDOW // 4), index % (WINDOW // 4)
            near, row_in = index // share, index % share
            far = far_place(near, chips.bit_length() - 1)
            device = meta.place ^ (piece // 2 + piece % 2 * 2 + far * 4)
            place = device * share + row_in
            moved = (row == place + start - WINDOW).astype(jnp.bfloat16)
            part = (WINDOW // 4, HD)
            keys = jnp.concatenate([ref[...].reshape(part) for ref in key_refs], axis=0)
            values = jnp.concatenate([ref[...].reshape(part) for ref in value_refs], axis=0)
            history = jnp.dot(
                moved, jnp.concatenate([keys, values], axis=1), preferred_element_type=jnp.float32
            )
            for i in range(REACH + 1):
                rows = slice(i * TOK, (i + 1) * TOK)
                index = lax.broadcasted_iota(jnp.int32, (TOK, HD), 0) + i * TOK
                turn = index >= start
                key_s[rows, :] = jnp.where(
                    turn, band(i, 0).astype(jnp.float32), history[rows, :HD]
                ).astype(jnp.bfloat16)
                value_s[rows, :] = jnp.where(
                    turn, band(i, 1).astype(jnp.float32), history[rows, HD:]
                ).astype(jnp.bfloat16)

        @pl.when(needed & (start <= 0))
        def _():
            for i in range(REACH + 1):
                rows = slice(i * TOK, (i + 1) * TOK)
                key_s[rows, :] = band(i, 0)
                value_s[rows, :] = band(i, 1)

        for b in range(TOK // BLOCK):
            inside = (b * BLOCK + BLOCK > r) if resuming else (b * BLOCK < r)

            @pl.when(needed & inside)
            def _():
                rows = slice(b * BLOCK, b * BLOCK + SPAN)
                keys = jnp.concatenate([key_s[rows, :], sinks(sk_ref, session)], axis=0)
                values = jnp.concatenate([value_s[rows, :], sinks(sv_ref, session)], axis=0)
                tokens = slice(b * BLOCK, (b + 1) * BLOCK)
                queries = jnp.concatenate(
                    [q_ref[tokens, g * HD : (g + 1) * HD] for g in range(QH // KVH)], axis=0
                )
                scores = lax.dot_general(
                    queries, keys, (((1,), (1,)), ((), ())), preferred_element_type=jnp.float32
                )
                token = lax.broadcasted_iota(jnp.int32, (BLOCK, COLUMNS), 0)
                column = lax.broadcasted_iota(jnp.int32, (BLOCK, COLUMNS), 1)
                seen = (column > token) & (column <= token + WINDOW) & (column >= oldest - b * BLOCK)
                seen = (seen & (column < SPAN)) | ((column >= SPAN) & (column < SPAN + SINKS))
                bias = jnp.where(seen, 0.0, NEG)
                weights, sums = [], []
                for g in range(QH // KVH):
                    score = scores[g * BLOCK : (g + 1) * BLOCK] * factor + bias
                    weight = jnp.exp(score - jnp.max(score, axis=1, keepdims=True))
                    sums.append(jnp.sum(weight, axis=1, keepdims=True))
                    weights.append(weight.astype(jnp.bfloat16))
                mixed = jnp.dot(
                    jnp.concatenate(weights, axis=0), values, preferred_element_type=jnp.float32
                )
                for g in range(QH // KVH):
                    result = mixed[g * BLOCK : (g + 1) * BLOCK] / sums[g]
                    lanes = slice(g * HD, (g + 1) * HD)
                    if resuming:
                        index = lax.broadcasted_iota(jnp.int32, (BLOCK, HD), 0) + b * BLOCK
                        before = out_ref[tokens, lanes].astype(jnp.float32)
                        result = jnp.where(index >= r, result, before)
                    out_ref[tokens, lanes] = result.astype(jnp.bfloat16)

    one_session(opening, history_refs[0:4], history_refs[4:8], False, r > 0)
    one_session(closing, history_refs[8:12], history_refs[12:], True, r >= 0)


def attend(meta, queries, bands, pieces, half, sink_keys, sink_values, idle):
    chips = pieces[0].shape[0]
    share = WINDOW // (4 * chips)
    lanes = QH // KVH * HD

    def history_spec(which, last):
        def index(j, *m):
            known = Scalars(*m)
            session = known.session_at(known.place * TOK + (TOK - 1 if last else 0))
            session = session - (known.place >= half).astype(jnp.int32)
            return (0, (which * 2 + session) * KVH + j, 0)

        return pl.BlockSpec((chips, share, HD), index)

    pad = SEQS, SINKS, HD
    return pl.pallas_call(
        scalars(attend_kernel),
        out_shape=[jax.ShapeDtypeStruct((TOK, QH * HD), jnp.bfloat16), TOKEN],
        grid_spec=pltpu.PrefetchScalarGridSpec(
            num_scalar_prefetch=1,
            grid=(KVH,),
            in_specs=[pl.BlockSpec((TOK, lanes), lambda j, *m: (0, j))]
            + [pl.BlockSpec((2, TOK, HD), lambda j, *m: (0, 0, j))] * len(bands)
            + [history_spec(0, False)] * 4
            + [history_spec(1, False)] * 4
            + [history_spec(0, True)] * 4
            + [history_spec(1, True)] * 4
            + [pl.BlockSpec(pad, lambda j, *m: (0, 0, j))] * 2
            + [idle_spec(a) for a in idle],
            out_specs=[
                pl.BlockSpec((TOK, lanes), lambda j, *m: (0, j)),
                pl.BlockSpec(TOKEN.shape, lambda j, *m: (0, 0)),
            ],
            scratch_shapes=[
                pltpu.VMEM(((REACH + 1) * TOK, HD), jnp.bfloat16),
                pltpu.VMEM(((REACH + 1) * TOK, HD), jnp.bfloat16),
            ],
        ),
        compiler_params=params(),
        cost_estimate=LONG,
        name="attend",
    )(
        meta, queries, *bands, *pieces, *pieces, *pieces, *pieces, sink_keys, sink_values, *idle
    )


def shifted(block, axis, distance):
    devices = range(lax.axis_size(axis))
    return lax.ppermute(block, axis, [(i - distance, i) for i in devices if i - distance in devices])


def shards(
    mamba_input,
    step_size,
    decay_log,
    state_write,
    state_read,
    skip_gain,
    saved_states,
    home_slot,
    turn_lengths,
    history_lengths,
    queries,
    turn_keys,
    turn_values,
    cache_keys,
    cache_values,
    sink_keys,
    sink_values,
):
    place = lax.axis_index("ctx")
    group = lax.axis_index("sess")
    groups = lax.axis_size("sess")
    devices = lax.axis_size("ctx")
    local = saved_states.shape[2]
    width = local * N
    chips = devices // 2
    same_core = [list(range(core, devices, 2)) for core in range(2)]
    meta = jnp.concatenate(
        [jnp.stack([place, group]).astype(jnp.int32), turn_lengths[0], history_lengths[0], home_slot]
    )
    x, rates, steps = mamba_input[0], decay_log[0].T, step_size[0].T
    writes, reads = state_write[0], state_read[0]
    def apart(block, distance):
        return lax.ppermute(block, "ctx", [(i, i ^ distance) for i in range(devices)])

    def exchanged(block):
        return lax.all_to_all(block, "ctx", 0, 0, axis_index_groups=same_core, tiled=True)

    parcel = (1, 4 * KVH * cache_keys.shape[2], HD)
    band = (2, TOK, KVH * HD)
    near, away, key_value = whole(
        scalars(pack_kernel, devices // 2),
        "pack",
        meta,
        [cache_keys[0], cache_values[0], turn_keys[0], turn_values[0]],
        [(parcel, jnp.bfloat16), (parcel, jnp.bfloat16), (band, jnp.bfloat16)],
        mib=60,
    )
    distance = devices // 2
    moved = apart(away, distance)
    four = shifted(key_value, "ctx", 4)

    keep, send = summaries(meta, x, rates, steps, writes, local, away)
    got = apart(send, 1)

    def joined(array):
        return ((2 * array.shape[0], *array.shape[1:]), jnp.bfloat16)

    near, two = whole(
        scalars(join_two_kernel),
        "join_two",
        meta,
        [near, moved, key_value, four],
        [joined(near), (band, jnp.bfloat16)],
        idle=[got],
    )
    distance //= 2
    moved = apart(near, distance)

    [turned] = whole(
        scalars(turn_kernel, local),
        "turn",
        meta,
        [saved_states[0].reshape(SEQS, local, P_SIZE, N)],
        [((SEQS, width, P_SIZE), jnp.float32)],
        idle=[two],
    )
    stored = [turned]
    for j in range(1, groups):
        route = [((i + j) % groups, i) for i in range(groups)]
        stored.append(lax.ppermute(turned, "sess", route))
    two = apart(two, 2)
    [chip] = whole(
        scalars(combine_kernel, local),
        "combine",
        meta,
        [keep, got],
        [(keep.shape, jnp.bfloat16)],
        idle=[turned, two],
    )
    total = exchanged(chip)
    after = chip
    while distance > 2:
        [near] = whole(scalars(join_kernel), "join", meta, [near, moved], [joined(near)], idle=[after])
        after = near
        distance //= 2
        moved = apart(near, distance)
    beside = moved
    resumed, restored = whole(
        scalars(restore_kernel, groups),
        "restore",
        meta,
        stored,
        [((chips, width, P_SIZE), jnp.bfloat16), ((SEQS, width, P_SIZE), jnp.float32)],
        idle=[after],
    )
    mine = exchanged(resumed)
    part, token = intra(meta, skip_gain, x, rates, steps, writes, reads, restored)

    entering, after = whole(
        scalars(recurrence_kernel, local),
        "recurrence",
        meta,
        [total, restored],
        [((chips, width, P_SIZE), jnp.bfloat16), (TOKEN.shape, TOKEN.dtype)],
        idle=[token, beside, mine],
    )
    entering = exchanged(entering)
    pieces = [near, beside, apart(near, 1), apart(beside, 1)]
    bands = [four, two, key_value]
    bands += [apart(block, 1) for block in bands]
    theirs = apart(mine, 1)
    low = apart(keep, 1)
    attended, token = attend(
        meta, queries[0], bands, pieces, devices // 2, sink_keys[0], sink_values[0], [after, theirs, low]
    )
    other = apart(entering, 1)
    mixed = finish(meta, part, rates, reads, entering, other, mine, theirs, low, got, local, token)
    return mixed[None], attended[None]


def solution(mesh):
    token = P("sess", "ctx", None)
    return jax.shard_map(
        shards,
        mesh=mesh,
        in_specs=(
            token,
            token,
            token,
            token,
            token,
            P(),
            P("sess", None, "ctx", None),
            P(),
            P("sess", None),
            P("sess", None),
            token,
            token,
            token,
            P("sess", None, "ctx", None),
            P("sess", None, "ctx", None),
            P("sess", None, None, None),
            P("sess", None, None, None),
        ),
        out_specs=(token, token),
        check_vma=False,
    )
```

```python
import math

import jax
import jax.numpy as jnp
from jax import lax
from jax.experimental import pallas as pl
from jax.experimental.pallas import tpu as pltpu
from jax.sharding import PartitionSpec as P

REACH = 4
SEQS = 3
SINKS = 4
H = 64
P_SIZE = 128
N = 64
G = 8
QH = 32
KVH = 4
HD = 128
WINDOW = 512
TOK = 128

HEADS_PER = H // G
PAIR = 2 * HEADS_PER
STEPS = H // PAIR
EXTRA = 16
BLOCK = 64
SPAN = WINDOW + BLOCK
COLUMNS = SPAN + 64
NEG = -1e30
TOKEN = jax.ShapeDtypeStruct((8, 128), jnp.float32)
SHORT = pl.CostEstimate(flops=1024, bytes_accessed=1024, transcendentals=0)
LONG = pl.CostEstimate(flops=1 << 35, bytes_accessed=1 << 20, transcendentals=0)


class Scalars:
    def __init__(self, ids):
        self.place, self.group = ids[0], ids[1]
        self.one = ids[2]
        self.two = ids[2] + ids[3]
        self.ids = ids
        self.even = self.place % 2 == 0

    def history(self, session):
        return self.ids[2 + SEQS + session]

    def home(self, number):
        return self.ids[2 + 2 * SEQS + number]

    def session_at(self, position):
        return (position >= self.one).astype(jnp.int32) + (position >= self.two).astype(jnp.int32)

    def start_of(self, session):
        return jnp.where(session == 0, 0, jnp.where(session == 1, self.one, self.two))

    def last_start(self):
        first = self.place * TOK
        return jnp.maximum(self.start_of(self.session_at(first + TOK - 1)) - first, 0)


def scalars(kernel, *options):
    def body(ids, *refs):
        kernel(*options, Scalars(ids), *refs)

    return body


def params(mib=60):
    return pltpu.CompilerParams(vmem_limit_bytes=mib * 1024 * 1024)


def running_rows(dl_ref):
    k = lax.broadcasted_iota(jnp.int32, (TOK, TOK), 0)
    u = lax.broadcasted_iota(jnp.int32, (TOK, TOK), 1)
    upto = (k <= u).astype(jnp.bfloat16)
    running = jnp.dot(dl_ref[...], upto, preferred_element_type=jnp.float32)
    return dl_ref[...].astype(jnp.float32), running


def summary_kernel(
    local, meta, x_ref, dl_ref, step_ref, write_ref, keep_ref, send_ref, coef_s, factor_s, write_s
):
    step = pl.program_id(0)

    @pl.when(step == 0)
    def _():
        rates, running = running_rows(dl_ref)
        steps = step_ref[...].astype(jnp.float32)
        r = meta.last_start()
        lane = lax.broadcasted_iota(jnp.int32, (H, TOK), 1)
        last = running[:, TOK - 1 :]
        base = jnp.sum(jnp.where(lane < r, rates, 0.0), axis=1, keepdims=True)
        coef_s[...] = jnp.where(lane >= r, jnp.exp(last - running) * steps, 0.0)
        factor_s[...] = jnp.broadcast_to(jnp.exp(last - base), (H, TOK))
        write_s[...] = write_ref[...].astype(jnp.float32).T

    even = meta.even
    coef = coef_s[pl.ds(pl.multiple_of(step * PAIR, PAIR), PAIR), :]
    factor = factor_s[pl.ds(pl.multiple_of(step * PAIR, PAIR), PAIR), :]
    writes = write_s[pl.ds(pl.multiple_of(step * 2 * N, 2 * N), 2 * N), :]

    def summary(k):
        group = k // HEADS_PER
        loading = (writes[group * N : (group + 1) * N] * coef[k : k + 1]).astype(jnp.bfloat16)
        return jnp.dot(
            loading, x_ref[:, k * P_SIZE : (k + 1) * P_SIZE], preferred_element_type=jnp.float32
        )

    for chip in range(PAIR // (2 * local)):
        low, high = 2 * local * chip, 2 * local * chip + local
        for k in range(local):
            first, second = summary(low + k), summary(high + k)
            rows = slice(k * N, (k + 1) * N)
            keep_ref[chip, rows, :] = jnp.where(even, first, second).astype(jnp.bfloat16)
            send_ref[chip, rows, :] = jnp.where(even, second, first).astype(jnp.bfloat16)
        first, second = factor[low : low + local], factor[high : high + local]
        keep_ref[chip, local * N :, :] = factor_rows(jnp.where(even, first, second))
        send_ref[chip, local * N :, :] = factor_rows(jnp.where(even, second, first))


def factor_rows(rows):
    high = rows.astype(jnp.bfloat16).astype(jnp.float32)
    parts = [high, rows - high]
    if EXTRA > 2 * rows.shape[0]:
        parts.append(jnp.zeros((EXTRA - 2 * rows.shape[0], TOK), jnp.float32))
    return jnp.concatenate(parts, axis=0).astype(jnp.bfloat16)


def factors_of(block, local):
    block = block.astype(jnp.float32)
    return block[:local] + block[local : 2 * local]


def summaries(meta, x, rates, steps, writes, local):
    chips = H // (2 * local)
    rows = local * N + EXTRA
    shape = jax.ShapeDtypeStruct((chips, rows, P_SIZE), jnp.bfloat16)
    spec = pl.BlockSpec((PAIR // (2 * local), rows, P_SIZE), lambda i, *m: (i, 0, 0))
    return pl.pallas_call(
        scalars(summary_kernel, local),
        out_shape=[shape, shape],
        grid_spec=pltpu.PrefetchScalarGridSpec(
            num_scalar_prefetch=1,
            grid=(STEPS,),
            in_specs=[
                pl.BlockSpec((TOK, PAIR * P_SIZE), lambda i, *m: (0, i)),
                pl.BlockSpec((H, TOK), lambda i, *m: (0, 0)),
                pl.BlockSpec((H, TOK), lambda i, *m: (0, 0)),
                pl.BlockSpec((TOK, G * N), lambda i, *m: (0, 0)),
            ],
            out_specs=[spec, spec],
            scratch_shapes=[
                pltpu.VMEM((H, TOK), jnp.float32),
                pltpu.VMEM((H, TOK), jnp.float32),
                pltpu.VMEM((G * N, TOK), jnp.float32),
            ],
        ),
        compiler_params=params(),
        cost_estimate=LONG,
        name="summaries",
    )(meta, x, rates, steps, writes)


def idle_spec(array):
    return pl.BlockSpec(memory_space=pl.ANY)


def whole(kernel, name, meta, arrays, shapes, idle=(), mib=16, scratch=()):
    def spec(shape):
        return pl.BlockSpec(shape, lambda i, *m: (0,) * len(shape))

    return pl.pallas_call(
        kernel,
        out_shape=[jax.ShapeDtypeStruct(s, t) for s, t in shapes],
        grid_spec=pltpu.PrefetchScalarGridSpec(
            num_scalar_prefetch=1,
            grid=(1,),
            in_specs=[spec(a.shape) for a in arrays] + [idle_spec(a) for a in idle],
            out_specs=[spec(s) for s, _ in shapes],
            scratch_shapes=scratch,
        ),
        compiler_params=params(mib),
        cost_estimate=LONG,
        name=name,
    )(meta, *arrays, *idle)


def restore_kernel(local, half, groups, meta, *refs):
    stored, (keys_ref, values_ref, turn_keys_ref, turn_values_ref) = refs[:groups], refs[groups : groups + 4]
    home_ref, away_ref, band_ref, restored_ref = refs[-4:]
    band_ref[0] = turn_keys_ref[...]
    band_ref[1] = turn_values_ref[...]
    for s in range(SEQS):
        slot = meta.home(meta.group * SEQS + s)
        source = (slot // SEQS - meta.group + groups) % groups
        for k in range(local):
            state = stored[0][slot % SEQS, k]
            for j in range(1, groups):
                state = jnp.where(source == j, stored[j][slot % SEQS, k], state)
            restored_ref[s, k * N : (k + 1) * N, :] = state.T
    rows = keys_ref.shape[1]
    upper = (meta.place >= half).astype(jnp.int32)
    for out_ref, first in ((home_ref, upper), (away_ref, 1 - upper)):
        for which, ref in enumerate((keys_ref, values_ref)):
            for s in range(2):
                for j in range(KVH):
                    place = ((which * 2 + s) * KVH + j) * rows
                    out_ref[0, place : place + rows, :] = ref[first + s, :, j * HD : (j + 1) * HD]
        out_ref[0, 4 * KVH * rows :, :] = restored_ref[first + 1].astype(jnp.bfloat16)


def copy_kernel(meta, array_ref, *refs):
    refs[-1][...] = array_ref[...]


def join_kernel(meta, first_ref, second_ref, *refs):
    out_ref = refs[-1]
    count = first_ref.shape[0]
    out_ref[:count] = first_ref[...]
    out_ref[count:] = second_ref[...]


def join_two_kernel(meta, first_ref, second_ref, key_value_ref, four_ref, *refs):
    out_ref, two_ref = refs[-2:]
    count = first_ref.shape[0]
    out_ref[:count] = first_ref[...]
    out_ref[count:] = second_ref[...]
    two_ref[...] = jnp.where(meta.place // 2 % 2 == 0, key_value_ref[...], four_ref[...])


def far_place(distance, bits):
    place = distance * 0
    for k in range(bits):
        place = place + ((distance // (1 << k)) % 2) * (1 << (bits - 1 - k))
    return place


def combine_kernel(local, meta, keep_ref, got_ref, *refs):
    out_ref = refs[-1]
    even = meta.even
    second = (meta.place // 2 * 2 + 1) * TOK
    closes = meta.start_of(meta.session_at(second + TOK - 1)) >= second
    width = local * N
    for chip in range(keep_ref.shape[0]):
        keep = factors_of(keep_ref[chip, width:, :], local)
        got = factors_of(got_ref[chip, width:, :], local)
        f0, f1 = jnp.where(even, keep, got), jnp.where(even, got, keep)
        out_ref[chip, width:, :] = factor_rows(jnp.where(closes, f1, f0 * f1))
        carry = jnp.where(closes, 0.0, f1)
        for k in range(local):
            rows = slice(k * N, (k + 1) * N)
            keep = keep_ref[chip, rows, :].astype(jnp.float32)
            got = got_ref[chip, rows, :].astype(jnp.float32)
            s0, s1 = jnp.where(even, keep, got), jnp.where(even, got, keep)
            out_ref[chip, rows, :] = (carry[k : k + 1] * s0 + s1).astype(jnp.bfloat16)


def recurrence_kernel(local, meta, got_ref, restored_ref, *refs):
    out_ref, token_ref = refs[-2:]
    token_ref[...] = jnp.zeros_like(token_ref)
    width = local * N
    span = 2 * TOK
    state = [jnp.zeros((N, P_SIZE), jnp.float32) for _ in range(local)]
    for c in range(got_ref.shape[0]):
        first = c * span
        opening = meta.session_at(first)
        closing = meta.session_at(first + span - 1)
        opens = meta.start_of(opening) >= first
        closes = meta.start_of(closing) >= first
        factor = factors_of(got_ref[c, width:, :], local)
        for k in range(local):
            rows = slice(k * N, (k + 1) * N)
            entering = jnp.where(opens, restored_ref[opening, rows, :], state[k])
            out_ref[c, rows, :] = entering.astype(jnp.bfloat16)
            source = jnp.where(closes, restored_ref[closing, rows, :], state[k])
            state[k] = factor[k : k + 1] * source + got_ref[c, rows, :].astype(jnp.float32)


def intra_kernel(meta, skip, x_ref, dl_ref, step_ref, write_ref, read_ref, _, out_ref, token_ref, run_s, step_s):
    step = pl.program_id(0)

    @pl.when(step == 0)
    def _():
        _, running = running_rows(dl_ref)
        run_s[...] = running
        step_s[...] = step_ref[...].astype(jnp.float32)

    token_ref[...] = jnp.zeros_like(token_ref)
    heads = pl.ds(pl.multiple_of(step * PAIR, PAIR), PAIR)
    running = run_s[heads, :]
    sizes = step_s[heads, :]
    columns = running.T
    r = meta.last_start()
    t = lax.broadcasted_iota(jnp.int32, (TOK, TOK), 0)
    u = lax.broadcasted_iota(jnp.int32, (TOK, TOK), 1)
    causal = (u <= t) & ((u >= r) | (t < r))
    for group in range(2):
        part = slice(group * N, (group + 1) * N)
        products = lax.dot_general(
            read_ref[:, part], write_ref[:, part], (((1,), (1,)), ((), ())),
            preferred_element_type=jnp.float32,
        )
        products = jnp.where(causal, products, 0.0)
        for k in range(group * HEADS_PER, (group + 1) * HEADS_PER):
            difference = columns[:, k : k + 1] - running[k : k + 1]
            decay = jnp.exp(jnp.minimum(difference, 0.0))
            mixing = (products * decay * sizes[k : k + 1]).astype(jnp.bfloat16)
            place = slice(k * P_SIZE, (k + 1) * P_SIZE)
            x = x_ref[:, place]
            mixed = jnp.dot(mixing, x, preferred_element_type=jnp.float32)
            out_ref[:, place] = mixed + skip[step * PAIR + k] * x.astype(jnp.float32)


def intra(meta, skip, x, rates, steps, writes, reads, idle):
    return pl.pallas_call(
        scalars(intra_kernel),
        out_shape=[jax.ShapeDtypeStruct((TOK, H * P_SIZE), jnp.float32), TOKEN],
        grid_spec=pltpu.PrefetchScalarGridSpec(
            num_scalar_prefetch=2,
            grid=(STEPS,),
            in_specs=[
                pl.BlockSpec((TOK, PAIR * P_SIZE), lambda i, *m: (0, i)),
                pl.BlockSpec((H, TOK), lambda i, *m: (0, 0)),
                pl.BlockSpec((H, TOK), lambda i, *m: (0, 0)),
                pl.BlockSpec((TOK, 2 * N), lambda i, *m: (0, i)),
                pl.BlockSpec((TOK, 2 * N), lambda i, *m: (0, i)),
                pl.BlockSpec(memory_space=pl.ANY),
            ],
            out_specs=[
                pl.BlockSpec((TOK, PAIR * P_SIZE), lambda i, *m: (0, i)),
                pl.BlockSpec(TOKEN.shape, lambda i, *m: (0, 0)),
            ],
            scratch_shapes=[
                pltpu.VMEM((H, TOK), jnp.float32),
                pltpu.VMEM((H, TOK), jnp.float32),
            ],
        ),
        compiler_params=params(),
        cost_estimate=LONG,
        name="intra",
    )(meta, skip, x, rates, steps, writes, reads, idle)


def finish_kernel(
    local, meta, part_ref, dl_ref, read_ref, own_ref, other_ref, low_ref, high_ref, *refs,
):
    pieces, (out_ref, factor_s) = refs[:4], refs[-2:]
    bits = pieces[0].shape[0].bit_length() - 1
    step = pl.program_id(0)
    even = meta.even
    r = meta.last_start()
    first = meta.place // 2 * 2 * TOK
    second = first + TOK
    start = meta.start_of(meta.session_at(second + TOK - 1))
    closes = (start > first) & (start < second)
    opens = start == second
    width = local * N

    @pl.when(step == 0)
    def _():
        rates, running = running_rows(dl_ref)
        lane = lax.broadcasted_iota(jnp.int32, (H, TOK), 1)
        base = jnp.sum(jnp.where(lane < r, rates, 0.0), axis=1, keepdims=True)
        factor_s[...] = jnp.exp(jnp.minimum(running - jnp.where(lane >= r, base, 0.0), 0.0))

    factor = factor_s[pl.ds(pl.multiple_of(step * PAIR, PAIR), PAIR), :].T
    token = lax.broadcasted_iota(jnp.int32, (TOK, N), 0)
    resumed = (token >= r) & (r > 0)
    decays = [[factors_of(ref[chip, width:, :], local) for ref in (low_ref, high_ref)] for chip in range(own_ref.shape[0])]
    for group in range(2):
        reads = read_ref[:, group * N : (group + 1) * N].astype(jnp.float32)
        left = jnp.where(resumed, 0.0, reads)
        right = jnp.where(resumed, reads, 0.0)
        reads = jnp.concatenate([left, right], axis=1).astype(jnp.bfloat16)
        for k in range(group * HEADS_PER, (group + 1) * HEADS_PER):
            chip, half, head = k // (2 * local), k // local % 2, k % local
            rows = slice(head * N, (head + 1) * N)
            own = even if half == 0 else jnp.logical_not(even)
            entering = jnp.where(own, own_ref[chip, rows, :], other_ref[chip, rows, :]).astype(jnp.float32)
            distance = (step * own_ref.shape[0] + chip) ^ (meta.place // 2)
            far, near = far_place(distance // 2, bits), distance % 2 == 0
            found = [piece[far, rows, :] for piece in pieces]
            restored = jnp.where(own, jnp.where(near, found[0], found[1]), jnp.where(near, found[2], found[3]))
            whole_state = restored.astype(jnp.float32)
            summary = (low_ref, high_ref)[half][chip, rows, :].astype(jnp.float32)
            middle = decays[chip][half][head : head + 1] * jnp.where(closes, whole_state, entering) + summary
            middle = jnp.where(opens, whole_state, middle)
            entering = jnp.where(even, entering, middle).astype(jnp.bfloat16)
            states = jnp.concatenate([entering, restored], axis=0)
            carried = jnp.dot(reads, states, preferred_element_type=jnp.float32)
            place = slice(k * P_SIZE, (k + 1) * P_SIZE)
            out_ref[:, place] = (part_ref[:, place] + factor[:, k : k + 1] * carried).astype(jnp.bfloat16)


def finish(meta, part, rates, reads, own, other, low, high, pieces, local):
    chips = PAIR // (2 * local)
    count, length, _ = pieces[0].shape
    resumed = pl.BlockSpec((count, local * N, P_SIZE), lambda i, *m: (0, length // (local * N) - 1, 0))
    states = pl.BlockSpec((chips, local * N, P_SIZE), lambda i, *m: (i, 0, 0))
    stretch = pl.BlockSpec((chips, local * N + EXTRA, P_SIZE), lambda i, *m: (i, 0, 0))
    return pl.pallas_call(
        scalars(finish_kernel, local),
        out_shape=jax.ShapeDtypeStruct((TOK, H * P_SIZE), jnp.bfloat16),
        grid_spec=pltpu.PrefetchScalarGridSpec(
            num_scalar_prefetch=1,
            grid=(STEPS,),
            in_specs=[
                pl.BlockSpec((TOK, PAIR * P_SIZE), lambda i, *m: (0, i)),
                pl.BlockSpec((H, TOK), lambda i, *m: (0, 0)),
                pl.BlockSpec((TOK, 2 * N), lambda i, *m: (0, i)),
                states,
                states,
                stretch,
                stretch,
            ]
            + [resumed] * 4,
            out_specs=pl.BlockSpec((TOK, PAIR * P_SIZE), lambda i, *m: (0, i)),
            scratch_shapes=[pltpu.VMEM((H, TOK), jnp.float32)],
        ),
        compiler_params=params(),
        cost_estimate=LONG,
        name="finish",
    )(meta, part, rates, reads, own, other, low, high, *pieces)


def attend_kernel(
    meta, q_ref, four, two, now, four_across, two_across, now_across, *refs,
):
    history_refs, (sk_ref, sv_ref), (out_ref, token_ref, key_s, value_s) = refs[:16], refs[16:18], refs[-4:]
    factor = 1.0 / math.sqrt(HD)
    first = meta.place * TOK
    r = meta.last_start()
    opening = meta.session_at(first)
    closing = meta.session_at(first + TOK - 1)
    even = meta.even

    def band(number, part):
        if number == 0:
            return four[part]
        if number == 1:
            return jnp.where(even, four_across[part], two_across[part])
        if number == 2:
            return two[part]
        if number == 3:
            return jnp.where(even, two_across[part], now_across[part])
        return now[part]

    token_ref[...] = jnp.zeros_like(token_ref)

    def sinks(ref, session):
        rows = ref[session].astype(jnp.float32)
        spare = jnp.zeros((COLUMNS - SPAN - SINKS, HD), jnp.float32)
        return jnp.concatenate([rows, spare], axis=0).astype(jnp.bfloat16)

    length = (REACH + 1) * TOK

    def one_session(session, key_refs, value_refs, resuming, needed):
        start = meta.start_of(session) - first + WINDOW
        oldest = start - WINDOW + jnp.maximum(SINKS + WINDOW - meta.history(session), 0)

        @pl.when(needed & (start > 0))
        def _():
            row = lax.broadcasted_iota(jnp.int32, (length, WINDOW), 0)
            chips, share, _ = key_refs[0].shape
            index = lax.broadcasted_iota(jnp.int32, (1, WINDOW), 1)
            piece, index = index // (WINDOW // 4), index % (WINDOW // 4)
            near, row_in = index // share, index % share
            far = far_place(near, chips.bit_length() - 1)
            device = meta.place ^ (piece // 2 + piece % 2 * 2 + far * 4)
            place = device * share + row_in
            moved = (row == place + start - WINDOW).astype(jnp.bfloat16)
            part = (WINDOW // 4, HD)
            keys = jnp.concatenate([ref[...].reshape(part) for ref in key_refs], axis=0)
            values = jnp.concatenate([ref[...].reshape(part) for ref in value_refs], axis=0)
            history = jnp.dot(
                moved, jnp.concatenate([keys, values], axis=1), preferred_element_type=jnp.float32
            )
            for i in range(REACH + 1):
                rows = slice(i * TOK, (i + 1) * TOK)
                index = lax.broadcasted_iota(jnp.int32, (TOK, HD), 0) + i * TOK
                turn = index >= start
                key_s[rows, :] = jnp.where(
                    turn, band(i, 0).astype(jnp.float32), history[rows, :HD]
                ).astype(jnp.bfloat16)
                value_s[rows, :] = jnp.where(
                    turn, band(i, 1).astype(jnp.float32), history[rows, HD:]
                ).astype(jnp.bfloat16)

        @pl.when(needed & (start <= 0))
        def _():
            for i in range(REACH + 1):
                rows = slice(i * TOK, (i + 1) * TOK)
                key_s[rows, :] = band(i, 0)
                value_s[rows, :] = band(i, 1)

        for b in range(TOK // BLOCK):
            inside = (b * BLOCK + BLOCK > r) if resuming else (b * BLOCK < r)

            @pl.when(needed & inside)
            def _():
                rows = slice(b * BLOCK, b * BLOCK + SPAN)
                keys = jnp.concatenate([key_s[rows, :], sinks(sk_ref, session)], axis=0)
                values = jnp.concatenate([value_s[rows, :], sinks(sv_ref, session)], axis=0)
                tokens = slice(b * BLOCK, (b + 1) * BLOCK)
                queries = jnp.concatenate(
                    [q_ref[tokens, g * HD : (g + 1) * HD] for g in range(QH // KVH)], axis=0
                )
                scores = lax.dot_general(
                    queries, keys, (((1,), (1,)), ((), ())), preferred_element_type=jnp.float32
                )
                token = lax.broadcasted_iota(jnp.int32, (BLOCK, COLUMNS), 0)
                column = lax.broadcasted_iota(jnp.int32, (BLOCK, COLUMNS), 1)
                seen = (column > token) & (column <= token + WINDOW) & (column >= oldest - b * BLOCK)
                seen = (seen & (column < SPAN)) | ((column >= SPAN) & (column < SPAN + SINKS))
                bias = jnp.where(seen, 0.0, NEG)
                weights, sums = [], []
                for g in range(QH // KVH):
                    score = scores[g * BLOCK : (g + 1) * BLOCK] * factor + bias
                    weight = jnp.exp(score - jnp.max(score, axis=1, keepdims=True))
                    sums.append(jnp.sum(weight, axis=1, keepdims=True))
                    weights.append(weight.astype(jnp.bfloat16))
                mixed = jnp.dot(
                    jnp.concatenate(weights, axis=0), values, preferred_element_type=jnp.float32
                )
                for g in range(QH // KVH):
                    result = mixed[g * BLOCK : (g + 1) * BLOCK] / sums[g]
                    lanes = slice(g * HD, (g + 1) * HD)
                    if resuming:
                        index = lax.broadcasted_iota(jnp.int32, (BLOCK, HD), 0) + b * BLOCK
                        before = out_ref[tokens, lanes].astype(jnp.float32)
                        result = jnp.where(index >= r, result, before)
                    out_ref[tokens, lanes] = result.astype(jnp.bfloat16)

    one_session(opening, history_refs[0:4], history_refs[4:8], False, r > 0)
    one_session(closing, history_refs[8:12], history_refs[12:], True, r >= 0)


def attend(meta, queries, bands, pieces, half, sink_keys, sink_values, idle):
    chips = pieces[0].shape[0]
    share = WINDOW // (4 * chips)
    lanes = QH // KVH * HD

    def history_spec(which, last):
        def index(j, *m):
            known = Scalars(*m)
            session = known.session_at(known.place * TOK + (TOK - 1 if last else 0))
            session = session - (known.place >= half).astype(jnp.int32)
            return (0, (which * 2 + session) * KVH + j, 0)

        return pl.BlockSpec((chips, share, HD), index)

    pad = SEQS, SINKS, HD
    return pl.pallas_call(
        scalars(attend_kernel),
        out_shape=[jax.ShapeDtypeStruct((TOK, QH * HD), jnp.bfloat16), TOKEN],
        grid_spec=pltpu.PrefetchScalarGridSpec(
            num_scalar_prefetch=1,
            grid=(KVH,),
            in_specs=[pl.BlockSpec((TOK, lanes), lambda j, *m: (0, j))]
            + [pl.BlockSpec((2, TOK, HD), lambda j, *m: (0, 0, j))] * len(bands)
            + [history_spec(0, False)] * 4
            + [history_spec(1, False)] * 4
            + [history_spec(0, True)] * 4
            + [history_spec(1, True)] * 4
            + [pl.BlockSpec(pad, lambda j, *m: (0, 0, j))] * 2
            + [idle_spec(a) for a in idle],
            out_specs=[
                pl.BlockSpec((TOK, lanes), lambda j, *m: (0, j)),
                pl.BlockSpec(TOKEN.shape, lambda j, *m: (0, 0)),
            ],
            scratch_shapes=[
                pltpu.VMEM(((REACH + 1) * TOK, HD), jnp.bfloat16),
                pltpu.VMEM(((REACH + 1) * TOK, HD), jnp.bfloat16),
            ],
        ),
        compiler_params=params(),
        cost_estimate=SHORT,
        name="attend",
    )(
        meta, queries, *bands, *pieces, *pieces, *pieces, *pieces, sink_keys, sink_values, *idle
    )


def shifted(block, axis, distance):
    devices = range(lax.axis_size(axis))
    return lax.ppermute(block, axis, [(i - distance, i) for i in devices if i - distance in devices])


def shards(
    mamba_input,
    step_size,
    decay_log,
    state_write,
    state_read,
    skip_gain,
    saved_states,
    home_slot,
    turn_lengths,
    history_lengths,
    queries,
    turn_keys,
    turn_values,
    cache_keys,
    cache_values,
    sink_keys,
    sink_values,
):
    place = lax.axis_index("ctx")
    group = lax.axis_index("sess")
    groups = lax.axis_size("sess")
    devices = lax.axis_size("ctx")
    local = saved_states.shape[2]
    width = local * N
    chips = devices // 2
    same_core = [list(range(core, devices, 2)) for core in range(2)]
    meta = jnp.concatenate(
        [jnp.stack([place, group]).astype(jnp.int32), turn_lengths[0], history_lengths[0], home_slot]
    )
    x, rates, steps = mamba_input[0], decay_log[0].T, step_size[0].T
    writes, reads = state_write[0], state_read[0]
    def apart(block, distance):
        return lax.ppermute(block, "ctx", [(i, i ^ distance) for i in range(devices)])

    def exchanged(block):
        return lax.all_to_all(block, "ctx", 0, 0, axis_index_groups=same_core, tiled=True)

    stored = [saved_states[0]]
    for j in range(1, groups):
        route = [((i + j) % groups, i) for i in range(groups)]
        stored.append(lax.ppermute(saved_states[0], "sess", route))
    stored = [block.reshape(SEQS, local, P_SIZE, N) for block in stored]

    keep, send = summaries(meta, x, rates, steps, writes, local)
    got = apart(send, 1)

    parcel = (1, 4 * KVH * cache_keys.shape[2] + width, HD)
    band = (2, TOK, KVH * HD)
    near, away, key_value, restored = whole(
        scalars(restore_kernel, local, devices // 2, groups),
        "restore",
        meta,
        [*stored, cache_keys[0], cache_values[0], turn_keys[0], turn_values[0]],
        [
            (parcel, jnp.bfloat16),
            (parcel, jnp.bfloat16),
            (band, jnp.bfloat16),
            ((SEQS, width, P_SIZE), jnp.float32),
        ],
        idle=[send],
        mib=60,
    )
    distance = devices // 2
    moved = apart(away, distance)
    four = shifted(key_value, "ctx", 4)
    [chip] = whole(
        scalars(combine_kernel, local),
        "combine",
        meta,
        [keep, got],
        [(keep.shape, jnp.bfloat16)],
        idle=[key_value],
    )
    total = exchanged(chip)

    def joined(array):
        return ((2 * array.shape[0], *array.shape[1:]), jnp.bfloat16)

    near, two = whole(
        scalars(join_two_kernel),
        "join_two",
        meta,
        [near, moved, key_value, four],
        [joined(near), (band, jnp.bfloat16)],
        idle=[chip],
    )
    distance //= 2
    moved = apart(near, distance)
    two = apart(two, 2)
    part, token = intra(meta, skip_gain, x, rates, steps, writes, reads, near)
    after = token
    while distance > 2:
        [near] = whole(scalars(join_kernel), "join", meta, [near, moved], [joined(near)], idle=[after])
        after = near
        distance //= 2
        moved = apart(near, distance)
    beside = moved

    entering, after = whole(
        scalars(recurrence_kernel, local),
        "recurrence",
        meta,
        [total, restored],
        [((chips, width, P_SIZE), jnp.bfloat16), (TOKEN.shape, TOKEN.dtype)],
        idle=[after, two],
    )
    entering = exchanged(entering)
    pieces = [near, beside, apart(near, 1), apart(beside, 1)]
    bands = [four, two, key_value]
    bands += [apart(block, 1) for block in bands]
    low = apart(keep, 1)
    attended, token = attend(
        meta, queries[0], bands, pieces, devices // 2, sink_keys[0], sink_values[0], [after, low]
    )
    [entering] = whole(
        scalars(copy_kernel), "copy", meta, [entering], [((chips, width, P_SIZE), jnp.bfloat16)], idle=[token]
    )
    other = apart(entering, 1)
    mixed = finish(meta, part, rates, reads, entering, other, low, got, pieces, local)
    return mixed[None], attended[None]


def solution(mesh):
    token = P("sess", "ctx", None)
    return jax.shard_map(
        shards,
        mesh=mesh,
        in_specs=(
            token,
            token,
            token,
            token,
            token,
            P(),
            P("sess", None, "ctx", None),
            P(),
            P("sess", None),
            P("sess", None),
            token,
            token,
            token,
            P("sess", None, "ctx", None),
            P("sess", None, "ctx", None),
            P("sess", None, None, None),
            P("sess", None, None, None),
        ),
        out_specs=(token, token),
        check_vma=False,
    )
```

```python
import math

import jax
import jax.numpy as jnp
from jax import lax
from jax.experimental import pallas as pl
from jax.experimental.pallas import tpu as pltpu
from jax.sharding import PartitionSpec as P

REACH = 4
SEQS = 3
SINKS = 4
H = 64
P_SIZE = 128
N = 64
G = 8
QH = 32
KVH = 4
HD = 128
WINDOW = 512
TOK = 128

HEADS_PER = H // G
PAIR = 2 * HEADS_PER
STEPS = H // PAIR
EXTRA = 16
BLOCK = 64
SPAN = WINDOW + BLOCK
COLUMNS = SPAN + 64
NEG = -1e30
TOKEN = jax.ShapeDtypeStruct((8, 128), jnp.float32)
SHORT = pl.CostEstimate(flops=1024, bytes_accessed=1024, transcendentals=0)
LONG = pl.CostEstimate(flops=1 << 35, bytes_accessed=1 << 20, transcendentals=0)


class Scalars:
    def __init__(self, ids):
        self.place, self.group = ids[0], ids[1]
        self.one = ids[2]
        self.two = ids[2] + ids[3]
        self.ids = ids
        self.even = self.place % 2 == 0

    def history(self, session):
        return self.ids[2 + SEQS + session]

    def home(self, number):
        return self.ids[2 + 2 * SEQS + number]

    def session_at(self, position):
        return (position >= self.one).astype(jnp.int32) + (position >= self.two).astype(jnp.int32)

    def start_of(self, session):
        return jnp.where(session == 0, 0, jnp.where(session == 1, self.one, self.two))

    def last_start(self):
        first = self.place * TOK
        return jnp.maximum(self.start_of(self.session_at(first + TOK - 1)) - first, 0)


def scalars(kernel, *options):
    def body(ids, *refs):
        kernel(*options, Scalars(ids), *refs)

    return body


def params(mib=60):
    return pltpu.CompilerParams(vmem_limit_bytes=mib * 1024 * 1024)


def running_rows(dl_ref):
    k = lax.broadcasted_iota(jnp.int32, (TOK, TOK), 0)
    u = lax.broadcasted_iota(jnp.int32, (TOK, TOK), 1)
    upto = (k <= u).astype(jnp.bfloat16)
    running = jnp.dot(dl_ref[...], upto, preferred_element_type=jnp.float32)
    return dl_ref[...].astype(jnp.float32), running


def summary_kernel(
    local, meta, x_ref, dl_ref, step_ref, write_ref, keep_ref, send_ref, coef_s, factor_s, write_s
):
    step = pl.program_id(0)

    @pl.when(step == 0)
    def _():
        rates, running = running_rows(dl_ref)
        steps = step_ref[...].astype(jnp.float32)
        r = meta.last_start()
        lane = lax.broadcasted_iota(jnp.int32, (H, TOK), 1)
        last = running[:, TOK - 1 :]
        base = jnp.sum(jnp.where(lane < r, rates, 0.0), axis=1, keepdims=True)
        coef_s[...] = jnp.where(lane >= r, jnp.exp(last - running) * steps, 0.0)
        factor_s[...] = jnp.broadcast_to(jnp.exp(last - base), (H, TOK))
        write_s[...] = write_ref[...].astype(jnp.float32).T

    even = meta.even
    coef = coef_s[pl.ds(pl.multiple_of(step * PAIR, PAIR), PAIR), :]
    factor = factor_s[pl.ds(pl.multiple_of(step * PAIR, PAIR), PAIR), :]
    writes = write_s[pl.ds(pl.multiple_of(step * 2 * N, 2 * N), 2 * N), :]

    def summary(k):
        group = k // HEADS_PER
        loading = (writes[group * N : (group + 1) * N] * coef[k : k + 1]).astype(jnp.bfloat16)
        return jnp.dot(
            loading, x_ref[:, k * P_SIZE : (k + 1) * P_SIZE], preferred_element_type=jnp.float32
        )

    for chip in range(PAIR // (2 * local)):
        low, high = 2 * local * chip, 2 * local * chip + local
        for k in range(local):
            first, second = summary(low + k), summary(high + k)
            rows = slice(k * N, (k + 1) * N)
            keep_ref[chip, rows, :] = jnp.where(even, first, second).astype(jnp.bfloat16)
            send_ref[chip, rows, :] = jnp.where(even, second, first).astype(jnp.bfloat16)
        first, second = factor[low : low + local], factor[high : high + local]
        keep_ref[chip, local * N :, :] = factor_rows(jnp.where(even, first, second))
        send_ref[chip, local * N :, :] = factor_rows(jnp.where(even, second, first))


def factor_rows(rows):
    high = rows.astype(jnp.bfloat16).astype(jnp.float32)
    parts = [high, rows - high]
    if EXTRA > 2 * rows.shape[0]:
        parts.append(jnp.zeros((EXTRA - 2 * rows.shape[0], TOK), jnp.float32))
    return jnp.concatenate(parts, axis=0).astype(jnp.bfloat16)


def factors_of(block, local):
    block = block.astype(jnp.float32)
    return block[:local] + block[local : 2 * local]


def summaries(meta, x, rates, steps, writes, local):
    chips = H // (2 * local)
    rows = local * N + EXTRA
    shape = jax.ShapeDtypeStruct((chips, rows, P_SIZE), jnp.bfloat16)
    spec = pl.BlockSpec((PAIR // (2 * local), rows, P_SIZE), lambda i, *m: (i, 0, 0))
    return pl.pallas_call(
        scalars(summary_kernel, local),
        out_shape=[shape, shape],
        grid_spec=pltpu.PrefetchScalarGridSpec(
            num_scalar_prefetch=1,
            grid=(STEPS,),
            in_specs=[
                pl.BlockSpec((TOK, PAIR * P_SIZE), lambda i, *m: (0, i)),
                pl.BlockSpec((H, TOK), lambda i, *m: (0, 0)),
                pl.BlockSpec((H, TOK), lambda i, *m: (0, 0)),
                pl.BlockSpec((TOK, G * N), lambda i, *m: (0, 0)),
            ],
            out_specs=[spec, spec],
            scratch_shapes=[
                pltpu.VMEM((H, TOK), jnp.float32),
                pltpu.VMEM((H, TOK), jnp.float32),
                pltpu.VMEM((G * N, TOK), jnp.float32),
            ],
        ),
        compiler_params=params(),
        cost_estimate=LONG,
        name="summaries",
    )(meta, x, rates, steps, writes)


def idle_spec(array):
    return pl.BlockSpec(memory_space=pl.ANY)


def whole(kernel, name, meta, arrays, shapes, idle=(), mib=16, scratch=()):
    def spec(shape):
        return pl.BlockSpec(shape, lambda i, *m: (0,) * len(shape))

    return pl.pallas_call(
        kernel,
        out_shape=[jax.ShapeDtypeStruct(s, t) for s, t in shapes],
        grid_spec=pltpu.PrefetchScalarGridSpec(
            num_scalar_prefetch=1,
            grid=(1,),
            in_specs=[spec(a.shape) for a in arrays] + [idle_spec(a) for a in idle],
            out_specs=[spec(s) for s, _ in shapes],
            scratch_shapes=scratch,
        ),
        compiler_params=params(mib),
        cost_estimate=LONG,
        name=name,
    )(meta, *arrays, *idle)


def restore_kernel(local, half, groups, meta, *refs):
    stored, (keys_ref, values_ref, turn_keys_ref, turn_values_ref) = refs[:groups], refs[groups : groups + 4]
    home_ref, away_ref, band_ref, restored_ref = refs[-4:]
    band_ref[0] = turn_keys_ref[...]
    band_ref[1] = turn_values_ref[...]
    for s in range(SEQS):
        slot = meta.home(meta.group * SEQS + s)
        source = (slot // SEQS - meta.group + groups) % groups
        for k in range(local):
            state = stored[0][slot % SEQS, k]
            for j in range(1, groups):
                state = jnp.where(source == j, stored[j][slot % SEQS, k], state)
            restored_ref[s, k * N : (k + 1) * N, :] = state.T
    rows = keys_ref.shape[1]
    upper = (meta.place >= half).astype(jnp.int32)
    for out_ref, first in ((home_ref, upper), (away_ref, 1 - upper)):
        for which, ref in enumerate((keys_ref, values_ref)):
            for s in range(2):
                for j in range(KVH):
                    place = ((which * 2 + s) * KVH + j) * rows
                    out_ref[0, place : place + rows, :] = ref[first + s, :, j * HD : (j + 1) * HD]
        out_ref[0, 4 * KVH * rows :, :] = restored_ref[first + 1].astype(jnp.bfloat16)


def copy_kernel(meta, array_ref, *refs):
    refs[-1][...] = array_ref[...]


def join_kernel(meta, first_ref, second_ref, *refs):
    out_ref = refs[-1]
    count = first_ref.shape[0]
    out_ref[:count] = first_ref[...]
    out_ref[count:] = second_ref[...]


def join_two_kernel(meta, first_ref, second_ref, key_value_ref, four_ref, *refs):
    out_ref, two_ref = refs[-2:]
    count = first_ref.shape[0]
    out_ref[:count] = first_ref[...]
    out_ref[count:] = second_ref[...]
    two_ref[...] = jnp.where(meta.place // 2 % 2 == 0, key_value_ref[...], four_ref[...])


def far_place(distance, bits):
    place = distance * 0
    for k in range(bits):
        place = place + ((distance // (1 << k)) % 2) * (1 << (bits - 1 - k))
    return place


def combine_kernel(local, meta, keep_ref, got_ref, *refs):
    out_ref = refs[-1]
    even = meta.even
    second = (meta.place // 2 * 2 + 1) * TOK
    closes = meta.start_of(meta.session_at(second + TOK - 1)) >= second
    width = local * N
    for chip in range(keep_ref.shape[0]):
        keep = factors_of(keep_ref[chip, width:, :], local)
        got = factors_of(got_ref[chip, width:, :], local)
        f0, f1 = jnp.where(even, keep, got), jnp.where(even, got, keep)
        out_ref[chip, width:, :] = factor_rows(jnp.where(closes, f1, f0 * f1))
        carry = jnp.where(closes, 0.0, f1)
        for k in range(local):
            rows = slice(k * N, (k + 1) * N)
            keep = keep_ref[chip, rows, :].astype(jnp.float32)
            got = got_ref[chip, rows, :].astype(jnp.float32)
            s0, s1 = jnp.where(even, keep, got), jnp.where(even, got, keep)
            out_ref[chip, rows, :] = (carry[k : k + 1] * s0 + s1).astype(jnp.bfloat16)


def recurrence_kernel(local, meta, got_ref, restored_ref, *refs):
    out_ref, token_ref = refs[-2:]
    token_ref[...] = jnp.zeros_like(token_ref)
    width = local * N
    span = 2 * TOK
    state = [jnp.zeros((N, P_SIZE), jnp.float32) for _ in range(local)]
    for c in range(got_ref.shape[0]):
        first = c * span
        opening = meta.session_at(first)
        closing = meta.session_at(first + span - 1)
        opens = meta.start_of(opening) >= first
        closes = meta.start_of(closing) >= first
        factor = factors_of(got_ref[c, width:, :], local)
        for k in range(local):
            rows = slice(k * N, (k + 1) * N)
            entering = jnp.where(opens, restored_ref[opening, rows, :], state[k])
            out_ref[c, rows, :] = entering.astype(jnp.bfloat16)
            source = jnp.where(closes, restored_ref[closing, rows, :], state[k])
            state[k] = factor[k : k + 1] * source + got_ref[c, rows, :].astype(jnp.float32)


def intra_kernel(meta, skip, x_ref, dl_ref, step_ref, write_ref, read_ref, _, out_ref, token_ref, run_s, step_s):
    step = pl.program_id(0)

    @pl.when(step == 0)
    def _():
        _, running = running_rows(dl_ref)
        run_s[...] = running
        step_s[...] = step_ref[...].astype(jnp.float32)

    token_ref[...] = jnp.zeros_like(token_ref)
    heads = pl.ds(pl.multiple_of(step * PAIR, PAIR), PAIR)
    running = run_s[heads, :]
    sizes = step_s[heads, :]
    columns = running.T
    r = meta.last_start()
    t = lax.broadcasted_iota(jnp.int32, (TOK, TOK), 0)
    u = lax.broadcasted_iota(jnp.int32, (TOK, TOK), 1)
    causal = (u <= t) & ((u >= r) | (t < r))
    for group in range(2):
        part = slice(group * N, (group + 1) * N)
        products = lax.dot_general(
            read_ref[:, part], write_ref[:, part], (((1,), (1,)), ((), ())),
            preferred_element_type=jnp.float32,
        )
        products = jnp.where(causal, products, 0.0)
        for k in range(group * HEADS_PER, (group + 1) * HEADS_PER):
            difference = columns[:, k : k + 1] - running[k : k + 1]
            decay = jnp.exp(jnp.minimum(difference, 0.0))
            mixing = (products * decay * sizes[k : k + 1]).astype(jnp.bfloat16)
            place = slice(k * P_SIZE, (k + 1) * P_SIZE)
            x = x_ref[:, place]
            mixed = jnp.dot(mixing, x, preferred_element_type=jnp.float32)
            out_ref[:, place] = mixed + skip[step * PAIR + k] * x.astype(jnp.float32)


def intra(meta, skip, x, rates, steps, writes, reads, idle):
    return pl.pallas_call(
        scalars(intra_kernel),
        out_shape=[jax.ShapeDtypeStruct((TOK, H * P_SIZE), jnp.float32), TOKEN],
        grid_spec=pltpu.PrefetchScalarGridSpec(
            num_scalar_prefetch=2,
            grid=(STEPS,),
            in_specs=[
                pl.BlockSpec((TOK, PAIR * P_SIZE), lambda i, *m: (0, i)),
                pl.BlockSpec((H, TOK), lambda i, *m: (0, 0)),
                pl.BlockSpec((H, TOK), lambda i, *m: (0, 0)),
                pl.BlockSpec((TOK, 2 * N), lambda i, *m: (0, i)),
                pl.BlockSpec((TOK, 2 * N), lambda i, *m: (0, i)),
                pl.BlockSpec(memory_space=pl.ANY),
            ],
            out_specs=[
                pl.BlockSpec((TOK, PAIR * P_SIZE), lambda i, *m: (0, i)),
                pl.BlockSpec(TOKEN.shape, lambda i, *m: (0, 0)),
            ],
            scratch_shapes=[
                pltpu.VMEM((H, TOK), jnp.float32),
                pltpu.VMEM((H, TOK), jnp.float32),
            ],
        ),
        compiler_params=params(),
        cost_estimate=LONG,
        name="intra",
    )(meta, skip, x, rates, steps, writes, reads, idle)


def finish_kernel(
    local, meta, part_ref, dl_ref, read_ref, own_ref, other_ref, low_ref, high_ref, *refs,
):
    pieces, (out_ref, factor_s) = refs[:8], refs[-2:]
    bits = pieces[0].shape[0].bit_length() - 1
    step = pl.program_id(0)
    even = meta.even
    r = meta.last_start()
    first = meta.place // 2 * 2 * TOK
    second = first + TOK
    start = meta.start_of(meta.session_at(second + TOK - 1))
    closes = (start > first) & (start < second)
    opens = start == second
    width = local * N

    @pl.when(step == 0)
    def _():
        rates, running = running_rows(dl_ref)
        lane = lax.broadcasted_iota(jnp.int32, (H, TOK), 1)
        base = jnp.sum(jnp.where(lane < r, rates, 0.0), axis=1, keepdims=True)
        factor_s[...] = jnp.exp(jnp.minimum(running - jnp.where(lane >= r, base, 0.0), 0.0))

    factor = factor_s[pl.ds(pl.multiple_of(step * PAIR, PAIR), PAIR), :].T
    token = lax.broadcasted_iota(jnp.int32, (TOK, N), 0)
    resumed = (token >= r) & (r > 0)
    decays = [[factors_of(ref[chip, width:, :], local) for ref in (low_ref, high_ref)] for chip in range(own_ref.shape[0])]
    for group in range(2):
        reads = read_ref[:, group * N : (group + 1) * N].astype(jnp.float32)
        left = jnp.where(resumed, 0.0, reads)
        right = jnp.where(resumed, reads, 0.0)
        reads = jnp.concatenate([left, right], axis=1).astype(jnp.bfloat16)
        for k in range(group * HEADS_PER, (group + 1) * HEADS_PER):
            chip, half, head = k // (2 * local), k // local % 2, k % local
            rows = slice(head * N, (head + 1) * N)
            own = even if half == 0 else jnp.logical_not(even)
            entering = jnp.where(own, own_ref[chip, rows, :], other_ref[chip, rows, :]).astype(jnp.float32)
            distance = (step * own_ref.shape[0] + chip) ^ (meta.place // 2)
            far = far_place(distance // 4, bits)
            near, low_bit = distance % 2 == 0, distance // 2 % 2 == 0
            found = [piece[far, rows, :] for piece in pieces]
            found = [jnp.where(low_bit, found[i], found[i + 1]) for i in range(0, 8, 2)]
            restored = jnp.where(own, jnp.where(near, found[0], found[1]), jnp.where(near, found[2], found[3]))
            whole_state = restored.astype(jnp.float32)
            summary = (low_ref, high_ref)[half][chip, rows, :].astype(jnp.float32)
            middle = decays[chip][half][head : head + 1] * jnp.where(closes, whole_state, entering) + summary
            middle = jnp.where(opens, whole_state, middle)
            entering = jnp.where(even, entering, middle).astype(jnp.bfloat16)
            states = jnp.concatenate([entering, restored], axis=0)
            carried = jnp.dot(reads, states, preferred_element_type=jnp.float32)
            place = slice(k * P_SIZE, (k + 1) * P_SIZE)
            out_ref[:, place] = (part_ref[:, place] + factor[:, k : k + 1] * carried).astype(jnp.bfloat16)


def finish(meta, part, rates, reads, own, other, low, high, pieces, local):
    chips = PAIR // (2 * local)
    count, length, _ = pieces[0].shape
    resumed = pl.BlockSpec((count, local * N, P_SIZE), lambda i, *m: (0, length // (local * N) - 1, 0))
    states = pl.BlockSpec((chips, local * N, P_SIZE), lambda i, *m: (i, 0, 0))
    stretch = pl.BlockSpec((chips, local * N + EXTRA, P_SIZE), lambda i, *m: (i, 0, 0))
    return pl.pallas_call(
        scalars(finish_kernel, local),
        out_shape=jax.ShapeDtypeStruct((TOK, H * P_SIZE), jnp.bfloat16),
        grid_spec=pltpu.PrefetchScalarGridSpec(
            num_scalar_prefetch=1,
            grid=(STEPS,),
            in_specs=[
                pl.BlockSpec((TOK, PAIR * P_SIZE), lambda i, *m: (0, i)),
                pl.BlockSpec((H, TOK), lambda i, *m: (0, 0)),
                pl.BlockSpec((TOK, 2 * N), lambda i, *m: (0, i)),
                states,
                states,
                stretch,
                stretch,
            ]
            + [resumed] * 8,
            out_specs=pl.BlockSpec((TOK, PAIR * P_SIZE), lambda i, *m: (0, i)),
            scratch_shapes=[pltpu.VMEM((H, TOK), jnp.float32)],
        ),
        compiler_params=params(),
        cost_estimate=LONG,
        name="finish",
    )(meta, part, rates, reads, own, other, low, high, *pieces)


def attend_kernel(
    meta, q_ref, four, two, now, four_across, two_across, now_across, *refs,
):
    history_refs, (sk_ref, sv_ref), (out_ref, token_ref, key_s, value_s) = refs[:32], refs[32:34], refs[-4:]
    factor = 1.0 / math.sqrt(HD)
    first = meta.place * TOK
    r = meta.last_start()
    opening = meta.session_at(first)
    closing = meta.session_at(first + TOK - 1)
    even = meta.even

    def band(number, part):
        if number == 0:
            return four[part]
        if number == 1:
            return jnp.where(even, four_across[part], two_across[part])
        if number == 2:
            return two[part]
        if number == 3:
            return jnp.where(even, two_across[part], now_across[part])
        return now[part]

    token_ref[...] = jnp.zeros_like(token_ref)

    def sinks(ref, session):
        rows = ref[session].astype(jnp.float32)
        spare = jnp.zeros((COLUMNS - SPAN - SINKS, HD), jnp.float32)
        return jnp.concatenate([rows, spare], axis=0).astype(jnp.bfloat16)

    length = (REACH + 1) * TOK

    def one_session(session, key_refs, value_refs, resuming, needed):
        start = meta.start_of(session) - first + WINDOW
        oldest = start - WINDOW + jnp.maximum(SINKS + WINDOW - meta.history(session), 0)

        @pl.when(needed & (start > 0))
        def _():
            row = lax.broadcasted_iota(jnp.int32, (length, WINDOW), 0)
            chips, share, _ = key_refs[0].shape
            index = lax.broadcasted_iota(jnp.int32, (1, WINDOW), 1)
            piece, index = index // (WINDOW // 8), index % (WINDOW // 8)
            near, row_in = index // share, index % share
            far = far_place(near, chips.bit_length() - 1)
            device = meta.place ^ (piece // 4 + piece // 2 % 2 * 2 + piece % 2 * 4 + far * 8)
            place = device * share + row_in
            moved = (row == place + start - WINDOW).astype(jnp.bfloat16)
            part = (WINDOW // 8, HD)
            keys = jnp.concatenate([ref[...].reshape(part) for ref in key_refs], axis=0)
            values = jnp.concatenate([ref[...].reshape(part) for ref in value_refs], axis=0)
            history = jnp.dot(
                moved, jnp.concatenate([keys, values], axis=1), preferred_element_type=jnp.float32
            )
            for i in range(REACH + 1):
                rows = slice(i * TOK, (i + 1) * TOK)
                index = lax.broadcasted_iota(jnp.int32, (TOK, HD), 0) + i * TOK
                turn = index >= start
                key_s[rows, :] = jnp.where(
                    turn, band(i, 0).astype(jnp.float32), history[rows, :HD]
                ).astype(jnp.bfloat16)
                value_s[rows, :] = jnp.where(
                    turn, band(i, 1).astype(jnp.float32), history[rows, HD:]
                ).astype(jnp.bfloat16)

        @pl.when(needed & (start <= 0))
        def _():
            for i in range(REACH + 1):
                rows = slice(i * TOK, (i + 1) * TOK)
                key_s[rows, :] = band(i, 0)
                value_s[rows, :] = band(i, 1)

        for b in range(TOK // BLOCK):
            inside = (b * BLOCK + BLOCK > r) if resuming else (b * BLOCK < r)

            @pl.when(needed & inside)
            def _():
                rows = slice(b * BLOCK, b * BLOCK + SPAN)
                keys = jnp.concatenate([key_s[rows, :], sinks(sk_ref, session)], axis=0)
                values = jnp.concatenate([value_s[rows, :], sinks(sv_ref, session)], axis=0)
                tokens = slice(b * BLOCK, (b + 1) * BLOCK)
                queries = jnp.concatenate(
                    [q_ref[tokens, g * HD : (g + 1) * HD] for g in range(QH // KVH)], axis=0
                )
                scores = lax.dot_general(
                    queries, keys, (((1,), (1,)), ((), ())), preferred_element_type=jnp.float32
                )
                token = lax.broadcasted_iota(jnp.int32, (BLOCK, COLUMNS), 0)
                column = lax.broadcasted_iota(jnp.int32, (BLOCK, COLUMNS), 1)
                seen = (column > token) & (column <= token + WINDOW) & (column >= oldest - b * BLOCK)
                seen = (seen & (column < SPAN)) | ((column >= SPAN) & (column < SPAN + SINKS))
                bias = jnp.where(seen, 0.0, NEG)
                weights, sums = [], []
                for g in range(QH // KVH):
                    score = scores[g * BLOCK : (g + 1) * BLOCK] * factor + bias
                    weight = jnp.exp(score - jnp.max(score, axis=1, keepdims=True))
                    sums.append(jnp.sum(weight, axis=1, keepdims=True))
                    weights.append(weight.astype(jnp.bfloat16))
                mixed = jnp.dot(
                    jnp.concatenate(weights, axis=0), values, preferred_element_type=jnp.float32
                )
                for g in range(QH // KVH):
                    result = mixed[g * BLOCK : (g + 1) * BLOCK] / sums[g]
                    lanes = slice(g * HD, (g + 1) * HD)
                    if resuming:
                        index = lax.broadcasted_iota(jnp.int32, (BLOCK, HD), 0) + b * BLOCK
                        before = out_ref[tokens, lanes].astype(jnp.float32)
                        result = jnp.where(index >= r, result, before)
                    out_ref[tokens, lanes] = result.astype(jnp.bfloat16)

    one_session(opening, history_refs[0:8], history_refs[8:16], False, r > 0)
    one_session(closing, history_refs[16:24], history_refs[24:], True, r >= 0)


def attend(meta, queries, bands, pieces, half, sink_keys, sink_values, idle):
    chips = pieces[0].shape[0]
    share = WINDOW // (8 * chips)
    lanes = QH // KVH * HD

    def history_spec(which, last):
        def index(j, *m):
            known = Scalars(*m)
            session = known.session_at(known.place * TOK + (TOK - 1 if last else 0))
            session = session - (known.place >= half).astype(jnp.int32)
            return (0, (which * 2 + session) * KVH + j, 0)

        return pl.BlockSpec((chips, share, HD), index)

    pad = SEQS, SINKS, HD
    return pl.pallas_call(
        scalars(attend_kernel),
        out_shape=[jax.ShapeDtypeStruct((TOK, QH * HD), jnp.bfloat16), TOKEN],
        grid_spec=pltpu.PrefetchScalarGridSpec(
            num_scalar_prefetch=1,
            grid=(KVH,),
            in_specs=[pl.BlockSpec((TOK, lanes), lambda j, *m: (0, j))]
            + [pl.BlockSpec((2, TOK, HD), lambda j, *m: (0, 0, j))] * len(bands)
            + [history_spec(0, False)] * 8
            + [history_spec(1, False)] * 8
            + [history_spec(0, True)] * 8
            + [history_spec(1, True)] * 8
            + [pl.BlockSpec(pad, lambda j, *m: (0, 0, j))] * 2
            + [idle_spec(a) for a in idle],
            out_specs=[
                pl.BlockSpec((TOK, lanes), lambda j, *m: (0, j)),
                pl.BlockSpec(TOKEN.shape, lambda j, *m: (0, 0)),
            ],
            scratch_shapes=[
                pltpu.VMEM(((REACH + 1) * TOK, HD), jnp.bfloat16),
                pltpu.VMEM(((REACH + 1) * TOK, HD), jnp.bfloat16),
            ],
        ),
        compiler_params=params(),
        cost_estimate=SHORT,
        name="attend",
    )(
        meta, queries, *bands, *pieces, *pieces, *pieces, *pieces, sink_keys, sink_values, *idle
    )


def shifted(block, axis, distance):
    devices = range(lax.axis_size(axis))
    return lax.ppermute(block, axis, [(i - distance, i) for i in devices if i - distance in devices])


def shards(
    mamba_input,
    step_size,
    decay_log,
    state_write,
    state_read,
    skip_gain,
    saved_states,
    home_slot,
    turn_lengths,
    history_lengths,
    queries,
    turn_keys,
    turn_values,
    cache_keys,
    cache_values,
    sink_keys,
    sink_values,
):
    place = lax.axis_index("ctx")
    group = lax.axis_index("sess")
    groups = lax.axis_size("sess")
    devices = lax.axis_size("ctx")
    local = saved_states.shape[2]
    width = local * N
    chips = devices // 2
    same_core = [list(range(core, devices, 2)) for core in range(2)]
    meta = jnp.concatenate(
        [jnp.stack([place, group]).astype(jnp.int32), turn_lengths[0], history_lengths[0], home_slot]
    )
    x, rates, steps = mamba_input[0], decay_log[0].T, step_size[0].T
    writes, reads = state_write[0], state_read[0]
    def apart(block, distance):
        return lax.ppermute(block, "ctx", [(i, i ^ distance) for i in range(devices)])

    def exchanged(block):
        return lax.all_to_all(block, "ctx", 0, 0, axis_index_groups=same_core, tiled=True)

    stored = [saved_states[0]]
    for j in range(1, groups):
        route = [((i + j) % groups, i) for i in range(groups)]
        stored.append(lax.ppermute(saved_states[0], "sess", route))
    stored = [block.reshape(SEQS, local, P_SIZE, N) for block in stored]

    keep, send = summaries(meta, x, rates, steps, writes, local)
    got = apart(send, 1)

    parcel = (1, 4 * KVH * cache_keys.shape[2] + width, HD)
    band = (2, TOK, KVH * HD)
    near, away, key_value, restored = whole(
        scalars(restore_kernel, local, devices // 2, groups),
        "restore",
        meta,
        [*stored, cache_keys[0], cache_values[0], turn_keys[0], turn_values[0]],
        [
            (parcel, jnp.bfloat16),
            (parcel, jnp.bfloat16),
            (band, jnp.bfloat16),
            ((SEQS, width, P_SIZE), jnp.float32),
        ],
        idle=[send],
        mib=60,
    )
    distance = devices // 2
    moved = apart(away, distance)
    four = shifted(key_value, "ctx", 4)

    def joined(array):
        return ((2 * array.shape[0], *array.shape[1:]), jnp.bfloat16)

    after = got
    while distance > 8:
        [near] = whole(scalars(join_kernel), "join", meta, [near, moved], [joined(near)], idle=[after])
        after = near
        distance //= 2
        moved = apart(near, distance)
    near, two = whole(
        scalars(join_two_kernel),
        "join_two",
        meta,
        [near, moved, key_value, four],
        [joined(near), (band, jnp.bfloat16)],
        idle=[after],
    )
    moved = apart(near, 4)
    two = apart(two, 2)
    beside = apart(near, 2)
    [chip] = whole(
        scalars(combine_kernel, local),
        "combine",
        meta,
        [keep, got],
        [(keep.shape, jnp.bfloat16)],
        idle=[near],
    )
    total = exchanged(chip)
    part, token = intra(meta, skip_gain, x, rates, steps, writes, reads, chip)
    pieces = [near, moved, beside, apart(moved, 2)]
    bands = [four, two, key_value]
    across = [apart(block, 1) for block in bands]
    low = apart(keep, 1)

    entering, after = whole(
        scalars(recurrence_kernel, local),
        "recurrence",
        meta,
        [total, restored],
        [((chips, width, P_SIZE), jnp.bfloat16), (TOKEN.shape, TOKEN.dtype)],
        idle=[token, low, *across, *pieces],
    )
    entering = exchanged(entering)
    pieces += [apart(piece, 1) for piece in pieces]
    attended, token = attend(
        meta, queries[0], bands + across, pieces, devices // 2, sink_keys[0], sink_values[0], [after]
    )
    [entering] = whole(
        scalars(copy_kernel), "copy", meta, [entering], [((chips, width, P_SIZE), jnp.bfloat16)], idle=[token]
    )
    other = apart(entering, 1)
    mixed = finish(meta, part, rates, reads, entering, other, low, got, pieces, local)
    return mixed[None], attended[None]


def solution(mesh):
    token = P("sess", "ctx", None)
    return jax.shard_map(
        shards,
        mesh=mesh,
        in_specs=(
            token,
            token,
            token,
            token,
            token,
            P(),
            P("sess", None, "ctx", None),
            P(),
            P("sess", None),
            P("sess", None),
            token,
            token,
            token,
            P("sess", None, "ctx", None),
            P("sess", None, "ctx", None),
            P("sess", None, None, None),
            P("sess", None, None, None),
        ),
        out_specs=(token, token),
        check_vma=False,
    )
```

```python
import math

import jax
import jax.numpy as jnp
from jax import lax
from jax.experimental import pallas as pl
from jax.experimental.pallas import tpu as pltpu
from jax.sharding import PartitionSpec as P

REACH = 4
SEQS = 3
SINKS = 4
H = 64
P_SIZE = 128
N = 64
G = 8
QH = 32
KVH = 4
HD = 128
WINDOW = 512
TOK = 128

HEADS_PER = H // G
PAIR = 2 * HEADS_PER
STEPS = H // PAIR
EXTRA = 16
BLOCK = 64
SPAN = WINDOW + BLOCK
COLUMNS = SPAN + 64
NEG = -1e30
TOKEN = jax.ShapeDtypeStruct((8, 128), jnp.float32)
SHORT = pl.CostEstimate(flops=1024, bytes_accessed=1024, transcendentals=0)
LONG = pl.CostEstimate(flops=1 << 35, bytes_accessed=1 << 20, transcendentals=0)


class Scalars:
    def __init__(self, ids):
        self.place, self.group = ids[0], ids[1]
        self.one = ids[2]
        self.two = ids[2] + ids[3]
        self.ids = ids
        self.even = self.place % 2 == 0

    def history(self, session):
        return self.ids[2 + SEQS + session]

    def home(self, number):
        return self.ids[2 + 2 * SEQS + number]

    def session_at(self, position):
        return (position >= self.one).astype(jnp.int32) + (position >= self.two).astype(jnp.int32)

    def start_of(self, session):
        return jnp.where(session == 0, 0, jnp.where(session == 1, self.one, self.two))

    def last_start(self):
        first = self.place * TOK
        return jnp.maximum(self.start_of(self.session_at(first + TOK - 1)) - first, 0)


def scalars(kernel, *options):
    def body(ids, *refs):
        kernel(*options, Scalars(ids), *refs)

    return body


def params(mib=60):
    return pltpu.CompilerParams(vmem_limit_bytes=mib * 1024 * 1024)


def running_rows(dl_ref):
    k = lax.broadcasted_iota(jnp.int32, (TOK, TOK), 0)
    u = lax.broadcasted_iota(jnp.int32, (TOK, TOK), 1)
    upto = (k <= u).astype(jnp.bfloat16)
    running = jnp.dot(dl_ref[...], upto, preferred_element_type=jnp.float32)
    return dl_ref[...].astype(jnp.float32), running


def summary_kernel(
    local, meta, x_ref, dl_ref, step_ref, write_ref, _, keep_ref, send_ref, coef_s, factor_s, write_s
):
    step = pl.program_id(0)

    @pl.when(step == 0)
    def _():
        rates, running = running_rows(dl_ref)
        steps = step_ref[...].astype(jnp.float32)
        r = meta.last_start()
        lane = lax.broadcasted_iota(jnp.int32, (H, TOK), 1)
        last = running[:, TOK - 1 :]
        base = jnp.sum(jnp.where(lane < r, rates, 0.0), axis=1, keepdims=True)
        coef_s[...] = jnp.where(lane >= r, jnp.exp(last - running) * steps, 0.0)
        factor_s[...] = jnp.broadcast_to(jnp.exp(last - base), (H, TOK))
        write_s[...] = write_ref[...].astype(jnp.float32).T

    even = meta.even
    coef = coef_s[pl.ds(pl.multiple_of(step * PAIR, PAIR), PAIR), :]
    factor = factor_s[pl.ds(pl.multiple_of(step * PAIR, PAIR), PAIR), :]
    writes = write_s[pl.ds(pl.multiple_of(step * 2 * N, 2 * N), 2 * N), :]

    def summary(k):
        group = k // HEADS_PER
        loading = (writes[group * N : (group + 1) * N] * coef[k : k + 1]).astype(jnp.bfloat16)
        return jnp.dot(
            loading, x_ref[:, k * P_SIZE : (k + 1) * P_SIZE], preferred_element_type=jnp.float32
        )

    for chip in range(PAIR // (2 * local)):
        low, high = 2 * local * chip, 2 * local * chip + local
        for k in range(local):
            first, second = summary(low + k), summary(high + k)
            rows = slice(k * N, (k + 1) * N)
            keep_ref[chip, rows, :] = jnp.where(even, first, second).astype(jnp.bfloat16)
            send_ref[chip, rows, :] = jnp.where(even, second, first).astype(jnp.bfloat16)
        first, second = factor[low : low + local], factor[high : high + local]
        keep_ref[chip, local * N :, :] = factor_rows(jnp.where(even, first, second))
        send_ref[chip, local * N :, :] = factor_rows(jnp.where(even, second, first))


def factor_rows(rows):
    high = rows.astype(jnp.bfloat16).astype(jnp.float32)
    parts = [high, rows - high]
    if EXTRA > 2 * rows.shape[0]:
        parts.append(jnp.zeros((EXTRA - 2 * rows.shape[0], TOK), jnp.float32))
    return jnp.concatenate(parts, axis=0).astype(jnp.bfloat16)


def factors_of(block, local):
    block = block.astype(jnp.float32)
    return block[:local] + block[local : 2 * local]


def summaries(meta, x, rates, steps, writes, local, idle):
    chips = H // (2 * local)
    rows = local * N + EXTRA
    shape = jax.ShapeDtypeStruct((chips, rows, P_SIZE), jnp.bfloat16)
    spec = pl.BlockSpec((PAIR // (2 * local), rows, P_SIZE), lambda i, *m: (i, 0, 0))
    return pl.pallas_call(
        scalars(summary_kernel, local),
        out_shape=[shape, shape],
        grid_spec=pltpu.PrefetchScalarGridSpec(
            num_scalar_prefetch=1,
            grid=(STEPS,),
            in_specs=[
                pl.BlockSpec((TOK, PAIR * P_SIZE), lambda i, *m: (0, i)),
                pl.BlockSpec((H, TOK), lambda i, *m: (0, 0)),
                pl.BlockSpec((H, TOK), lambda i, *m: (0, 0)),
                pl.BlockSpec((TOK, G * N), lambda i, *m: (0, 0)),
                pl.BlockSpec(memory_space=pl.ANY),
            ],
            out_specs=[spec, spec],
            scratch_shapes=[
                pltpu.VMEM((H, TOK), jnp.float32),
                pltpu.VMEM((H, TOK), jnp.float32),
                pltpu.VMEM((G * N, TOK), jnp.float32),
            ],
        ),
        compiler_params=params(),
        cost_estimate=LONG,
        name="summaries",
    )(meta, x, rates, steps, writes, idle)


def idle_spec(array):
    return pl.BlockSpec(memory_space=pl.ANY)


def whole(kernel, name, meta, arrays, shapes, idle=(), mib=16, scratch=()):
    def spec(shape):
        return pl.BlockSpec(shape, lambda i, *m: (0,) * len(shape))

    return pl.pallas_call(
        kernel,
        out_shape=[jax.ShapeDtypeStruct(s, t) for s, t in shapes],
        grid_spec=pltpu.PrefetchScalarGridSpec(
            num_scalar_prefetch=1,
            grid=(1,),
            in_specs=[spec(a.shape) for a in arrays] + [idle_spec(a) for a in idle],
            out_specs=[spec(s) for s, _ in shapes],
            scratch_shapes=scratch,
        ),
        compiler_params=params(mib),
        cost_estimate=LONG,
        name=name,
    )(meta, *arrays, *idle)


def pack_kernel(half, meta, keys_ref, values_ref, turn_keys_ref, turn_values_ref, home_ref, away_ref, band_ref):
    band_ref[0] = turn_keys_ref[...]
    band_ref[1] = turn_values_ref[...]
    rows = keys_ref.shape[1]
    upper = (meta.place >= half).astype(jnp.int32)
    for out_ref, first in ((home_ref, upper), (away_ref, 1 - upper)):
        for which, ref in enumerate((keys_ref, values_ref)):
            for s in range(2):
                for j in range(KVH):
                    place = ((which * 2 + s) * KVH + j) * rows
                    out_ref[0, place : place + rows, :] = ref[first + s, :, j * HD : (j + 1) * HD]


def restore_kernel(local, half, groups, meta, *refs):
    stored, (home_ref, away_ref, restored_ref) = refs[:groups], refs[-3:]
    for s in range(SEQS):
        slot = meta.home(meta.group * SEQS + s)
        source = (slot // SEQS - meta.group + groups) % groups
        for k in range(local):
            state = stored[0][slot % SEQS, k]
            for j in range(1, groups):
                state = jnp.where(source == j, stored[j][slot % SEQS, k], state)
            restored_ref[s, k * N : (k + 1) * N, :] = state.T
    upper = (meta.place >= half).astype(jnp.int32)
    home_ref[0] = restored_ref[upper + 1].astype(jnp.bfloat16)
    away_ref[0] = restored_ref[2 - upper].astype(jnp.bfloat16)


def copy_kernel(meta, array_ref, *refs):
    refs[-1][...] = array_ref[...]


def join_kernel(meta, first_ref, second_ref, *refs):
    out_ref = refs[-1]
    count = first_ref.shape[0]
    out_ref[:count] = first_ref[...]
    out_ref[count:] = second_ref[...]


def join_two_kernel(
    meta, first_ref, second_ref, first_state_ref, second_state_ref, key_value_ref, four_ref, *refs
):
    out_ref, two_ref = refs[-2:]
    rows = first_ref.shape[1]
    for i, (parcel, state) in enumerate(((first_ref, first_state_ref), (second_ref, second_state_ref))):
        out_ref[i, :rows, :] = parcel[0]
        out_ref[i, rows:, :] = state[0]
    two_ref[...] = jnp.where(meta.place // 2 % 2 == 0, key_value_ref[...], four_ref[...])


def far_place(distance, bits):
    place = distance * 0
    for k in range(bits):
        place = place + ((distance // (1 << k)) % 2) * (1 << (bits - 1 - k))
    return place


def combine_kernel(local, meta, keep_ref, got_ref, *refs):
    out_ref = refs[-1]
    even = meta.even
    second = (meta.place // 2 * 2 + 1) * TOK
    closes = meta.start_of(meta.session_at(second + TOK - 1)) >= second
    width = local * N
    for chip in range(keep_ref.shape[0]):
        keep = factors_of(keep_ref[chip, width:, :], local)
        got = factors_of(got_ref[chip, width:, :], local)
        f0, f1 = jnp.where(even, keep, got), jnp.where(even, got, keep)
        out_ref[chip, width:, :] = factor_rows(jnp.where(closes, f1, f0 * f1))
        carry = jnp.where(closes, 0.0, f1)
        for k in range(local):
            rows = slice(k * N, (k + 1) * N)
            keep = keep_ref[chip, rows, :].astype(jnp.float32)
            got = got_ref[chip, rows, :].astype(jnp.float32)
            s0, s1 = jnp.where(even, keep, got), jnp.where(even, got, keep)
            out_ref[chip, rows, :] = (carry[k : k + 1] * s0 + s1).astype(jnp.bfloat16)


def recurrence_kernel(local, meta, got_ref, restored_ref, *refs):
    out_ref, token_ref = refs[-2:]
    token_ref[...] = jnp.zeros_like(token_ref)
    width = local * N
    span = 2 * TOK
    state = [jnp.zeros((N, P_SIZE), jnp.float32) for _ in range(local)]
    for c in range(got_ref.shape[0]):
        first = c * span
        opening = meta.session_at(first)
        closing = meta.session_at(first + span - 1)
        opens = meta.start_of(opening) >= first
        closes = meta.start_of(closing) >= first
        factor = factors_of(got_ref[c, width:, :], local)
        for k in range(local):
            rows = slice(k * N, (k + 1) * N)
            entering = jnp.where(opens, restored_ref[opening, rows, :], state[k])
            out_ref[c, rows, :] = entering.astype(jnp.bfloat16)
            source = jnp.where(closes, restored_ref[closing, rows, :], state[k])
            state[k] = factor[k : k + 1] * source + got_ref[c, rows, :].astype(jnp.float32)


def intra_kernel(meta, skip, x_ref, dl_ref, step_ref, write_ref, read_ref, _, out_ref, token_ref, run_s, step_s):
    step = pl.program_id(0)

    @pl.when(step == 0)
    def _():
        _, running = running_rows(dl_ref)
        run_s[...] = running
        step_s[...] = step_ref[...].astype(jnp.float32)

    token_ref[...] = jnp.zeros_like(token_ref)
    heads = pl.ds(pl.multiple_of(step * PAIR, PAIR), PAIR)
    running = run_s[heads, :]
    sizes = step_s[heads, :]
    columns = running.T
    r = meta.last_start()
    t = lax.broadcasted_iota(jnp.int32, (TOK, TOK), 0)
    u = lax.broadcasted_iota(jnp.int32, (TOK, TOK), 1)
    causal = (u <= t) & ((u >= r) | (t < r))
    for group in range(2):
        part = slice(group * N, (group + 1) * N)
        products = lax.dot_general(
            read_ref[:, part], write_ref[:, part], (((1,), (1,)), ((), ())),
            preferred_element_type=jnp.float32,
        )
        products = jnp.where(causal, products, 0.0)
        for k in range(group * HEADS_PER, (group + 1) * HEADS_PER):
            difference = columns[:, k : k + 1] - running[k : k + 1]
            decay = jnp.exp(jnp.minimum(difference, 0.0))
            mixing = (products * decay * sizes[k : k + 1]).astype(jnp.bfloat16)
            place = slice(k * P_SIZE, (k + 1) * P_SIZE)
            x = x_ref[:, place]
            mixed = jnp.dot(mixing, x, preferred_element_type=jnp.float32)
            out_ref[:, place] = mixed + skip[step * PAIR + k] * x.astype(jnp.float32)


def intra(meta, skip, x, rates, steps, writes, reads, idle):
    return pl.pallas_call(
        scalars(intra_kernel),
        out_shape=[jax.ShapeDtypeStruct((TOK, H * P_SIZE), jnp.float32), TOKEN],
        grid_spec=pltpu.PrefetchScalarGridSpec(
            num_scalar_prefetch=2,
            grid=(STEPS,),
            in_specs=[
                pl.BlockSpec((TOK, PAIR * P_SIZE), lambda i, *m: (0, i)),
                pl.BlockSpec((H, TOK), lambda i, *m: (0, 0)),
                pl.BlockSpec((H, TOK), lambda i, *m: (0, 0)),
                pl.BlockSpec((TOK, 2 * N), lambda i, *m: (0, i)),
                pl.BlockSpec((TOK, 2 * N), lambda i, *m: (0, i)),
                pl.BlockSpec(memory_space=pl.ANY),
            ],
            out_specs=[
                pl.BlockSpec((TOK, PAIR * P_SIZE), lambda i, *m: (0, i)),
                pl.BlockSpec(TOKEN.shape, lambda i, *m: (0, 0)),
            ],
            scratch_shapes=[
                pltpu.VMEM((H, TOK), jnp.float32),
                pltpu.VMEM((H, TOK), jnp.float32),
            ],
        ),
        compiler_params=params(),
        cost_estimate=LONG,
        name="intra",
    )(meta, skip, x, rates, steps, writes, reads, idle)


def finish_kernel(
    local, meta, part_ref, dl_ref, read_ref, own_ref, other_ref, low_ref, high_ref, *refs,
):
    pieces, (out_ref, factor_s) = refs[:8], refs[-2:]
    bits = pieces[0].shape[0].bit_length() - 1
    step = pl.program_id(0)
    even = meta.even
    r = meta.last_start()
    first = meta.place // 2 * 2 * TOK
    second = first + TOK
    start = meta.start_of(meta.session_at(second + TOK - 1))
    closes = (start > first) & (start < second)
    opens = start == second
    width = local * N

    @pl.when(step == 0)
    def _():
        rates, running = running_rows(dl_ref)
        lane = lax.broadcasted_iota(jnp.int32, (H, TOK), 1)
        base = jnp.sum(jnp.where(lane < r, rates, 0.0), axis=1, keepdims=True)
        factor_s[...] = jnp.exp(jnp.minimum(running - jnp.where(lane >= r, base, 0.0), 0.0))

    factor = factor_s[pl.ds(pl.multiple_of(step * PAIR, PAIR), PAIR), :].T
    token = lax.broadcasted_iota(jnp.int32, (TOK, N), 0)
    resumed = (token >= r) & (r > 0)
    decays = [[factors_of(ref[chip, width:, :], local) for ref in (low_ref, high_ref)] for chip in range(own_ref.shape[0])]
    for group in range(2):
        reads = read_ref[:, group * N : (group + 1) * N].astype(jnp.float32)
        left = jnp.where(resumed, 0.0, reads)
        right = jnp.where(resumed, reads, 0.0)
        reads = jnp.concatenate([left, right], axis=1).astype(jnp.bfloat16)
        for k in range(group * HEADS_PER, (group + 1) * HEADS_PER):
            chip, half, head = k // (2 * local), k // local % 2, k % local
            rows = slice(head * N, (head + 1) * N)
            own = even if half == 0 else jnp.logical_not(even)
            entering = jnp.where(own, own_ref[chip, rows, :], other_ref[chip, rows, :]).astype(jnp.float32)
            distance = (step * own_ref.shape[0] + chip) ^ (meta.place // 2)
            far = far_place(distance // 4, bits)
            near, low_bit = distance % 2 == 0, distance // 2 % 2 == 0
            found = [piece[far, rows, :] for piece in pieces]
            found = [jnp.where(low_bit, found[i], found[i + 1]) for i in range(0, 8, 2)]
            restored = jnp.where(own, jnp.where(near, found[0], found[1]), jnp.where(near, found[2], found[3]))
            whole_state = restored.astype(jnp.float32)
            summary = (low_ref, high_ref)[half][chip, rows, :].astype(jnp.float32)
            middle = decays[chip][half][head : head + 1] * jnp.where(closes, whole_state, entering) + summary
            middle = jnp.where(opens, whole_state, middle)
            entering = jnp.where(even, entering, middle).astype(jnp.bfloat16)
            states = jnp.concatenate([entering, restored], axis=0)
            carried = jnp.dot(reads, states, preferred_element_type=jnp.float32)
            place = slice(k * P_SIZE, (k + 1) * P_SIZE)
            out_ref[:, place] = (part_ref[:, place] + factor[:, k : k + 1] * carried).astype(jnp.bfloat16)


def finish(meta, part, rates, reads, own, other, low, high, pieces, local):
    chips = PAIR // (2 * local)
    count, length, _ = pieces[0].shape
    resumed = pl.BlockSpec((count, local * N, P_SIZE), lambda i, *m: (0, length // (local * N) - 1, 0))
    states = pl.BlockSpec((chips, local * N, P_SIZE), lambda i, *m: (i, 0, 0))
    stretch = pl.BlockSpec((chips, local * N + EXTRA, P_SIZE), lambda i, *m: (i, 0, 0))
    return pl.pallas_call(
        scalars(finish_kernel, local),
        out_shape=jax.ShapeDtypeStruct((TOK, H * P_SIZE), jnp.bfloat16),
        grid_spec=pltpu.PrefetchScalarGridSpec(
            num_scalar_prefetch=1,
            grid=(STEPS,),
            in_specs=[
                pl.BlockSpec((TOK, PAIR * P_SIZE), lambda i, *m: (0, i)),
                pl.BlockSpec((H, TOK), lambda i, *m: (0, 0)),
                pl.BlockSpec((TOK, 2 * N), lambda i, *m: (0, i)),
                states,
                states,
                stretch,
                stretch,
            ]
            + [resumed] * 8,
            out_specs=pl.BlockSpec((TOK, PAIR * P_SIZE), lambda i, *m: (0, i)),
            scratch_shapes=[pltpu.VMEM((H, TOK), jnp.float32)],
        ),
        compiler_params=params(),
        cost_estimate=LONG,
        name="finish",
    )(meta, part, rates, reads, own, other, low, high, *pieces)


def attend_kernel(
    meta, q_ref, four, two, now, four_across, two_across, now_across, *refs,
):
    history_refs, (sk_ref, sv_ref), (out_ref, token_ref, key_s, value_s) = refs[:32], refs[32:34], refs[-4:]
    factor = 1.0 / math.sqrt(HD)
    first = meta.place * TOK
    r = meta.last_start()
    opening = meta.session_at(first)
    closing = meta.session_at(first + TOK - 1)
    even = meta.even

    def band(number, part):
        if number == 0:
            return four[part]
        if number == 1:
            return jnp.where(even, four_across[part], two_across[part])
        if number == 2:
            return two[part]
        if number == 3:
            return jnp.where(even, two_across[part], now_across[part])
        return now[part]

    token_ref[...] = jnp.zeros_like(token_ref)

    def sinks(ref, session):
        rows = ref[session].astype(jnp.float32)
        spare = jnp.zeros((COLUMNS - SPAN - SINKS, HD), jnp.float32)
        return jnp.concatenate([rows, spare], axis=0).astype(jnp.bfloat16)

    length = (REACH + 1) * TOK

    def one_session(session, key_refs, value_refs, resuming, needed):
        start = meta.start_of(session) - first + WINDOW
        oldest = start - WINDOW + jnp.maximum(SINKS + WINDOW - meta.history(session), 0)

        @pl.when(needed & (start > 0))
        def _():
            row = lax.broadcasted_iota(jnp.int32, (length, WINDOW), 0)
            chips, share, _ = key_refs[0].shape
            index = lax.broadcasted_iota(jnp.int32, (1, WINDOW), 1)
            piece, index = index // (WINDOW // 8), index % (WINDOW // 8)
            near, row_in = index // share, index % share
            far = far_place(near, chips.bit_length() - 1)
            device = meta.place ^ (piece // 4 + piece // 2 % 2 * 2 + piece % 2 * 4 + far * 8)
            place = device * share + row_in
            moved = (row == place + start - WINDOW).astype(jnp.bfloat16)
            part = (WINDOW // 8, HD)
            keys = jnp.concatenate([ref[...].reshape(part) for ref in key_refs], axis=0)
            values = jnp.concatenate([ref[...].reshape(part) for ref in value_refs], axis=0)
            history = jnp.dot(
                moved, jnp.concatenate([keys, values], axis=1), preferred_element_type=jnp.float32
            )
            for i in range(REACH + 1):
                rows = slice(i * TOK, (i + 1) * TOK)
                index = lax.broadcasted_iota(jnp.int32, (TOK, HD), 0) + i * TOK
                turn = index >= start
                key_s[rows, :] = jnp.where(
                    turn, band(i, 0).astype(jnp.float32), history[rows, :HD]
                ).astype(jnp.bfloat16)
                value_s[rows, :] = jnp.where(
                    turn, band(i, 1).astype(jnp.float32), history[rows, HD:]
                ).astype(jnp.bfloat16)

        @pl.when(needed & (start <= 0))
        def _():
            for i in range(REACH + 1):
                rows = slice(i * TOK, (i + 1) * TOK)
                key_s[rows, :] = band(i, 0)
                value_s[rows, :] = band(i, 1)

        for b in range(TOK // BLOCK):
            inside = (b * BLOCK + BLOCK > r) if resuming else (b * BLOCK < r)

            @pl.when(needed & inside)
            def _():
                rows = slice(b * BLOCK, b * BLOCK + SPAN)
                keys = jnp.concatenate([key_s[rows, :], sinks(sk_ref, session)], axis=0)
                values = jnp.concatenate([value_s[rows, :], sinks(sv_ref, session)], axis=0)
                tokens = slice(b * BLOCK, (b + 1) * BLOCK)
                queries = jnp.concatenate(
                    [q_ref[tokens, g * HD : (g + 1) * HD] for g in range(QH // KVH)], axis=0
                )
                scores = lax.dot_general(
                    queries, keys, (((1,), (1,)), ((), ())), preferred_element_type=jnp.float32
                )
                token = lax.broadcasted_iota(jnp.int32, (BLOCK, COLUMNS), 0)
                column = lax.broadcasted_iota(jnp.int32, (BLOCK, COLUMNS), 1)
                seen = (column > token) & (column <= token + WINDOW) & (column >= oldest - b * BLOCK)
                seen = (seen & (column < SPAN)) | ((column >= SPAN) & (column < SPAN + SINKS))
                bias = jnp.where(seen, 0.0, NEG)
                weights, sums = [], []
                for g in range(QH // KVH):
                    score = scores[g * BLOCK : (g + 1) * BLOCK] * factor + bias
                    weight = jnp.exp(score - jnp.max(score, axis=1, keepdims=True))
                    sums.append(jnp.sum(weight, axis=1, keepdims=True))
                    weights.append(weight.astype(jnp.bfloat16))
                mixed = jnp.dot(
                    jnp.concatenate(weights, axis=0), values, preferred_element_type=jnp.float32
                )
                for g in range(QH // KVH):
                    result = mixed[g * BLOCK : (g + 1) * BLOCK] / sums[g]
                    lanes = slice(g * HD, (g + 1) * HD)
                    if resuming:
                        index = lax.broadcasted_iota(jnp.int32, (BLOCK, HD), 0) + b * BLOCK
                        before = out_ref[tokens, lanes].astype(jnp.float32)
                        result = jnp.where(index >= r, result, before)
                    out_ref[tokens, lanes] = result.astype(jnp.bfloat16)

    one_session(opening, history_refs[0:8], history_refs[8:16], False, r > 0)
    one_session(closing, history_refs[16:24], history_refs[24:], True, r >= 0)


def attend(meta, queries, bands, pieces, half, sink_keys, sink_values, idle):
    chips = pieces[0].shape[0]
    share = WINDOW // (8 * chips)
    lanes = QH // KVH * HD

    def history_spec(which, last):
        def index(j, *m):
            known = Scalars(*m)
            session = known.session_at(known.place * TOK + (TOK - 1 if last else 0))
            session = session - (known.place >= half).astype(jnp.int32)
            return (0, (which * 2 + session) * KVH + j, 0)

        return pl.BlockSpec((chips, share, HD), index)

    pad = SEQS, SINKS, HD
    return pl.pallas_call(
        scalars(attend_kernel),
        out_shape=[jax.ShapeDtypeStruct((TOK, QH * HD), jnp.bfloat16), TOKEN],
        grid_spec=pltpu.PrefetchScalarGridSpec(
            num_scalar_prefetch=1,
            grid=(KVH,),
            in_specs=[pl.BlockSpec((TOK, lanes), lambda j, *m: (0, j))]
            + [pl.BlockSpec((2, TOK, HD), lambda j, *m: (0, 0, j))] * len(bands)
            + [history_spec(0, False)] * 8
            + [history_spec(1, False)] * 8
            + [history_spec(0, True)] * 8
            + [history_spec(1, True)] * 8
            + [pl.BlockSpec(pad, lambda j, *m: (0, 0, j))] * 2
            + [idle_spec(a) for a in idle],
            out_specs=[
                pl.BlockSpec((TOK, lanes), lambda j, *m: (0, j)),
                pl.BlockSpec(TOKEN.shape, lambda j, *m: (0, 0)),
            ],
            scratch_shapes=[
                pltpu.VMEM(((REACH + 1) * TOK, HD), jnp.bfloat16),
                pltpu.VMEM(((REACH + 1) * TOK, HD), jnp.bfloat16),
            ],
        ),
        compiler_params=params(),
        cost_estimate=SHORT,
        name="attend",
    )(
        meta, queries, *bands, *pieces, *pieces, *pieces, *pieces, sink_keys, sink_values, *idle
    )


def shifted(block, axis, distance):
    devices = range(lax.axis_size(axis))
    return lax.ppermute(block, axis, [(i - distance, i) for i in devices if i - distance in devices])


def shards(
    mamba_input,
    step_size,
    decay_log,
    state_write,
    state_read,
    skip_gain,
    saved_states,
    home_slot,
    turn_lengths,
    history_lengths,
    queries,
    turn_keys,
    turn_values,
    cache_keys,
    cache_values,
    sink_keys,
    sink_values,
):
    place = lax.axis_index("ctx")
    group = lax.axis_index("sess")
    groups = lax.axis_size("sess")
    devices = lax.axis_size("ctx")
    local = saved_states.shape[2]
    width = local * N
    chips = devices // 2
    same_core = [list(range(core, devices, 2)) for core in range(2)]
    meta = jnp.concatenate(
        [jnp.stack([place, group]).astype(jnp.int32), turn_lengths[0], history_lengths[0], home_slot]
    )
    x, rates, steps = mamba_input[0], decay_log[0].T, step_size[0].T
    writes, reads = state_write[0], state_read[0]
    def apart(block, distance):
        return lax.ppermute(block, "ctx", [(i, i ^ distance) for i in range(devices)])

    def exchanged(block):
        return lax.all_to_all(block, "ctx", 0, 0, axis_index_groups=same_core, tiled=True)

    stored = [saved_states[0]]
    for j in range(1, groups):
        route = [((i + j) % groups, i) for i in range(groups)]
        stored.append(lax.ppermute(saved_states[0], "sess", route))
    stored = [block.reshape(SEQS, local, P_SIZE, N) for block in stored]

    parcel = (1, 4 * KVH * cache_keys.shape[2], HD)
    band = (2, TOK, KVH * HD)
    near, away, key_value = whole(
        scalars(pack_kernel, devices // 2),
        "pack",
        meta,
        [cache_keys[0], cache_values[0], turn_keys[0], turn_values[0]],
        [(parcel, jnp.bfloat16), (parcel, jnp.bfloat16), (band, jnp.bfloat16)],
        mib=60,
    )
    moved = apart(away, devices // 2)
    four = shifted(key_value, "ctx", 4)

    keep, send = summaries(meta, x, rates, steps, writes, local, away)
    got = apart(send, 1)

    one = (1, width, P_SIZE)
    home, away, restored = whole(
        scalars(restore_kernel, local, devices // 2, groups),
        "restore",
        meta,
        stored,
        [(one, jnp.bfloat16), (one, jnp.bfloat16), ((SEQS, width, P_SIZE), jnp.float32)],
        idle=[send],
    )
    away = apart(away, devices // 2)
    near, two = whole(
        scalars(join_two_kernel),
        "join_two",
        meta,
        [near, moved, home, away, key_value, four],
        [((2, parcel[1] + width, HD), jnp.bfloat16), (band, jnp.bfloat16)],
        idle=[got],
    )
    distance = devices // 4
    while distance > 4:
        joined = (2 * near.shape[0], *near.shape[1:])
        [near] = whole(scalars(join_kernel), "join", meta, [near, apart(near, distance)], [(joined, jnp.bfloat16)])
        distance //= 2
    moved = apart(near, 4)
    two = apart(two, 2)
    beside = apart(near, 2)
    [chip] = whole(
        scalars(combine_kernel, local),
        "combine",
        meta,
        [keep, got],
        [(keep.shape, jnp.bfloat16)],
        idle=[near],
    )
    total = exchanged(chip)
    part, token = intra(meta, skip_gain, x, rates, steps, writes, reads, chip)
    pieces = [near, moved, beside, apart(moved, 2)]
    bands = [four, two, key_value]
    across = [apart(block, 1) for block in bands]
    low = apart(keep, 1)

    entering, after = whole(
        scalars(recurrence_kernel, local),
        "recurrence",
        meta,
        [total, restored],
        [((chips, width, P_SIZE), jnp.bfloat16), (TOKEN.shape, TOKEN.dtype)],
        idle=[token, low, *across, *pieces],
    )
    entering = exchanged(entering)
    pieces += [apart(piece, 1) for piece in pieces]
    attended, token = attend(
        meta, queries[0], bands + across, pieces, devices // 2, sink_keys[0], sink_values[0], [after]
    )
    [entering] = whole(
        scalars(copy_kernel), "copy", meta, [entering], [((chips, width, P_SIZE), jnp.bfloat16)], idle=[token]
    )
    other = apart(entering, 1)
    mixed = finish(meta, part, rates, reads, entering, other, low, got, pieces, local)
    return mixed[None], attended[None]


def solution(mesh):
    token = P("sess", "ctx", None)
    return jax.shard_map(
        shards,
        mesh=mesh,
        in_specs=(
            token,
            token,
            token,
            token,
            token,
            P(),
            P("sess", None, "ctx", None),
            P(),
            P("sess", None),
            P("sess", None),
            token,
            token,
            token,
            P("sess", None, "ctx", None),
            P("sess", None, "ctx", None),
            P("sess", None, None, None),
            P("sess", None, None, None),
        ),
        out_specs=(token, token),
        check_vma=False,
    )
```

```python
import math

import jax
import jax.numpy as jnp
from jax import lax
from jax.experimental import pallas as pl
from jax.experimental.pallas import tpu as pltpu
from jax.sharding import PartitionSpec as P

REACH = 4
SEQS = 3
SINKS = 4
H = 64
P_SIZE = 128
N = 64
G = 8
QH = 32
KVH = 4
HD = 128
WINDOW = 512
TOK = 128

HEADS_PER = H // G
PAIR = 2 * HEADS_PER
STEPS = H // PAIR
EXTRA = 16
BLOCK = 64
SPAN = WINDOW + BLOCK
COLUMNS = SPAN + 64
NEG = -1e30
TOKEN = jax.ShapeDtypeStruct((8, 128), jnp.float32)
SHORT = pl.CostEstimate(flops=1024, bytes_accessed=1024, transcendentals=0)
LONG = pl.CostEstimate(flops=1 << 35, bytes_accessed=1 << 20, transcendentals=0)


class Scalars:
    def __init__(self, ids):
        self.place, self.group = ids[0], ids[1]
        self.one = ids[2]
        self.two = ids[2] + ids[3]
        self.ids = ids
        self.even = self.place % 2 == 0

    def history(self, session):
        return self.ids[2 + SEQS + session]

    def home(self, number):
        return self.ids[2 + 2 * SEQS + number]

    def session_at(self, position):
        return (position >= self.one).astype(jnp.int32) + (position >= self.two).astype(jnp.int32)

    def start_of(self, session):
        return jnp.where(session == 0, 0, jnp.where(session == 1, self.one, self.two))

    def last_start(self):
        first = self.place * TOK
        return jnp.maximum(self.start_of(self.session_at(first + TOK - 1)) - first, 0)


def scalars(kernel, *options):
    def body(ids, *refs):
        kernel(*options, Scalars(ids), *refs)

    return body


def params(mib=60):
    return pltpu.CompilerParams(vmem_limit_bytes=mib * 1024 * 1024)


def running_rows(dl_ref):
    k = lax.broadcasted_iota(jnp.int32, (TOK, TOK), 0)
    u = lax.broadcasted_iota(jnp.int32, (TOK, TOK), 1)
    upto = (k <= u).astype(jnp.bfloat16)
    running = jnp.dot(dl_ref[...], upto, preferred_element_type=jnp.float32)
    return dl_ref[...].astype(jnp.float32), running


def summary_kernel(
    local, meta, x_ref, dl_ref, step_ref, write_ref, _, keep_ref, send_ref, coef_s, factor_s, write_s
):
    step = pl.program_id(0)

    @pl.when(step == 0)
    def _():
        rates, running = running_rows(dl_ref)
        steps = step_ref[...].astype(jnp.float32)
        r = meta.last_start()
        lane = lax.broadcasted_iota(jnp.int32, (H, TOK), 1)
        last = running[:, TOK - 1 :]
        base = jnp.sum(jnp.where(lane < r, rates, 0.0), axis=1, keepdims=True)
        coef_s[...] = jnp.where(lane >= r, jnp.exp(last - running) * steps, 0.0)
        factor_s[...] = jnp.broadcast_to(jnp.exp(last - base), (H, TOK))
        write_s[...] = write_ref[...].astype(jnp.float32).T

    even = meta.even
    coef = coef_s[pl.ds(pl.multiple_of(step * PAIR, PAIR), PAIR), :]
    factor = factor_s[pl.ds(pl.multiple_of(step * PAIR, PAIR), PAIR), :]
    writes = write_s[pl.ds(pl.multiple_of(step * 2 * N, 2 * N), 2 * N), :]

    def summary(k):
        group = k // HEADS_PER
        loading = (writes[group * N : (group + 1) * N] * coef[k : k + 1]).astype(jnp.bfloat16)
        return jnp.dot(
            loading, x_ref[:, k * P_SIZE : (k + 1) * P_SIZE], preferred_element_type=jnp.float32
        )

    for chip in range(PAIR // (2 * local)):
        low, high = 2 * local * chip, 2 * local * chip + local
        for k in range(local):
            first, second = summary(low + k), summary(high + k)
            rows = slice(k * N, (k + 1) * N)
            keep_ref[chip, rows, :] = jnp.where(even, first, second).astype(jnp.bfloat16)
            send_ref[chip, rows, :] = jnp.where(even, second, first).astype(jnp.bfloat16)
        first, second = factor[low : low + local], factor[high : high + local]
        keep_ref[chip, local * N :, :] = factor_rows(jnp.where(even, first, second))
        send_ref[chip, local * N :, :] = factor_rows(jnp.where(even, second, first))


def factor_rows(rows):
    high = rows.astype(jnp.bfloat16).astype(jnp.float32)
    parts = [high, rows - high]
    if EXTRA > 2 * rows.shape[0]:
        parts.append(jnp.zeros((EXTRA - 2 * rows.shape[0], TOK), jnp.float32))
    return jnp.concatenate(parts, axis=0).astype(jnp.bfloat16)


def factors_of(block, local):
    block = block.astype(jnp.float32)
    return block[:local] + block[local : 2 * local]


def summaries(meta, x, rates, steps, writes, local, idle):
    chips = H // (2 * local)
    rows = local * N + EXTRA
    shape = jax.ShapeDtypeStruct((chips, rows, P_SIZE), jnp.bfloat16)
    spec = pl.BlockSpec((PAIR // (2 * local), rows, P_SIZE), lambda i, *m: (i, 0, 0))
    return pl.pallas_call(
        scalars(summary_kernel, local),
        out_shape=[shape, shape],
        grid_spec=pltpu.PrefetchScalarGridSpec(
            num_scalar_prefetch=1,
            grid=(STEPS,),
            in_specs=[
                pl.BlockSpec((TOK, PAIR * P_SIZE), lambda i, *m: (0, i)),
                pl.BlockSpec((H, TOK), lambda i, *m: (0, 0)),
                pl.BlockSpec((H, TOK), lambda i, *m: (0, 0)),
                pl.BlockSpec((TOK, G * N), lambda i, *m: (0, 0)),
                pl.BlockSpec(memory_space=pl.ANY),
            ],
            out_specs=[spec, spec],
            scratch_shapes=[
                pltpu.VMEM((H, TOK), jnp.float32),
                pltpu.VMEM((H, TOK), jnp.float32),
                pltpu.VMEM((G * N, TOK), jnp.float32),
            ],
        ),
        compiler_params=params(),
        cost_estimate=LONG,
        name="summaries",
    )(meta, x, rates, steps, writes, idle)


def idle_spec(array):
    return pl.BlockSpec(memory_space=pl.ANY)


def whole(kernel, name, meta, arrays, shapes, idle=(), mib=16, scratch=()):
    def spec(shape):
        return pl.BlockSpec(shape, lambda i, *m: (0,) * len(shape))

    return pl.pallas_call(
        kernel,
        out_shape=[jax.ShapeDtypeStruct(s, t) for s, t in shapes],
        grid_spec=pltpu.PrefetchScalarGridSpec(
            num_scalar_prefetch=1,
            grid=(1,),
            in_specs=[spec(a.shape) for a in arrays] + [idle_spec(a) for a in idle],
            out_specs=[spec(s) for s, _ in shapes],
            scratch_shapes=scratch,
        ),
        compiler_params=params(mib),
        cost_estimate=LONG,
        name=name,
    )(meta, *arrays, *idle)


def pack_kernel(half, meta, keys_ref, values_ref, turn_keys_ref, turn_values_ref, home_ref, away_ref, band_ref):
    band_ref[0] = turn_keys_ref[...]
    band_ref[1] = turn_values_ref[...]
    rows = keys_ref.shape[1]
    upper = (meta.place >= half).astype(jnp.int32)
    for out_ref, first in ((home_ref, upper), (away_ref, 1 - upper)):
        for which, ref in enumerate((keys_ref, values_ref)):
            for s in range(2):
                for j in range(KVH):
                    place = ((which * 2 + s) * KVH + j) * rows
                    out_ref[0, place : place + rows, :] = ref[first + s, :, j * HD : (j + 1) * HD]


def restore_kernel(local, half, groups, meta, *refs):
    stored, (home_ref, away_ref, restored_ref) = refs[:groups], refs[-3:]
    for s in range(SEQS):
        slot = meta.home(meta.group * SEQS + s)
        source = (slot // SEQS - meta.group + groups) % groups
        for k in range(local):
            state = stored[0][slot % SEQS, k]
            for j in range(1, groups):
                state = jnp.where(source == j, stored[j][slot % SEQS, k], state)
            restored_ref[s, k * N : (k + 1) * N, :] = state.T
    upper = (meta.place >= half).astype(jnp.int32)
    home_ref[0] = restored_ref[upper + 1].astype(jnp.bfloat16)
    away_ref[0] = restored_ref[2 - upper].astype(jnp.bfloat16)


def copy_kernel(meta, array_ref, *refs):
    refs[-1][...] = array_ref[...]


def join_kernel(meta, first_ref, second_ref, *refs):
    out_ref = refs[-1]
    count = first_ref.shape[0]
    out_ref[:count] = first_ref[...]
    out_ref[count:] = second_ref[...]


def join_two_kernel(
    meta, first_ref, second_ref, first_state_ref, second_state_ref, key_value_ref, four_ref, *refs
):
    out_ref, two_ref = refs[-2:]
    rows = first_ref.shape[1]
    for i, (parcel, state) in enumerate(((first_ref, first_state_ref), (second_ref, second_state_ref))):
        out_ref[i, :rows, :] = parcel[0]
        out_ref[i, rows:, :] = state[0]
    two_ref[...] = jnp.where(meta.place // 2 % 2 == 0, key_value_ref[...], four_ref[...])


def far_place(distance, bits):
    place = distance * 0
    for k in range(bits):
        place = place + ((distance // (1 << k)) % 2) * (1 << (bits - 1 - k))
    return place


def combine_kernel(local, meta, keep_ref, got_ref, *refs):
    out_ref = refs[-1]
    even = meta.even
    second = (meta.place // 2 * 2 + 1) * TOK
    closes = meta.start_of(meta.session_at(second + TOK - 1)) >= second
    width = local * N
    for chip in range(keep_ref.shape[0]):
        keep = factors_of(keep_ref[chip, width:, :], local)
        got = factors_of(got_ref[chip, width:, :], local)
        f0, f1 = jnp.where(even, keep, got), jnp.where(even, got, keep)
        out_ref[chip, width:, :] = factor_rows(jnp.where(closes, f1, f0 * f1))
        carry = jnp.where(closes, 0.0, f1)
        for k in range(local):
            rows = slice(k * N, (k + 1) * N)
            keep = keep_ref[chip, rows, :].astype(jnp.float32)
            got = got_ref[chip, rows, :].astype(jnp.float32)
            s0, s1 = jnp.where(even, keep, got), jnp.where(even, got, keep)
            out_ref[chip, rows, :] = (carry[k : k + 1] * s0 + s1).astype(jnp.bfloat16)


def recurrence_kernel(local, meta, got_ref, restored_ref, *refs):
    out_ref, token_ref = refs[-2:]
    token_ref[...] = jnp.zeros_like(token_ref)
    width = local * N
    span = 2 * TOK
    state = [jnp.zeros((N, P_SIZE), jnp.float32) for _ in range(local)]
    for c in range(got_ref.shape[0]):
        first = c * span
        opening = meta.session_at(first)
        closing = meta.session_at(first + span - 1)
        opens = meta.start_of(opening) >= first
        closes = meta.start_of(closing) >= first
        factor = factors_of(got_ref[c, width:, :], local)
        for k in range(local):
            rows = slice(k * N, (k + 1) * N)
            entering = jnp.where(opens, restored_ref[opening, rows, :], state[k])
            out_ref[c, rows, :] = entering.astype(jnp.bfloat16)
            source = jnp.where(closes, restored_ref[closing, rows, :], state[k])
            state[k] = factor[k : k + 1] * source + got_ref[c, rows, :].astype(jnp.float32)


def intra_kernel(meta, skip, x_ref, dl_ref, step_ref, write_ref, read_ref, _, out_ref, token_ref, run_s, step_s):
    step = pl.program_id(0)

    @pl.when(step == 0)
    def _():
        _, running = running_rows(dl_ref)
        run_s[...] = running
        step_s[...] = step_ref[...].astype(jnp.float32)

    token_ref[...] = jnp.zeros_like(token_ref)
    heads = pl.ds(pl.multiple_of(step * PAIR, PAIR), PAIR)
    running = run_s[heads, :]
    sizes = step_s[heads, :]
    columns = running.T
    r = meta.last_start()
    t = lax.broadcasted_iota(jnp.int32, (TOK, TOK), 0)
    u = lax.broadcasted_iota(jnp.int32, (TOK, TOK), 1)
    causal = (u <= t) & ((u >= r) | (t < r))
    for group in range(2):
        part = slice(group * N, (group + 1) * N)
        products = lax.dot_general(
            read_ref[:, part], write_ref[:, part], (((1,), (1,)), ((), ())),
            preferred_element_type=jnp.float32,
        )
        products = jnp.where(causal, products, 0.0)
        for k in range(group * HEADS_PER, (group + 1) * HEADS_PER):
            difference = columns[:, k : k + 1] - running[k : k + 1]
            decay = jnp.exp(jnp.minimum(difference, 0.0))
            mixing = (products * decay * sizes[k : k + 1]).astype(jnp.bfloat16)
            place = slice(k * P_SIZE, (k + 1) * P_SIZE)
            x = x_ref[:, place]
            mixed = jnp.dot(mixing, x, preferred_element_type=jnp.float32)
            out_ref[:, place] = mixed + skip[step * PAIR + k] * x.astype(jnp.float32)


def intra(meta, skip, x, rates, steps, writes, reads, idle):
    return pl.pallas_call(
        scalars(intra_kernel),
        out_shape=[jax.ShapeDtypeStruct((TOK, H * P_SIZE), jnp.float32), TOKEN],
        grid_spec=pltpu.PrefetchScalarGridSpec(
            num_scalar_prefetch=2,
            grid=(STEPS,),
            in_specs=[
                pl.BlockSpec((TOK, PAIR * P_SIZE), lambda i, *m: (0, i)),
                pl.BlockSpec((H, TOK), lambda i, *m: (0, 0)),
                pl.BlockSpec((H, TOK), lambda i, *m: (0, 0)),
                pl.BlockSpec((TOK, 2 * N), lambda i, *m: (0, i)),
                pl.BlockSpec((TOK, 2 * N), lambda i, *m: (0, i)),
                pl.BlockSpec(memory_space=pl.ANY),
            ],
            out_specs=[
                pl.BlockSpec((TOK, PAIR * P_SIZE), lambda i, *m: (0, i)),
                pl.BlockSpec(TOKEN.shape, lambda i, *m: (0, 0)),
            ],
            scratch_shapes=[
                pltpu.VMEM((H, TOK), jnp.float32),
                pltpu.VMEM((H, TOK), jnp.float32),
            ],
        ),
        compiler_params=params(),
        cost_estimate=LONG,
        name="intra",
    )(meta, skip, x, rates, steps, writes, reads, idle)


def finish_kernel(
    local, meta, part_ref, dl_ref, read_ref, own_ref, other_ref, low_ref, high_ref, *refs,
):
    pieces, (out_ref, factor_s) = refs[:8], refs[-2:]
    bits = pieces[0].shape[0].bit_length() - 1
    step = pl.program_id(0)
    even = meta.even
    r = meta.last_start()
    first = meta.place // 2 * 2 * TOK
    second = first + TOK
    start = meta.start_of(meta.session_at(second + TOK - 1))
    closes = (start > first) & (start < second)
    opens = start == second
    width = local * N

    @pl.when(step == 0)
    def _():
        rates, running = running_rows(dl_ref)
        lane = lax.broadcasted_iota(jnp.int32, (H, TOK), 1)
        base = jnp.sum(jnp.where(lane < r, rates, 0.0), axis=1, keepdims=True)
        factor_s[...] = jnp.exp(jnp.minimum(running - jnp.where(lane >= r, base, 0.0), 0.0))

    factor = factor_s[pl.ds(pl.multiple_of(step * PAIR, PAIR), PAIR), :].T
    token = lax.broadcasted_iota(jnp.int32, (TOK, N), 0)
    resumed = (token >= r) & (r > 0)
    decays = [[factors_of(ref[chip, width:, :], local) for ref in (low_ref, high_ref)] for chip in range(own_ref.shape[0])]
    for group in range(2):
        reads = read_ref[:, group * N : (group + 1) * N].astype(jnp.float32)
        left = jnp.where(resumed, 0.0, reads)
        right = jnp.where(resumed, reads, 0.0)
        reads = jnp.concatenate([left, right], axis=1).astype(jnp.bfloat16)
        for k in range(group * HEADS_PER, (group + 1) * HEADS_PER):
            chip, half, head = k // (2 * local), k // local % 2, k % local
            rows = slice(head * N, (head + 1) * N)
            own = even if half == 0 else jnp.logical_not(even)
            entering = jnp.where(own, own_ref[chip, rows, :], other_ref[chip, rows, :]).astype(jnp.float32)
            distance = (step * own_ref.shape[0] + chip) ^ (meta.place // 2)
            far = far_place(distance // 4, bits)
            near, low_bit = distance % 2 == 0, distance // 2 % 2 == 0
            found = [piece[far, rows, :] for piece in pieces]
            found = [jnp.where(low_bit, found[i], found[i + 1]) for i in range(0, 8, 2)]
            restored = jnp.where(own, jnp.where(near, found[0], found[1]), jnp.where(near, found[2], found[3]))
            whole_state = restored.astype(jnp.float32)
            summary = (low_ref, high_ref)[half][chip, rows, :].astype(jnp.float32)
            middle = decays[chip][half][head : head + 1] * jnp.where(closes, whole_state, entering) + summary
            middle = jnp.where(opens, whole_state, middle)
            entering = jnp.where(even, entering, middle).astype(jnp.bfloat16)
            states = jnp.concatenate([entering, restored], axis=0)
            carried = jnp.dot(reads, states, preferred_element_type=jnp.float32)
            place = slice(k * P_SIZE, (k + 1) * P_SIZE)
            out_ref[:, place] = (part_ref[:, place] + factor[:, k : k + 1] * carried).astype(jnp.bfloat16)


def finish(meta, part, rates, reads, own, other, low, high, pieces, local):
    chips = PAIR // (2 * local)
    count, length, _ = pieces[0].shape
    resumed = pl.BlockSpec((count, local * N, P_SIZE), lambda i, *m: (0, length // (local * N) - 1, 0))
    states = pl.BlockSpec((chips, local * N, P_SIZE), lambda i, *m: (i, 0, 0))
    stretch = pl.BlockSpec((chips, local * N + EXTRA, P_SIZE), lambda i, *m: (i, 0, 0))
    return pl.pallas_call(
        scalars(finish_kernel, local),
        out_shape=jax.ShapeDtypeStruct((TOK, H * P_SIZE), jnp.bfloat16),
        grid_spec=pltpu.PrefetchScalarGridSpec(
            num_scalar_prefetch=1,
            grid=(STEPS,),
            in_specs=[
                pl.BlockSpec((TOK, PAIR * P_SIZE), lambda i, *m: (0, i)),
                pl.BlockSpec((H, TOK), lambda i, *m: (0, 0)),
                pl.BlockSpec((TOK, 2 * N), lambda i, *m: (0, i)),
                states,
                states,
                stretch,
                stretch,
            ]
            + [resumed] * 8,
            out_specs=pl.BlockSpec((TOK, PAIR * P_SIZE), lambda i, *m: (0, i)),
            scratch_shapes=[pltpu.VMEM((H, TOK), jnp.float32)],
        ),
        compiler_params=params(),
        cost_estimate=LONG,
        name="finish",
    )(meta, part, rates, reads, own, other, low, high, *pieces)


def attend_kernel(
    meta, q_ref, four, two, now, four_across, two_across, now_across, *refs,
):
    history_refs, (sk_ref, sv_ref), (out_ref, token_ref, key_s, value_s) = refs[:32], refs[32:34], refs[-4:]
    factor = 1.0 / math.sqrt(HD)
    first = meta.place * TOK
    r = meta.last_start()
    opening = meta.session_at(first)
    closing = meta.session_at(first + TOK - 1)
    even = meta.even

    def band(number, part):
        if number == 0:
            return four[part]
        if number == 1:
            return jnp.where(even, four_across[part], two_across[part])
        if number == 2:
            return two[part]
        if number == 3:
            return jnp.where(even, two_across[part], now_across[part])
        return now[part]

    token_ref[...] = jnp.zeros_like(token_ref)

    def sinks(ref, session):
        rows = ref[session].astype(jnp.float32)
        spare = jnp.zeros((COLUMNS - SPAN - SINKS, HD), jnp.float32)
        return jnp.concatenate([rows, spare], axis=0).astype(jnp.bfloat16)

    length = (REACH + 1) * TOK

    def one_session(session, key_refs, value_refs, resuming, needed):
        start = meta.start_of(session) - first + WINDOW
        oldest = start - WINDOW + jnp.maximum(SINKS + WINDOW - meta.history(session), 0)

        @pl.when(needed & (start > 0))
        def _():
            row = lax.broadcasted_iota(jnp.int32, (length, WINDOW), 0)
            chips, share, _ = key_refs[0].shape
            index = lax.broadcasted_iota(jnp.int32, (1, WINDOW), 1)
            piece, index = index // (WINDOW // 8), index % (WINDOW // 8)
            near, row_in = index // share, index % share
            far = far_place(near, chips.bit_length() - 1)
            device = meta.place ^ (piece // 4 + piece // 2 % 2 * 2 + piece % 2 * 4 + far * 8)
            place = device * share + row_in
            moved = (row == place + start - WINDOW).astype(jnp.bfloat16)
            part = (WINDOW // 8, HD)
            keys = jnp.concatenate([ref[...].reshape(part) for ref in key_refs], axis=0)
            values = jnp.concatenate([ref[...].reshape(part) for ref in value_refs], axis=0)
            history = jnp.dot(
                moved, jnp.concatenate([keys, values], axis=1), preferred_element_type=jnp.float32
            )
            for i in range(REACH + 1):
                rows = slice(i * TOK, (i + 1) * TOK)
                index = lax.broadcasted_iota(jnp.int32, (TOK, HD), 0) + i * TOK
                turn = index >= start
                key_s[rows, :] = jnp.where(
                    turn, band(i, 0).astype(jnp.float32), history[rows, :HD]
                ).astype(jnp.bfloat16)
                value_s[rows, :] = jnp.where(
                    turn, band(i, 1).astype(jnp.float32), history[rows, HD:]
                ).astype(jnp.bfloat16)

        @pl.when(needed & (start <= 0))
        def _():
            for i in range(REACH + 1):
                rows = slice(i * TOK, (i + 1) * TOK)
                key_s[rows, :] = band(i, 0)
                value_s[rows, :] = band(i, 1)

        for b in range(TOK // BLOCK):
            inside = (b * BLOCK + BLOCK > r) if resuming else (b * BLOCK < r)

            @pl.when(needed & inside)
            def _():
                rows = slice(b * BLOCK, b * BLOCK + SPAN)
                keys = jnp.concatenate([key_s[rows, :], sinks(sk_ref, session)], axis=0)
                values = jnp.concatenate([value_s[rows, :], sinks(sv_ref, session)], axis=0)
                tokens = slice(b * BLOCK, (b + 1) * BLOCK)
                queries = jnp.concatenate(
                    [q_ref[tokens, g * HD : (g + 1) * HD] for g in range(QH // KVH)], axis=0
                )
                scores = lax.dot_general(
                    queries, keys, (((1,), (1,)), ((), ())), preferred_element_type=jnp.float32
                )
                token = lax.broadcasted_iota(jnp.int32, (BLOCK, COLUMNS), 0)
                column = lax.broadcasted_iota(jnp.int32, (BLOCK, COLUMNS), 1)
                seen = (column > token) & (column <= token + WINDOW) & (column >= oldest - b * BLOCK)
                seen = (seen & (column < SPAN)) | ((column >= SPAN) & (column < SPAN + SINKS))
                bias = jnp.where(seen, 0.0, NEG)
                weights, sums = [], []
                for g in range(QH // KVH):
                    score = scores[g * BLOCK : (g + 1) * BLOCK] * factor + bias
                    weight = jnp.exp(score - jnp.max(score, axis=1, keepdims=True))
                    sums.append(jnp.sum(weight, axis=1, keepdims=True))
                    weights.append(weight.astype(jnp.bfloat16))
                mixed = jnp.dot(
                    jnp.concatenate(weights, axis=0), values, preferred_element_type=jnp.float32
                )
                for g in range(QH // KVH):
                    result = mixed[g * BLOCK : (g + 1) * BLOCK] / sums[g]
                    lanes = slice(g * HD, (g + 1) * HD)
                    if resuming:
                        index = lax.broadcasted_iota(jnp.int32, (BLOCK, HD), 0) + b * BLOCK
                        before = out_ref[tokens, lanes].astype(jnp.float32)
                        result = jnp.where(index >= r, result, before)
                    out_ref[tokens, lanes] = result.astype(jnp.bfloat16)

    one_session(opening, history_refs[0:8], history_refs[8:16], False, r > 0)
    one_session(closing, history_refs[16:24], history_refs[24:], True, r >= 0)


def attend(meta, queries, bands, pieces, half, sink_keys, sink_values, idle):
    chips = pieces[0].shape[0]
    share = WINDOW // (8 * chips)
    lanes = QH // KVH * HD

    def history_spec(which, last):
        def index(j, *m):
            known = Scalars(*m)
            session = known.session_at(known.place * TOK + (TOK - 1 if last else 0))
            session = session - (known.place >= half).astype(jnp.int32)
            return (0, (which * 2 + session) * KVH + j, 0)

        return pl.BlockSpec((chips, share, HD), index)

    pad = SEQS, SINKS, HD
    return pl.pallas_call(
        scalars(attend_kernel),
        out_shape=[jax.ShapeDtypeStruct((TOK, QH * HD), jnp.bfloat16), TOKEN],
        grid_spec=pltpu.PrefetchScalarGridSpec(
            num_scalar_prefetch=1,
            grid=(KVH,),
            in_specs=[pl.BlockSpec((TOK, lanes), lambda j, *m: (0, j))]
            + [pl.BlockSpec((2, TOK, HD), lambda j, *m: (0, 0, j))] * len(bands)
            + [history_spec(0, False)] * 8
            + [history_spec(1, False)] * 8
            + [history_spec(0, True)] * 8
            + [history_spec(1, True)] * 8
            + [pl.BlockSpec(pad, lambda j, *m: (0, 0, j))] * 2
            + [idle_spec(a) for a in idle],
            out_specs=[
                pl.BlockSpec((TOK, lanes), lambda j, *m: (0, j)),
                pl.BlockSpec(TOKEN.shape, lambda j, *m: (0, 0)),
            ],
            scratch_shapes=[
                pltpu.VMEM(((REACH + 1) * TOK, HD), jnp.bfloat16),
                pltpu.VMEM(((REACH + 1) * TOK, HD), jnp.bfloat16),
            ],
        ),
        compiler_params=params(),
        cost_estimate=SHORT,
        name="attend",
    )(
        meta, queries, *bands, *pieces, *pieces, *pieces, *pieces, sink_keys, sink_values, *idle
    )


def shifted(block, axis, distance):
    devices = range(lax.axis_size(axis))
    return lax.ppermute(block, axis, [(i - distance, i) for i in devices if i - distance in devices])


def shards(
    mamba_input,
    step_size,
    decay_log,
    state_write,
    state_read,
    skip_gain,
    saved_states,
    home_slot,
    turn_lengths,
    history_lengths,
    queries,
    turn_keys,
    turn_values,
    cache_keys,
    cache_values,
    sink_keys,
    sink_values,
):
    place = lax.axis_index("ctx")
    group = lax.axis_index("sess")
    groups = lax.axis_size("sess")
    devices = lax.axis_size("ctx")
    local = saved_states.shape[2]
    width = local * N
    chips = devices // 2
    same_core = [list(range(core, devices, 2)) for core in range(2)]
    meta = jnp.concatenate(
        [jnp.stack([place, group]).astype(jnp.int32), turn_lengths[0], history_lengths[0], home_slot]
    )
    x, rates, steps = mamba_input[0], decay_log[0].T, step_size[0].T
    writes, reads = state_write[0], state_read[0]
    def apart(block, distance):
        return lax.ppermute(block, "ctx", [(i, i ^ distance) for i in range(devices)])

    def exchanged(block):
        return lax.all_to_all(block, "ctx", 0, 0, axis_index_groups=same_core, tiled=True)

    stored = [saved_states[0]]
    for j in range(1, groups):
        route = [((i + j) % groups, i) for i in range(groups)]
        stored.append(lax.ppermute(saved_states[0], "sess", route))
    stored = [block.reshape(SEQS, local, P_SIZE, N) for block in stored]

    parcel = (1, 4 * KVH * cache_keys.shape[2], HD)
    band = (2, TOK, KVH * HD)
    near, away, key_value = whole(
        scalars(pack_kernel, devices // 2),
        "pack",
        meta,
        [cache_keys[0], cache_values[0], turn_keys[0], turn_values[0]],
        [(parcel, jnp.bfloat16), (parcel, jnp.bfloat16), (band, jnp.bfloat16)],
        mib=60,
    )
    moved = apart(away, devices // 2)
    four = shifted(key_value, "ctx", 4)

    one = (1, width, P_SIZE)
    home, away, restored = whole(
        scalars(restore_kernel, local, devices // 2, groups),
        "restore",
        meta,
        stored,
        [(one, jnp.bfloat16), (one, jnp.bfloat16), ((SEQS, width, P_SIZE), jnp.float32)],
        idle=[key_value],
    )
    away = apart(away, devices // 2)
    keep, send = summaries(meta, x, rates, steps, writes, local, home)
    got = apart(send, 1)

    near, two = whole(
        scalars(join_two_kernel),
        "join_two",
        meta,
        [near, moved, home, away, key_value, four],
        [((2, parcel[1] + width, HD), jnp.bfloat16), (band, jnp.bfloat16)],
        idle=[send],
    )
    distance = devices // 4
    while distance > 4:
        joined = (2 * near.shape[0], *near.shape[1:])
        [near] = whole(scalars(join_kernel), "join", meta, [near, apart(near, distance)], [(joined, jnp.bfloat16)])
        distance //= 2
    moved = apart(near, 4)
    two = apart(two, 2)
    beside = apart(near, 2)
    [chip] = whole(
        scalars(combine_kernel, local),
        "combine",
        meta,
        [keep, got],
        [(keep.shape, jnp.bfloat16)],
        idle=[near],
    )
    total = exchanged(chip)
    part, token = intra(meta, skip_gain, x, rates, steps, writes, reads, chip)
    pieces = [near, moved, beside, apart(moved, 2)]
    bands = [four, two, key_value]
    across = [apart(block, 1) for block in bands]
    low = apart(keep, 1)

    entering, after = whole(
        scalars(recurrence_kernel, local),
        "recurrence",
        meta,
        [total, restored],
        [((chips, width, P_SIZE), jnp.bfloat16), (TOKEN.shape, TOKEN.dtype)],
        idle=[token, low, *across, *pieces],
    )
    entering = exchanged(entering)
    pieces += [apart(piece, 1) for piece in pieces]
    attended, token = attend(
        meta, queries[0], bands + across, pieces, devices // 2, sink_keys[0], sink_values[0], [after]
    )
    [entering] = whole(
        scalars(copy_kernel), "copy", meta, [entering], [((chips, width, P_SIZE), jnp.bfloat16)], idle=[token]
    )
    other = apart(entering, 1)
    mixed = finish(meta, part, rates, reads, entering, other, low, got, pieces, local)
    return mixed[None], attended[None]


def solution(mesh):
    token = P("sess", "ctx", None)
    return jax.shard_map(
        shards,
        mesh=mesh,
        in_specs=(
            token,
            token,
            token,
            token,
            token,
            P(),
            P("sess", None, "ctx", None),
            P(),
            P("sess", None),
            P("sess", None),
            token,
            token,
            token,
            P("sess", None, "ctx", None),
            P("sess", None, "ctx", None),
            P("sess", None, None, None),
            P("sess", None, None, None),
        ),
        out_specs=(token, token),
        check_vma=False,
    )
```

```python
import math

import jax
import jax.numpy as jnp
from jax import lax
from jax.experimental import pallas as pl
from jax.experimental.pallas import tpu as pltpu
from jax.sharding import PartitionSpec as P

REACH = 4
SEQS = 3
SINKS = 4
H = 64
P_SIZE = 128
N = 64
G = 8
QH = 32
KVH = 4
HD = 128
WINDOW = 512
TOK = 128

HEADS_PER = H // G
PAIR = 2 * HEADS_PER
STEPS = H // PAIR
EXTRA = 16
BLOCK = 64
SPAN = WINDOW + BLOCK
COLUMNS = SPAN + 64
NEG = -1e30
TOKEN = jax.ShapeDtypeStruct((8, 128), jnp.float32)
SHORT = pl.CostEstimate(flops=1024, bytes_accessed=1024, transcendentals=0)
LONG = pl.CostEstimate(flops=1 << 35, bytes_accessed=1 << 20, transcendentals=0)


class Scalars:
    def __init__(self, ids):
        self.place, self.group = ids[0], ids[1]
        self.one = ids[2]
        self.two = ids[2] + ids[3]
        self.ids = ids
        self.even = self.place % 2 == 0

    def history(self, session):
        return self.ids[2 + SEQS + session]

    def home(self, number):
        return self.ids[2 + 2 * SEQS + number]

    def session_at(self, position):
        return (position >= self.one).astype(jnp.int32) + (position >= self.two).astype(jnp.int32)

    def start_of(self, session):
        return jnp.where(session == 0, 0, jnp.where(session == 1, self.one, self.two))

    def last_start(self):
        first = self.place * TOK
        return jnp.maximum(self.start_of(self.session_at(first + TOK - 1)) - first, 0)


def scalars(kernel, *options):
    def body(ids, *refs):
        kernel(*options, Scalars(ids), *refs)

    return body


def params(mib=60):
    return pltpu.CompilerParams(vmem_limit_bytes=mib * 1024 * 1024)


def running_rows(dl_ref):
    k = lax.broadcasted_iota(jnp.int32, (TOK, TOK), 0)
    u = lax.broadcasted_iota(jnp.int32, (TOK, TOK), 1)
    upto = (k <= u).astype(jnp.bfloat16)
    running = jnp.dot(dl_ref[...], upto, preferred_element_type=jnp.float32)
    return dl_ref[...].astype(jnp.float32), running


def summary_kernel(
    local, meta, x_ref, dl_ref, step_ref, write_ref, _, keep_ref, send_ref, coef_s, factor_s, write_s
):
    step = pl.program_id(0)

    @pl.when(step == 0)
    def _():
        rates, running = running_rows(dl_ref)
        steps = step_ref[...].astype(jnp.float32)
        r = meta.last_start()
        lane = lax.broadcasted_iota(jnp.int32, (H, TOK), 1)
        last = running[:, TOK - 1 :]
        base = jnp.sum(jnp.where(lane < r, rates, 0.0), axis=1, keepdims=True)
        coef_s[...] = jnp.where(lane >= r, jnp.exp(last - running) * steps, 0.0)
        factor_s[...] = jnp.broadcast_to(jnp.exp(last - base), (H, TOK))
        write_s[...] = write_ref[...].astype(jnp.float32).T

    even = meta.even
    coef = coef_s[pl.ds(pl.multiple_of(step * PAIR, PAIR), PAIR), :]
    factor = factor_s[pl.ds(pl.multiple_of(step * PAIR, PAIR), PAIR), :]
    writes = write_s[pl.ds(pl.multiple_of(step * 2 * N, 2 * N), 2 * N), :]

    def summary(k):
        group = k // HEADS_PER
        loading = (writes[group * N : (group + 1) * N] * coef[k : k + 1]).astype(jnp.bfloat16)
        return jnp.dot(
            loading, x_ref[:, k * P_SIZE : (k + 1) * P_SIZE], preferred_element_type=jnp.float32
        )

    for chip in range(PAIR // (2 * local)):
        low, high = 2 * local * chip, 2 * local * chip + local
        for k in range(local):
            first, second = summary(low + k), summary(high + k)
            rows = slice(k * N, (k + 1) * N)
            keep_ref[chip, rows, :] = jnp.where(even, first, second).astype(jnp.bfloat16)
            send_ref[chip, rows, :] = jnp.where(even, second, first).astype(jnp.bfloat16)
        first, second = factor[low : low + local], factor[high : high + local]
        keep_ref[chip, local * N :, :] = factor_rows(jnp.where(even, first, second))
        send_ref[chip, local * N :, :] = factor_rows(jnp.where(even, second, first))


def factor_rows(rows):
    high = rows.astype(jnp.bfloat16).astype(jnp.float32)
    parts = [high, rows - high]
    if EXTRA > 2 * rows.shape[0]:
        parts.append(jnp.zeros((EXTRA - 2 * rows.shape[0], TOK), jnp.float32))
    return jnp.concatenate(parts, axis=0).astype(jnp.bfloat16)


def factors_of(block, local):
    block = block.astype(jnp.float32)
    return block[:local] + block[local : 2 * local]


def summaries(meta, x, rates, steps, writes, local, idle):
    chips = H // (2 * local)
    rows = local * N + EXTRA
    shape = jax.ShapeDtypeStruct((chips, rows, P_SIZE), jnp.bfloat16)
    spec = pl.BlockSpec((PAIR // (2 * local), rows, P_SIZE), lambda i, *m: (i, 0, 0))
    return pl.pallas_call(
        scalars(summary_kernel, local),
        out_shape=[shape, shape],
        grid_spec=pltpu.PrefetchScalarGridSpec(
            num_scalar_prefetch=1,
            grid=(STEPS,),
            in_specs=[
                pl.BlockSpec((TOK, PAIR * P_SIZE), lambda i, *m: (0, i)),
                pl.BlockSpec((H, TOK), lambda i, *m: (0, 0)),
                pl.BlockSpec((H, TOK), lambda i, *m: (0, 0)),
                pl.BlockSpec((TOK, G * N), lambda i, *m: (0, 0)),
                pl.BlockSpec(memory_space=pl.ANY),
            ],
            out_specs=[spec, spec],
            scratch_shapes=[
                pltpu.VMEM((H, TOK), jnp.float32),
                pltpu.VMEM((H, TOK), jnp.float32),
                pltpu.VMEM((G * N, TOK), jnp.float32),
            ],
        ),
        compiler_params=params(),
        cost_estimate=LONG,
        name="summaries",
    )(meta, x, rates, steps, writes, idle)


def idle_spec(array):
    return pl.BlockSpec(memory_space=pl.ANY)


def whole(kernel, name, meta, arrays, shapes, idle=(), mib=16, scratch=()):
    def spec(shape):
        return pl.BlockSpec(shape, lambda i, *m: (0,) * len(shape))

    return pl.pallas_call(
        kernel,
        out_shape=[jax.ShapeDtypeStruct(s, t) for s, t in shapes],
        grid_spec=pltpu.PrefetchScalarGridSpec(
            num_scalar_prefetch=1,
            grid=(1,),
            in_specs=[spec(a.shape) for a in arrays] + [idle_spec(a) for a in idle],
            out_specs=[spec(s) for s, _ in shapes],
            scratch_shapes=scratch,
        ),
        compiler_params=params(mib),
        cost_estimate=LONG,
        name=name,
    )(meta, *arrays, *idle)


def pack_kernel(half, meta, keys_ref, values_ref, turn_keys_ref, turn_values_ref, home_ref, away_ref, band_ref):
    band_ref[0] = turn_keys_ref[...]
    band_ref[1] = turn_values_ref[...]
    rows = keys_ref.shape[1]
    upper = (meta.place >= half).astype(jnp.int32)
    for out_ref, first in ((home_ref, upper), (away_ref, 1 - upper)):
        for which, ref in enumerate((keys_ref, values_ref)):
            for s in range(2):
                for j in range(KVH):
                    place = ((which * 2 + s) * KVH + j) * rows
                    out_ref[0, place : place + rows, :] = ref[first + s, :, j * HD : (j + 1) * HD]


def restore_kernel(local, half, groups, meta, *refs):
    stored, (home_ref, away_ref, restored_ref) = refs[:groups], refs[-3:]
    for s in range(SEQS):
        slot = meta.home(meta.group * SEQS + s)
        source = (slot // SEQS - meta.group + groups) % groups
        for k in range(local):
            state = stored[0][slot % SEQS, k]
            for j in range(1, groups):
                state = jnp.where(source == j, stored[j][slot % SEQS, k], state)
            restored_ref[s, k * N : (k + 1) * N, :] = state.T
    upper = (meta.place >= half).astype(jnp.int32)
    home_ref[0] = restored_ref[upper + 1].astype(jnp.bfloat16)
    away_ref[0] = restored_ref[2 - upper].astype(jnp.bfloat16)


def copy_kernel(meta, array_ref, *refs):
    refs[-1][...] = array_ref[...]


def join_kernel(meta, first_ref, second_ref, *refs):
    out_ref = refs[-1]
    count = first_ref.shape[0]
    out_ref[:count] = first_ref[...]
    out_ref[count:] = second_ref[...]


def join_two_kernel(
    meta, first_ref, second_ref, first_state_ref, second_state_ref, key_value_ref, four_ref, *refs
):
    out_ref, two_ref = refs[-2:]
    rows = first_ref.shape[1]
    for i, (parcel, state) in enumerate(((first_ref, first_state_ref), (second_ref, second_state_ref))):
        out_ref[i, :rows, :] = parcel[0]
        out_ref[i, rows:, :] = state[0]
    two_ref[...] = jnp.where(meta.place // 2 % 2 == 0, key_value_ref[...], four_ref[...])


def far_place(distance, bits):
    place = distance * 0
    for k in range(bits):
        place = place + ((distance // (1 << k)) % 2) * (1 << (bits - 1 - k))
    return place


def combine_kernel(local, meta, keep_ref, got_ref, *refs):
    out_ref = refs[-1]
    even = meta.even
    second = (meta.place // 2 * 2 + 1) * TOK
    closes = meta.start_of(meta.session_at(second + TOK - 1)) >= second
    width = local * N
    for chip in range(keep_ref.shape[0]):
        keep = factors_of(keep_ref[chip, width:, :], local)
        got = factors_of(got_ref[chip, width:, :], local)
        f0, f1 = jnp.where(even, keep, got), jnp.where(even, got, keep)
        out_ref[chip, width:, :] = factor_rows(jnp.where(closes, f1, f0 * f1))
        carry = jnp.where(closes, 0.0, f1)
        for k in range(local):
            rows = slice(k * N, (k + 1) * N)
            keep = keep_ref[chip, rows, :].astype(jnp.float32)
            got = got_ref[chip, rows, :].astype(jnp.float32)
            s0, s1 = jnp.where(even, keep, got), jnp.where(even, got, keep)
            out_ref[chip, rows, :] = (carry[k : k + 1] * s0 + s1).astype(jnp.bfloat16)


def recurrence_kernel(local, meta, got_ref, restored_ref, *refs):
    out_ref, token_ref = refs[-2:]
    token_ref[...] = jnp.zeros_like(token_ref)
    width = local * N
    span = 2 * TOK
    state = [jnp.zeros((N, P_SIZE), jnp.float32) for _ in range(local)]
    for c in range(got_ref.shape[0]):
        first = c * span
        opening = meta.session_at(first)
        closing = meta.session_at(first + span - 1)
        opens = meta.start_of(opening) >= first
        closes = meta.start_of(closing) >= first
        factor = factors_of(got_ref[c, width:, :], local)
        for k in range(local):
            rows = slice(k * N, (k + 1) * N)
            entering = jnp.where(opens, restored_ref[opening, rows, :], state[k])
            out_ref[c, rows, :] = entering.astype(jnp.bfloat16)
            source = jnp.where(closes, restored_ref[closing, rows, :], state[k])
            state[k] = factor[k : k + 1] * source + got_ref[c, rows, :].astype(jnp.float32)


def intra_kernel(meta, skip, x_ref, dl_ref, step_ref, write_ref, read_ref, _, out_ref, token_ref, run_s, step_s):
    step = pl.program_id(0)

    @pl.when(step == 0)
    def _():
        _, running = running_rows(dl_ref)
        run_s[...] = running
        step_s[...] = step_ref[...].astype(jnp.float32)

    token_ref[...] = jnp.zeros_like(token_ref)
    heads = pl.ds(pl.multiple_of(step * PAIR, PAIR), PAIR)
    running = run_s[heads, :]
    sizes = step_s[heads, :]
    columns = running.T
    r = meta.last_start()
    t = lax.broadcasted_iota(jnp.int32, (TOK, TOK), 0)
    u = lax.broadcasted_iota(jnp.int32, (TOK, TOK), 1)
    causal = (u <= t) & ((u >= r) | (t < r))
    for group in range(2):
        part = slice(group * N, (group + 1) * N)
        products = lax.dot_general(
            read_ref[:, part], write_ref[:, part], (((1,), (1,)), ((), ())),
            preferred_element_type=jnp.float32,
        )
        products = jnp.where(causal, products, 0.0)
        for k in range(group * HEADS_PER, (group + 1) * HEADS_PER):
            difference = columns[:, k : k + 1] - running[k : k + 1]
            decay = jnp.exp(jnp.minimum(difference, 0.0))
            mixing = (products * decay * sizes[k : k + 1]).astype(jnp.bfloat16)
            place = slice(k * P_SIZE, (k + 1) * P_SIZE)
            x = x_ref[:, place]
            mixed = jnp.dot(mixing, x, preferred_element_type=jnp.float32)
            out_ref[:, place] = mixed + skip[step * PAIR + k] * x.astype(jnp.float32)


def intra(meta, skip, x, rates, steps, writes, reads, idle):
    return pl.pallas_call(
        scalars(intra_kernel),
        out_shape=[jax.ShapeDtypeStruct((TOK, H * P_SIZE), jnp.float32), TOKEN],
        grid_spec=pltpu.PrefetchScalarGridSpec(
            num_scalar_prefetch=2,
            grid=(STEPS,),
            in_specs=[
                pl.BlockSpec((TOK, PAIR * P_SIZE), lambda i, *m: (0, i)),
                pl.BlockSpec((H, TOK), lambda i, *m: (0, 0)),
                pl.BlockSpec((H, TOK), lambda i, *m: (0, 0)),
                pl.BlockSpec((TOK, 2 * N), lambda i, *m: (0, i)),
                pl.BlockSpec((TOK, 2 * N), lambda i, *m: (0, i)),
                pl.BlockSpec(memory_space=pl.ANY),
            ],
            out_specs=[
                pl.BlockSpec((TOK, PAIR * P_SIZE), lambda i, *m: (0, i)),
                pl.BlockSpec(TOKEN.shape, lambda i, *m: (0, 0)),
            ],
            scratch_shapes=[
                pltpu.VMEM((H, TOK), jnp.float32),
                pltpu.VMEM((H, TOK), jnp.float32),
            ],
        ),
        compiler_params=params(),
        cost_estimate=LONG,
        name="intra",
    )(meta, skip, x, rates, steps, writes, reads, idle)


def finish_kernel(
    local, meta, part_ref, dl_ref, read_ref, own_ref, other_ref, low_ref, high_ref, *refs,
):
    pieces, (out_ref, factor_s) = refs[:8], refs[-2:]
    bits = pieces[0].shape[0].bit_length() - 1
    step = pl.program_id(0)
    even = meta.even
    r = meta.last_start()
    first = meta.place // 2 * 2 * TOK
    second = first + TOK
    start = meta.start_of(meta.session_at(second + TOK - 1))
    closes = (start > first) & (start < second)
    opens = start == second
    width = local * N

    @pl.when(step == 0)
    def _():
        rates, running = running_rows(dl_ref)
        lane = lax.broadcasted_iota(jnp.int32, (H, TOK), 1)
        base = jnp.sum(jnp.where(lane < r, rates, 0.0), axis=1, keepdims=True)
        factor_s[...] = jnp.exp(jnp.minimum(running - jnp.where(lane >= r, base, 0.0), 0.0))

    factor = factor_s[pl.ds(pl.multiple_of(step * PAIR, PAIR), PAIR), :].T
    token = lax.broadcasted_iota(jnp.int32, (TOK, N), 0)
    resumed = (token >= r) & (r > 0)
    decays = [[factors_of(ref[chip, width:, :], local) for ref in (low_ref, high_ref)] for chip in range(own_ref.shape[0])]
    for group in range(2):
        reads = read_ref[:, group * N : (group + 1) * N].astype(jnp.float32)
        left = jnp.where(resumed, 0.0, reads)
        right = jnp.where(resumed, reads, 0.0)
        reads = jnp.concatenate([left, right], axis=1).astype(jnp.bfloat16)
        for k in range(group * HEADS_PER, (group + 1) * HEADS_PER):
            chip, half, head = k // (2 * local), k // local % 2, k % local
            rows = slice(head * N, (head + 1) * N)
            own = even if half == 0 else jnp.logical_not(even)
            entering = jnp.where(own, own_ref[chip, rows, :], other_ref[chip, rows, :]).astype(jnp.float32)
            distance = (step * own_ref.shape[0] + chip) ^ (meta.place // 2)
            far = far_place(distance // 4, bits)
            near, low_bit = distance % 2 == 0, distance // 2 % 2 == 0
            found = [piece[far, rows, :] for piece in pieces]
            found = [jnp.where(low_bit, found[i], found[i + 1]) for i in range(0, 8, 2)]
            restored = jnp.where(own, jnp.where(near, found[0], found[1]), jnp.where(near, found[2], found[3]))
            whole_state = restored.astype(jnp.float32)
            summary = (low_ref, high_ref)[half][chip, rows, :].astype(jnp.float32)
            middle = decays[chip][half][head : head + 1] * jnp.where(closes, whole_state, entering) + summary
            middle = jnp.where(opens, whole_state, middle)
            entering = jnp.where(even, entering, middle).astype(jnp.bfloat16)
            states = jnp.concatenate([entering, restored], axis=0)
            carried = jnp.dot(reads, states, preferred_element_type=jnp.float32)
            place = slice(k * P_SIZE, (k + 1) * P_SIZE)
            out_ref[:, place] = (part_ref[:, place] + factor[:, k : k + 1] * carried).astype(jnp.bfloat16)


def finish(meta, part, rates, reads, own, other, low, high, pieces, local):
    chips = PAIR // (2 * local)
    count, length, _ = pieces[0].shape
    resumed = pl.BlockSpec((count, local * N, P_SIZE), lambda i, *m: (0, length // (local * N) - 1, 0))
    states = pl.BlockSpec((chips, local * N, P_SIZE), lambda i, *m: (i, 0, 0))
    stretch = pl.BlockSpec((chips, local * N + EXTRA, P_SIZE), lambda i, *m: (i, 0, 0))
    return pl.pallas_call(
        scalars(finish_kernel, local),
        out_shape=jax.ShapeDtypeStruct((TOK, H * P_SIZE), jnp.bfloat16),
        grid_spec=pltpu.PrefetchScalarGridSpec(
            num_scalar_prefetch=1,
            grid=(STEPS,),
            in_specs=[
                pl.BlockSpec((TOK, PAIR * P_SIZE), lambda i, *m: (0, i)),
                pl.BlockSpec((H, TOK), lambda i, *m: (0, 0)),
                pl.BlockSpec((TOK, 2 * N), lambda i, *m: (0, i)),
                states,
                states,
                stretch,
                stretch,
            ]
            + [resumed] * 8,
            out_specs=pl.BlockSpec((TOK, PAIR * P_SIZE), lambda i, *m: (0, i)),
            scratch_shapes=[pltpu.VMEM((H, TOK), jnp.float32)],
        ),
        compiler_params=params(),
        cost_estimate=LONG,
        name="finish",
    )(meta, part, rates, reads, own, other, low, high, *pieces)


def attend_kernel(
    meta, q_ref, four, two, now, four_across, two_across, now_across, *refs,
):
    history_refs, (sk_ref, sv_ref), (out_ref, token_ref, key_s, value_s) = refs[:32], refs[32:34], refs[-4:]
    factor = 1.0 / math.sqrt(HD)
    first = meta.place * TOK
    r = meta.last_start()
    opening = meta.session_at(first)
    closing = meta.session_at(first + TOK - 1)
    even = meta.even

    def band(number, part):
        if number == 0:
            return four[part]
        if number == 1:
            return jnp.where(even, four_across[part], two_across[part])
        if number == 2:
            return two[part]
        if number == 3:
            return jnp.where(even, two_across[part], now_across[part])
        return now[part]

    token_ref[...] = jnp.zeros_like(token_ref)

    def sinks(ref, session):
        rows = ref[session].astype(jnp.float32)
        spare = jnp.zeros((COLUMNS - SPAN - SINKS, HD), jnp.float32)
        return jnp.concatenate([rows, spare], axis=0).astype(jnp.bfloat16)

    length = (REACH + 1) * TOK

    def one_session(session, key_refs, value_refs, resuming, needed):
        start = meta.start_of(session) - first + WINDOW
        oldest = start - WINDOW + jnp.maximum(SINKS + WINDOW - meta.history(session), 0)

        @pl.when(needed & (start > 0))
        def _():
            row = lax.broadcasted_iota(jnp.int32, (length, WINDOW), 0)
            chips, share, _ = key_refs[0].shape
            index = lax.broadcasted_iota(jnp.int32, (1, WINDOW), 1)
            piece, index = index // (WINDOW // 8), index % (WINDOW // 8)
            near, row_in = index // share, index % share
            far = far_place(near, chips.bit_length() - 1)
            device = meta.place ^ (piece // 4 + piece // 2 % 2 * 2 + piece % 2 * 4 + far * 8)
            place = device * share + row_in
            moved = (row == place + start - WINDOW).astype(jnp.bfloat16)
            part = (WINDOW // 8, HD)
            keys = jnp.concatenate([ref[...].reshape(part) for ref in key_refs], axis=0)
            values = jnp.concatenate([ref[...].reshape(part) for ref in value_refs], axis=0)
            history = jnp.dot(
                moved, jnp.concatenate([keys, values], axis=1), preferred_element_type=jnp.float32
            )
            for i in range(REACH + 1):
                rows = slice(i * TOK, (i + 1) * TOK)
                index = lax.broadcasted_iota(jnp.int32, (TOK, HD), 0) + i * TOK
                turn = index >= start
                key_s[rows, :] = jnp.where(
                    turn, band(i, 0).astype(jnp.float32), history[rows, :HD]
                ).astype(jnp.bfloat16)
                value_s[rows, :] = jnp.where(
                    turn, band(i, 1).astype(jnp.float32), history[rows, HD:]
                ).astype(jnp.bfloat16)

        @pl.when(needed & (start <= 0))
        def _():
            for i in range(REACH + 1):
                rows = slice(i * TOK, (i + 1) * TOK)
                key_s[rows, :] = band(i, 0)
                value_s[rows, :] = band(i, 1)

        for b in range(TOK // BLOCK):
            inside = (b * BLOCK + BLOCK > r) if resuming else (b * BLOCK < r)

            @pl.when(needed & inside)
            def _():
                rows = slice(b * BLOCK, b * BLOCK + SPAN)
                keys = jnp.concatenate([key_s[rows, :], sinks(sk_ref, session)], axis=0)
                values = jnp.concatenate([value_s[rows, :], sinks(sv_ref, session)], axis=0)
                tokens = slice(b * BLOCK, (b + 1) * BLOCK)
                queries = jnp.concatenate(
                    [q_ref[tokens, g * HD : (g + 1) * HD] for g in range(QH // KVH)], axis=0
                )
                scores = lax.dot_general(
                    keys, queries, (((1,), (1,)), ((), ())), preferred_element_type=jnp.float32
                )
                column = lax.broadcasted_iota(jnp.int32, (COLUMNS, 2 * BLOCK), 0)
                token = lax.broadcasted_iota(jnp.int32, (COLUMNS, 2 * BLOCK), 1) % BLOCK
                seen = (column > token) & (column <= token + WINDOW) & (column >= oldest - b * BLOCK)
                seen = (seen & (column < SPAN)) | ((column >= SPAN) & (column < SPAN + SINKS))
                bias = jnp.where(seen, 0.0, NEG)
                weights, shares = [], []
                for j in range(QH // KVH // 2):
                    score = scores[:, j * 2 * BLOCK : (j + 1) * 2 * BLOCK] * factor + bias
                    weight = jnp.exp(score - jnp.max(score, axis=0, keepdims=True))
                    shares.append(1.0 / jnp.sum(weight, axis=0, keepdims=True))
                    weights.append(weight.astype(jnp.bfloat16))
                mixed = lax.dot_general(
                    values, jnp.concatenate(weights, axis=1), (((0,), (0,)), ((), ())),
                    preferred_element_type=jnp.float32,
                )
                for j in range(QH // KVH // 2):
                    pair = (mixed[:, j * 2 * BLOCK : (j + 1) * 2 * BLOCK] * shares[j]).T
                    for g in range(2):
                        result = pair[g * BLOCK : (g + 1) * BLOCK]
                        lanes = slice((2 * j + g) * HD, (2 * j + g + 1) * HD)
                        if resuming:
                            index = lax.broadcasted_iota(jnp.int32, (BLOCK, HD), 0) + b * BLOCK
                            before = out_ref[tokens, lanes].astype(jnp.float32)
                            result = jnp.where(index >= r, result, before)
                        out_ref[tokens, lanes] = result.astype(jnp.bfloat16)

    one_session(opening, history_refs[0:8], history_refs[8:16], False, r > 0)
    one_session(closing, history_refs[16:24], history_refs[24:], True, r >= 0)


def attend(meta, queries, bands, pieces, half, sink_keys, sink_values, idle):
    chips = pieces[0].shape[0]
    share = WINDOW // (8 * chips)
    lanes = QH // KVH * HD

    def history_spec(which, last):
        def index(j, *m):
            known = Scalars(*m)
            session = known.session_at(known.place * TOK + (TOK - 1 if last else 0))
            session = session - (known.place >= half).astype(jnp.int32)
            return (0, (which * 2 + session) * KVH + j, 0)

        return pl.BlockSpec((chips, share, HD), index)

    pad = SEQS, SINKS, HD
    return pl.pallas_call(
        scalars(attend_kernel),
        out_shape=[jax.ShapeDtypeStruct((TOK, QH * HD), jnp.bfloat16), TOKEN],
        grid_spec=pltpu.PrefetchScalarGridSpec(
            num_scalar_prefetch=1,
            grid=(KVH,),
            in_specs=[pl.BlockSpec((TOK, lanes), lambda j, *m: (0, j))]
            + [pl.BlockSpec((2, TOK, HD), lambda j, *m: (0, 0, j))] * len(bands)
            + [history_spec(0, False)] * 8
            + [history_spec(1, False)] * 8
            + [history_spec(0, True)] * 8
            + [history_spec(1, True)] * 8
            + [pl.BlockSpec(pad, lambda j, *m: (0, 0, j))] * 2
            + [idle_spec(a) for a in idle],
            out_specs=[
                pl.BlockSpec((TOK, lanes), lambda j, *m: (0, j)),
                pl.BlockSpec(TOKEN.shape, lambda j, *m: (0, 0)),
            ],
            scratch_shapes=[
                pltpu.VMEM(((REACH + 1) * TOK, HD), jnp.bfloat16),
                pltpu.VMEM(((REACH + 1) * TOK, HD), jnp.bfloat16),
            ],
        ),
        compiler_params=params(),
        cost_estimate=SHORT,
        name="attend",
    )(
        meta, queries, *bands, *pieces, *pieces, *pieces, *pieces, sink_keys, sink_values, *idle
    )


def shifted(block, axis, distance):
    devices = range(lax.axis_size(axis))
    return lax.ppermute(block, axis, [(i - distance, i) for i in devices if i - distance in devices])


def shards(
    mamba_input,
    step_size,
    decay_log,
    state_write,
    state_read,
    skip_gain,
    saved_states,
    home_slot,
    turn_lengths,
    history_lengths,
    queries,
    turn_keys,
    turn_values,
    cache_keys,
    cache_values,
    sink_keys,
    sink_values,
):
    place = lax.axis_index("ctx")
    group = lax.axis_index("sess")
    groups = lax.axis_size("sess")
    devices = lax.axis_size("ctx")
    local = saved_states.shape[2]
    width = local * N
    chips = devices // 2
    same_core = [list(range(core, devices, 2)) for core in range(2)]
    meta = jnp.concatenate(
        [jnp.stack([place, group]).astype(jnp.int32), turn_lengths[0], history_lengths[0], home_slot]
    )
    x, rates, steps = mamba_input[0], decay_log[0].T, step_size[0].T
    writes, reads = state_write[0], state_read[0]
    def apart(block, distance):
        return lax.ppermute(block, "ctx", [(i, i ^ distance) for i in range(devices)])

    def exchanged(block):
        return lax.all_to_all(block, "ctx", 0, 0, axis_index_groups=same_core, tiled=True)

    stored = [saved_states[0]]
    for j in range(1, groups):
        route = [((i + j) % groups, i) for i in range(groups)]
        stored.append(lax.ppermute(saved_states[0], "sess", route))
    stored = [block.reshape(SEQS, local, P_SIZE, N) for block in stored]

    parcel = (1, 4 * KVH * cache_keys.shape[2], HD)
    band = (2, TOK, KVH * HD)
    near, away, key_value = whole(
        scalars(pack_kernel, devices // 2),
        "pack",
        meta,
        [cache_keys[0], cache_values[0], turn_keys[0], turn_values[0]],
        [(parcel, jnp.bfloat16), (parcel, jnp.bfloat16), (band, jnp.bfloat16)],
        mib=60,
    )
    moved = apart(away, devices // 2)
    four = shifted(key_value, "ctx", 4)

    keep, send = summaries(meta, x, rates, steps, writes, local, away)
    got = apart(send, 1)

    one = (1, width, P_SIZE)
    home, away, restored = whole(
        scalars(restore_kernel, local, devices // 2, groups),
        "restore",
        meta,
        stored,
        [(one, jnp.bfloat16), (one, jnp.bfloat16), ((SEQS, width, P_SIZE), jnp.float32)],
        idle=[send],
    )
    away = apart(away, devices // 2)
    near, two = whole(
        scalars(join_two_kernel),
        "join_two",
        meta,
        [near, moved, home, away, key_value, four],
        [((2, parcel[1] + width, HD), jnp.bfloat16), (band, jnp.bfloat16)],
        idle=[got],
    )
    distance = devices // 4
    while distance > 4:
        joined = (2 * near.shape[0], *near.shape[1:])
        [near] = whole(scalars(join_kernel), "join", meta, [near, apart(near, distance)], [(joined, jnp.bfloat16)])
        distance //= 2
    moved = apart(near, 4)
    two = apart(two, 2)
    beside = apart(near, 2)
    [chip] = whole(
        scalars(combine_kernel, local),
        "combine",
        meta,
        [keep, got],
        [(keep.shape, jnp.bfloat16)],
        idle=[near],
    )
    total = exchanged(chip)
    part, token = intra(meta, skip_gain, x, rates, steps, writes, reads, chip)
    pieces = [near, moved, beside, apart(moved, 2)]
    bands = [four, two, key_value]
    across = [apart(block, 1) for block in bands]
    low = apart(keep, 1)

    entering, after = whole(
        scalars(recurrence_kernel, local),
        "recurrence",
        meta,
        [total, restored],
        [((chips, width, P_SIZE), jnp.bfloat16), (TOKEN.shape, TOKEN.dtype)],
        idle=[token, low, *across, *pieces],
    )
    entering = exchanged(entering)
    pieces += [apart(piece, 1) for piece in pieces]
    attended, token = attend(
        meta, queries[0], bands + across, pieces, devices // 2, sink_keys[0], sink_values[0], [after]
    )
    [entering] = whole(
        scalars(copy_kernel), "copy", meta, [entering], [((chips, width, P_SIZE), jnp.bfloat16)], idle=[token]
    )
    other = apart(entering, 1)
    mixed = finish(meta, part, rates, reads, entering, other, low, got, pieces, local)
    return mixed[None], attended[None]


def solution(mesh):
    token = P("sess", "ctx", None)
    return jax.shard_map(
        shards,
        mesh=mesh,
        in_specs=(
            token,
            token,
            token,
            token,
            token,
            P(),
            P("sess", None, "ctx", None),
            P(),
            P("sess", None),
            P("sess", None),
            token,
            token,
            token,
            P("sess", None, "ctx", None),
            P("sess", None, "ctx", None),
            P("sess", None, None, None),
            P("sess", None, None, None),
        ),
        out_specs=(token, token),
        check_vma=False,
    )
```

```python
import math

import jax
import jax.numpy as jnp
from jax import lax
from jax.experimental import pallas as pl
from jax.experimental.pallas import tpu as pltpu
from jax.sharding import PartitionSpec as P

REACH = 4
SEQS = 3
SINKS = 4
H = 64
P_SIZE = 128
N = 64
G = 8
QH = 32
KVH = 4
HD = 128
WINDOW = 512
TOK = 128

HEADS_PER = H // G
PAIR = 2 * HEADS_PER
STEPS = H // PAIR
EXTRA = 16
BLOCK = 64
SPAN = WINDOW + BLOCK
COLUMNS = SPAN + 64
NEG = -1e30
TOKEN = jax.ShapeDtypeStruct((8, 128), jnp.float32)
SHORT = pl.CostEstimate(flops=1024, bytes_accessed=1024, transcendentals=0)
LONG = pl.CostEstimate(flops=1 << 35, bytes_accessed=1 << 20, transcendentals=0)


class Scalars:
    def __init__(self, ids):
        self.place, self.group = ids[0], ids[1]
        self.one = ids[2]
        self.two = ids[2] + ids[3]
        self.ids = ids
        self.even = self.place % 2 == 0

    def history(self, session):
        return self.ids[2 + SEQS + session]

    def home(self, number):
        return self.ids[2 + 2 * SEQS + number]

    def session_at(self, position):
        return (position >= self.one).astype(jnp.int32) + (position >= self.two).astype(jnp.int32)

    def start_of(self, session):
        return jnp.where(session == 0, 0, jnp.where(session == 1, self.one, self.two))

    def last_start(self):
        first = self.place * TOK
        return jnp.maximum(self.start_of(self.session_at(first + TOK - 1)) - first, 0)


def scalars(kernel, *options):
    def body(ids, *refs):
        kernel(*options, Scalars(ids), *refs)

    return body


def params(mib=60):
    return pltpu.CompilerParams(vmem_limit_bytes=mib * 1024 * 1024)


def running_rows(dl_ref):
    k = lax.broadcasted_iota(jnp.int32, (TOK, TOK), 0)
    u = lax.broadcasted_iota(jnp.int32, (TOK, TOK), 1)
    upto = (k <= u).astype(jnp.bfloat16)
    running = jnp.dot(dl_ref[...], upto, preferred_element_type=jnp.float32)
    return dl_ref[...].astype(jnp.float32), running


def summary_kernel(
    local, meta, x_ref, dl_ref, step_ref, write_ref, _, keep_ref, send_ref, coef_s, factor_s, write_s
):
    step = pl.program_id(0)

    @pl.when(step == 0)
    def _():
        rates, running = running_rows(dl_ref)
        steps = step_ref[...].astype(jnp.float32)
        r = meta.last_start()
        lane = lax.broadcasted_iota(jnp.int32, (H, TOK), 1)
        last = running[:, TOK - 1 :]
        base = jnp.sum(jnp.where(lane < r, rates, 0.0), axis=1, keepdims=True)
        coef_s[...] = jnp.where(lane >= r, jnp.exp(last - running) * steps, 0.0)
        factor_s[...] = jnp.broadcast_to(jnp.exp(last - base), (H, TOK))
        write_s[...] = write_ref[...].astype(jnp.float32).T

    even = meta.even
    coef = coef_s[pl.ds(pl.multiple_of(step * PAIR, PAIR), PAIR), :]
    factor = factor_s[pl.ds(pl.multiple_of(step * PAIR, PAIR), PAIR), :]
    writes = write_s[pl.ds(pl.multiple_of(step * 2 * N, 2 * N), 2 * N), :]

    def summary(k):
        group = k // HEADS_PER
        loading = (writes[group * N : (group + 1) * N] * coef[k : k + 1]).astype(jnp.bfloat16)
        return jnp.dot(
            loading, x_ref[:, k * P_SIZE : (k + 1) * P_SIZE], preferred_element_type=jnp.float32
        )

    for chip in range(PAIR // (2 * local)):
        low, high = 2 * local * chip, 2 * local * chip + local
        for k in range(local):
            first, second = summary(low + k), summary(high + k)
            rows = slice(k * N, (k + 1) * N)
            keep_ref[chip, rows, :] = jnp.where(even, first, second).astype(jnp.bfloat16)
            send_ref[chip, rows, :] = jnp.where(even, second, first).astype(jnp.bfloat16)
        first, second = factor[low : low + local], factor[high : high + local]
        keep_ref[chip, local * N :, :] = factor_rows(jnp.where(even, first, second))
        send_ref[chip, local * N :, :] = factor_rows(jnp.where(even, second, first))


def factor_rows(rows):
    high = rows.astype(jnp.bfloat16).astype(jnp.float32)
    parts = [high, rows - high]
    if EXTRA > 2 * rows.shape[0]:
        parts.append(jnp.zeros((EXTRA - 2 * rows.shape[0], TOK), jnp.float32))
    return jnp.concatenate(parts, axis=0).astype(jnp.bfloat16)


def factors_of(block, local):
    block = block.astype(jnp.float32)
    return block[:local] + block[local : 2 * local]


def summaries(meta, x, rates, steps, writes, local, idle):
    chips = H // (2 * local)
    rows = local * N + EXTRA
    shape = jax.ShapeDtypeStruct((chips, rows, P_SIZE), jnp.bfloat16)
    spec = pl.BlockSpec((PAIR // (2 * local), rows, P_SIZE), lambda i, *m: (i, 0, 0))
    return pl.pallas_call(
        scalars(summary_kernel, local),
        out_shape=[shape, shape],
        grid_spec=pltpu.PrefetchScalarGridSpec(
            num_scalar_prefetch=1,
            grid=(STEPS,),
            in_specs=[
                pl.BlockSpec((TOK, PAIR * P_SIZE), lambda i, *m: (0, i)),
                pl.BlockSpec((H, TOK), lambda i, *m: (0, 0)),
                pl.BlockSpec((H, TOK), lambda i, *m: (0, 0)),
                pl.BlockSpec((TOK, G * N), lambda i, *m: (0, 0)),
                pl.BlockSpec(memory_space=pl.ANY),
            ],
            out_specs=[spec, spec],
            scratch_shapes=[
                pltpu.VMEM((H, TOK), jnp.float32),
                pltpu.VMEM((H, TOK), jnp.float32),
                pltpu.VMEM((G * N, TOK), jnp.float32),
            ],
        ),
        compiler_params=params(),
        cost_estimate=LONG,
        name="summaries",
    )(meta, x, rates, steps, writes, idle)


def idle_spec(array):
    return pl.BlockSpec(memory_space=pl.ANY)


def whole(kernel, name, meta, arrays, shapes, idle=(), mib=16, scratch=()):
    def spec(shape):
        return pl.BlockSpec(shape, lambda i, *m: (0,) * len(shape))

    return pl.pallas_call(
        kernel,
        out_shape=[jax.ShapeDtypeStruct(s, t) for s, t in shapes],
        grid_spec=pltpu.PrefetchScalarGridSpec(
            num_scalar_prefetch=1,
            grid=(1,),
            in_specs=[spec(a.shape) for a in arrays] + [idle_spec(a) for a in idle],
            out_specs=[spec(s) for s, _ in shapes],
            scratch_shapes=scratch,
        ),
        compiler_params=params(mib),
        cost_estimate=LONG,
        name=name,
    )(meta, *arrays, *idle)


def pack_kernel(half, meta, keys_ref, values_ref, turn_keys_ref, turn_values_ref, home_ref, away_ref, band_ref):
    band_ref[0] = turn_keys_ref[...]
    band_ref[1] = turn_values_ref[...]
    rows = keys_ref.shape[1]
    upper = (meta.place >= half).astype(jnp.int32)
    for out_ref, first in ((home_ref, upper), (away_ref, 1 - upper)):
        for which, ref in enumerate((keys_ref, values_ref)):
            for s in range(2):
                for j in range(KVH):
                    place = ((which * 2 + s) * KVH + j) * rows
                    out_ref[0, place : place + rows, :] = ref[first + s, :, j * HD : (j + 1) * HD]


def restore_kernel(local, half, groups, meta, *refs):
    stored, (home_ref, away_ref, restored_ref) = refs[:groups], refs[-3:]
    for s in range(SEQS):
        slot = meta.home(meta.group * SEQS + s)
        source = (slot // SEQS - meta.group + groups) % groups
        for k in range(local):
            state = stored[0][slot % SEQS, k]
            for j in range(1, groups):
                state = jnp.where(source == j, stored[j][slot % SEQS, k], state)
            restored_ref[s, k * N : (k + 1) * N, :] = state.T
    upper = (meta.place >= half).astype(jnp.int32)
    home_ref[0] = restored_ref[upper + 1].astype(jnp.bfloat16)
    away_ref[0] = restored_ref[2 - upper].astype(jnp.bfloat16)


def copy_kernel(meta, array_ref, *refs):
    refs[-1][...] = array_ref[...]


def join_kernel(meta, first_ref, second_ref, *refs):
    out_ref = refs[-1]
    count = first_ref.shape[0]
    out_ref[:count] = first_ref[...]
    out_ref[count:] = second_ref[...]


def parcels_kernel(meta, first_ref, second_ref, first_state_ref, second_state_ref, *refs):
    out_ref = refs[-1]
    rows = first_ref.shape[1]
    for i, (parcel, state) in enumerate(((first_ref, first_state_ref), (second_ref, second_state_ref))):
        out_ref[i, :rows, :] = parcel[0]
        out_ref[i, rows:, :] = state[0]


def two_kernel(meta, key_value_ref, four_ref, *refs):
    refs[-1][...] = jnp.where(meta.place // 2 % 2 == 0, key_value_ref[...], four_ref[...])


def far_place(distance, bits):
    place = distance * 0
    for k in range(bits):
        place = place + ((distance // (1 << k)) % 2) * (1 << (bits - 1 - k))
    return place


def combine_kernel(local, meta, keep_ref, got_ref, *refs):
    out_ref = refs[-1]
    even = meta.even
    second = (meta.place // 2 * 2 + 1) * TOK
    closes = meta.start_of(meta.session_at(second + TOK - 1)) >= second
    width = local * N
    for chip in range(keep_ref.shape[0]):
        keep = factors_of(keep_ref[chip, width:, :], local)
        got = factors_of(got_ref[chip, width:, :], local)
        f0, f1 = jnp.where(even, keep, got), jnp.where(even, got, keep)
        out_ref[chip, width:, :] = factor_rows(jnp.where(closes, f1, f0 * f1))
        carry = jnp.where(closes, 0.0, f1)
        for k in range(local):
            rows = slice(k * N, (k + 1) * N)
            keep = keep_ref[chip, rows, :].astype(jnp.float32)
            got = got_ref[chip, rows, :].astype(jnp.float32)
            s0, s1 = jnp.where(even, keep, got), jnp.where(even, got, keep)
            out_ref[chip, rows, :] = (carry[k : k + 1] * s0 + s1).astype(jnp.bfloat16)


def recurrence_kernel(local, meta, got_ref, restored_ref, *refs):
    out_ref, token_ref = refs[-2:]
    token_ref[...] = jnp.zeros_like(token_ref)
    width = local * N
    span = 2 * TOK
    state = [jnp.zeros((N, P_SIZE), jnp.float32) for _ in range(local)]
    for c in range(got_ref.shape[0]):
        first = c * span
        opening = meta.session_at(first)
        closing = meta.session_at(first + span - 1)
        opens = meta.start_of(opening) >= first
        closes = meta.start_of(closing) >= first
        factor = factors_of(got_ref[c, width:, :], local)
        for k in range(local):
            rows = slice(k * N, (k + 1) * N)
            entering = jnp.where(opens, restored_ref[opening, rows, :], state[k])
            out_ref[c, rows, :] = entering.astype(jnp.bfloat16)
            source = jnp.where(closes, restored_ref[closing, rows, :], state[k])
            state[k] = factor[k : k + 1] * source + got_ref[c, rows, :].astype(jnp.float32)


def intra_kernel(meta, skip, x_ref, dl_ref, step_ref, write_ref, read_ref, _, out_ref, token_ref, run_s, step_s):
    step = pl.program_id(0)

    @pl.when(step == 0)
    def _():
        _, running = running_rows(dl_ref)
        run_s[...] = running
        step_s[...] = step_ref[...].astype(jnp.float32)

    token_ref[...] = jnp.zeros_like(token_ref)
    heads = pl.ds(pl.multiple_of(step * PAIR, PAIR), PAIR)
    running = run_s[heads, :]
    sizes = step_s[heads, :]
    columns = running.T
    r = meta.last_start()
    t = lax.broadcasted_iota(jnp.int32, (TOK, TOK), 0)
    u = lax.broadcasted_iota(jnp.int32, (TOK, TOK), 1)
    causal = (u <= t) & ((u >= r) | (t < r))
    for group in range(2):
        part = slice(group * N, (group + 1) * N)
        products = lax.dot_general(
            read_ref[:, part], write_ref[:, part], (((1,), (1,)), ((), ())),
            preferred_element_type=jnp.float32,
        )
        products = jnp.where(causal, products, 0.0)
        for k in range(group * HEADS_PER, (group + 1) * HEADS_PER):
            difference = columns[:, k : k + 1] - running[k : k + 1]
            decay = jnp.exp(jnp.minimum(difference, 0.0))
            mixing = (products * decay * sizes[k : k + 1]).astype(jnp.bfloat16)
            place = slice(k * P_SIZE, (k + 1) * P_SIZE)
            x = x_ref[:, place]
            mixed = jnp.dot(mixing, x, preferred_element_type=jnp.float32)
            out_ref[:, place] = mixed + skip[step * PAIR + k] * x.astype(jnp.float32)


def intra(meta, skip, x, rates, steps, writes, reads, idle):
    return pl.pallas_call(
        scalars(intra_kernel),
        out_shape=[jax.ShapeDtypeStruct((TOK, H * P_SIZE), jnp.float32), TOKEN],
        grid_spec=pltpu.PrefetchScalarGridSpec(
            num_scalar_prefetch=2,
            grid=(STEPS,),
            in_specs=[
                pl.BlockSpec((TOK, PAIR * P_SIZE), lambda i, *m: (0, i)),
                pl.BlockSpec((H, TOK), lambda i, *m: (0, 0)),
                pl.BlockSpec((H, TOK), lambda i, *m: (0, 0)),
                pl.BlockSpec((TOK, 2 * N), lambda i, *m: (0, i)),
                pl.BlockSpec((TOK, 2 * N), lambda i, *m: (0, i)),
                pl.BlockSpec(memory_space=pl.ANY),
            ],
            out_specs=[
                pl.BlockSpec((TOK, PAIR * P_SIZE), lambda i, *m: (0, i)),
                pl.BlockSpec(TOKEN.shape, lambda i, *m: (0, 0)),
            ],
            scratch_shapes=[
                pltpu.VMEM((H, TOK), jnp.float32),
                pltpu.VMEM((H, TOK), jnp.float32),
            ],
        ),
        compiler_params=params(),
        cost_estimate=LONG,
        name="intra",
    )(meta, skip, x, rates, steps, writes, reads, idle)


def finish_kernel(
    local, meta, part_ref, dl_ref, read_ref, own_ref, other_ref, low_ref, high_ref, *refs,
):
    pieces, (out_ref, factor_s) = refs[:8], refs[-2:]
    bits = pieces[0].shape[0].bit_length() - 1
    step = pl.program_id(0)
    even = meta.even
    r = meta.last_start()
    first = meta.place // 2 * 2 * TOK
    second = first + TOK
    start = meta.start_of(meta.session_at(second + TOK - 1))
    closes = (start > first) & (start < second)
    opens = start == second
    width = local * N

    @pl.when(step == 0)
    def _():
        rates, running = running_rows(dl_ref)
        lane = lax.broadcasted_iota(jnp.int32, (H, TOK), 1)
        base = jnp.sum(jnp.where(lane < r, rates, 0.0), axis=1, keepdims=True)
        factor_s[...] = jnp.exp(jnp.minimum(running - jnp.where(lane >= r, base, 0.0), 0.0))

    factor = factor_s[pl.ds(pl.multiple_of(step * PAIR, PAIR), PAIR), :].T
    token = lax.broadcasted_iota(jnp.int32, (TOK, N), 0)
    resumed = (token >= r) & (r > 0)
    decays = [[factors_of(ref[chip, width:, :], local) for ref in (low_ref, high_ref)] for chip in range(own_ref.shape[0])]
    for group in range(2):
        reads = read_ref[:, group * N : (group + 1) * N].astype(jnp.float32)
        left = jnp.where(resumed, 0.0, reads)
        right = jnp.where(resumed, reads, 0.0)
        reads = jnp.concatenate([left, right], axis=1).astype(jnp.bfloat16)
        for k in range(group * HEADS_PER, (group + 1) * HEADS_PER):
            chip, half, head = k // (2 * local), k // local % 2, k % local
            rows = slice(head * N, (head + 1) * N)
            own = even if half == 0 else jnp.logical_not(even)
            entering = jnp.where(own, own_ref[chip, rows, :], other_ref[chip, rows, :]).astype(jnp.float32)
            distance = (step * own_ref.shape[0] + chip) ^ (meta.place // 2)
            far = far_place(distance // 4, bits)
            near, low_bit = distance % 2 == 0, distance // 2 % 2 == 0
            found = [piece[far, rows, :] for piece in pieces]
            found = [jnp.where(low_bit, found[i], found[i + 1]) for i in range(0, 8, 2)]
            restored = jnp.where(own, jnp.where(near, found[0], found[1]), jnp.where(near, found[2], found[3]))
            whole_state = restored.astype(jnp.float32)
            summary = (low_ref, high_ref)[half][chip, rows, :].astype(jnp.float32)
            middle = decays[chip][half][head : head + 1] * jnp.where(closes, whole_state, entering) + summary
            middle = jnp.where(opens, whole_state, middle)
            entering = jnp.where(even, entering, middle).astype(jnp.bfloat16)
            states = jnp.concatenate([entering, restored], axis=0)
            carried = jnp.dot(reads, states, preferred_element_type=jnp.float32)
            place = slice(k * P_SIZE, (k + 1) * P_SIZE)
            out_ref[:, place] = (part_ref[:, place] + factor[:, k : k + 1] * carried).astype(jnp.bfloat16)


def finish(meta, part, rates, reads, own, other, low, high, pieces, local):
    chips = PAIR // (2 * local)
    count, length, _ = pieces[0].shape
    resumed = pl.BlockSpec((count, local * N, P_SIZE), lambda i, *m: (0, length // (local * N) - 1, 0))
    states = pl.BlockSpec((chips, local * N, P_SIZE), lambda i, *m: (i, 0, 0))
    stretch = pl.BlockSpec((chips, local * N + EXTRA, P_SIZE), lambda i, *m: (i, 0, 0))
    return pl.pallas_call(
        scalars(finish_kernel, local),
        out_shape=jax.ShapeDtypeStruct((TOK, H * P_SIZE), jnp.bfloat16),
        grid_spec=pltpu.PrefetchScalarGridSpec(
            num_scalar_prefetch=1,
            grid=(STEPS,),
            in_specs=[
                pl.BlockSpec((TOK, PAIR * P_SIZE), lambda i, *m: (0, i)),
                pl.BlockSpec((H, TOK), lambda i, *m: (0, 0)),
                pl.BlockSpec((TOK, 2 * N), lambda i, *m: (0, i)),
                states,
                states,
                stretch,
                stretch,
            ]
            + [resumed] * 8,
            out_specs=pl.BlockSpec((TOK, PAIR * P_SIZE), lambda i, *m: (0, i)),
            scratch_shapes=[pltpu.VMEM((H, TOK), jnp.float32)],
        ),
        compiler_params=params(),
        cost_estimate=LONG,
        name="finish",
    )(meta, part, rates, reads, own, other, low, high, *pieces)


def attend_kernel(
    meta, q_ref, four, two, now, four_across, two_across, now_across, *refs,
):
    history_refs, (sk_ref, sv_ref), (out_ref, token_ref, key_s, value_s) = refs[:32], refs[32:34], refs[-4:]
    factor = 1.0 / math.sqrt(HD)
    first = meta.place * TOK
    r = meta.last_start()
    opening = meta.session_at(first)
    closing = meta.session_at(first + TOK - 1)
    even = meta.even

    def band(number, part):
        if number == 0:
            return four[part]
        if number == 1:
            return jnp.where(even, four_across[part], two_across[part])
        if number == 2:
            return two[part]
        if number == 3:
            return jnp.where(even, two_across[part], now_across[part])
        return now[part]

    token_ref[...] = jnp.zeros_like(token_ref)

    def sinks(ref, session):
        rows = ref[session].astype(jnp.float32)
        spare = jnp.zeros((COLUMNS - SPAN - SINKS, HD), jnp.float32)
        return jnp.concatenate([rows, spare], axis=0).astype(jnp.bfloat16)

    length = (REACH + 1) * TOK

    def one_session(session, key_refs, value_refs, resuming, needed):
        start = meta.start_of(session) - first + WINDOW
        oldest = start - WINDOW + jnp.maximum(SINKS + WINDOW - meta.history(session), 0)

        @pl.when(needed & (start > 0))
        def _():
            row = lax.broadcasted_iota(jnp.int32, (length, WINDOW), 0)
            chips, share, _ = key_refs[0].shape
            index = lax.broadcasted_iota(jnp.int32, (1, WINDOW), 1)
            piece, index = index // (WINDOW // 8), index % (WINDOW // 8)
            near, row_in = index // share, index % share
            far = far_place(near, chips.bit_length() - 1)
            device = meta.place ^ (piece // 4 + piece // 2 % 2 * 2 + piece % 2 * 4 + far * 8)
            place = device * share + row_in
            moved = (row == place + start - WINDOW).astype(jnp.bfloat16)
            part = (WINDOW // 8, HD)
            keys = jnp.concatenate([ref[...].reshape(part) for ref in key_refs], axis=0)
            values = jnp.concatenate([ref[...].reshape(part) for ref in value_refs], axis=0)
            history = jnp.dot(
                moved, jnp.concatenate([keys, values], axis=1), preferred_element_type=jnp.float32
            )
            for i in range(REACH + 1):
                rows = slice(i * TOK, (i + 1) * TOK)
                index = lax.broadcasted_iota(jnp.int32, (TOK, HD), 0) + i * TOK
                turn = index >= start
                key_s[rows, :] = jnp.where(
                    turn, band(i, 0).astype(jnp.float32), history[rows, :HD]
                ).astype(jnp.bfloat16)
                value_s[rows, :] = jnp.where(
                    turn, band(i, 1).astype(jnp.float32), history[rows, HD:]
                ).astype(jnp.bfloat16)

        @pl.when(needed & (start <= 0))
        def _():
            for i in range(REACH + 1):
                rows = slice(i * TOK, (i + 1) * TOK)
                key_s[rows, :] = band(i, 0)
                value_s[rows, :] = band(i, 1)

        for b in range(TOK // BLOCK):
            inside = (b * BLOCK + BLOCK > r) if resuming else (b * BLOCK < r)

            @pl.when(needed & inside)
            def _():
                rows = slice(b * BLOCK, b * BLOCK + SPAN)
                keys = jnp.concatenate([key_s[rows, :], sinks(sk_ref, session)], axis=0)
                values = jnp.concatenate([value_s[rows, :], sinks(sv_ref, session)], axis=0)
                tokens = slice(b * BLOCK, (b + 1) * BLOCK)
                queries = jnp.concatenate(
                    [q_ref[tokens, g * HD : (g + 1) * HD] for g in range(QH // KVH)], axis=0
                )
                scores = lax.dot_general(
                    keys, queries, (((1,), (1,)), ((), ())), preferred_element_type=jnp.float32
                )
                column = lax.broadcasted_iota(jnp.int32, (COLUMNS, 2 * BLOCK), 0)
                token = lax.broadcasted_iota(jnp.int32, (COLUMNS, 2 * BLOCK), 1) % BLOCK
                seen = (column > token) & (column <= token + WINDOW) & (column >= oldest - b * BLOCK)
                seen = (seen & (column < SPAN)) | ((column >= SPAN) & (column < SPAN + SINKS))
                bias = jnp.where(seen, 0.0, NEG)
                weights, shares = [], []
                for j in range(QH // KVH // 2):
                    score = scores[:, j * 2 * BLOCK : (j + 1) * 2 * BLOCK] * factor + bias
                    weight = jnp.exp(score - jnp.max(score, axis=0, keepdims=True))
                    shares.append(1.0 / jnp.sum(weight, axis=0, keepdims=True))
                    weights.append(weight.astype(jnp.bfloat16))
                mixed = lax.dot_general(
                    values, jnp.concatenate(weights, axis=1), (((0,), (0,)), ((), ())),
                    preferred_element_type=jnp.float32,
                )
                for j in range(QH // KVH // 2):
                    pair = (mixed[:, j * 2 * BLOCK : (j + 1) * 2 * BLOCK] * shares[j]).T
                    for g in range(2):
                        result = pair[g * BLOCK : (g + 1) * BLOCK]
                        lanes = slice((2 * j + g) * HD, (2 * j + g + 1) * HD)
                        if resuming:
                            index = lax.broadcasted_iota(jnp.int32, (BLOCK, HD), 0) + b * BLOCK
                            before = out_ref[tokens, lanes].astype(jnp.float32)
                            result = jnp.where(index >= r, result, before)
                        out_ref[tokens, lanes] = result.astype(jnp.bfloat16)

    one_session(opening, history_refs[0:8], history_refs[8:16], False, r > 0)
    one_session(closing, history_refs[16:24], history_refs[24:], True, r >= 0)


def attend(meta, queries, bands, pieces, half, sink_keys, sink_values, idle):
    chips = pieces[0].shape[0]
    share = WINDOW // (8 * chips)
    lanes = QH // KVH * HD

    def history_spec(which, last):
        def index(j, *m):
            known = Scalars(*m)
            session = known.session_at(known.place * TOK + (TOK - 1 if last else 0))
            session = session - (known.place >= half).astype(jnp.int32)
            return (0, (which * 2 + session) * KVH + j, 0)

        return pl.BlockSpec((chips, share, HD), index)

    pad = SEQS, SINKS, HD
    return pl.pallas_call(
        scalars(attend_kernel),
        out_shape=[jax.ShapeDtypeStruct((TOK, QH * HD), jnp.bfloat16), TOKEN],
        grid_spec=pltpu.PrefetchScalarGridSpec(
            num_scalar_prefetch=1,
            grid=(KVH,),
            in_specs=[pl.BlockSpec((TOK, lanes), lambda j, *m: (0, j))]
            + [pl.BlockSpec((2, TOK, HD), lambda j, *m: (0, 0, j))] * len(bands)
            + [history_spec(0, False)] * 8
            + [history_spec(1, False)] * 8
            + [history_spec(0, True)] * 8
            + [history_spec(1, True)] * 8
            + [pl.BlockSpec(pad, lambda j, *m: (0, 0, j))] * 2
            + [idle_spec(a) for a in idle],
            out_specs=[
                pl.BlockSpec((TOK, lanes), lambda j, *m: (0, j)),
                pl.BlockSpec(TOKEN.shape, lambda j, *m: (0, 0)),
            ],
            scratch_shapes=[
                pltpu.VMEM(((REACH + 1) * TOK, HD), jnp.bfloat16),
                pltpu.VMEM(((REACH + 1) * TOK, HD), jnp.bfloat16),
            ],
        ),
        compiler_params=params(),
        cost_estimate=SHORT,
        name="attend",
    )(
        meta, queries, *bands, *pieces, *pieces, *pieces, *pieces, sink_keys, sink_values, *idle
    )


def shifted(block, axis, distance):
    devices = range(lax.axis_size(axis))
    return lax.ppermute(block, axis, [(i - distance, i) for i in devices if i - distance in devices])


def shards(
    mamba_input,
    step_size,
    decay_log,
    state_write,
    state_read,
    skip_gain,
    saved_states,
    home_slot,
    turn_lengths,
    history_lengths,
    queries,
    turn_keys,
    turn_values,
    cache_keys,
    cache_values,
    sink_keys,
    sink_values,
):
    place = lax.axis_index("ctx")
    group = lax.axis_index("sess")
    groups = lax.axis_size("sess")
    devices = lax.axis_size("ctx")
    local = saved_states.shape[2]
    width = local * N
    chips = devices // 2
    same_core = [list(range(core, devices, 2)) for core in range(2)]
    meta = jnp.concatenate(
        [jnp.stack([place, group]).astype(jnp.int32), turn_lengths[0], history_lengths[0], home_slot]
    )
    x, rates, steps = mamba_input[0], decay_log[0].T, step_size[0].T
    writes, reads = state_write[0], state_read[0]
    def apart(block, distance):
        return lax.ppermute(block, "ctx", [(i, i ^ distance) for i in range(devices)])

    def exchanged(block):
        return lax.all_to_all(block, "ctx", 0, 0, axis_index_groups=same_core, tiled=True)

    stored = [saved_states[0]]
    for j in range(1, groups):
        route = [((i + j) % groups, i) for i in range(groups)]
        stored.append(lax.ppermute(saved_states[0], "sess", route))
    stored = [block.reshape(SEQS, local, P_SIZE, N) for block in stored]

    parcel = (1, 4 * KVH * cache_keys.shape[2], HD)
    band = (2, TOK, KVH * HD)
    near, away, key_value = whole(
        scalars(pack_kernel, devices // 2),
        "pack",
        meta,
        [cache_keys[0], cache_values[0], turn_keys[0], turn_values[0]],
        [(parcel, jnp.bfloat16), (parcel, jnp.bfloat16), (band, jnp.bfloat16)],
        mib=60,
    )
    moved = apart(away, devices // 2)
    four = shifted(key_value, "ctx", 4)

    keep, send = summaries(meta, x, rates, steps, writes, local, away)
    got = apart(send, 1)

    [two] = whole(
        scalars(two_kernel), "two", meta, [key_value, four], [(band, jnp.bfloat16)], idle=[send]
    )

    one = (1, width, P_SIZE)
    home, away, restored = whole(
        scalars(restore_kernel, local, devices // 2, groups),
        "restore",
        meta,
        stored,
        [(one, jnp.bfloat16), (one, jnp.bfloat16), ((SEQS, width, P_SIZE), jnp.float32)],
        idle=[two],
    )
    two = apart(two, 2)
    away = apart(away, devices // 2)
    [near] = whole(
        scalars(parcels_kernel),
        "parcels",
        meta,
        [near, moved, home, away],
        [((2, parcel[1] + width, HD), jnp.bfloat16)],
        idle=[got],
    )
    distance = devices // 4
    while distance > 4:
        joined = (2 * near.shape[0], *near.shape[1:])
        [near] = whole(scalars(join_kernel), "join", meta, [near, apart(near, distance)], [(joined, jnp.bfloat16)])
        distance //= 2
    moved = apart(near, 4)
    beside = apart(near, 2)
    [chip] = whole(
        scalars(combine_kernel, local),
        "combine",
        meta,
        [keep, got],
        [(keep.shape, jnp.bfloat16)],
        idle=[near],
    )
    total = exchanged(chip)
    part, token = intra(meta, skip_gain, x, rates, steps, writes, reads, chip)
    pieces = [near, moved, beside, apart(moved, 2)]
    bands = [four, two, key_value]
    across = [apart(block, 1) for block in bands]
    low = apart(keep, 1)

    entering, after = whole(
        scalars(recurrence_kernel, local),
        "recurrence",
        meta,
        [total, restored],
        [((chips, width, P_SIZE), jnp.bfloat16), (TOKEN.shape, TOKEN.dtype)],
        idle=[token, low, *across, *pieces],
    )
    entering = exchanged(entering)
    pieces += [apart(piece, 1) for piece in pieces]
    attended, token = attend(
        meta, queries[0], bands + across, pieces, devices // 2, sink_keys[0], sink_values[0], [after]
    )
    [entering] = whole(
        scalars(copy_kernel), "copy", meta, [entering], [((chips, width, P_SIZE), jnp.bfloat16)], idle=[token]
    )
    other = apart(entering, 1)
    mixed = finish(meta, part, rates, reads, entering, other, low, got, pieces, local)
    return mixed[None], attended[None]


def solution(mesh):
    token = P("sess", "ctx", None)
    return jax.shard_map(
        shards,
        mesh=mesh,
        in_specs=(
            token,
            token,
            token,
            token,
            token,
            P(),
            P("sess", None, "ctx", None),
            P(),
            P("sess", None),
            P("sess", None),
            token,
            token,
            token,
            P("sess", None, "ctx", None),
            P("sess", None, "ctx", None),
            P("sess", None, None, None),
            P("sess", None, None, None),
        ),
        out_specs=(token, token),
        check_vma=False,
    )
```

```python
import math

import jax
import jax.numpy as jnp
from jax import lax
from jax.experimental import pallas as pl
from jax.experimental.pallas import tpu as pltpu
from jax.sharding import PartitionSpec as P

REACH = 4
SEQS = 3
SINKS = 4
H = 64
P_SIZE = 128
N = 64
G = 8
QH = 32
KVH = 4
HD = 128
WINDOW = 512
TOK = 128

HEADS_PER = H // G
PAIR = 2 * HEADS_PER
STEPS = H // PAIR
EXTRA = 16
BLOCK = 64
SPAN = WINDOW + BLOCK
COLUMNS = SPAN + 64
NEG = -1e30
TOKEN = jax.ShapeDtypeStruct((8, 128), jnp.float32)
SHORT = pl.CostEstimate(flops=1024, bytes_accessed=1024, transcendentals=0)
LONG = pl.CostEstimate(flops=1 << 35, bytes_accessed=1 << 20, transcendentals=0)


class Scalars:
    def __init__(self, ids):
        self.place, self.group = ids[0], ids[1]
        self.one = ids[2]
        self.two = ids[2] + ids[3]
        self.ids = ids
        self.even = self.place % 2 == 0

    def history(self, session):
        return self.ids[2 + SEQS + session]

    def home(self, number):
        return self.ids[2 + 2 * SEQS + number]

    def session_at(self, position):
        return (position >= self.one).astype(jnp.int32) + (position >= self.two).astype(jnp.int32)

    def start_of(self, session):
        return jnp.where(session == 0, 0, jnp.where(session == 1, self.one, self.two))

    def last_start(self):
        first = self.place * TOK
        return jnp.maximum(self.start_of(self.session_at(first + TOK - 1)) - first, 0)


def scalars(kernel, *options):
    def body(ids, *refs):
        kernel(*options, Scalars(ids), *refs)

    return body


def params(mib=60):
    return pltpu.CompilerParams(vmem_limit_bytes=mib * 1024 * 1024)


def running_rows(dl_ref):
    k = lax.broadcasted_iota(jnp.int32, (TOK, TOK), 0)
    u = lax.broadcasted_iota(jnp.int32, (TOK, TOK), 1)
    upto = (k <= u).astype(jnp.bfloat16)
    running = jnp.dot(dl_ref[...], upto, preferred_element_type=jnp.float32)
    return dl_ref[...].astype(jnp.float32), running


def summary_kernel(
    local, meta, x_ref, dl_ref, step_ref, write_ref, _, keep_ref, send_ref, coef_s, factor_s, write_s
):
    step = pl.program_id(0)

    @pl.when(step == 0)
    def _():
        rates, running = running_rows(dl_ref)
        steps = step_ref[...].astype(jnp.float32)
        r = meta.last_start()
        lane = lax.broadcasted_iota(jnp.int32, (H, TOK), 1)
        last = running[:, TOK - 1 :]
        base = jnp.sum(jnp.where(lane < r, rates, 0.0), axis=1, keepdims=True)
        coef_s[...] = jnp.where(lane >= r, jnp.exp(last - running) * steps, 0.0)
        factor_s[...] = jnp.broadcast_to(jnp.exp(last - base), (H, TOK))
        write_s[...] = write_ref[...].astype(jnp.float32).T

    even = meta.even
    coef = coef_s[pl.ds(pl.multiple_of(step * PAIR, PAIR), PAIR), :]
    factor = factor_s[pl.ds(pl.multiple_of(step * PAIR, PAIR), PAIR), :]
    writes = write_s[pl.ds(pl.multiple_of(step * 2 * N, 2 * N), 2 * N), :]

    def summary(k):
        group = k // HEADS_PER
        loading = (writes[group * N : (group + 1) * N] * coef[k : k + 1]).astype(jnp.bfloat16)
        return jnp.dot(
            loading, x_ref[:, k * P_SIZE : (k + 1) * P_SIZE], preferred_element_type=jnp.float32
        )

    for chip in range(PAIR // (2 * local)):
        low, high = 2 * local * chip, 2 * local * chip + local
        for k in range(local):
            first, second = summary(low + k), summary(high + k)
            rows = slice(k * N, (k + 1) * N)
            keep_ref[chip, rows, :] = jnp.where(even, first, second).astype(jnp.bfloat16)
            send_ref[chip, rows, :] = jnp.where(even, second, first).astype(jnp.bfloat16)
        first, second = factor[low : low + local], factor[high : high + local]
        keep_ref[chip, local * N :, :] = factor_rows(jnp.where(even, first, second))
        send_ref[chip, local * N :, :] = factor_rows(jnp.where(even, second, first))


def factor_rows(rows):
    high = rows.astype(jnp.bfloat16).astype(jnp.float32)
    parts = [high, rows - high]
    if EXTRA > 2 * rows.shape[0]:
        parts.append(jnp.zeros((EXTRA - 2 * rows.shape[0], TOK), jnp.float32))
    return jnp.concatenate(parts, axis=0).astype(jnp.bfloat16)


def factors_of(block, local):
    block = block.astype(jnp.float32)
    return block[:local] + block[local : 2 * local]


def summaries(meta, x, rates, steps, writes, local, idle):
    chips = H // (2 * local)
    rows = local * N + EXTRA
    shape = jax.ShapeDtypeStruct((chips, rows, P_SIZE), jnp.bfloat16)
    spec = pl.BlockSpec((PAIR // (2 * local), rows, P_SIZE), lambda i, *m: (i, 0, 0))
    return pl.pallas_call(
        scalars(summary_kernel, local),
        out_shape=[shape, shape],
        grid_spec=pltpu.PrefetchScalarGridSpec(
            num_scalar_prefetch=1,
            grid=(STEPS,),
            in_specs=[
                pl.BlockSpec((TOK, PAIR * P_SIZE), lambda i, *m: (0, i)),
                pl.BlockSpec((H, TOK), lambda i, *m: (0, 0)),
                pl.BlockSpec((H, TOK), lambda i, *m: (0, 0)),
                pl.BlockSpec((TOK, G * N), lambda i, *m: (0, 0)),
                pl.BlockSpec(memory_space=pl.ANY),
            ],
            out_specs=[spec, spec],
            scratch_shapes=[
                pltpu.VMEM((H, TOK), jnp.float32),
                pltpu.VMEM((H, TOK), jnp.float32),
                pltpu.VMEM((G * N, TOK), jnp.float32),
            ],
        ),
        compiler_params=params(),
        cost_estimate=LONG,
        name="summaries",
    )(meta, x, rates, steps, writes, idle)


def idle_spec(array):
    return pl.BlockSpec(memory_space=pl.ANY)


def whole(kernel, name, meta, arrays, shapes, idle=(), mib=16, scratch=()):
    def spec(shape):
        return pl.BlockSpec(shape, lambda i, *m: (0,) * len(shape))

    return pl.pallas_call(
        kernel,
        out_shape=[jax.ShapeDtypeStruct(s, t) for s, t in shapes],
        grid_spec=pltpu.PrefetchScalarGridSpec(
            num_scalar_prefetch=1,
            grid=(1,),
            in_specs=[spec(a.shape) for a in arrays] + [idle_spec(a) for a in idle],
            out_specs=[spec(s) for s, _ in shapes],
            scratch_shapes=scratch,
        ),
        compiler_params=params(mib),
        cost_estimate=LONG,
        name=name,
    )(meta, *arrays, *idle)


def pack_kernel(half, meta, keys_ref, values_ref, turn_keys_ref, turn_values_ref, home_ref, away_ref, band_ref):
    band_ref[0] = turn_keys_ref[...]
    band_ref[1] = turn_values_ref[...]
    rows = keys_ref.shape[1]
    upper = (meta.place >= half).astype(jnp.int32)
    for out_ref, first in ((home_ref, upper), (away_ref, 1 - upper)):
        for which, ref in enumerate((keys_ref, values_ref)):
            for s in range(2):
                for j in range(KVH):
                    place = ((which * 2 + s) * KVH + j) * rows
                    out_ref[0, place : place + rows, :] = ref[first + s, :, j * HD : (j + 1) * HD]


def restore_kernel(local, half, groups, meta, *refs):
    stored, (home_ref, away_ref, restored_ref) = refs[:groups], refs[-3:]
    for s in range(SEQS):
        slot = meta.home(meta.group * SEQS + s)
        source = (slot // SEQS - meta.group + groups) % groups
        for k in range(local):
            state = stored[0][slot % SEQS, k]
            for j in range(1, groups):
                state = jnp.where(source == j, stored[j][slot % SEQS, k], state)
            restored_ref[s, k * N : (k + 1) * N, :] = state.T
    upper = (meta.place >= half).astype(jnp.int32)
    home_ref[0] = restored_ref[upper + 1].astype(jnp.bfloat16)
    away_ref[0] = restored_ref[2 - upper].astype(jnp.bfloat16)


def copy_kernel(meta, array_ref, *refs):
    refs[-1][...] = array_ref[...]


def join_kernel(meta, first_ref, second_ref, *refs):
    out_ref = refs[-1]
    count = first_ref.shape[0]
    out_ref[:count] = first_ref[...]
    out_ref[count:] = second_ref[...]


def join_two_kernel(
    meta, first_ref, second_ref, first_state_ref, second_state_ref, key_value_ref, four_ref, *refs
):
    out_ref, two_ref = refs[-2:]
    rows = first_ref.shape[1]
    for i, (parcel, state) in enumerate(((first_ref, first_state_ref), (second_ref, second_state_ref))):
        out_ref[i, :rows, :] = parcel[0]
        out_ref[i, rows:, :] = state[0]
    two_ref[...] = jnp.where(meta.place // 2 % 2 == 0, key_value_ref[...], four_ref[...])


def far_place(distance, bits):
    place = distance * 0
    for k in range(bits):
        place = place + ((distance // (1 << k)) % 2) * (1 << (bits - 1 - k))
    return place


def combine_kernel(local, meta, keep_ref, got_ref, *refs):
    out_ref = refs[-1]
    even = meta.even
    second = (meta.place // 2 * 2 + 1) * TOK
    closes = meta.start_of(meta.session_at(second + TOK - 1)) >= second
    width = local * N
    for chip in range(keep_ref.shape[0]):
        keep = factors_of(keep_ref[chip, width:, :], local)
        got = factors_of(got_ref[chip, width:, :], local)
        f0, f1 = jnp.where(even, keep, got), jnp.where(even, got, keep)
        out_ref[chip, width:, :] = factor_rows(jnp.where(closes, f1, f0 * f1))
        carry = jnp.where(closes, 0.0, f1)
        for k in range(local):
            rows = slice(k * N, (k + 1) * N)
            keep = keep_ref[chip, rows, :].astype(jnp.float32)
            got = got_ref[chip, rows, :].astype(jnp.float32)
            s0, s1 = jnp.where(even, keep, got), jnp.where(even, got, keep)
            out_ref[chip, rows, :] = (carry[k : k + 1] * s0 + s1).astype(jnp.bfloat16)


def recurrence_kernel(local, meta, got_ref, restored_ref, *refs):
    out_ref, token_ref = refs[-2:]
    token_ref[...] = jnp.zeros_like(token_ref)
    width = local * N
    span = 2 * TOK
    state = [jnp.zeros((N, P_SIZE), jnp.float32) for _ in range(local)]
    for c in range(got_ref.shape[0]):
        first = c * span
        opening = meta.session_at(first)
        closing = meta.session_at(first + span - 1)
        opens = meta.start_of(opening) >= first
        closes = meta.start_of(closing) >= first
        factor = factors_of(got_ref[c, width:, :], local)
        for k in range(local):
            rows = slice(k * N, (k + 1) * N)
            entering = jnp.where(opens, restored_ref[opening, rows, :], state[k])
            out_ref[c, rows, :] = entering.astype(jnp.bfloat16)
            source = jnp.where(closes, restored_ref[closing, rows, :], state[k])
            state[k] = factor[k : k + 1] * source + got_ref[c, rows, :].astype(jnp.float32)


def intra_kernel(meta, skip, x_ref, dl_ref, step_ref, write_ref, read_ref, _, out_ref, token_ref, run_s, step_s):
    step = pl.program_id(0)

    @pl.when(step == 0)
    def _():
        _, running = running_rows(dl_ref)
        run_s[...] = running
        step_s[...] = step_ref[...].astype(jnp.float32)

    token_ref[...] = jnp.zeros_like(token_ref)
    heads = pl.ds(pl.multiple_of(step * PAIR, PAIR), PAIR)
    running = run_s[heads, :]
    sizes = step_s[heads, :]
    columns = running.T
    r = meta.last_start()
    t = lax.broadcasted_iota(jnp.int32, (TOK, TOK), 0)
    u = lax.broadcasted_iota(jnp.int32, (TOK, TOK), 1)
    causal = (u <= t) & ((u >= r) | (t < r))
    for group in range(2):
        part = slice(group * N, (group + 1) * N)
        products = lax.dot_general(
            read_ref[:, part], write_ref[:, part], (((1,), (1,)), ((), ())),
            preferred_element_type=jnp.float32,
        )
        products = jnp.where(causal, products, 0.0)
        for k in range(group * HEADS_PER, (group + 1) * HEADS_PER):
            difference = columns[:, k : k + 1] - running[k : k + 1]
            decay = jnp.exp(jnp.minimum(difference, 0.0))
            mixing = (products * decay * sizes[k : k + 1]).astype(jnp.bfloat16)
            place = slice(k * P_SIZE, (k + 1) * P_SIZE)
            x = x_ref[:, place]
            mixed = jnp.dot(mixing, x, preferred_element_type=jnp.float32)
            out_ref[:, place] = mixed + skip[step * PAIR + k] * x.astype(jnp.float32)


def intra(meta, skip, x, rates, steps, writes, reads, idle):
    return pl.pallas_call(
        scalars(intra_kernel),
        out_shape=[jax.ShapeDtypeStruct((TOK, H * P_SIZE), jnp.float32), TOKEN],
        grid_spec=pltpu.PrefetchScalarGridSpec(
            num_scalar_prefetch=2,
            grid=(STEPS,),
            in_specs=[
                pl.BlockSpec((TOK, PAIR * P_SIZE), lambda i, *m: (0, i)),
                pl.BlockSpec((H, TOK), lambda i, *m: (0, 0)),
                pl.BlockSpec((H, TOK), lambda i, *m: (0, 0)),
                pl.BlockSpec((TOK, 2 * N), lambda i, *m: (0, i)),
                pl.BlockSpec((TOK, 2 * N), lambda i, *m: (0, i)),
                pl.BlockSpec(memory_space=pl.ANY),
            ],
            out_specs=[
                pl.BlockSpec((TOK, PAIR * P_SIZE), lambda i, *m: (0, i)),
                pl.BlockSpec(TOKEN.shape, lambda i, *m: (0, 0)),
            ],
            scratch_shapes=[
                pltpu.VMEM((H, TOK), jnp.float32),
                pltpu.VMEM((H, TOK), jnp.float32),
            ],
        ),
        compiler_params=params(),
        cost_estimate=LONG,
        name="intra",
    )(meta, skip, x, rates, steps, writes, reads, idle)


def finish_kernel(
    local, meta, part_ref, dl_ref, read_ref, own_ref, other_ref, low_ref, high_ref, *refs,
):
    pieces, (out_ref, factor_s) = refs[:8], refs[-2:]
    bits = pieces[0].shape[0].bit_length() - 1
    step = pl.program_id(0)
    even = meta.even
    r = meta.last_start()
    first = meta.place // 2 * 2 * TOK
    second = first + TOK
    start = meta.start_of(meta.session_at(second + TOK - 1))
    closes = (start > first) & (start < second)
    opens = start == second
    width = local * N

    @pl.when(step == 0)
    def _():
        rates, running = running_rows(dl_ref)
        lane = lax.broadcasted_iota(jnp.int32, (H, TOK), 1)
        base = jnp.sum(jnp.where(lane < r, rates, 0.0), axis=1, keepdims=True)
        factor_s[...] = jnp.exp(jnp.minimum(running - jnp.where(lane >= r, base, 0.0), 0.0))

    factor = factor_s[pl.ds(pl.multiple_of(step * PAIR, PAIR), PAIR), :].T
    token = lax.broadcasted_iota(jnp.int32, (TOK, N), 0)
    resumed = (token >= r) & (r > 0)
    decays = [[factors_of(ref[chip, width:, :], local) for ref in (low_ref, high_ref)] for chip in range(own_ref.shape[0])]
    for group in range(2):
        reads = read_ref[:, group * N : (group + 1) * N].astype(jnp.float32)
        left = jnp.where(resumed, 0.0, reads)
        right = jnp.where(resumed, reads, 0.0)
        reads = jnp.concatenate([left, right], axis=1).astype(jnp.bfloat16)
        for k in range(group * HEADS_PER, (group + 1) * HEADS_PER):
            chip, half, head = k // (2 * local), k // local % 2, k % local
            rows = slice(head * N, (head + 1) * N)
            own = even if half == 0 else jnp.logical_not(even)
            entering = jnp.where(own, own_ref[chip, rows, :], other_ref[chip, rows, :]).astype(jnp.float32)
            distance = (step * own_ref.shape[0] + chip) ^ (meta.place // 2)
            far = far_place(distance // 4, bits)
            near, low_bit = distance % 2 == 0, distance // 2 % 2 == 0
            found = [piece[far, rows, :] for piece in pieces]
            found = [jnp.where(low_bit, found[i], found[i + 1]) for i in range(0, 8, 2)]
            restored = jnp.where(own, jnp.where(near, found[0], found[1]), jnp.where(near, found[2], found[3]))
            whole_state = restored.astype(jnp.float32)
            summary = (low_ref, high_ref)[half][chip, rows, :].astype(jnp.float32)
            middle = decays[chip][half][head : head + 1] * jnp.where(closes, whole_state, entering) + summary
            middle = jnp.where(opens, whole_state, middle)
            entering = jnp.where(even, entering, middle).astype(jnp.bfloat16)
            states = jnp.concatenate([entering, restored], axis=0)
            carried = jnp.dot(reads, states, preferred_element_type=jnp.float32)
            place = slice(k * P_SIZE, (k + 1) * P_SIZE)
            out_ref[:, place] = (part_ref[:, place] + factor[:, k : k + 1] * carried).astype(jnp.bfloat16)


def finish(meta, part, rates, reads, own, other, low, high, pieces, local):
    chips = PAIR // (2 * local)
    count, length, _ = pieces[0].shape
    resumed = pl.BlockSpec((count, local * N, P_SIZE), lambda i, *m: (0, length // (local * N) - 1, 0))
    states = pl.BlockSpec((chips, local * N, P_SIZE), lambda i, *m: (i, 0, 0))
    stretch = pl.BlockSpec((chips, local * N + EXTRA, P_SIZE), lambda i, *m: (i, 0, 0))
    return pl.pallas_call(
        scalars(finish_kernel, local),
        out_shape=jax.ShapeDtypeStruct((TOK, H * P_SIZE), jnp.bfloat16),
        grid_spec=pltpu.PrefetchScalarGridSpec(
            num_scalar_prefetch=1,
            grid=(STEPS,),
            in_specs=[
                pl.BlockSpec((TOK, PAIR * P_SIZE), lambda i, *m: (0, i)),
                pl.BlockSpec((H, TOK), lambda i, *m: (0, 0)),
                pl.BlockSpec((TOK, 2 * N), lambda i, *m: (0, i)),
                states,
                states,
                stretch,
                stretch,
            ]
            + [resumed] * 8,
            out_specs=pl.BlockSpec((TOK, PAIR * P_SIZE), lambda i, *m: (0, i)),
            scratch_shapes=[pltpu.VMEM((H, TOK), jnp.float32)],
        ),
        compiler_params=params(),
        cost_estimate=LONG,
        name="finish",
    )(meta, part, rates, reads, own, other, low, high, *pieces)


def attend_kernel(
    meta, q_ref, four, two, now, four_across, two_across, now_across, *refs,
):
    history_refs, (sk_ref, sv_ref), (out_ref, token_ref, key_s, value_s) = refs[:32], refs[32:34], refs[-4:]
    factor = 1.0 / math.sqrt(HD)
    first = meta.place * TOK
    r = meta.last_start()
    opening = meta.session_at(first)
    closing = meta.session_at(first + TOK - 1)
    even = meta.even

    def band(number, part):
        if number == 0:
            return four[part]
        if number == 1:
            return jnp.where(even, four_across[part], two_across[part])
        if number == 2:
            return two[part]
        if number == 3:
            return jnp.where(even, two_across[part], now_across[part])
        return now[part]

    token_ref[...] = jnp.zeros_like(token_ref)

    def sinks(ref, session):
        rows = ref[session].astype(jnp.float32)
        spare = jnp.zeros((COLUMNS - SPAN - SINKS, HD), jnp.float32)
        return jnp.concatenate([rows, spare], axis=0).astype(jnp.bfloat16)

    length = (REACH + 1) * TOK

    def one_session(session, key_refs, value_refs, resuming, needed):
        start = meta.start_of(session) - first + WINDOW
        oldest = start - WINDOW + jnp.maximum(SINKS + WINDOW - meta.history(session), 0)

        @pl.when(needed & (start > 0))
        def _():
            row = lax.broadcasted_iota(jnp.int32, (length, WINDOW), 0)
            chips, share, _ = key_refs[0].shape
            index = lax.broadcasted_iota(jnp.int32, (1, WINDOW), 1)
            piece, index = index // (WINDOW // 8), index % (WINDOW // 8)
            near, row_in = index // share, index % share
            far = far_place(near, chips.bit_length() - 1)
            device = meta.place ^ (piece // 4 + piece // 2 % 2 * 2 + piece % 2 * 4 + far * 8)
            place = device * share + row_in
            moved = (row == place + start - WINDOW).astype(jnp.bfloat16)
            part = (WINDOW // 8, HD)
            keys = jnp.concatenate([ref[...].reshape(part) for ref in key_refs], axis=0)
            values = jnp.concatenate([ref[...].reshape(part) for ref in value_refs], axis=0)
            history = jnp.dot(
                moved, jnp.concatenate([keys, values], axis=1), preferred_element_type=jnp.float32
            )
            for i in range(REACH + 1):
                rows = slice(i * TOK, (i + 1) * TOK)
                index = lax.broadcasted_iota(jnp.int32, (TOK, HD), 0) + i * TOK
                turn = index >= start
                key_s[rows, :] = jnp.where(
                    turn, band(i, 0).astype(jnp.float32), history[rows, :HD]
                ).astype(jnp.bfloat16)
                value_s[rows, :] = jnp.where(
                    turn, band(i, 1).astype(jnp.float32), history[rows, HD:]
                ).astype(jnp.bfloat16)

        @pl.when(needed & (start <= 0))
        def _():
            for i in range(REACH + 1):
                rows = slice(i * TOK, (i + 1) * TOK)
                key_s[rows, :] = band(i, 0)
                value_s[rows, :] = band(i, 1)

        for b in range(TOK // BLOCK):
            inside = (b * BLOCK + BLOCK > r) if resuming else (b * BLOCK < r)

            @pl.when(needed & inside)
            def _():
                rows = slice(b * BLOCK, b * BLOCK + SPAN)
                keys = jnp.concatenate([key_s[rows, :], sinks(sk_ref, session)], axis=0)
                values = jnp.concatenate([value_s[rows, :], sinks(sv_ref, session)], axis=0)
                tokens = slice(b * BLOCK, (b + 1) * BLOCK)
                queries = jnp.concatenate(
                    [q_ref[tokens, g * HD : (g + 1) * HD] for g in range(QH // KVH)], axis=0
                )
                scores = lax.dot_general(
                    keys, queries, (((1,), (1,)), ((), ())), preferred_element_type=jnp.float32
                )
                column = lax.broadcasted_iota(jnp.int32, (COLUMNS, 2 * BLOCK), 0)
                token = lax.broadcasted_iota(jnp.int32, (COLUMNS, 2 * BLOCK), 1) % BLOCK
                seen = (column > token) & (column <= token + WINDOW) & (column >= oldest - b * BLOCK)
                seen = (seen & (column < SPAN)) | ((column >= SPAN) & (column < SPAN + SINKS))
                bias = jnp.where(seen, 0.0, NEG)
                weights, shares = [], []
                for j in range(QH // KVH // 2):
                    score = scores[:, j * 2 * BLOCK : (j + 1) * 2 * BLOCK] * factor + bias
                    weight = jnp.exp(score - jnp.max(score, axis=0, keepdims=True))
                    shares.append(1.0 / jnp.sum(weight, axis=0, keepdims=True))
                    weights.append(weight.astype(jnp.bfloat16))
                mixed = lax.dot_general(
                    values, jnp.concatenate(weights, axis=1), (((0,), (0,)), ((), ())),
                    preferred_element_type=jnp.float32,
                )
                for j in range(QH // KVH // 2):
                    pair = (mixed[:, j * 2 * BLOCK : (j + 1) * 2 * BLOCK] * shares[j]).T
                    for g in range(2):
                        result = pair[g * BLOCK : (g + 1) * BLOCK]
                        lanes = slice((2 * j + g) * HD, (2 * j + g + 1) * HD)
                        if resuming:
                            index = lax.broadcasted_iota(jnp.int32, (BLOCK, HD), 0) + b * BLOCK
                            before = out_ref[tokens, lanes].astype(jnp.float32)
                            result = jnp.where(index >= r, result, before)
                        out_ref[tokens, lanes] = result.astype(jnp.bfloat16)

    one_session(opening, history_refs[0:8], history_refs[8:16], False, r > 0)
    one_session(closing, history_refs[16:24], history_refs[24:], True, r >= 0)


def attend(meta, queries, bands, pieces, half, sink_keys, sink_values, idle):
    chips = pieces[0].shape[0]
    share = WINDOW // (8 * chips)
    lanes = QH // KVH * HD

    def history_spec(which, last):
        def index(j, *m):
            known = Scalars(*m)
            session = known.session_at(known.place * TOK + (TOK - 1 if last else 0))
            session = session - (known.place >= half).astype(jnp.int32)
            return (0, (which * 2 + session) * KVH + j, 0)

        return pl.BlockSpec((chips, share, HD), index)

    pad = SEQS, SINKS, HD
    return pl.pallas_call(
        scalars(attend_kernel),
        out_shape=[jax.ShapeDtypeStruct((TOK, QH * HD), jnp.bfloat16), TOKEN],
        grid_spec=pltpu.PrefetchScalarGridSpec(
            num_scalar_prefetch=1,
            grid=(KVH,),
            in_specs=[pl.BlockSpec((TOK, lanes), lambda j, *m: (0, j))]
            + [pl.BlockSpec((2, TOK, HD), lambda j, *m: (0, 0, j))] * len(bands)
            + [history_spec(0, False)] * 8
            + [history_spec(1, False)] * 8
            + [history_spec(0, True)] * 8
            + [history_spec(1, True)] * 8
            + [pl.BlockSpec(pad, lambda j, *m: (0, 0, j))] * 2
            + [idle_spec(a) for a in idle],
            out_specs=[
                pl.BlockSpec((TOK, lanes), lambda j, *m: (0, j)),
                pl.BlockSpec(TOKEN.shape, lambda j, *m: (0, 0)),
            ],
            scratch_shapes=[
                pltpu.VMEM(((REACH + 1) * TOK, HD), jnp.bfloat16),
                pltpu.VMEM(((REACH + 1) * TOK, HD), jnp.bfloat16),
            ],
        ),
        compiler_params=params(),
        cost_estimate=SHORT,
        name="attend",
    )(
        meta, queries, *bands, *pieces, *pieces, *pieces, *pieces, sink_keys, sink_values, *idle
    )


def shifted(block, axis, distance):
    devices = range(lax.axis_size(axis))
    return lax.ppermute(block, axis, [(i - distance, i) for i in devices if i - distance in devices])


def shards(
    mamba_input,
    step_size,
    decay_log,
    state_write,
    state_read,
    skip_gain,
    saved_states,
    home_slot,
    turn_lengths,
    history_lengths,
    queries,
    turn_keys,
    turn_values,
    cache_keys,
    cache_values,
    sink_keys,
    sink_values,
):
    place = lax.axis_index("ctx")
    group = lax.axis_index("sess")
    groups = lax.axis_size("sess")
    devices = lax.axis_size("ctx")
    local = saved_states.shape[2]
    width = local * N
    chips = devices // 2
    same_core = [list(range(core, devices, 2)) for core in range(2)]
    meta = jnp.concatenate(
        [jnp.stack([place, group]).astype(jnp.int32), turn_lengths[0], history_lengths[0], home_slot]
    )
    x, rates, steps = mamba_input[0], decay_log[0].T, step_size[0].T
    writes, reads = state_write[0], state_read[0]
    def apart(block, distance):
        return lax.ppermute(block, "ctx", [(i, i ^ distance) for i in range(devices)])

    def exchanged(block):
        return lax.all_to_all(block, "ctx", 0, 0, axis_index_groups=same_core, tiled=True)

    stored = [saved_states[0]]
    for j in range(1, groups):
        route = [((i + j) % groups, i) for i in range(groups)]
        stored.append(lax.ppermute(saved_states[0], "sess", route))
    stored = [block.reshape(SEQS, local, P_SIZE, N) for block in stored]

    parcel = (1, 4 * KVH * cache_keys.shape[2], HD)
    band = (2, TOK, KVH * HD)
    near, away, key_value = whole(
        scalars(pack_kernel, devices // 2),
        "pack",
        meta,
        [cache_keys[0], cache_values[0], turn_keys[0], turn_values[0]],
        [(parcel, jnp.bfloat16), (parcel, jnp.bfloat16), (band, jnp.bfloat16)],
        mib=60,
    )
    moved = apart(away, devices // 2)
    four = shifted(key_value, "ctx", 4)

    keep, send = summaries(meta, x, rates, steps, writes, local, away)
    got = apart(send, 1)

    one = (1, width, P_SIZE)
    home, away, restored = whole(
        scalars(restore_kernel, local, devices // 2, groups),
        "restore",
        meta,
        stored,
        [(one, jnp.bfloat16), (one, jnp.bfloat16), ((SEQS, width, P_SIZE), jnp.float32)],
        idle=[send],
    )
    away = apart(away, devices // 2)
    near, two = whole(
        scalars(join_two_kernel),
        "join_two",
        meta,
        [near, moved, home, away, key_value, four],
        [((2, parcel[1] + width, HD), jnp.bfloat16), (band, jnp.bfloat16)],
        idle=[got],
    )
    distance = devices // 4
    while distance > 4:
        joined = (2 * near.shape[0], *near.shape[1:])
        [near] = whole(scalars(join_kernel), "join", meta, [near, apart(near, distance)], [(joined, jnp.bfloat16)])
        distance //= 2
    moved = apart(near, 4)
    two = apart(two, 2)
    beside = apart(near, 2)
    [chip] = whole(
        scalars(combine_kernel, local),
        "combine",
        meta,
        [keep, got],
        [(keep.shape, jnp.bfloat16)],
        idle=[near],
    )
    total = exchanged(chip)
    part, token = intra(meta, skip_gain, x, rates, steps, writes, reads, chip)
    pieces = [near, moved, beside, apart(moved, 2)]
    bands = [four, two, key_value]
    across = [apart(block, 1) for block in bands]
    low = apart(keep, 1)

    entering, after = whole(
        scalars(recurrence_kernel, local),
        "recurrence",
        meta,
        [total, restored],
        [((chips, width, P_SIZE), jnp.bfloat16), (TOKEN.shape, TOKEN.dtype)],
        idle=[token, low, *across, *pieces[:3]],
    )
    entering = exchanged(entering)
    pieces += [apart(piece, 1) for piece in pieces]
    attended, token = attend(
        meta, queries[0], bands + across, pieces, devices // 2, sink_keys[0], sink_values[0], [after]
    )
    [entering] = whole(
        scalars(copy_kernel), "copy", meta, [entering], [((chips, width, P_SIZE), jnp.bfloat16)], idle=[token]
    )
    other = apart(entering, 1)
    mixed = finish(meta, part, rates, reads, entering, other, low, got, pieces, local)
    return mixed[None], attended[None]


def solution(mesh):
    token = P("sess", "ctx", None)
    return jax.shard_map(
        shards,
        mesh=mesh,
        in_specs=(
            token,
            token,
            token,
            token,
            token,
            P(),
            P("sess", None, "ctx", None),
            P(),
            P("sess", None),
            P("sess", None),
            token,
            token,
            token,
            P("sess", None, "ctx", None),
            P("sess", None, "ctx", None),
            P("sess", None, None, None),
            P("sess", None, None, None),
        ),
        out_specs=(token, token),
        check_vma=False,
    )
```

```python
import math

import jax
import jax.numpy as jnp
from jax import lax
from jax.experimental import pallas as pl
from jax.experimental.pallas import tpu as pltpu
from jax.sharding import PartitionSpec as P

REACH = 4
SEQS = 3
SINKS = 4
H = 64
P_SIZE = 128
N = 64
G = 8
QH = 32
KVH = 4
HD = 128
WINDOW = 512
TOK = 128

HEADS_PER = H // G
PAIR = 2 * HEADS_PER
STEPS = H // PAIR
EXTRA = 16
BLOCK = 64
SPAN = WINDOW + BLOCK
COLUMNS = SPAN + 16
NEG = -1e30
TOKEN = jax.ShapeDtypeStruct((8, 128), jnp.float32)
SHORT = pl.CostEstimate(flops=1024, bytes_accessed=1024, transcendentals=0)
LONG = pl.CostEstimate(flops=1 << 35, bytes_accessed=1 << 20, transcendentals=0)


class Scalars:
    def __init__(self, ids):
        self.place, self.group = ids[0], ids[1]
        self.one = ids[2]
        self.two = ids[2] + ids[3]
        self.ids = ids
        self.even = self.place % 2 == 0

    def history(self, session):
        return self.ids[2 + SEQS + session]

    def home(self, number):
        return self.ids[2 + 2 * SEQS + number]

    def session_at(self, position):
        return (position >= self.one).astype(jnp.int32) + (position >= self.two).astype(jnp.int32)

    def start_of(self, session):
        return jnp.where(session == 0, 0, jnp.where(session == 1, self.one, self.two))

    def last_start(self):
        first = self.place * TOK
        return jnp.maximum(self.start_of(self.session_at(first + TOK - 1)) - first, 0)


def scalars(kernel, *options):
    def body(ids, *refs):
        kernel(*options, Scalars(ids), *refs)

    return body


def params(mib=60):
    return pltpu.CompilerParams(vmem_limit_bytes=mib * 1024 * 1024)


def running_rows(dl_ref):
    k = lax.broadcasted_iota(jnp.int32, (TOK, TOK), 0)
    u = lax.broadcasted_iota(jnp.int32, (TOK, TOK), 1)
    upto = (k <= u).astype(jnp.bfloat16)
    running = jnp.dot(dl_ref[...], upto, preferred_element_type=jnp.float32)
    return dl_ref[...].astype(jnp.float32), running


def summary_kernel(
    local, meta, x_ref, dl_ref, step_ref, write_ref, _, keep_ref, send_ref, coef_s, factor_s, write_s
):
    step = pl.program_id(0)

    @pl.when(step == 0)
    def _():
        rates, running = running_rows(dl_ref)
        steps = step_ref[...].astype(jnp.float32)
        r = meta.last_start()
        lane = lax.broadcasted_iota(jnp.int32, (H, TOK), 1)
        last = running[:, TOK - 1 :]
        base = jnp.sum(jnp.where(lane < r, rates, 0.0), axis=1, keepdims=True)
        coef_s[...] = jnp.where(lane >= r, jnp.exp(last - running) * steps, 0.0)
        factor_s[...] = jnp.broadcast_to(jnp.exp(last - base), (H, TOK))
        write_s[...] = write_ref[...].astype(jnp.float32).T

    even = meta.even
    coef = coef_s[pl.ds(pl.multiple_of(step * PAIR, PAIR), PAIR), :]
    factor = factor_s[pl.ds(pl.multiple_of(step * PAIR, PAIR), PAIR), :]
    writes = write_s[pl.ds(pl.multiple_of(step * 2 * N, 2 * N), 2 * N), :]

    def summary(k):
        group = k // HEADS_PER
        loading = (writes[group * N : (group + 1) * N] * coef[k : k + 1]).astype(jnp.bfloat16)
        return jnp.dot(
            loading, x_ref[:, k * P_SIZE : (k + 1) * P_SIZE], preferred_element_type=jnp.float32
        )

    for chip in range(PAIR // (2 * local)):
        low, high = 2 * local * chip, 2 * local * chip + local
        for k in range(local):
            first, second = summary(low + k), summary(high + k)
            rows = slice(k * N, (k + 1) * N)
            keep_ref[chip, rows, :] = jnp.where(even, first, second).astype(jnp.bfloat16)
            send_ref[chip, rows, :] = jnp.where(even, second, first).astype(jnp.bfloat16)
        first, second = factor[low : low + local], factor[high : high + local]
        keep_ref[chip, local * N :, :] = factor_rows(jnp.where(even, first, second))
        send_ref[chip, local * N :, :] = factor_rows(jnp.where(even, second, first))


def factor_rows(rows):
    high = rows.astype(jnp.bfloat16).astype(jnp.float32)
    parts = [high, rows - high]
    if EXTRA > 2 * rows.shape[0]:
        parts.append(jnp.zeros((EXTRA - 2 * rows.shape[0], TOK), jnp.float32))
    return jnp.concatenate(parts, axis=0).astype(jnp.bfloat16)


def factors_of(block, local):
    block = block.astype(jnp.float32)
    return block[:local] + block[local : 2 * local]


def summaries(meta, x, rates, steps, writes, local, idle):
    chips = H // (2 * local)
    rows = local * N + EXTRA
    shape = jax.ShapeDtypeStruct((chips, rows, P_SIZE), jnp.bfloat16)
    spec = pl.BlockSpec((PAIR // (2 * local), rows, P_SIZE), lambda i, *m: (i, 0, 0))
    return pl.pallas_call(
        scalars(summary_kernel, local),
        out_shape=[shape, shape],
        grid_spec=pltpu.PrefetchScalarGridSpec(
            num_scalar_prefetch=1,
            grid=(STEPS,),
            in_specs=[
                pl.BlockSpec((TOK, PAIR * P_SIZE), lambda i, *m: (0, i)),
                pl.BlockSpec((H, TOK), lambda i, *m: (0, 0)),
                pl.BlockSpec((H, TOK), lambda i, *m: (0, 0)),
                pl.BlockSpec((TOK, G * N), lambda i, *m: (0, 0)),
                pl.BlockSpec(memory_space=pl.ANY),
            ],
            out_specs=[spec, spec],
            scratch_shapes=[
                pltpu.VMEM((H, TOK), jnp.float32),
                pltpu.VMEM((H, TOK), jnp.float32),
                pltpu.VMEM((G * N, TOK), jnp.float32),
            ],
        ),
        compiler_params=params(),
        cost_estimate=LONG,
        name="summaries",
    )(meta, x, rates, steps, writes, idle)


def idle_spec(array):
    return pl.BlockSpec(memory_space=pl.ANY)


def whole(kernel, name, meta, arrays, shapes, idle=(), mib=16, scratch=()):
    def spec(shape):
        return pl.BlockSpec(shape, lambda i, *m: (0,) * len(shape))

    return pl.pallas_call(
        kernel,
        out_shape=[jax.ShapeDtypeStruct(s, t) for s, t in shapes],
        grid_spec=pltpu.PrefetchScalarGridSpec(
            num_scalar_prefetch=1,
            grid=(1,),
            in_specs=[spec(a.shape) for a in arrays] + [idle_spec(a) for a in idle],
            out_specs=[spec(s) for s, _ in shapes],
            scratch_shapes=scratch,
        ),
        compiler_params=params(mib),
        cost_estimate=LONG,
        name=name,
    )(meta, *arrays, *idle)


def pack_kernel(half, meta, keys_ref, values_ref, turn_keys_ref, turn_values_ref, home_ref, away_ref, band_ref):
    band_ref[0] = turn_keys_ref[...]
    band_ref[1] = turn_values_ref[...]
    rows = keys_ref.shape[1]
    upper = (meta.place >= half).astype(jnp.int32)
    for out_ref, first in ((home_ref, upper), (away_ref, 1 - upper)):
        for which, ref in enumerate((keys_ref, values_ref)):
            for s in range(2):
                for j in range(KVH):
                    place = ((which * 2 + s) * KVH + j) * rows
                    out_ref[0, place : place + rows, :] = ref[first + s, :, j * HD : (j + 1) * HD]


def restore_kernel(local, half, groups, meta, *refs):
    stored, (home_ref, away_ref, restored_ref) = refs[:groups], refs[-3:]
    for s in range(SEQS):
        slot = meta.home(meta.group * SEQS + s)
        source = (slot // SEQS - meta.group + groups) % groups
        for k in range(local):
            state = stored[0][slot % SEQS, k]
            for j in range(1, groups):
                state = jnp.where(source == j, stored[j][slot % SEQS, k], state)
            restored_ref[s, k * N : (k + 1) * N, :] = state.T
    upper = (meta.place >= half).astype(jnp.int32)
    home_ref[0] = restored_ref[upper + 1].astype(jnp.bfloat16)
    away_ref[0] = restored_ref[2 - upper].astype(jnp.bfloat16)


def copy_kernel(meta, array_ref, *refs):
    refs[-1][...] = array_ref[...]


def join_kernel(meta, first_ref, second_ref, *refs):
    out_ref = refs[-1]
    count = first_ref.shape[0]
    out_ref[:count] = first_ref[...]
    out_ref[count:] = second_ref[...]


def join_two_kernel(
    meta, first_ref, second_ref, first_state_ref, second_state_ref, key_value_ref, four_ref, *refs
):
    out_ref, two_ref = refs[-2:]
    rows = first_ref.shape[1]
    for i, (parcel, state) in enumerate(((first_ref, first_state_ref), (second_ref, second_state_ref))):
        out_ref[i, :rows, :] = parcel[0]
        out_ref[i, rows:, :] = state[0]
    two_ref[...] = jnp.where(meta.place // 2 % 2 == 0, key_value_ref[...], four_ref[...])


def far_place(distance, bits):
    place = distance * 0
    for k in range(bits):
        place = place + ((distance // (1 << k)) % 2) * (1 << (bits - 1 - k))
    return place


def combine_kernel(local, meta, keep_ref, got_ref, *refs):
    out_ref = refs[-1]
    even = meta.even
    second = (meta.place // 2 * 2 + 1) * TOK
    closes = meta.start_of(meta.session_at(second + TOK - 1)) >= second
    width = local * N
    for chip in range(keep_ref.shape[0]):
        keep = factors_of(keep_ref[chip, width:, :], local)
        got = factors_of(got_ref[chip, width:, :], local)
        f0, f1 = jnp.where(even, keep, got), jnp.where(even, got, keep)
        out_ref[chip, width:, :] = factor_rows(jnp.where(closes, f1, f0 * f1))
        carry = jnp.where(closes, 0.0, f1)
        for k in range(local):
            rows = slice(k * N, (k + 1) * N)
            keep = keep_ref[chip, rows, :].astype(jnp.float32)
            got = got_ref[chip, rows, :].astype(jnp.float32)
            s0, s1 = jnp.where(even, keep, got), jnp.where(even, got, keep)
            out_ref[chip, rows, :] = (carry[k : k + 1] * s0 + s1).astype(jnp.bfloat16)


def recurrence_kernel(local, meta, got_ref, restored_ref, *refs):
    out_ref, token_ref = refs[-2:]
    token_ref[...] = jnp.zeros_like(token_ref)
    width = local * N
    span = 2 * TOK
    state = [jnp.zeros((N, P_SIZE), jnp.float32) for _ in range(local)]
    for c in range(got_ref.shape[0]):
        first = c * span
        opening = meta.session_at(first)
        closing = meta.session_at(first + span - 1)
        opens = meta.start_of(opening) >= first
        closes = meta.start_of(closing) >= first
        factor = factors_of(got_ref[c, width:, :], local)
        for k in range(local):
            rows = slice(k * N, (k + 1) * N)
            entering = jnp.where(opens, restored_ref[opening, rows, :], state[k])
            out_ref[c, rows, :] = entering.astype(jnp.bfloat16)
            source = jnp.where(closes, restored_ref[closing, rows, :], state[k])
            state[k] = factor[k : k + 1] * source + got_ref[c, rows, :].astype(jnp.float32)


def intra_kernel(meta, skip, x_ref, dl_ref, step_ref, write_ref, read_ref, _, out_ref, token_ref, run_s, step_s):
    step = pl.program_id(0)

    @pl.when(step == 0)
    def _():
        _, running = running_rows(dl_ref)
        run_s[...] = running
        step_s[...] = step_ref[...].astype(jnp.float32)

    token_ref[...] = jnp.zeros_like(token_ref)
    heads = pl.ds(pl.multiple_of(step * PAIR, PAIR), PAIR)
    running = run_s[heads, :]
    sizes = step_s[heads, :]
    columns = running.T
    r = meta.last_start()
    t = lax.broadcasted_iota(jnp.int32, (TOK, TOK), 0)
    u = lax.broadcasted_iota(jnp.int32, (TOK, TOK), 1)
    causal = (u <= t) & ((u >= r) | (t < r))
    for group in range(2):
        part = slice(group * N, (group + 1) * N)
        products = lax.dot_general(
            read_ref[:, part], write_ref[:, part], (((1,), (1,)), ((), ())),
            preferred_element_type=jnp.float32,
        )
        products = jnp.where(causal, products, 0.0)
        for k in range(group * HEADS_PER, (group + 1) * HEADS_PER):
            difference = columns[:, k : k + 1] - running[k : k + 1]
            decay = jnp.exp(jnp.minimum(difference, 0.0))
            mixing = (products * decay * sizes[k : k + 1]).astype(jnp.bfloat16)
            place = slice(k * P_SIZE, (k + 1) * P_SIZE)
            x = x_ref[:, place]
            mixed = jnp.dot(mixing, x, preferred_element_type=jnp.float32)
            out_ref[:, place] = mixed + skip[step * PAIR + k] * x.astype(jnp.float32)


def intra(meta, skip, x, rates, steps, writes, reads, idle):
    return pl.pallas_call(
        scalars(intra_kernel),
        out_shape=[jax.ShapeDtypeStruct((TOK, H * P_SIZE), jnp.float32), TOKEN],
        grid_spec=pltpu.PrefetchScalarGridSpec(
            num_scalar_prefetch=2,
            grid=(STEPS,),
            in_specs=[
                pl.BlockSpec((TOK, PAIR * P_SIZE), lambda i, *m: (0, i)),
                pl.BlockSpec((H, TOK), lambda i, *m: (0, 0)),
                pl.BlockSpec((H, TOK), lambda i, *m: (0, 0)),
                pl.BlockSpec((TOK, 2 * N), lambda i, *m: (0, i)),
                pl.BlockSpec((TOK, 2 * N), lambda i, *m: (0, i)),
                pl.BlockSpec(memory_space=pl.ANY),
            ],
            out_specs=[
                pl.BlockSpec((TOK, PAIR * P_SIZE), lambda i, *m: (0, i)),
                pl.BlockSpec(TOKEN.shape, lambda i, *m: (0, 0)),
            ],
            scratch_shapes=[
                pltpu.VMEM((H, TOK), jnp.float32),
                pltpu.VMEM((H, TOK), jnp.float32),
            ],
        ),
        compiler_params=params(),
        cost_estimate=LONG,
        name="intra",
    )(meta, skip, x, rates, steps, writes, reads, idle)


def finish_kernel(
    local, meta, part_ref, dl_ref, read_ref, own_ref, other_ref, low_ref, high_ref, *refs,
):
    pieces, (out_ref, factor_s) = refs[:8], refs[-2:]
    bits = pieces[0].shape[0].bit_length() - 1
    step = pl.program_id(0)
    even = meta.even
    r = meta.last_start()
    first = meta.place // 2 * 2 * TOK
    second = first + TOK
    start = meta.start_of(meta.session_at(second + TOK - 1))
    closes = (start > first) & (start < second)
    opens = start == second
    width = local * N

    @pl.when(step == 0)
    def _():
        rates, running = running_rows(dl_ref)
        lane = lax.broadcasted_iota(jnp.int32, (H, TOK), 1)
        base = jnp.sum(jnp.where(lane < r, rates, 0.0), axis=1, keepdims=True)
        factor_s[...] = jnp.exp(jnp.minimum(running - jnp.where(lane >= r, base, 0.0), 0.0))

    factor = factor_s[pl.ds(pl.multiple_of(step * PAIR, PAIR), PAIR), :].T
    token = lax.broadcasted_iota(jnp.int32, (TOK, N), 0)
    resumed = (token >= r) & (r > 0)
    decays = [[factors_of(ref[chip, width:, :], local) for ref in (low_ref, high_ref)] for chip in range(own_ref.shape[0])]
    for group in range(2):
        reads = read_ref[:, group * N : (group + 1) * N].astype(jnp.float32)
        left = jnp.where(resumed, 0.0, reads)
        right = jnp.where(resumed, reads, 0.0)
        reads = jnp.concatenate([left, right], axis=1).astype(jnp.bfloat16)
        for k in range(group * HEADS_PER, (group + 1) * HEADS_PER):
            chip, half, head = k // (2 * local), k // local % 2, k % local
            rows = slice(head * N, (head + 1) * N)
            own = even if half == 0 else jnp.logical_not(even)
            entering = jnp.where(own, own_ref[chip, rows, :], other_ref[chip, rows, :]).astype(jnp.float32)
            distance = (step * own_ref.shape[0] + chip) ^ (meta.place // 2)
            far = far_place(distance // 4, bits)
            near, low_bit = distance % 2 == 0, distance // 2 % 2 == 0
            found = [piece[far, rows, :] for piece in pieces]
            found = [jnp.where(low_bit, found[i], found[i + 1]) for i in range(0, 8, 2)]
            restored = jnp.where(own, jnp.where(near, found[0], found[1]), jnp.where(near, found[2], found[3]))
            whole_state = restored.astype(jnp.float32)
            summary = (low_ref, high_ref)[half][chip, rows, :].astype(jnp.float32)
            middle = decays[chip][half][head : head + 1] * jnp.where(closes, whole_state, entering) + summary
            middle = jnp.where(opens, whole_state, middle)
            entering = jnp.where(even, entering, middle).astype(jnp.bfloat16)
            states = jnp.concatenate([entering, restored], axis=0)
            carried = jnp.dot(reads, states, preferred_element_type=jnp.float32)
            place = slice(k * P_SIZE, (k + 1) * P_SIZE)
            out_ref[:, place] = (part_ref[:, place] + factor[:, k : k + 1] * carried).astype(jnp.bfloat16)


def finish(meta, part, rates, reads, own, other, low, high, pieces, local):
    chips = PAIR // (2 * local)
    count, length, _ = pieces[0].shape
    resumed = pl.BlockSpec((count, local * N, P_SIZE), lambda i, *m: (0, length // (local * N) - 1, 0))
    states = pl.BlockSpec((chips, local * N, P_SIZE), lambda i, *m: (i, 0, 0))
    stretch = pl.BlockSpec((chips, local * N + EXTRA, P_SIZE), lambda i, *m: (i, 0, 0))
    return pl.pallas_call(
        scalars(finish_kernel, local),
        out_shape=jax.ShapeDtypeStruct((TOK, H * P_SIZE), jnp.bfloat16),
        grid_spec=pltpu.PrefetchScalarGridSpec(
            num_scalar_prefetch=1,
            grid=(STEPS,),
            in_specs=[
                pl.BlockSpec((TOK, PAIR * P_SIZE), lambda i, *m: (0, i)),
                pl.BlockSpec((H, TOK), lambda i, *m: (0, 0)),
                pl.BlockSpec((TOK, 2 * N), lambda i, *m: (0, i)),
                states,
                states,
                stretch,
                stretch,
            ]
            + [resumed] * 8,
            out_specs=pl.BlockSpec((TOK, PAIR * P_SIZE), lambda i, *m: (0, i)),
            scratch_shapes=[pltpu.VMEM((H, TOK), jnp.float32)],
        ),
        compiler_params=params(),
        cost_estimate=LONG,
        name="finish",
    )(meta, part, rates, reads, own, other, low, high, *pieces)


def attend_kernel(
    meta, q_ref, four, two, now, four_across, two_across, now_across, *refs,
):
    history_refs, (sk_ref, sv_ref), (out_ref, token_ref, key_s, value_s) = refs[:32], refs[32:34], refs[-4:]
    factor = 1.0 / math.sqrt(HD)
    first = meta.place * TOK
    r = meta.last_start()
    opening = meta.session_at(first)
    closing = meta.session_at(first + TOK - 1)
    even = meta.even

    def band(number, part):
        if number == 0:
            return four[part]
        if number == 1:
            return jnp.where(even, four_across[part], two_across[part])
        if number == 2:
            return two[part]
        if number == 3:
            return jnp.where(even, two_across[part], now_across[part])
        return now[part]

    token_ref[...] = jnp.zeros_like(token_ref)

    def sinks(ref, session):
        rows = ref[session].astype(jnp.float32)
        spare = jnp.zeros((COLUMNS - SPAN - SINKS, HD), jnp.float32)
        return jnp.concatenate([rows, spare], axis=0).astype(jnp.bfloat16)

    length = (REACH + 1) * TOK

    def one_session(session, key_refs, value_refs, resuming, needed):
        start = meta.start_of(session) - first + WINDOW
        oldest = start - WINDOW + jnp.maximum(SINKS + WINDOW - meta.history(session), 0)

        @pl.when(needed & (start > 0))
        def _():
            row = lax.broadcasted_iota(jnp.int32, (length, WINDOW), 0)
            chips, share, _ = key_refs[0].shape
            index = lax.broadcasted_iota(jnp.int32, (1, WINDOW), 1)
            piece, index = index // (WINDOW // 8), index % (WINDOW // 8)
            near, row_in = index // share, index % share
            far = far_place(near, chips.bit_length() - 1)
            device = meta.place ^ (piece // 4 + piece // 2 % 2 * 2 + piece % 2 * 4 + far * 8)
            place = device * share + row_in
            moved = (row == place + start - WINDOW).astype(jnp.bfloat16)
            part = (WINDOW // 8, HD)
            keys = jnp.concatenate([ref[...].reshape(part) for ref in key_refs], axis=0)
            values = jnp.concatenate([ref[...].reshape(part) for ref in value_refs], axis=0)
            history = jnp.dot(
                moved, jnp.concatenate([keys, values], axis=1), preferred_element_type=jnp.float32
            )
            for i in range(REACH + 1):
                rows = slice(i * TOK, (i + 1) * TOK)
                index = lax.broadcasted_iota(jnp.int32, (TOK, HD), 0) + i * TOK
                turn = index >= start
                key_s[rows, :] = jnp.where(
                    turn, band(i, 0).astype(jnp.float32), history[rows, :HD]
                ).astype(jnp.bfloat16)
                value_s[rows, :] = jnp.where(
                    turn, band(i, 1).astype(jnp.float32), history[rows, HD:]
                ).astype(jnp.bfloat16)

        @pl.when(needed & (start <= 0))
        def _():
            for i in range(REACH + 1):
                rows = slice(i * TOK, (i + 1) * TOK)
                key_s[rows, :] = band(i, 0)
                value_s[rows, :] = band(i, 1)

        for b in range(TOK // BLOCK):
            inside = (b * BLOCK + BLOCK > r) if resuming else (b * BLOCK < r)

            @pl.when(needed & inside)
            def _():
                rows = slice(b * BLOCK, b * BLOCK + SPAN)
                keys = jnp.concatenate([key_s[rows, :], sinks(sk_ref, session)], axis=0)
                values = jnp.concatenate([value_s[rows, :], sinks(sv_ref, session)], axis=0)
                tokens = slice(b * BLOCK, (b + 1) * BLOCK)
                queries = jnp.concatenate(
                    [q_ref[tokens, g * HD : (g + 1) * HD] for g in range(QH // KVH)], axis=0
                )
                scores = lax.dot_general(
                    keys, queries, (((1,), (1,)), ((), ())), preferred_element_type=jnp.float32
                )
                column = lax.broadcasted_iota(jnp.int32, (COLUMNS, 2 * BLOCK), 0)
                token = lax.broadcasted_iota(jnp.int32, (COLUMNS, 2 * BLOCK), 1) % BLOCK
                seen = (column > token) & (column <= token + WINDOW) & (column >= oldest - b * BLOCK)
                seen = (seen & (column < SPAN)) | ((column >= SPAN) & (column < SPAN + SINKS))
                bias = jnp.where(seen, 0.0, NEG)
                weights, shares = [], []
                for j in range(QH // KVH // 2):
                    score = scores[:, j * 2 * BLOCK : (j + 1) * 2 * BLOCK] * factor + bias
                    weight = jnp.exp(score - jnp.max(score, axis=0, keepdims=True))
                    shares.append(1.0 / jnp.sum(weight, axis=0, keepdims=True))
                    weights.append(weight.astype(jnp.bfloat16))
                mixed = lax.dot_general(
                    values, jnp.concatenate(weights, axis=1), (((0,), (0,)), ((), ())),
                    preferred_element_type=jnp.float32,
                )
                for j in range(QH // KVH // 2):
                    pair = (mixed[:, j * 2 * BLOCK : (j + 1) * 2 * BLOCK] * shares[j]).T
                    for g in range(2):
                        result = pair[g * BLOCK : (g + 1) * BLOCK]
                        lanes = slice((2 * j + g) * HD, (2 * j + g + 1) * HD)
                        if resuming:
                            index = lax.broadcasted_iota(jnp.int32, (BLOCK, HD), 0) + b * BLOCK
                            before = out_ref[tokens, lanes].astype(jnp.float32)
                            result = jnp.where(index >= r, result, before)
                        out_ref[tokens, lanes] = result.astype(jnp.bfloat16)

    one_session(opening, history_refs[0:8], history_refs[8:16], False, r > 0)
    one_session(closing, history_refs[16:24], history_refs[24:], True, r >= 0)


def attend(meta, queries, bands, pieces, half, sink_keys, sink_values, idle):
    chips = pieces[0].shape[0]
    share = WINDOW // (8 * chips)
    lanes = QH // KVH * HD

    def history_spec(which, last):
        def index(j, *m):
            known = Scalars(*m)
            session = known.session_at(known.place * TOK + (TOK - 1 if last else 0))
            session = session - (known.place >= half).astype(jnp.int32)
            return (0, (which * 2 + session) * KVH + j, 0)

        return pl.BlockSpec((chips, share, HD), index)

    pad = SEQS, SINKS, HD
    return pl.pallas_call(
        scalars(attend_kernel),
        out_shape=[jax.ShapeDtypeStruct((TOK, QH * HD), jnp.bfloat16), TOKEN],
        grid_spec=pltpu.PrefetchScalarGridSpec(
            num_scalar_prefetch=1,
            grid=(KVH,),
            in_specs=[pl.BlockSpec((TOK, lanes), lambda j, *m: (0, j))]
            + [pl.BlockSpec((2, TOK, HD), lambda j, *m: (0, 0, j))] * len(bands)
            + [history_spec(0, False)] * 8
            + [history_spec(1, False)] * 8
            + [history_spec(0, True)] * 8
            + [history_spec(1, True)] * 8
            + [pl.BlockSpec(pad, lambda j, *m: (0, 0, j))] * 2
            + [idle_spec(a) for a in idle],
            out_specs=[
                pl.BlockSpec((TOK, lanes), lambda j, *m: (0, j)),
                pl.BlockSpec(TOKEN.shape, lambda j, *m: (0, 0)),
            ],
            scratch_shapes=[
                pltpu.VMEM(((REACH + 1) * TOK, HD), jnp.bfloat16),
                pltpu.VMEM(((REACH + 1) * TOK, HD), jnp.bfloat16),
            ],
        ),
        compiler_params=params(),
        cost_estimate=SHORT,
        name="attend",
    )(
        meta, queries, *bands, *pieces, *pieces, *pieces, *pieces, sink_keys, sink_values, *idle
    )


def shifted(block, axis, distance):
    devices = range(lax.axis_size(axis))
    return lax.ppermute(block, axis, [(i - distance, i) for i in devices if i - distance in devices])


def shards(
    mamba_input,
    step_size,
    decay_log,
    state_write,
    state_read,
    skip_gain,
    saved_states,
    home_slot,
    turn_lengths,
    history_lengths,
    queries,
    turn_keys,
    turn_values,
    cache_keys,
    cache_values,
    sink_keys,
    sink_values,
):
    place = lax.axis_index("ctx")
    group = lax.axis_index("sess")
    groups = lax.axis_size("sess")
    devices = lax.axis_size("ctx")
    local = saved_states.shape[2]
    width = local * N
    chips = devices // 2
    same_core = [list(range(core, devices, 2)) for core in range(2)]
    meta = jnp.concatenate(
        [jnp.stack([place, group]).astype(jnp.int32), turn_lengths[0], history_lengths[0], home_slot]
    )
    x, rates, steps = mamba_input[0], decay_log[0].T, step_size[0].T
    writes, reads = state_write[0], state_read[0]
    def apart(block, distance):
        return lax.ppermute(block, "ctx", [(i, i ^ distance) for i in range(devices)])

    def exchanged(block):
        return lax.all_to_all(block, "ctx", 0, 0, axis_index_groups=same_core, tiled=True)

    stored = [saved_states[0]]
    for j in range(1, groups):
        route = [((i + j) % groups, i) for i in range(groups)]
        stored.append(lax.ppermute(saved_states[0], "sess", route))
    stored = [block.reshape(SEQS, local, P_SIZE, N) for block in stored]

    parcel = (1, 4 * KVH * cache_keys.shape[2], HD)
    band = (2, TOK, KVH * HD)
    near, away, key_value = whole(
        scalars(pack_kernel, devices // 2),
        "pack",
        meta,
        [cache_keys[0], cache_values[0], turn_keys[0], turn_values[0]],
        [(parcel, jnp.bfloat16), (parcel, jnp.bfloat16), (band, jnp.bfloat16)],
        mib=60,
    )
    moved = apart(away, devices // 2)
    four = shifted(key_value, "ctx", 4)

    keep, send = summaries(meta, x, rates, steps, writes, local, away)
    got = apart(send, 1)

    one = (1, width, P_SIZE)
    home, away, restored = whole(
        scalars(restore_kernel, local, devices // 2, groups),
        "restore",
        meta,
        stored,
        [(one, jnp.bfloat16), (one, jnp.bfloat16), ((SEQS, width, P_SIZE), jnp.float32)],
        idle=[send],
    )
    away = apart(away, devices // 2)
    near, two = whole(
        scalars(join_two_kernel),
        "join_two",
        meta,
        [near, moved, home, away, key_value, four],
        [((2, parcel[1] + width, HD), jnp.bfloat16), (band, jnp.bfloat16)],
        idle=[got],
    )
    distance = devices // 4
    while distance > 4:
        joined = (2 * near.shape[0], *near.shape[1:])
        [near] = whole(scalars(join_kernel), "join", meta, [near, apart(near, distance)], [(joined, jnp.bfloat16)])
        distance //= 2
    moved = apart(near, 4)
    two = apart(two, 2)
    beside = apart(near, 2)
    [chip] = whole(
        scalars(combine_kernel, local),
        "combine",
        meta,
        [keep, got],
        [(keep.shape, jnp.bfloat16)],
        idle=[near],
    )
    total = exchanged(chip)
    part, token = intra(meta, skip_gain, x, rates, steps, writes, reads, chip)
    pieces = [near, moved, beside, apart(moved, 2)]
    bands = [four, two, key_value]
    across = [apart(block, 1) for block in bands]
    low = apart(keep, 1)

    entering, after = whole(
        scalars(recurrence_kernel, local),
        "recurrence",
        meta,
        [total, restored],
        [((chips, width, P_SIZE), jnp.bfloat16), (TOKEN.shape, TOKEN.dtype)],
        idle=[token, low, *across, *pieces],
    )
    entering = exchanged(entering)
    pieces += [apart(piece, 1) for piece in pieces]
    attended, token = attend(
        meta, queries[0], bands + across, pieces, devices // 2, sink_keys[0], sink_values[0], [after]
    )
    [entering] = whole(
        scalars(copy_kernel), "copy", meta, [entering], [((chips, width, P_SIZE), jnp.bfloat16)], idle=[token]
    )
    other = apart(entering, 1)
    mixed = finish(meta, part, rates, reads, entering, other, low, got, pieces, local)
    return mixed[None], attended[None]


def solution(mesh):
    token = P("sess", "ctx", None)
    return jax.shard_map(
        shards,
        mesh=mesh,
        in_specs=(
            token,
            token,
            token,
            token,
            token,
            P(),
            P("sess", None, "ctx", None),
            P(),
            P("sess", None),
            P("sess", None),
            token,
            token,
            token,
            P("sess", None, "ctx", None),
            P("sess", None, "ctx", None),
            P("sess", None, None, None),
            P("sess", None, None, None),
        ),
        out_specs=(token, token),
        check_vma=False,
    )
```
